32 devices in a mesh: clip: 8 (over y, x, core), frame: 4 (over z).
Axes of the slice: x: 2, y: 2, z: 4, core: 2. Of those that a mesh axis runs over, the one named last changes fastest.
Arguments:
- inputs: bfloat16 [16, 16, 256, 768], P('clip', 'frame'), may hold values from -6 to 6
- cotangent: bfloat16 [16, 16, 256, 768], P('clip', 'frame'), may hold values from -6 to 6
- time_steps: int32 [16], P('clip'), may hold values from 0 to 999
- weight_index: int32 [16], P('clip'), may hold values from 0 to 7
- ada_weight: bfloat16 [768, 6912], P(('clip', 'frame')), may hold values from -0.4375 to 0.4375
- ada_bias: bfloat16 [6912], P(('clip', 'frame')), may hold values from -2.390625 to 2.390625
- space_qkv: bfloat16 [768, 2304], P(('clip', 'frame')), may hold values from -0.21875 to 0.21875
- space_out: bfloat16 [768, 768], P(('clip', 'frame')), may hold values from -0.875 to 0.875
- space_out_bias: bfloat16 [768], P(('clip', 'frame')), may hold values from -3 to 3
- time_qkv: bfloat16 [768, 2304], P(('clip', 'frame')), may hold values from -0.21875 to 0.21875
- time_out: bfloat16 [768, 768], P(('clip', 'frame')), may hold values from -0.4375 to 0.4375
- time_out_bias: bfloat16 [768], P(('clip', 'frame')), may hold values from -3 to 3
- up_weight: bfloat16 [768, 3072], P(('clip', 'frame')), may hold values from -0.21875 to 0.21875
- up_bias: bfloat16 [3072], P(('clip', 'frame')), may hold values from -3 to 3
- down_weight: bfloat16 [3072, 768], P(('clip', 'frame')), may hold values from -0.109375 to 0.109375
- down_bias: bfloat16 [768], P(('clip', 'frame')), may hold values from -3 to 3
Outputs:
- block_output: bfloat16 [16, 16, 256, 768], P('clip', 'frame')
- input_grad: float32 [16, 16, 256, 768], P('clip', 'frame')
- grad_ada_weight: float32 [768, 6912], P(('clip', 'frame'))
- grad_ada_bias: float32 [6912], P(('clip', 'frame'))
- grad_space_qkv: float32 [768, 2304], P(('clip', 'frame'))
- grad_space_out: float32 [768, 768], P(('clip', 'frame'))
- grad_space_out_bias: float32 [768], P(('clip', 'frame'))
- grad_time_qkv: float32 [768, 2304], P(('clip', 'frame'))
- grad_time_out: float32 [768, 768], P(('clip', 'frame'))
- grad_time_out_bias: float32 [768], P(('clip', 'frame'))
- grad_up_weight: float32 [768, 3072], P(('clip', 'frame'))
- grad_up_bias: float32 [3072], P(('clip', 'frame'))
- grad_down_weight: float32 [3072, 768], P(('clip', 'frame'))
- grad_down_bias: float32 [768], P(('clip', 'frame'))
The draws below stay inside these ranges and needn't reach their ends.
All inputs are finite; a program needn't handle non-finite values.
Results may differ from the reference program's by a relative error of at most 0.02.
Values may be sent and summed in bfloat16 or wider, within the bound.
A program may use at most 320 MiB of HBM per device.

```python
import math
import jax
import jax.numpy as jnp
import numpy as np
from jax import lax

D = 768
HEADS = 12
HEAD = 64
FF = 3072
P_SIZE = 256
FRAMES = 16
CLIPS = 16


def set_ends(drawn, own_key, smallest, high):
    index_at = [jax.random.randint(jax.random.fold_in(own_key, axis), (), 0, length) for axis, length in enumerate(drawn.shape)]
    longest = drawn.shape.index(max(drawn.shape))
    neighbour = index_at[:longest] + [(index_at[longest] + 1) % drawn.shape[longest]] + index_at[longest + 1:]
    return drawn.at[tuple(index_at)].set(smallest).at[tuple(neighbour)].set(high)


def levels(stream_key, shape, shards, least, largest):
    def one(dim, shards_of):
        heights = jax.random.uniform(jax.random.fold_in(jax.random.fold_in(stream_key, 6), dim), (shards_of,), jnp.float32, least / len(shards), largest / len(shards))
        return jnp.repeat(jnp.exp(heights), shape[dim] // shards_of).reshape((-1,) + (1,) * (len(shape) - dim - 1))

    gain = one(*shards[0])
    for cut in shards[1:]:
        gain = gain * one(*cut)
    return gain


def cumulative_ranks(number_of, slope):
    portions = [(1 << 20) // math.isqrt(rank ** slope) + 1 for rank in range(1, number_of + 1)]
    scale = 1 + sum(portions) // (1 << 30)
    return np.cumsum(np.array([max(1, weight // scale) for weight in portions]))


def ranked_ids(rng, shape, count, lean):
    grid = cumulative_ranks(count, lean)
    ticket = jax.random.randint(jax.random.fold_in(rng, 1), shape, 0, int(grid[count - 1]))
    rank = jnp.searchsorted(jnp.asarray(grid, jnp.int32), ticket, side="right")
    return jax.random.permutation(jax.random.fold_in(rng, 2), count)[rank].astype(jnp.int32)


def noise(key, dims, deviation, bound, shards=(), kind=jnp.bfloat16):
    loudness = levels(key, dims, shards, -0.22, 0.18) if shards else 1.0
    result = jax.random.normal(key, dims, jnp.float32) * deviation * loudness
    return jnp.minimum(jnp.maximum(result, -bound), bound).astype(kind)


def setup_inputs(seed: int = 0) -> dict:
    arg_keys = jax.random.split(jax.random.key(seed), 17)
    return {
        "inputs": noise(arg_keys[0], (CLIPS, FRAMES, P_SIZE, D), 1.0, 6.0, ((0, 8), (1, 4))),
        "cotangent": noise(arg_keys[1], (CLIPS, FRAMES, P_SIZE, D), 1.0, 6.0, ((0, 8), (1, 4))),
        "time_steps": set_ends(jax.random.randint(arg_keys[2], (CLIPS,), 0, 1000), jax.random.fold_in(arg_keys[2], 1), 0, 999).astype(jnp.int32),
        "weight_index": set_ends(ranked_ids(arg_keys[3], (CLIPS,), 8, 2), jax.random.fold_in(arg_keys[3], 3), 0, 7).astype(jnp.int32),
        "ada_weight": noise(arg_keys[4], (D, 9 * D), (D // 4) ** -0.5, 0.4375, ((0, 32),)),
        "ada_bias": noise(arg_keys[5], (9 * D,), 0.4, 2.390625, ((0, 32),)),
        "space_qkv": noise(arg_keys[6], (D, 3 * D), D ** -0.5, 0.21875, ((0, 32),)),
        "space_out": noise(arg_keys[7], (D, D), (D // 16) ** -0.5, 0.875, ((0, 32),)),
        "space_out_bias": noise(arg_keys[8], (D,), 0.5, 3.0, ((0, 32),)),
        "time_qkv": noise(arg_keys[9], (D, 3 * D), D ** -0.5, 0.21875, ((0, 32),)),
        "time_out": noise(arg_keys[10], (D, D), (D // 4) ** -0.5, 0.4375, ((0, 32),)),
        "time_out_bias": noise(arg_keys[11], (D,), 0.5, 3.0, ((0, 32),)),
        "up_weight": noise(arg_keys[12], (D, FF), D ** -0.5, 0.21875, ((0, 32),)),
        "up_bias": noise(arg_keys[13], (FF,), 0.5, 3.0, ((0, 32),)),
        "down_weight": noise(arg_keys[14], (FF, D), FF ** -0.5, 0.109375, ((0, 32),)),
        "down_bias": noise(arg_keys[15], (D,), 0.5, 3.0, ((0, 32),)),
    }


@jax.custom_vjp
def low(v):
    return lax.optimization_barrier(v.astype(jnp.bfloat16)).astype(jnp.float32)

@jax.custom_vjp
def low_back(v):
    return v

def low_keep(v):
    return (low(v), None)

def low_pass(kept, grad):
    return (grad,)

def back_keep(v):
    return (v, None)

def back_low(kept, grad):
    return (low(grad),)
low.defvjp(low_keep, low_pass)
low_back.defvjp(back_keep, back_low)
highest = lax.Precision.HIGHEST

def embed_steps(time_steps, model_width):
    half_width = model_width // 2
    frequencies = jnp.exp(-math.log(10000.0) * jnp.arange(half_width, dtype=jnp.float32) / half_width)
    angles = time_steps.astype(jnp.float32)[:, None] * frequencies[None, :]
    return jnp.concatenate([jnp.cos(angles), jnp.sin(angles)], axis=1)

def modulated_norm(values, scaling, offset):
    centred = values - lax.optimization_barrier(jnp.mean(values, axis=-1, keepdims=True))
    variance = lax.optimization_barrier(jnp.mean(centred * centred, axis=-1, keepdims=True))
    return centred * lax.rsqrt(variance + 1e-06) * (1.0 + scaling) + offset

def gelu_tanh(values):
    return jax.nn.gelu(values, approximate=True)

def attend_ref(queries, keys_all, values_all):
    scores = low_back(jnp.einsum('abihe,abjhe->abhij', queries, keys_all, precision=highest) * 0.125)
    row_peak = lax.optimization_barrier(jnp.max(scores, axis=-1, keepdims=True))
    terms = jnp.exp(scores - row_peak)
    attention = low(terms / lax.optimization_barrier(jnp.sum(terms, axis=-1, keepdims=True)))
    return jnp.einsum('abhij,abjhe->abihe', attention, values_all, precision=highest)

def block(clip_in, clip_mod, w_sqkv, w_sout, b_sout, w_tqkv, w_tout, b_tout, w_up, b_up, w_down, b_down):
    pieces = [clip_mod[number * D:(number + 1) * D] for number in range(9)]
    hidden_one = low(modulated_norm(clip_in, pieces[1], pieces[0]))
    qkv_one = low(low_back(jnp.einsum('fpd,dk->fpk', hidden_one, w_sqkv, precision=highest)))
    split_one = qkv_one.reshape(1, FRAMES, P_SIZE, 3, HEADS, HEAD)
    mixed_one = attend_ref(split_one[:, :, :, 0], split_one[:, :, :, 1], split_one[:, :, :, 2])
    flat_one = low(low_back(mixed_one.reshape(FRAMES, P_SIZE, D)))
    branch_one = low_back(jnp.einsum('fpd,de->fpe', flat_one, w_sout, precision=highest) + b_sout)
    after_one = clip_in + pieces[2] * branch_one
    hidden_two = low(low_back(modulated_norm(after_one, pieces[4], pieces[3])))
    qkv_two = low(low_back(jnp.einsum('fpd,dk->fpk', hidden_two, w_tqkv, precision=highest)))
    split_two = jnp.swapaxes(qkv_two.reshape(1, FRAMES, P_SIZE, 3, HEADS, HEAD), 1, 2)
    mixed_two = jnp.swapaxes(attend_ref(split_two[:, :, :, 0], split_two[:, :, :, 1], split_two[:, :, :, 2]), 1, 2)
    flat_two = low(low_back(mixed_two.reshape(FRAMES, P_SIZE, D)))
    branch_two = low_back(jnp.einsum('fpd,de->fpe', flat_two, w_tout, precision=highest) + b_tout)
    after_two = after_one + pieces[5] * branch_two
    hidden_three = low(modulated_norm(after_two, pieces[7], pieces[6]))
    upper = low_back(jnp.einsum('fpd,dk->fpk', hidden_three, w_up, precision=highest) + b_up)
    activated = low(gelu_tanh(upper))
    branch_three = low_back(jnp.einsum('fpk,kd->fpd', activated, w_down, precision=highest) + b_down)
    return after_two + pieces[8] * branch_three

def reference(inputs, cotangent, time_steps, weight_index, ada_weight, ada_bias, space_qkv, space_out, space_out_bias, time_qkv, time_out, time_out_bias, up_weight, up_bias, down_weight, down_bias):
    silu_embed = jax.nn.silu(embed_steps(time_steps, D))
    loss_scale = jnp.exp2(weight_index.astype(jnp.float32) * 0.5 - 1.0)

    def forward(values, w_ada, b_ada, w_sqkv, w_sout, b_sout, w_tqkv, w_tout, b_tout, w_up, b_up, w_down, b_down):
        modulation = jnp.dot(low(silu_embed), w_ada, precision=highest) + b_ada

        def one_clip(carry, pair):
            return (carry, block(pair[0], pair[1], w_sqkv, w_sout, b_sout, w_tqkv, w_tout, b_tout, w_up, b_up, w_down, b_down))
        final, outputs = lax.scan(jax.checkpoint(one_clip), jnp.zeros((), jnp.float32), (values, modulation))
        return outputs
    outputs, pullback = jax.vjp(forward, inputs.astype(jnp.float32), ada_weight.astype(jnp.float32), ada_bias.astype(jnp.float32), space_qkv.astype(jnp.float32), space_out.astype(jnp.float32), space_out_bias.astype(jnp.float32), time_qkv.astype(jnp.float32), time_out.astype(jnp.float32), time_out_bias.astype(jnp.float32), up_weight.astype(jnp.float32), up_bias.astype(jnp.float32), down_weight.astype(jnp.float32), down_bias.astype(jnp.float32))
    grads = pullback(cotangent.astype(jnp.float32) * loss_scale[:, None, None, None])
    return (outputs.astype(jnp.bfloat16), grads[0], grads[1], grads[2], grads[3], grads[4], grads[5], grads[6], grads[7], grads[8], grads[9], grads[10], grads[11], grads[12])
```

```python
import functools
import math

import jax
import jax.numpy as jnp
from jax import lax
from jax.experimental import pallas as pl
from jax.experimental.pallas import tpu as pltpu
from jax.sharding import PartitionSpec as P

HEADS = 12
HEAD = 64
PAIRS = HEADS // 2
ROWS = 32
GELU_C = math.sqrt(2.0 / math.pi)
GELU_A = 0.044715
VMEM_LIMIT = 58 << 20

f32 = jnp.float32
bf16 = jnp.bfloat16
highest = lax.Precision.HIGHEST
MESH = pl.DeviceIdType.MESH
VMEM = pltpu.VMEM
DMA = pltpu.SemaphoreType.DMA


def embed_steps(time_steps, model_width):
    half_width = model_width // 2
    frequencies = jnp.exp(
        -math.log(10000.0) * jnp.arange(half_width, dtype=f32) / half_width
    )
    angles = time_steps.astype(f32)[:, None] * frequencies[None, :]
    return jnp.concatenate([jnp.cos(angles), jnp.sin(angles)], axis=1)


def dot(left, right, left_dim, right_dim):
    return lax.dot_general(
        left, right, (((left_dim,), (right_dim,)), ((), ())), preferred_element_type=f32
    )


def flip(index, mask):
    bit = 1
    while bit <= mask:
        if mask & bit:
            index = index + bit * (1 - 2 * ((index // bit) % 2))
        bit *= 2
    return index


def span(masks):
    out = [0]
    for mask in masks:
        out = out + [entry ^ mask for entry in out]
    return out


def frame_masks(frames):
    masks, bit = [], 1
    while bit < frames:
        masks.append(bit)
        bit *= 2
    if len(masks) > 1:
        masks = [frames - 1] + masks[:-1]
    return masks


def clip_tail_masks(clips):
    masks, bit = [], 2
    while bit < clips:
        masks.append(bit)
        bit *= 2
    return masks


def greet(clips, frames):
    clip, frame = lax.axis_index("clip"), lax.axis_index("frame")
    barrier = pltpu.get_barrier_semaphore()
    for step in range(1, clips):
        pl.semaphore_signal(
            barrier, inc=1, device_id={"clip": lax.rem(clip + step, clips)}, device_id_type=MESH
        )
    for step in range(1, frames):
        pl.semaphore_signal(
            barrier, inc=1, device_id={"frame": lax.rem(frame + step, frames)}, device_id_type=MESH
        )
    pl.semaphore_wait(barrier, clips + frames - 2)


def spread(axis, size, source_of, target, send_sems, recv_sems):
    me = lax.axis_index(axis)
    copies = []
    for step in range(1, size):
        peer = lax.rem(me + step, size)
        copy = pltpu.make_async_remote_copy(
            src_ref=source_of(peer),
            dst_ref=target.at[me],
            send_sem=send_sems.at[step - 1],
            recv_sem=recv_sems.at[step - 1],
            device_id={axis: peer},
            device_id_type=MESH,
        )
        copy.start()
        copies.append(copy)
    return copies


def start_kernel(
    clips, frames, clip_count,
    x_ref, cotangent, sh_c, sh_b, sh_u, sh_d, embed, select, ada, bias,
    w_c, w_b, w_u, w_d, mod, chosen, totals, hidden_out, qkv_out, mixed_out, branch_out,
    after_first, after_later, cot_first,
    v_c, z_c, z_b, z_u, z_d, st_w, b_c, b_b, b_u, b_d,
    embeds, parts, terms, arrived, held, lined, hidden, qkv, mixed, branch, after,
    zs, zr, cs, cr, xs, xr, ls, es, er, ps, pr, fs, fr, ts, tr, hs, hr, os, ws,
):
    clip, frame = lax.axis_index("clip"), lax.axis_index("frame")
    shards_in = (sh_c, sh_b, sh_u, sh_d)
    zoned = (z_c, z_b, z_u, z_d)
    blocks = (b_c, b_b, b_u, b_d)
    wholes = (v_c, w_b, w_u, w_d)
    width = mod.shape[1]
    frame_count, tokens = x_ref.shape[1], x_ref.shape[2]
    part = tokens // frames
    greet(clips, frames)
    masks = frame_masks(frames)
    sends = []
    stage = {}

    def frame_step(group, step):
        number = (1 << step) - 1
        copies = []
        for offset in span(masks[:step]):
            slot = flip(frame, offset)
            source = shards_in[group] if offset == 0 else zoned[group].at[slot]
            copy = pltpu.make_async_remote_copy(
                src_ref=source,
                dst_ref=zoned[group].at[slot],
                send_sem=zs.at[group, number],
                recv_sem=zr.at[group, number],
                device_id={"frame": flip(frame, masks[step])},
                device_id_type=MESH,
            )
            copy.start()
            copies.append(copy)
            number += 1
        sends.extend(copies)
        stage[group] = copies

    def frame_rest(group):
        for step in range(1, len(masks)):
            for copy in stage[group]:
                copy.wait_recv()
            frame_step(group, step)

    tail = clip_tail_masks(clips)
    steps = len(tail)
    orders = (tail, tail[::-1])
    moving = {}

    def block_send(group, half, step, position, offset):
        whole = wholes[group]
        block_rows = whole.shape[0] // clips
        columns = whole.shape[1] // 2
        rows = pl.ds(pl.multiple_of(flip(clip, offset) * block_rows, block_rows), block_rows)
        lanes = pl.ds(half * columns, columns)
        target = whole.at[rows, lanes]
        number = (1 << step) - 1 + position
        copy = pltpu.make_async_remote_copy(
            src_ref=blocks[group].at[:, lanes] if offset == 0 else target,
            dst_ref=target,
            send_sem=xs.at[group, half, number],
            recv_sem=xr.at[group, half, number],
            device_id={"clip": flip(clip, orders[half][step])},
            device_id_type=MESH,
        )
        copy.start()
        moving[group, half, number] = copy

    core_copies = {group: [] for group in range(4)}

    def core_send(group, offset):
        whole = wholes[group]
        block_rows = whole.shape[0] // clips
        rows = pl.ds(pl.multiple_of(flip(clip, offset) * block_rows, block_rows), block_rows)
        number = len(core_copies[group])
        copy = pltpu.make_async_remote_copy(
            src_ref=blocks[group] if offset == 0 else whole.at[rows, :],
            dst_ref=whole.at[rows, :],
            send_sem=cs.at[group, number],
            recv_sem=cr.at[group, number],
            device_id={"clip": flip(clip, 1)},
            device_id_type=MESH,
        )
        copy.start()
        core_copies[group].append(copy)

    local_copies = []

    def block_ready(group):
        for copy in stage[group]:
            copy.wait_recv()
        rows, columns = shards_in[group].shape
        block_rows = frames * rows
        if rows % 16:
            for slot in range(frames):
                st_w[slot * rows : (slot + 1) * rows, :columns] = zoned[group][slot].astype(f32)
            blocks[group][...] = st_w[:block_rows, :columns].astype(bf16)
        else:
            for slot in range(frames):
                blocks[group][slot * rows : (slot + 1) * rows, :] = zoned[group][slot]
        for step in range(steps):
            for half in range(2):
                block_send(group, half, step, 0, 0)
        core_send(group, 0)
        place = pl.ds(pl.multiple_of(clip * block_rows, block_rows), block_rows)
        keep = pltpu.make_async_copy(blocks[group], wholes[group].at[place, :], ls.at[group])
        keep.start()
        local_copies.append(keep)

    def block_forward(group):
        for step in range(1, steps):
            for half in range(2):
                for position in range(1 << (step - 1), 1 << step):
                    moving[group, half, position - 1].wait_recv()
                for later in range(step, steps):
                    for position, offset in enumerate(span(orders[half][:later])):
                        if (1 << (step - 1)) <= position < (1 << step):
                            block_send(group, half, later, position, offset)

    def block_finish(group):
        last = (1 << (steps - 1)) - 1
        for half in range(2):
            for number in range(last, (1 << steps) - 1):
                moving[group, half, number].wait_recv()
        for offset in span(tail)[1:]:
            core_send(group, offset)

    def core_finish(group):
        for copy in core_copies[group]:
            copy.wait_recv()

    for group in range(4):
        frame_step(group, 0)
    own = spread("clip", clips, lambda peer: embed, embeds, es, er)
    sends.extend(own)
    embeds[clip] = embed[...]
    for group in range(4):
        zoned[group][frame] = shards_in[group][...]
    for copy in own:
        copy.wait_recv()
    picked = dot(embeds[...].reshape(clips * 16, width), select[...], 1, 0).astype(bf16)
    chosen[...] = picked
    parts[...] = dot(picked, ada[...], 1, 0)
    for peer in range(clips):
        for local in range(clip_count):
            row = peer * 16 + local
            for piece in range(9):
                terms[peer, local * 9 + piece : local * 9 + piece + 1, :] = (
                    parts[row : row + 1, piece * width : (piece + 1) * width]
                    + bias[piece : piece + 1, :]
                )
        base = clip_count * 9
        terms[peer, base : base + 7, :] = bias[9:16, :]
        if base + 7 < ROWS:
            terms[peer, base + 7 : ROWS, :] = jnp.zeros((ROWS - base - 7, width), f32)
    own = spread("clip", clips, lambda peer: terms.at[peer], arrived, ps, pr)
    sends.extend(own)
    arrived[clip] = terms[clip]
    frame_rest(0)
    for copy in own:
        copy.wait_recv()
    total = arrived[0]
    for peer in range(1, clips):
        total = total + arrived[peer]
    held[...] = total
    own = spread("frame", frames, lambda peer: held, lined, fs, fr)
    sends.extend(own)
    lined[frame] = total
    block_ready(0)
    for group in range(1, 4):
        frame_rest(group)

    cot_copies = []
    for step in range(1, frames):
        peer = lax.rem(frame + step, frames)
        copy = pltpu.make_async_remote_copy(
            src_ref=cotangent.at[0, :, pl.ds(pl.multiple_of(peer * part, part), part), :],
            dst_ref=cot_first.at[frame],
            send_sem=ts.at[step - 1],
            recv_sem=tr.at[step - 1],
            device_id={"frame": peer},
            device_id_type=MESH,
        )
        copy.start()
        cot_copies.append(copy)
    keep = pltpu.make_async_copy(
        cotangent.at[0, :, pl.ds(pl.multiple_of(frame * part, part), part), :],
        cot_first.at[frame],
        ls.at[4],
    )
    keep.start()
    local_copies.append(keep)

    for copy in own:
        copy.wait_recv()
    total = lined[0]
    for peer in range(1, frames):
        total = total + lined[peer]
    mod[...] = total
    block_forward(0)
    for group in range(1, 4):
        block_ready(group)
    block_finish(0)
    core_finish(0)
    local_copies[0].wait()

    keep = pltpu.make_async_copy(v_c, w_c, ls.at[5])
    keep.start()
    local_copies.append(keep)

    def after_copy(f, step):
        peer = lax.rem(frame + step, frames)
        return pltpu.make_async_remote_copy(
            src_ref=after.at[f, pl.ds(pl.multiple_of(peer * part, part), part), :],
            dst_ref=after_first.at[frame, f],
            send_sem=hs.at[f, step - 1],
            recv_sem=hr.at[f, step - 1],
            device_id={"frame": peer},
            device_id_type=MESH,
        )

    def own_after(f):
        return pltpu.make_async_copy(
            after.at[f, pl.ds(pl.multiple_of(frame * part, part), part), :],
            after_first.at[frame, f],
            os.at[f],
        )

    def later_after(f):
        return pltpu.make_async_copy(after.at[f], after_later.at[f - frame_count], os.at[f])

    kept = ((hidden, hidden_out), (qkv, qkv_out), (mixed, mixed_out), (branch, branch_out))

    def write_back(f):
        return [
            pltpu.make_async_copy(source.at[f], target.at[f], ws.at[number, f])
            for number, (source, target) in enumerate(kept)
        ]

    for local in range(clip_count):
        row = local * 9

        def one_frame(index, carry):
            f = local * frame_count + index
            values = x_ref[local, index].astype(f32)
            norm, _ = normed(values)
            scaled = norm * (1.0 + mod[row + 1 : row + 2, :]) + mod[row : row + 1, :]
            lowered = scaled.astype(bf16)
            hidden[f] = lowered
            qkv[f] = dot(lowered, v_c[:, : 3 * width], 1, 0).astype(bf16)
            attend(qkv.at[f], mixed.at[f], totals.at[f], width, None)
            grown = dot(mixed[f], v_c[:, 3 * width :], 1, 0) + mod[18:19, :]
            branch[f] = grown.astype(bf16)
            after[f] = (values + mod[row + 2 : row + 3, :] * grown).astype(bf16)
            if local == 0:
                for step in range(1, frames):
                    after_copy(f, step).start()
                own_after(f).start()
            else:
                later_after(f).start()
            for copy in write_back(f):
                copy.start()
            return carry

        lax.fori_loop(0, frame_count, one_frame, 0)
        if local == 0:
            block_forward(1)
    for group in range(2, 4):
        block_forward(group)
    for group in range(1, 4):
        block_finish(group)
    for group in range(1, 4):
        core_finish(group)

    def settle(f, carry):
        for step in range(1, frames):
            copy = after_copy(f, step)
            copy.wait_recv()
            copy.wait_send()
        own_after(f).wait()
        return carry

    lax.fori_loop(0, frame_count, settle, 0)

    def settle_later(f, carry):
        later_after(f).wait()
        return carry

    lax.fori_loop(frame_count, clip_count * frame_count, settle_later, 0)

    def settle_kept(f, carry):
        for copy in write_back(f):
            copy.wait()
        return carry

    lax.fori_loop(0, clip_count * frame_count, settle_kept, 0)
    for copy in cot_copies:
        copy.wait_recv()
        copy.wait_send()
    for copy in local_copies[1:]:
        copy.wait()
    for copy in moving.values():
        copy.wait_send()
    for group in range(4):
        for copy in core_copies[group]:
            copy.wait_send()
    for copy in sends:
        copy.wait_send()


def start_call(
    clips, frames, inputs, cotangent, sh_c, sh_b, sh_u, sh_d, embed, select, ada, bias
):
    clip_count, frame_count, tokens, width = inputs.shape
    rows, columns = sh_c.shape
    rows_d = sh_d.shape[0]
    block = frames * rows
    block_d = frames * rows_d
    peers = max(clips // 2 - 1, 1)
    total = clip_count * frame_count
    part = tokens // frames
    whole = jax.ShapeDtypeStruct((clips * block, columns), bf16)
    vmem = pl.BlockSpec(memory_space=VMEM)
    hbm = pl.BlockSpec(memory_space=pl.ANY)
    zoned = lambda height, lanes: VMEM((frames, height, lanes), bf16)
    saved = lambda lanes: jax.ShapeDtypeStruct((total, tokens, lanes), bf16)
    lent = lambda lanes: VMEM((total, tokens, lanes), bf16)
    traded = jax.ShapeDtypeStruct((frames, frame_count, part, width), bf16)
    return pl.pallas_call(
        functools.partial(start_kernel, clips, frames, clip_count),
        out_shape=(
            whole, whole, whole,
            jax.ShapeDtypeStruct((clips * block_d, width), bf16),
            jax.ShapeDtypeStruct((ROWS, width), f32),
            jax.ShapeDtypeStruct((clips * 16, 128), bf16),
            jax.ShapeDtypeStruct((total, 16, tokens), f32),
            saved(width), saved(3 * width), saved(width), saved(width),
            traded,
            jax.ShapeDtypeStruct(((clip_count - 1) * frame_count, tokens, width), bf16),
            traded,
        ),
        in_specs=[vmem, hbm] + [vmem] * 8,
        out_specs=(hbm, hbm, hbm, hbm, vmem, vmem, vmem) + (hbm,) * 7,
        scratch_shapes=[
            VMEM((clips * block, columns), bf16),
            zoned(rows, columns), zoned(rows, columns), zoned(rows, columns), zoned(rows_d, width),
            VMEM((max(block, block_d), columns), f32),
            VMEM((block, columns), bf16),
            VMEM((block, columns), bf16),
            VMEM((block, columns), bf16),
            VMEM((block_d, width), bf16),
            VMEM((clips, 16, width), bf16),
            VMEM((clips * 16, 9 * width), f32),
            VMEM((clips, ROWS, width), f32),
            VMEM((clips, ROWS, width), f32),
            VMEM((ROWS, width), f32),
            VMEM((frames, ROWS, width), f32),
            lent(width), lent(3 * width), lent(width), lent(width), lent(width),
            DMA((4, frames - 1)), DMA((4, frames - 1)),
            DMA((4, clips // 2)), DMA((4, clips // 2)),
            DMA((4, 2, peers)), DMA((4, 2, peers)),
            DMA((6,)),
            DMA((clips - 1,)), DMA((clips - 1,)),
            DMA((clips - 1,)), DMA((clips - 1,)),
            DMA((frames - 1,)), DMA((frames - 1,)),
            DMA((frames - 1,)), DMA((frames - 1,)),
            DMA((frame_count, frames - 1)), DMA((frame_count, frames - 1)),
            DMA((total,)),
            DMA((4, total)),
        ],
        compiler_params=pltpu.CompilerParams(
            collective_id=0, has_side_effects=True, vmem_limit_bytes=VMEM_LIMIT
        ),
    )(inputs, cotangent, sh_c, sh_b, sh_u, sh_d, embed, select, ada, bias)


def end_kernel(clips, frames, small, out, lined, held, fs, fr, ps, pr):
    clip, frame = lax.axis_index("clip"), lax.axis_index("frame")
    greet(clips, frames)
    first = spread("frame", frames, lambda peer: small, lined, fs, fr)
    lined[frame] = small[...]
    for copy in first:
        copy.wait_recv()
    total = lined[0]
    for peer in range(1, frames):
        total = total + lined[peer]
    held[...] = total
    second = spread("clip", clips, lambda peer: held, out, ps, pr)
    out[clip] = total
    for copy in second:
        copy.wait_recv()
    for copy in first + second:
        copy.wait_send()


def end_call(clips, frames, small):
    vmem = pl.BlockSpec(memory_space=VMEM)
    return pl.pallas_call(
        functools.partial(end_kernel, clips, frames),
        out_shape=jax.ShapeDtypeStruct((clips,) + small.shape, f32),
        in_specs=[vmem],
        out_specs=vmem,
        scratch_shapes=[
            VMEM((frames,) + small.shape, f32),
            VMEM(small.shape, f32),
            DMA((frames - 1,)), DMA((frames - 1,)),
            DMA((clips - 1,)), DMA((clips - 1,)),
        ],
        compiler_params=pltpu.CompilerParams(collective_id=1, has_side_effects=True),
    )(small)


def normed(values):
    centred = values - jnp.mean(values, axis=-1, keepdims=True)
    scale = lax.rsqrt(jnp.mean(centred * centred, axis=-1, keepdims=True) + 1e-06)
    return centred * scale, scale


def norm_back(grad, scaled, norm, scale):
    inner = grad * scaled
    return scale * (
        inner
        - jnp.mean(inner, axis=-1, keepdims=True)
        - norm * jnp.mean(inner * norm, axis=-1, keepdims=True)
    )


def column_sum(values):
    return jnp.sum(values, axis=0, keepdims=True)


def attend(qkv, mixed, totals, width, mask):
    tokens = qkv.shape[0]
    low = lax.broadcasted_iota(jnp.int32, (tokens, 128), 1) < HEAD
    for pair in range(PAIRS):
        at = pair * 128
        queries = qkv[:, at : at + 128] * bf16(0.125)
        keys = qkv[:, width + at : width + at + 128]
        values = qkv[:, 2 * width + at : 2 * width + at + 128]
        halves = []
        for half in range(2):
            own = jnp.where(low if half == 0 else ~low, queries, bf16(0))
            scores = dot(keys, own, 1, 1)
            if mask is not None:
                scores = scores + mask[...]
            peak = jnp.max(scores, axis=0, keepdims=True)
            terms = jnp.exp(scores - peak)
            total = jnp.sum(terms, axis=0, keepdims=True)
            weights = (terms * (1.0 / total)).astype(bf16)
            totals[2 * pair + half : 2 * pair + half + 1, :] = peak + jnp.log(total)
            halves.append(dot(weights, values, 0, 0))
        mixed[:, at : at + 128] = jnp.where(low, halves[0], halves[1]).astype(bf16)


def attend_back(qkv, grad_mixed, totals, grad_qkv, width, mask):
    tokens = qkv.shape[0]
    low = lax.broadcasted_iota(jnp.int32, (tokens, 128), 1) < HEAD
    for pair in range(PAIRS):
        at = pair * 128
        queries = qkv[:, at : at + 128]
        keys = qkv[:, width + at : width + at + 128]
        values = qkv[:, 2 * width + at : 2 * width + at + 128]
        grads = grad_mixed[:, at : at + 128]
        halves = []
        for half in range(2):
            pick = low if half == 0 else ~low
            own = jnp.where(pick, queries * bf16(0.125), bf16(0))
            own_grads = jnp.where(pick, grads, bf16(0))
            scores = dot(keys, own, 1, 1)
            if mask is not None:
                scores = scores + mask[...]
            weights = jnp.exp(scores - totals[2 * pair + half : 2 * pair + half + 1, :])
            grad_weights = dot(values, own_grads, 1, 1)
            inner = jnp.sum(weights * grad_weights, axis=0, keepdims=True)
            grad_scores = (weights * (grad_weights - inner)).astype(bf16)
            halves.append(
                (
                    dot(grad_scores, keys, 0, 0),
                    dot(grad_scores, queries, 1, 0),
                    dot(weights.astype(bf16), grads, 1, 0),
                )
            )
        for part, factor in ((0, 0.125), (1, 0.125), (2, 1.0)):
            joined = jnp.where(low, halves[0][part], halves[1][part]) * factor
            start = part * width + at
            grad_qkv[:, start : start + 128] = joined.astype(bf16)


def full(shape):
    return pl.BlockSpec(shape, lambda *_: (0,) * len(shape), pipeline_mode=pl.Buffered(1))


def middle_kernel(
    clip, after_ref, cot_ref, loss, mod, w_b, w_u, w_d,
    out_ref, grad_ref, act_ref, gup_ref, h3_ref, gb3_ref, mixed_ref, gb2_ref, h2_ref, gqkv_ref, sums,
    qkv, totals, mask, gmix,
):
    width = after_ref.shape[-1]
    group = after_ref.shape[2]
    tokens = after_ref.shape[0] * after_ref.shape[1] * group
    row = clip * 9
    piece = lambda number: mod[row + number : row + number + 1, :]

    @pl.when(pl.program_id(0) == 0)
    def _():
        sums[...] = jnp.zeros_like(sums)
        first = lax.broadcasted_iota(jnp.int32, (tokens, tokens), 0)
        second = lax.broadcasted_iota(jnp.int32, (tokens, tokens), 1)
        mask[...] = jnp.where(lax.rem(first, group) == lax.rem(second, group), 0.0, -1e30)

    def add(place, values):
        sums[place : place + 1, :] += values

    after = after_ref[...].reshape(tokens, width).astype(f32)
    norm, scale = normed(after)
    hidden = (norm * (1.0 + piece(4)) + piece(3)).astype(bf16)
    h2_ref[...] = hidden
    qkv[...] = dot(hidden, w_b[:, : 3 * width], 1, 0).astype(bf16)
    attend(qkv, mixed_ref, totals, width, mask)
    branch_two = dot(mixed_ref[...], w_b[:, 3 * width :], 1, 0) + mod[19:20, :]
    after_two = after + piece(5) * branch_two
    norm_three, scale_three = normed(after_two)
    hidden = (norm_three * (1.0 + piece(7)) + piece(6)).astype(bf16)
    h3_ref[...] = hidden
    grad_out = cot_ref[...].reshape(tokens, width).astype(f32) * loss[clip : clip + 1, :]
    grad_branch = (grad_out * piece(8)).astype(bf16)
    gb3_ref[...] = grad_branch
    add(11, column_sum(grad_branch.astype(f32)))
    branch_three = jnp.zeros((tokens, width), f32)
    grad_hidden = jnp.zeros((tokens, width), f32)
    for chunk in range(w_u.shape[1] // width):
        part = slice(chunk * width, (chunk + 1) * width)
        upper = dot(hidden, w_u[:, part], 1, 0) + mod[20 + chunk : 21 + chunk, :]
        square = upper * upper
        bend = jnp.tanh(upper * (GELU_C + (GELU_C * GELU_A) * square))
        half = 0.5 + 0.5 * bend
        act = (upper * half).astype(bf16)
        slope = half + (0.5 * upper) * (1.0 - bend * bend) * (
            GELU_C + (3.0 * GELU_C * GELU_A) * square
        )
        act_ref[:, part] = act
        branch_three += dot(act, w_d[part, :], 1, 0)
        grad_upper = (dot(grad_branch, w_d[part, :], 1, 1) * slope).astype(bf16)
        gup_ref[:, part] = grad_upper
        add(7 + chunk, column_sum(grad_upper.astype(f32)))
        grad_hidden += dot(grad_upper, w_u[:, part], 1, 1)
    branch_three += mod[24:25, :]
    out = (after_two + piece(8) * branch_three).astype(bf16)
    out_ref[...] = out.reshape(out_ref.shape)
    add(5, column_sum(grad_out * branch_three))
    add(3, column_sum(grad_hidden))
    add(4, column_sum(grad_hidden * norm_three))
    grad_two = grad_out + norm_back(grad_hidden, 1.0 + piece(7), norm_three, scale_three)
    add(2, column_sum(grad_two * branch_two))
    grad_branch = (grad_two * piece(5)).astype(bf16)
    gb2_ref[...] = grad_branch
    add(6, column_sum(grad_branch.astype(f32)))
    gmix[...] = dot(grad_branch, w_b[:, 3 * width :], 1, 1).astype(bf16)
    attend_back(qkv, gmix, totals, gqkv_ref, width, mask)
    grad_hidden = dot(gqkv_ref[...], w_b[:, : 3 * width], 1, 1).astype(bf16).astype(f32)
    add(0, column_sum(grad_hidden))
    add(1, column_sum(grad_hidden * norm))
    grad_one = grad_two + norm_back(grad_hidden, 1.0 + piece(4), norm, scale)
    grad_ref[...] = grad_one.astype(bf16).reshape(grad_ref.shape)


def middle_kernel_next(count, clip, *refs):
    middle_kernel(clip, *refs[:7], *refs[7 + count :])


def middle_call(clip, clip_count, after, cot, loss, mod, w_b, w_u, w_d, earlier):
    frames, frame_count, part, width = after.shape
    group = min(16, part)
    tiles = part // group
    tokens = frames * frame_count * group
    hidden_width = w_u.shape[1]
    block = pl.BlockSpec((frames, frame_count, group, width), lambda t: (0, 0, t, 0))
    widths = (hidden_width, hidden_width, width, width, width, width, width, 3 * width)
    own = lambda columns: pl.BlockSpec((tokens, columns), lambda t: (clip * tiles + t, 0))
    rows = tiles * tokens
    in_specs = [
        block, block, full(loss.shape), full(mod.shape), full(w_b.shape), full(w_u.shape),
        full(w_d.shape),
    ]
    args = [after, cot, loss, mod, w_b, w_u, w_d]
    body = functools.partial(middle_kernel, clip)
    aliases = {}
    if earlier is not None:
        in_specs += [pl.BlockSpec(memory_space=pl.ANY)] * len(earlier)
        args += list(earlier)
        aliases = {7 + number: 2 + number for number in range(len(earlier))}
        body = functools.partial(middle_kernel_next, len(earlier), clip)
    return pl.pallas_call(
        body,
        grid=(tiles,),
        in_specs=in_specs,
        out_specs=[block, block] + [own(columns) for columns in widths]
        + [pl.BlockSpec((16, width), lambda t: (0, 0))],
        out_shape=[
            jax.ShapeDtypeStruct(after.shape, bf16), jax.ShapeDtypeStruct(after.shape, bf16),
        ]
        + [jax.ShapeDtypeStruct((clip_count * rows, columns), bf16) for columns in widths]
        + [jax.ShapeDtypeStruct((16, width), f32)],
        scratch_shapes=[
            VMEM((tokens, 3 * width), bf16),
            VMEM((16, tokens), f32),
            VMEM((tokens, tokens), f32),
            VMEM((tokens, width), bf16),
        ],
        input_output_aliases=aliases,
        compiler_params=pltpu.CompilerParams(vmem_limit_bytes=VMEM_LIMIT),
        cost_estimate=pl.CostEstimate(
            flops=rows * 100_000_000, bytes_accessed=rows * 40_000, transcendentals=0
        ),
    )(*args)


def space_back_kernel(
    clip, grad_ref, x_ref, mod, w_c, qkv, branch, totals,
    out_ref, gb_ref, gqkv_ref, sums, gmix,
):
    width = x_ref.shape[-1]
    tokens = x_ref.shape[-2]
    row = clip * 9
    piece = lambda number: mod[row + number : row + number + 1, :]

    @pl.when(pl.program_id(0) == 0)
    def _():
        sums[...] = jnp.zeros_like(sums)

    grad = grad_ref[...].reshape(tokens, width).astype(f32)
    grad_branch = (grad * piece(2)).astype(bf16)
    gb_ref[...] = grad_branch
    sums[2:3, :] += column_sum(grad * branch[...].astype(f32))
    sums[3:4, :] += column_sum(grad_branch.astype(f32))
    gmix[...] = dot(grad_branch, w_c[:, 3 * width :], 1, 1).astype(bf16)
    attend_back(qkv, gmix, totals, gqkv_ref, width, None)
    grad_hidden = dot(gqkv_ref[...], w_c[:, : 3 * width], 1, 1)
    norm, scale = normed(x_ref[...].reshape(tokens, width).astype(f32))
    sums[0:1, :] += column_sum(grad_hidden)
    sums[1:2, :] += column_sum(grad_hidden * norm)
    result = grad + norm_back(grad_hidden, 1.0 + piece(1), norm, scale)
    out_ref[...] = result.reshape(out_ref.shape)


def space_back_next(count, clip, *refs):
    space_back_kernel(clip, *refs[:7], *refs[7 + count :])


def space_back_call(clip, grad, x, mod, w_c, qkv, branch, totals, earlier):
    clip_count, frame_count, tokens, width = x.shape
    frames = grad.shape[0]
    part = grad.shape[2]
    rows = frame_count * tokens
    by_frame = lambda columns: pl.BlockSpec(
        (None, tokens, columns), lambda f: (clip * frame_count + f, 0, 0)
    )
    own = lambda columns: pl.BlockSpec((tokens, columns), lambda f: (clip * frame_count + f, 0))
    in_specs = [
        pl.BlockSpec((frames, 1, part, width), lambda f: (0, f, 0, 0)),
        pl.BlockSpec((1, 1, tokens, width), lambda f: (clip, f, 0, 0)),
        full(mod.shape),
        full(w_c.shape),
        by_frame(3 * width),
        by_frame(width),
        pl.BlockSpec((None, 16, tokens), lambda f: (clip * frame_count + f, 0, 0)),
    ]
    args = [grad, x, mod, w_c, qkv, branch, totals]
    body = functools.partial(space_back_kernel, clip)
    aliases = {}
    if earlier is not None:
        in_specs += [pl.BlockSpec(memory_space=pl.ANY)] * len(earlier)
        args += list(earlier)
        aliases = {7 + number: number for number in range(len(earlier))}
        body = functools.partial(space_back_next, len(earlier), clip)
    return pl.pallas_call(
        body,
        grid=(frame_count,),
        in_specs=in_specs,
        out_specs=[
            pl.BlockSpec((1, 1, tokens, width), lambda f: (clip, f, 0, 0)),
            own(width),
            own(3 * width),
            pl.BlockSpec((8, width), lambda f: (0, 0)),
        ],
        out_shape=[
            jax.ShapeDtypeStruct(x.shape, f32),
            jax.ShapeDtypeStruct((clip_count * rows, width), bf16),
            jax.ShapeDtypeStruct((clip_count * rows, 3 * width), bf16),
            jax.ShapeDtypeStruct((8, width), f32),
        ],
        scratch_shapes=[VMEM((tokens, width), bf16)],
        input_output_aliases=aliases,
        compiler_params=pltpu.CompilerParams(vmem_limit_bytes=VMEM_LIMIT),
        cost_estimate=pl.CostEstimate(
            flops=rows * 20_000_000, bytes_accessed=rows * width * 20, transcendentals=0
        ),
    )(*args)


def scatter_rows(grad):
    return lax.psum_scatter(
        grad, ("clip", "frame"), scatter_dimension=0, tiled=True
    ).astype(f32)


def shards(
    inputs, cotangent, time_steps, weight_index, ada_weight, ada_bias, space_qkv, space_out,
    space_out_bias, time_qkv, time_out, time_out_bias, up_weight, up_bias, down_weight, down_bias,
):
    clip_count, frame_count, patch_count, width = inputs.shape
    clips, frames = lax.axis_size("clip"), lax.axis_size("frame")
    owners = clips * frames
    owner = lax.axis_index("clip") * frames + lax.axis_index("frame")
    part = patch_count // frames
    rows = ada_weight.shape[0]

    embed = jax.nn.silu(embed_steps(time_steps, width)).astype(bf16)
    embed = jnp.pad(embed, ((0, 16 - clip_count), (0, 0)))
    place = lax.broadcasted_iota(jnp.int32, (width, 128), 0) - owner * rows
    lane = lax.broadcasted_iota(jnp.int32, (width, 128), 1)
    select = ((place == lane) & (lane < rows)).astype(bf16)
    ada = jnp.pad(ada_weight, ((0, 128 - rows), (0, 0)))

    def spread_bias(vector):
        length = vector.shape[0]
        empty = jnp.zeros((owners * length,), f32)
        return lax.dynamic_update_slice(empty, vector.astype(f32), (owner * length,)).reshape(
            -1, width
        )

    bias = jnp.concatenate(
        [
            spread_bias(vector)
            for vector in (ada_bias, space_out_bias, time_out_bias, up_bias, down_bias)
        ],
        axis=0,
    )
    sh_c = jnp.concatenate([space_qkv, space_out], axis=1)
    sh_b = jnp.concatenate([time_qkv, time_out], axis=1)
    (
        w_c, w_b, w_u, w_d, mod, chosen, totals, hidden_one, qkv_one, mixed_one, branch_one,
        after_first, after_later, cot_first,
    ) = start_call(
        clips, frames, inputs, cotangent, sh_c, sh_b, up_weight, down_weight, embed, select, ada,
        bias,
    )

    def exchange(values):
        return lax.all_to_all(values, "frame", split_axis=0, concat_axis=0, tiled=True)

    loss = jnp.exp2(weight_index.astype(f32) * 0.5 - 1.0)
    loss = jnp.broadcast_to(loss[:, None], (clip_count, width))
    cots, afters = [cot_first], [after_first]
    for clip in range(1, clip_count):
        patches = cotangent[clip].reshape(frame_count, frames, part, width)
        cots.append(exchange(jnp.swapaxes(patches, 0, 1)))
        place = (clip - 1) * frame_count
        patches = after_later[place : place + frame_count]
        patches = patches.reshape(frame_count, frames, part, width)
        afters.append(exchange(jnp.swapaxes(patches, 0, 1)))

    earlier = None
    outs, grads, mid_sums = [], [], []
    for clip in range(clip_count):
        out, grad, *rest = middle_call(
            clip, clip_count, afters[clip], cots[clip], loss, mod, w_b, w_u, w_d, earlier
        )
        earlier = rest[:-1]
        mid_sums.append(rest[-1])
        outs.append(exchange(out))
        grads.append(exchange(grad))
    act, gup, h3, gb3, mixed_two, gb2, h2, gqkv_two = earlier
    grad_down = dot(act, gb3, 0, 0).astype(bf16)
    grad_up = dot(h3, gup, 0, 0).astype(bf16)
    grad_tout = dot(mixed_two, gb2, 0, 0).astype(bf16)
    grad_tqkv = dot(h2, gqkv_two, 0, 0).astype(bf16)

    earlier = None
    space_sums = []
    for clip in range(clip_count):
        *earlier, sums = space_back_call(
            clip, grads[clip], inputs, mod, w_c, qkv_one, branch_one, totals, earlier
        )
        space_sums.append(sums)
    input_grad, gb1, gqkv_one = earlier
    grad_sout = dot(mixed_one.reshape(-1, width), gb1, 0, 0).astype(bf16)
    grad_sqkv = dot(hidden_one.reshape(-1, width), gqkv_one, 0, 0).astype(bf16)

    pieces = []
    for clip in range(clip_count):
        pieces += [space_sums[clip][0:3], mid_sums[clip][0:6]]
    pieces.append(sum(entry[3:4] for entry in space_sums))
    pieces.append(sum(entry[6:12] for entry in mid_sums))
    small = jnp.concatenate(pieces, axis=0)
    small = jnp.pad(small, ((0, ROWS - small.shape[0]), (0, 0)))
    gathered = end_call(clips, frames, small)
    count = clip_count * 9
    grad_modulation = gathered[:, :count].reshape(clips * clip_count, 9 * width)
    picked = chosen.reshape(clips, 16, 128)[:, :clip_count, :rows].reshape(-1, rows)
    grad_ada = lax.dot_general(
        picked.astype(f32), grad_modulation, (((0,), (0,)), ((), ())), precision=highest
    )
    grad_ada_bias = jnp.sum(grad_modulation, axis=0)
    biases = jnp.sum(gathered[:, count : count + 7], axis=0)

    def own_slice(vector):
        length = vector.shape[0] // owners
        return lax.dynamic_slice_in_dim(vector, owner * length, length, 0)

    outputs = jnp.stack(
        [
            jnp.swapaxes(out, 0, 1).reshape(frame_count, patch_count, width)
            for out in outs
        ]
    )
    return (
        outputs,
        input_grad,
        grad_ada,
        own_slice(grad_ada_bias),
        scatter_rows(grad_sqkv),
        scatter_rows(grad_sout),
        own_slice(biases[0]),
        scatter_rows(grad_tqkv),
        scatter_rows(grad_tout),
        own_slice(biases[1]),
        scatter_rows(grad_up),
        own_slice(biases[2:6].reshape(-1)),
        scatter_rows(grad_down),
        own_slice(biases[6]),
    )


def solution(mesh):
    tokens = P("clip", "frame", None, None)
    matrix = P(("clip", "frame"), None)
    vector = P(("clip", "frame"))
    in_specs = (
        tokens, tokens, P("clip"), P("clip"), matrix, vector, matrix, matrix, vector, matrix,
        matrix, vector, matrix, vector, matrix, vector,
    )
    out_specs = (
        tokens, tokens, matrix, vector, matrix, matrix, vector, matrix, matrix, vector, matrix,
        vector, matrix, vector,
    )
    return jax.shard_map(shards, mesh=mesh, in_specs=in_specs, out_specs=out_specs, check_vma=False)
```

```python
import functools
import math

import jax
import jax.numpy as jnp
from jax import lax
from jax.experimental import pallas as pl
from jax.experimental.pallas import tpu as pltpu
from jax.sharding import PartitionSpec as P

HEADS = 12
HEAD = 64
PAIRS = HEADS // 2
ROWS = 32
GELU_C = math.sqrt(2.0 / math.pi)
GELU_A = 0.044715
VMEM_LIMIT = 58 << 20

f32 = jnp.float32
bf16 = jnp.bfloat16
highest = lax.Precision.HIGHEST
MESH = pl.DeviceIdType.MESH
VMEM = pltpu.VMEM
DMA = pltpu.SemaphoreType.DMA


def embed_steps(time_steps, model_width):
    half_width = model_width // 2
    frequencies = jnp.exp(
        -math.log(10000.0) * jnp.arange(half_width, dtype=f32) / half_width
    )
    angles = time_steps.astype(f32)[:, None] * frequencies[None, :]
    return jnp.concatenate([jnp.cos(angles), jnp.sin(angles)], axis=1)


def dot(left, right, left_dim, right_dim):
    return lax.dot_general(
        left, right, (((left_dim,), (right_dim,)), ((), ())), preferred_element_type=f32
    )


def flip(index, mask):
    bit = 1
    while bit <= mask:
        if mask & bit:
            index = index + bit * (1 - 2 * ((index // bit) % 2))
        bit *= 2
    return index


def span(masks):
    out = [0]
    for mask in masks:
        out = out + [entry ^ mask for entry in out]
    return out


def frame_masks(frames):
    masks, bit = [], 1
    while bit < frames:
        masks.append(bit)
        bit *= 2
    if len(masks) > 1:
        masks = [frames - 1] + masks[:-1]
    return masks


def clip_tail_masks(clips):
    masks, bit = [], 2
    while bit < clips:
        masks.append(bit)
        bit *= 2
    return masks


def greet(clips, frames):
    clip, frame = lax.axis_index("clip"), lax.axis_index("frame")
    barrier = pltpu.get_barrier_semaphore()
    for step in range(1, clips):
        pl.semaphore_signal(
            barrier, inc=1, device_id={"clip": lax.rem(clip + step, clips)}, device_id_type=MESH
        )
    for step in range(1, frames):
        pl.semaphore_signal(
            barrier, inc=1, device_id={"frame": lax.rem(frame + step, frames)}, device_id_type=MESH
        )
    pl.semaphore_wait(barrier, clips + frames - 2)


def spread(axis, size, source_of, target, send_sems, recv_sems):
    me = lax.axis_index(axis)
    copies = []
    for step in range(1, size):
        peer = lax.rem(me + step, size)
        copy = pltpu.make_async_remote_copy(
            src_ref=source_of(peer),
            dst_ref=target.at[me],
            send_sem=send_sems.at[step - 1],
            recv_sem=recv_sems.at[step - 1],
            device_id={axis: peer},
            device_id_type=MESH,
        )
        copy.start()
        copies.append(copy)
    return copies


def start_kernel(
    clips, frames, clip_count,
    x_ref, cotangent, sh_c, sh_b, sh_u, sh_d, embed, select, ada, bias,
    w_c, w_b, w_u, w_d, mod, chosen, totals, hidden_out, qkv_out, mixed_out, branch_out,
    after_first, after_later, cot_first,
    v_c, z_c, z_b, z_u, z_d, st_w, b_c, b_b, b_u, b_d,
    embeds, parts, terms, arrived, held, lined, hidden, qkv, mixed, branch, after,
    zs, zr, cs, cr, xs, xr, ls, es, er, ps, pr, fs, fr, ts, tr, hs, hr, os, ws,
):
    clip, frame = lax.axis_index("clip"), lax.axis_index("frame")
    shards_in = (sh_c, sh_b, sh_u, sh_d)
    zoned = (z_c, z_b, z_u, z_d)
    blocks = (b_c, b_b, b_u, b_d)
    wholes = (v_c, w_b, w_u, w_d)
    width = mod.shape[1]
    frame_count, tokens = x_ref.shape[1], x_ref.shape[2]
    part = tokens // frames
    greet(clips, frames)
    masks = frame_masks(frames)
    sends = []
    stage = {}

    def frame_step(group, step):
        number = (1 << step) - 1
        copies = []
        for offset in span(masks[:step]):
            slot = flip(frame, offset)
            source = shards_in[group] if offset == 0 else zoned[group].at[slot]
            copy = pltpu.make_async_remote_copy(
                src_ref=source,
                dst_ref=zoned[group].at[slot],
                send_sem=zs.at[group, number],
                recv_sem=zr.at[group, number],
                device_id={"frame": flip(frame, masks[step])},
                device_id_type=MESH,
            )
            copy.start()
            copies.append(copy)
            number += 1
        sends.extend(copies)
        stage[group] = copies

    def frame_rest(group):
        for step in range(1, len(masks)):
            for copy in stage[group]:
                copy.wait_recv()
            frame_step(group, step)

    tail = clip_tail_masks(clips)
    steps = len(tail)
    orders = (tail, tail[::-1])
    moving = {}

    def block_send(group, half, step, position, offset):
        whole = wholes[group]
        block_rows = whole.shape[0] // clips
        columns = whole.shape[1] // 2
        rows = pl.ds(pl.multiple_of(flip(clip, offset) * block_rows, block_rows), block_rows)
        lanes = pl.ds(half * columns, columns)
        target = whole.at[rows, lanes]
        number = (1 << step) - 1 + position
        copy = pltpu.make_async_remote_copy(
            src_ref=blocks[group].at[:, lanes] if offset == 0 else target,
            dst_ref=target,
            send_sem=xs.at[group, half, number],
            recv_sem=xr.at[group, half, number],
            device_id={"clip": flip(clip, orders[half][step])},
            device_id_type=MESH,
        )
        copy.start()
        moving[group, half, number] = copy

    core_copies = {group: [] for group in range(4)}

    def core_send(group, offset):
        whole = wholes[group]
        block_rows = whole.shape[0] // clips
        rows = pl.ds(pl.multiple_of(flip(clip, offset) * block_rows, block_rows), block_rows)
        number = len(core_copies[group])
        copy = pltpu.make_async_remote_copy(
            src_ref=blocks[group] if offset == 0 else whole.at[rows, :],
            dst_ref=whole.at[rows, :],
            send_sem=cs.at[group, number],
            recv_sem=cr.at[group, number],
            device_id={"clip": flip(clip, 1)},
            device_id_type=MESH,
        )
        copy.start()
        core_copies[group].append(copy)

    local_copies = []

    def block_ready(group):
        for copy in stage[group]:
            copy.wait_recv()
        rows, columns = shards_in[group].shape
        block_rows = frames * rows
        if rows % 16:
            for slot in range(frames):
                st_w[slot * rows : (slot + 1) * rows, :columns] = zoned[group][slot].astype(f32)
            blocks[group][...] = st_w[:block_rows, :columns].astype(bf16)
        else:
            for slot in range(frames):
                blocks[group][slot * rows : (slot + 1) * rows, :] = zoned[group][slot]
        for step in range(steps):
            for half in range(2):
                block_send(group, half, step, 0, 0)
        core_send(group, 0)
        place = pl.ds(pl.multiple_of(clip * block_rows, block_rows), block_rows)
        keep = pltpu.make_async_copy(blocks[group], wholes[group].at[place, :], ls.at[group])
        keep.start()
        local_copies.append(keep)

    def block_forward(group):
        for step in range(1, steps):
            for half in range(2):
                for position in range(1 << (step - 1), 1 << step):
                    moving[group, half, position - 1].wait_recv()
                for later in range(step, steps):
                    for position, offset in enumerate(span(orders[half][:later])):
                        if (1 << (step - 1)) <= position < (1 << step):
                            block_send(group, half, later, position, offset)

    def block_finish(group):
        last = (1 << (steps - 1)) - 1
        for half in range(2):
            for number in range(last, (1 << steps) - 1):
                moving[group, half, number].wait_recv()
        for offset in span(tail)[1:]:
            core_send(group, offset)

    def core_finish(group):
        for copy in core_copies[group]:
            copy.wait_recv()

    for group in range(4):
        frame_step(group, 0)
    own = spread("clip", clips, lambda peer: embed, embeds, es, er)
    sends.extend(own)
    embeds[clip] = embed[...]
    for group in range(4):
        zoned[group][frame] = shards_in[group][...]
    for copy in own:
        copy.wait_recv()
    picked = dot(embeds[...].reshape(clips * 16, width), select[...], 1, 0).astype(bf16)
    chosen[...] = picked
    parts[...] = dot(picked, ada[...], 1, 0)
    for peer in range(clips):
        for local in range(clip_count):
            row = peer * 16 + local
            for piece in range(9):
                terms[peer, local * 9 + piece : local * 9 + piece + 1, :] = (
                    parts[row : row + 1, piece * width : (piece + 1) * width]
                    + bias[piece : piece + 1, :]
                )
        base = clip_count * 9
        terms[peer, base : base + 7, :] = bias[9:16, :]
        if base + 7 < ROWS:
            terms[peer, base + 7 : ROWS, :] = jnp.zeros((ROWS - base - 7, width), f32)
    own = spread("clip", clips, lambda peer: terms.at[peer], arrived, ps, pr)
    sends.extend(own)
    arrived[clip] = terms[clip]
    frame_rest(0)
    for copy in own:
        copy.wait_recv()
    total = arrived[0]
    for peer in range(1, clips):
        total = total + arrived[peer]
    held[...] = total
    own = spread("frame", frames, lambda peer: held, lined, fs, fr)
    sends.extend(own)
    lined[frame] = total
    block_ready(0)
    for group in range(1, 4):
        frame_rest(group)

    cot_copies = []
    for step in range(1, frames):
        peer = lax.rem(frame + step, frames)
        copy = pltpu.make_async_remote_copy(
            src_ref=cotangent.at[0, :, pl.ds(pl.multiple_of(peer * part, part), part), :],
            dst_ref=cot_first.at[frame],
            send_sem=ts.at[step - 1],
            recv_sem=tr.at[step - 1],
            device_id={"frame": peer},
            device_id_type=MESH,
        )
        copy.start()
        cot_copies.append(copy)
    keep = pltpu.make_async_copy(
        cotangent.at[0, :, pl.ds(pl.multiple_of(frame * part, part), part), :],
        cot_first.at[frame],
        ls.at[4],
    )
    keep.start()
    local_copies.append(keep)

    for copy in own:
        copy.wait_recv()
    total = lined[0]
    for peer in range(1, frames):
        total = total + lined[peer]
    mod[...] = total
    block_forward(0)
    for group in range(1, 4):
        block_ready(group)
    block_finish(0)
    core_finish(0)
    local_copies[0].wait()

    keep = pltpu.make_async_copy(v_c, w_c, ls.at[5])
    keep.start()
    local_copies.append(keep)

    def after_copy(f, step):
        peer = lax.rem(frame + step, frames)
        return pltpu.make_async_remote_copy(
            src_ref=after.at[f, pl.ds(pl.multiple_of(peer * part, part), part), :],
            dst_ref=after_first.at[frame, f],
            send_sem=hs.at[f, step - 1],
            recv_sem=hr.at[f, step - 1],
            device_id={"frame": peer},
            device_id_type=MESH,
        )

    def own_after(f):
        return pltpu.make_async_copy(
            after.at[f, pl.ds(pl.multiple_of(frame * part, part), part), :],
            after_first.at[frame, f],
            os.at[f],
        )

    def later_after(f):
        return pltpu.make_async_copy(after.at[f], after_later.at[f - frame_count], os.at[f])

    kept = ((hidden, hidden_out), (qkv, qkv_out), (mixed, mixed_out), (branch, branch_out))

    def write_back(f):
        return [
            pltpu.make_async_copy(source.at[f], target.at[f], ws.at[number, f])
            for number, (source, target) in enumerate(kept)
        ]

    for local in range(clip_count):
        row = local * 9

        def one_frame(index, carry):
            f = local * frame_count + index
            values = x_ref[local, index].astype(f32)
            norm, _ = normed(values)
            scaled = norm * (1.0 + mod[row + 1 : row + 2, :]) + mod[row : row + 1, :]
            lowered = scaled.astype(bf16)
            hidden[f] = lowered
            qkv[f] = dot(lowered, v_c[:, : 3 * width], 1, 0).astype(bf16)
            attend(qkv.at[f], mixed.at[f], totals.at[f], width, None)
            grown = dot(mixed[f], v_c[:, 3 * width :], 1, 0) + mod[18:19, :]
            branch[f] = grown.astype(bf16)
            after[f] = (values + mod[row + 2 : row + 3, :] * grown).astype(bf16)
            if local == 0:
                for step in range(1, frames):
                    after_copy(f, step).start()
                own_after(f).start()
            else:
                later_after(f).start()
            for copy in write_back(f):
                copy.start()
            return carry

        lax.fori_loop(0, frame_count, one_frame, 0)
        if local == 0:
            block_forward(1)
    for group in range(2, 4):
        block_forward(group)
    for group in range(1, 4):
        block_finish(group)
    for group in range(1, 4):
        core_finish(group)

    def settle(f, carry):
        for step in range(1, frames):
            copy = after_copy(f, step)
            copy.wait_recv()
            copy.wait_send()
        own_after(f).wait()
        return carry

    lax.fori_loop(0, frame_count, settle, 0)

    def settle_later(f, carry):
        later_after(f).wait()
        return carry

    lax.fori_loop(frame_count, clip_count * frame_count, settle_later, 0)

    def settle_kept(f, carry):
        for copy in write_back(f):
            copy.wait()
        return carry

    lax.fori_loop(0, clip_count * frame_count, settle_kept, 0)
    for copy in cot_copies:
        copy.wait_recv()
        copy.wait_send()
    for copy in local_copies[1:]:
        copy.wait()
    for copy in moving.values():
        copy.wait_send()
    for group in range(4):
        for copy in core_copies[group]:
            copy.wait_send()
    for copy in sends:
        copy.wait_send()


def start_call(
    clips, frames, inputs, cotangent, sh_c, sh_b, sh_u, sh_d, embed, select, ada, bias
):
    clip_count, frame_count, tokens, width = inputs.shape
    rows, columns = sh_c.shape
    rows_d = sh_d.shape[0]
    block = frames * rows
    block_d = frames * rows_d
    peers = max(clips // 2 - 1, 1)
    total = clip_count * frame_count
    part = tokens // frames
    whole = jax.ShapeDtypeStruct((clips * block, columns), bf16)
    vmem = pl.BlockSpec(memory_space=VMEM)
    hbm = pl.BlockSpec(memory_space=pl.ANY)
    zoned = lambda height, lanes: VMEM((frames, height, lanes), bf16)
    saved = lambda lanes: jax.ShapeDtypeStruct((total, tokens, lanes), bf16)
    lent = lambda lanes: VMEM((total, tokens, lanes), bf16)
    traded = jax.ShapeDtypeStruct((frames, frame_count, part, width), bf16)
    return pl.pallas_call(
        functools.partial(start_kernel, clips, frames, clip_count),
        out_shape=(
            whole, whole, whole,
            jax.ShapeDtypeStruct((clips * block_d, width), bf16),
            jax.ShapeDtypeStruct((ROWS, width), f32),
            jax.ShapeDtypeStruct((clips * 16, 128), bf16),
            jax.ShapeDtypeStruct((total, 16, tokens), f32),
            saved(width), saved(3 * width), saved(width), saved(width),
            traded,
            jax.ShapeDtypeStruct(((clip_count - 1) * frame_count, tokens, width), bf16),
            traded,
        ),
        in_specs=[vmem, hbm] + [vmem] * 8,
        out_specs=(hbm, hbm, hbm, hbm, vmem, vmem, vmem) + (hbm,) * 7,
        scratch_shapes=[
            VMEM((clips * block, columns), bf16),
            zoned(rows, columns), zoned(rows, columns), zoned(rows, columns), zoned(rows_d, width),
            VMEM((max(block, block_d), columns), f32),
            VMEM((block, columns), bf16),
            VMEM((block, columns), bf16),
            VMEM((block, columns), bf16),
            VMEM((block_d, width), bf16),
            VMEM((clips, 16, width), bf16),
            VMEM((clips * 16, 9 * width), f32),
            VMEM((clips, ROWS, width), f32),
            VMEM((clips, ROWS, width), f32),
            VMEM((ROWS, width), f32),
            VMEM((frames, ROWS, width), f32),
            lent(width), lent(3 * width), lent(width), lent(width), lent(width),
            DMA((4, frames - 1)), DMA((4, frames - 1)),
            DMA((4, clips // 2)), DMA((4, clips // 2)),
            DMA((4, 2, peers)), DMA((4, 2, peers)),
            DMA((6,)),
            DMA((clips - 1,)), DMA((clips - 1,)),
            DMA((clips - 1,)), DMA((clips - 1,)),
            DMA((frames - 1,)), DMA((frames - 1,)),
            DMA((frames - 1,)), DMA((frames - 1,)),
            DMA((frame_count, frames - 1)), DMA((frame_count, frames - 1)),
            DMA((total,)),
            DMA((4, total)),
        ],
        compiler_params=pltpu.CompilerParams(
            collective_id=0, has_side_effects=True, vmem_limit_bytes=VMEM_LIMIT
        ),
    )(inputs, cotangent, sh_c, sh_b, sh_u, sh_d, embed, select, ada, bias)


STEP = 256


def grad_kernel(
    clips, frames,
    small, h3, gup, act, gb3, h2, gqkv2, mix2, gb2, h1, gqkv1, mix1, gb1,
    gathered, out_u, out_d, out_b, out_c,
    sum_w, sum_d, core_w, core_d, side_w, side_d, line_w, line_d, last_w, last_d,
    left, right, total, lined, held,
    lsem, rsem, cs, cr, xs, xr, zs, zr, fs, fr, ps, pr,
):
    clip, frame = lax.axis_index("clip"), lax.axis_index("frame")
    tokens = h3.shape[0]
    width = small.shape[1]
    wide = sum_w.shape[-1]
    narrow = sum_d.shape[-1]
    tail = clip_tail_masks(clips)
    orders = (tail, tail[::-1])
    masks = frame_masks(frames)
    greet(clips, frames)
    first = spread("frame", frames, lambda peer: small, lined, fs, fr)
    lined[frame] = small[...]

    chunks = [
        (1, 0, [(act, gb3, 0, 0, narrow)], out_d, 0),
        (1, 1, [(act, gb3, narrow, 0, narrow)], out_d, narrow),
        (0, 0, [(h3, gup, 0, 0, wide)], out_u, 0),
        (0, 1, [(h3, gup, wide, 0, wide)], out_u, wide),
        (0, 2, [(h2, gqkv2, 0, 0, wide)], out_b, 0),
        (0, 3, [(h2, gqkv2, wide, 0, width), (mix2, gb2, 0, width, width)], out_b, wide),
        (0, 4, [(h1, gqkv1, 0, 0, wide)], out_c, 0),
        (0, 5, [(h1, gqkv1, wide, 0, width), (mix1, gb1, 0, width, width)], out_c, wide),
    ]
    sums, cores, sides = (sum_w, sum_d), (core_w, core_d), (side_w, side_d)
    lines, lasts = (line_w, line_d), (last_w, last_d)
    flights = {}

    def multiply(number):
        kind, place, parts, _, _ = chunks[number]
        for one, other, begin, at, lanes in parts:
            height = one.shape[1]

            def load(step, slot):
                rows = pl.ds(pl.multiple_of(step * STEP, STEP), STEP)
                return (
                    pltpu.make_async_copy(
                        one.at[rows, :], left.at[slot, :, pl.ds(0, height)], lsem.at[slot]
                    ),
                    pltpu.make_async_copy(
                        other.at[rows, pl.ds(begin, lanes)],
                        right.at[slot, :, pl.ds(0, lanes)],
                        rsem.at[slot],
                    ),
                )

            for copy in load(0, 0):
                copy.start()
            steps = tokens // STEP

            def body(step, carry):
                slot = lax.rem(step, 2)

                @pl.when(step + 1 < steps)
                def _():
                    for copy in load(step + 1, lax.rem(step + 1, 2)):
                        copy.start()

                for copy in load(step, slot):
                    copy.wait()
                for group in range(height // width):
                    rows = slice(group * width, (group + 1) * width)
                    columns = slice(at + group * lanes, at + (group + 1) * lanes)
                    product = dot(left[slot, :, rows], right[slot, :, :lanes], 0, 0)

                    @pl.when(step == 0)
                    def _():
                        total[:, columns] = product

                    @pl.when(step > 0)
                    def _():
                        total[:, columns] += product

                return carry

            lax.fori_loop(0, steps, body, 0)
        rows, lanes = sums[kind].shape[2:]
        for block in range(clips):
            begin = block * rows
            column = begin // width * lanes
            begin = begin % width
            sums[kind][place, block] = total[begin : begin + rows, column : column + lanes].astype(
                bf16
            )

    def core_start(number):
        kind, place = chunks[number][:2]
        copies = []
        for position, offset in enumerate(span(tail)):
            copy = pltpu.make_async_remote_copy(
                src_ref=sums[kind].at[place, flip(clip, offset ^ 1)],
                dst_ref=cores[kind].at[place, position],
                send_sem=cs.at[number, position],
                recv_sem=cr.at[number, position],
                device_id={"clip": flip(clip, 1)},
                device_id_type=MESH,
            )
            copy.start()
            copies.append(copy)
        flights[number, "core"] = copies

    def half_of(kind, half):
        if kind:
            rows = sums[kind].shape[2] // 2
            return (slice(half * rows, (half + 1) * rows), slice(None))
        lanes = sums[kind].shape[3] // 2
        return (slice(None), slice(half * lanes, (half + 1) * lanes))

    def side_start(number, step):
        kind, place = chunks[number][:2]
        copies = []
        for half in range(2):
            mask = orders[half][step]
            for position, offset in enumerate(span(orders[half][:step])):
                entry = (1 << step) - 1 + position
                copy = pltpu.make_async_remote_copy(
                    src_ref=sums[kind].at[(place, flip(clip, offset ^ mask)) + half_of(kind, half)],
                    dst_ref=sides[kind].at[place, half, entry],
                    send_sem=xs.at[number, half, entry],
                    recv_sem=xr.at[number, half, entry],
                    device_id={"clip": flip(clip, mask)},
                    device_id_type=MESH,
                )
                copy.start()
                copies.append(copy)
        flights[number, "side", step] = copies

    def core_add(number):
        kind, place = chunks[number][:2]
        for copy in flights[number, "core"]:
            copy.wait_recv()
        for position, offset in enumerate(span(tail)):
            block = flip(clip, offset)
            sums[kind][place, block] = (
                sums[kind][place, block].astype(f32) + cores[kind][place, position].astype(f32)
            ).astype(bf16)
        side_start(number, len(tail) - 1)

    def side_add(number, step):
        kind, place = chunks[number][:2]
        for copy in flights[number, "side", step]:
            copy.wait_recv()
        for half in range(2):
            for position, offset in enumerate(span(orders[half][:step])):
                entry = (1 << step) - 1 + position
                block = flip(clip, offset)
                where = (place, block) + half_of(kind, half)
                sums[kind][where] = (
                    sums[kind][where].astype(f32) + sides[kind][place, half, entry].astype(f32)
                ).astype(bf16)
        if step:
            side_start(number, step - 1)
        else:
            rows = lines[kind].shape[2]
            block = sums[kind][place, clip].astype(f32)
            for slot in range(frames):
                lines[kind][place, slot] = block[slot * rows : (slot + 1) * rows, :].astype(bf16)
            line_start(number, len(masks) - 1)

    def line_start(number, step):
        kind, place = chunks[number][:2]
        copies = []
        for position, offset in enumerate(span(masks[:step])):
            entry = (1 << step) - 1 + position
            copy = pltpu.make_async_remote_copy(
                src_ref=lines[kind].at[place, flip(frame, offset ^ masks[step])],
                dst_ref=lasts[kind].at[place, entry],
                send_sem=zs.at[number, entry],
                recv_sem=zr.at[number, entry],
                device_id={"frame": flip(frame, masks[step])},
                device_id_type=MESH,
            )
            copy.start()
            copies.append(copy)
        flights[number, "line", step] = copies

    def line_add(number, step):
        kind, place, _, target, begin = chunks[number]
        for copy in flights[number, "line", step]:
            copy.wait_recv()
        for position, offset in enumerate(span(masks[:step])):
            entry = (1 << step) - 1 + position
            slot = flip(frame, offset)
            value = lines[kind][place, slot].astype(f32) + lasts[kind][place, entry].astype(f32)
            if step:
                lines[kind][place, slot] = value.astype(bf16)
            else:
                target[:, begin : begin + value.shape[1]] = value
        if step:
            line_start(number, step - 1)

    stages = [core_start, core_add]
    for step in range(len(tail))[::-1]:
        stages.append(functools.partial(side_add, step=step))
    for step in range(len(masks))[::-1]:
        stages.append(functools.partial(line_add, step=step))

    second = None
    for turn in range(len(chunks) + len(stages) - 1):
        for depth in range(len(stages))[::-1]:
            if depth > 0 and 0 <= turn - depth < len(chunks):
                stages[depth](turn - depth)
        if turn < len(chunks):
            multiply(turn)
            core_start(turn)
        if turn == 0:
            for copy in first:
                copy.wait_recv()
            summed = lined[0]
            for peer in range(1, frames):
                summed = summed + lined[peer]
            held[...] = summed
            second = spread("clip", clips, lambda peer: held, gathered, ps, pr)
            gathered[clip] = summed
    for copy in second:
        copy.wait_recv()
    for copy in first + second:
        copy.wait_send()
    for copies in flights.values():
        for copy in copies:
            copy.wait_send()


def grad_call(clips, frames, small, *operands):
    h3, gup, act = operands[:3]
    width, hidden = h3.shape[1], act.shape[1]
    owners = clips * frames
    wide, narrow = hidden // 2, width // 2
    rows_w, rows_d = width // owners, hidden // owners
    peers = max(clips // 2 - 1, 1)
    vmem = pl.BlockSpec(memory_space=VMEM)
    hbm = pl.BlockSpec(memory_space=pl.ANY)

    return pl.pallas_call(
        functools.partial(grad_kernel, clips, frames),
        out_shape=(
            jax.ShapeDtypeStruct((clips,) + small.shape, f32),
            jax.ShapeDtypeStruct((rows_w, hidden), f32),
            jax.ShapeDtypeStruct((rows_d, width), f32),
            jax.ShapeDtypeStruct((rows_w, hidden), f32),
            jax.ShapeDtypeStruct((rows_w, hidden), f32),
        ),
        in_specs=[vmem] + [hbm] * len(operands),
        out_specs=(vmem,) * 5,
        scratch_shapes=[
            VMEM((6, clips, rows_w * frames, wide), bf16),
            VMEM((2, clips, rows_d * frames, narrow), bf16),
            VMEM((6, clips // 2, rows_w * frames, wide), bf16),
            VMEM((2, clips // 2, rows_d * frames, narrow), bf16),
            VMEM((6, 2, peers, rows_w * frames, wide // 2), bf16),
            VMEM((2, 2, peers, rows_d * frames // 2, narrow), bf16),
            VMEM((6, frames, rows_w, wide), bf16),
            VMEM((2, frames, rows_d, narrow), bf16),
            VMEM((6, frames - 1, rows_w, wide), bf16),
            VMEM((2, frames - 1, rows_d, narrow), bf16),
            VMEM((2, STEP, hidden), bf16),
            VMEM((2, STEP, wide), bf16),
            VMEM((width, wide), f32),
            VMEM((frames,) + small.shape, f32),
            VMEM(small.shape, f32),
            DMA((2,)), DMA((2,)),
            DMA((8, clips // 2)), DMA((8, clips // 2)),
            DMA((8, 2, peers)), DMA((8, 2, peers)),
            DMA((8, frames - 1)), DMA((8, frames - 1)),
            DMA((frames - 1,)), DMA((frames - 1,)),
            DMA((clips - 1,)), DMA((clips - 1,)),
        ],
        compiler_params=pltpu.CompilerParams(
            collective_id=1, has_side_effects=True, vmem_limit_bytes=VMEM_LIMIT
        ),
    )(small, *operands)


def normed(values):
    centred = values - jnp.mean(values, axis=-1, keepdims=True)
    scale = lax.rsqrt(jnp.mean(centred * centred, axis=-1, keepdims=True) + 1e-06)
    return centred * scale, scale


def norm_back(grad, scaled, norm, scale):
    inner = grad * scaled
    return scale * (
        inner
        - jnp.mean(inner, axis=-1, keepdims=True)
        - norm * jnp.mean(inner * norm, axis=-1, keepdims=True)
    )


def column_sum(values):
    return jnp.sum(values, axis=0, keepdims=True)


def attend(qkv, mixed, totals, width, mask):
    tokens = qkv.shape[0]
    low = lax.broadcasted_iota(jnp.int32, (tokens, 128), 1) < HEAD
    for pair in range(PAIRS):
        at = pair * 128
        queries = qkv[:, at : at + 128] * bf16(0.125)
        keys = qkv[:, width + at : width + at + 128]
        values = qkv[:, 2 * width + at : 2 * width + at + 128]
        halves = []
        for half in range(2):
            own = jnp.where(low if half == 0 else ~low, queries, bf16(0))
            scores = dot(keys, own, 1, 1)
            if mask is not None:
                scores = scores + mask[...]
            peak = jnp.max(scores, axis=0, keepdims=True)
            terms = jnp.exp(scores - peak)
            total = jnp.sum(terms, axis=0, keepdims=True)
            weights = (terms * (1.0 / total)).astype(bf16)
            totals[2 * pair + half : 2 * pair + half + 1, :] = peak + jnp.log(total)
            halves.append(dot(weights, values, 0, 0))
        mixed[:, at : at + 128] = jnp.where(low, halves[0], halves[1]).astype(bf16)


def attend_back(qkv, grad_mixed, totals, grad_qkv, width, mask):
    tokens = qkv.shape[0]
    low = lax.broadcasted_iota(jnp.int32, (tokens, 128), 1) < HEAD
    for pair in range(PAIRS):
        at = pair * 128
        queries = qkv[:, at : at + 128]
        keys = qkv[:, width + at : width + at + 128]
        values = qkv[:, 2 * width + at : 2 * width + at + 128]
        grads = grad_mixed[:, at : at + 128]
        halves = []
        for half in range(2):
            pick = low if half == 0 else ~low
            own = jnp.where(pick, queries * bf16(0.125), bf16(0))
            own_grads = jnp.where(pick, grads, bf16(0))
            scores = dot(keys, own, 1, 1)
            if mask is not None:
                scores = scores + mask[...]
            weights = jnp.exp(scores - totals[2 * pair + half : 2 * pair + half + 1, :])
            grad_weights = dot(values, own_grads, 1, 1)
            inner = jnp.sum(weights * grad_weights, axis=0, keepdims=True)
            grad_scores = (weights * (grad_weights - inner)).astype(bf16)
            halves.append(
                (
                    dot(grad_scores, keys, 0, 0),
                    dot(grad_scores, queries, 1, 0),
                    dot(weights.astype(bf16), grads, 1, 0),
                )
            )
        for part, factor in ((0, 0.125), (1, 0.125), (2, 1.0)):
            joined = jnp.where(low, halves[0][part], halves[1][part]) * factor
            start = part * width + at
            grad_qkv[:, start : start + 128] = joined.astype(bf16)


def full(shape):
    return pl.BlockSpec(shape, lambda *_: (0,) * len(shape), pipeline_mode=pl.Buffered(1))


def middle_kernel(
    clip, after_ref, cot_ref, loss, mod, w_b, w_u, w_d,
    out_ref, grad_ref, act_ref, gup_ref, h3_ref, gb3_ref, mixed_ref, gb2_ref, h2_ref, gqkv_ref, sums,
    qkv, totals, mask, gmix,
):
    width = after_ref.shape[-1]
    group = after_ref.shape[2]
    tokens = after_ref.shape[0] * after_ref.shape[1] * group
    row = clip * 9
    piece = lambda number: mod[row + number : row + number + 1, :]

    @pl.when(pl.program_id(0) == 0)
    def _():
        sums[...] = jnp.zeros_like(sums)
        first = lax.broadcasted_iota(jnp.int32, (tokens, tokens), 0)
        second = lax.broadcasted_iota(jnp.int32, (tokens, tokens), 1)
        mask[...] = jnp.where(lax.rem(first, group) == lax.rem(second, group), 0.0, -1e30)

    def add(place, values):
        sums[place : place + 1, :] += values

    after = after_ref[...].reshape(tokens, width).astype(f32)
    norm, scale = normed(after)
    hidden = (norm * (1.0 + piece(4)) + piece(3)).astype(bf16)
    h2_ref[...] = hidden
    qkv[...] = dot(hidden, w_b[:, : 3 * width], 1, 0).astype(bf16)
    attend(qkv, mixed_ref, totals, width, mask)
    branch_two = dot(mixed_ref[...], w_b[:, 3 * width :], 1, 0) + mod[19:20, :]
    after_two = after + piece(5) * branch_two
    norm_three, scale_three = normed(after_two)
    hidden = (norm_three * (1.0 + piece(7)) + piece(6)).astype(bf16)
    h3_ref[...] = hidden
    grad_out = cot_ref[...].reshape(tokens, width).astype(f32) * loss[clip : clip + 1, :]
    grad_branch = (grad_out * piece(8)).astype(bf16)
    gb3_ref[...] = grad_branch
    add(11, column_sum(grad_branch.astype(f32)))
    branch_three = jnp.zeros((tokens, width), f32)
    grad_hidden = jnp.zeros((tokens, width), f32)
    for chunk in range(w_u.shape[1] // width):
        part = slice(chunk * width, (chunk + 1) * width)
        upper = dot(hidden, w_u[:, part], 1, 0) + mod[20 + chunk : 21 + chunk, :]
        square = upper * upper
        bend = jnp.tanh(upper * (GELU_C + (GELU_C * GELU_A) * square))
        half = 0.5 + 0.5 * bend
        act = (upper * half).astype(bf16)
        slope = half + (0.5 * upper) * (1.0 - bend * bend) * (
            GELU_C + (3.0 * GELU_C * GELU_A) * square
        )
        act_ref[:, part] = act
        branch_three += dot(act, w_d[part, :], 1, 0)
        grad_upper = (dot(grad_branch, w_d[part, :], 1, 1) * slope).astype(bf16)
        gup_ref[:, part] = grad_upper
        add(7 + chunk, column_sum(grad_upper.astype(f32)))
        grad_hidden += dot(grad_upper, w_u[:, part], 1, 1)
    branch_three += mod[24:25, :]
    out = (after_two + piece(8) * branch_three).astype(bf16)
    out_ref[...] = out.reshape(out_ref.shape)
    add(5, column_sum(grad_out * branch_three))
    add(3, column_sum(grad_hidden))
    add(4, column_sum(grad_hidden * norm_three))
    grad_two = grad_out + norm_back(grad_hidden, 1.0 + piece(7), norm_three, scale_three)
    add(2, column_sum(grad_two * branch_two))
    grad_branch = (grad_two * piece(5)).astype(bf16)
    gb2_ref[...] = grad_branch
    add(6, column_sum(grad_branch.astype(f32)))
    gmix[...] = dot(grad_branch, w_b[:, 3 * width :], 1, 1).astype(bf16)
    attend_back(qkv, gmix, totals, gqkv_ref, width, mask)
    grad_hidden = dot(gqkv_ref[...], w_b[:, : 3 * width], 1, 1).astype(bf16).astype(f32)
    add(0, column_sum(grad_hidden))
    add(1, column_sum(grad_hidden * norm))
    grad_one = grad_two + norm_back(grad_hidden, 1.0 + piece(4), norm, scale)
    grad_ref[...] = grad_one.astype(bf16).reshape(grad_ref.shape)


def middle_kernel_next(count, clip, *refs):
    middle_kernel(clip, *refs[:7], *refs[7 + count :])


def middle_call(clip, clip_count, after, cot, loss, mod, w_b, w_u, w_d, earlier):
    frames, frame_count, part, width = after.shape
    group = min(16, part)
    tiles = part // group
    tokens = frames * frame_count * group
    hidden_width = w_u.shape[1]
    block = pl.BlockSpec((frames, frame_count, group, width), lambda t: (0, 0, t, 0))
    widths = (hidden_width, hidden_width, width, width, width, width, width, 3 * width)
    own = lambda columns: pl.BlockSpec((tokens, columns), lambda t: (clip * tiles + t, 0))
    rows = tiles * tokens
    in_specs = [
        block, block, full(loss.shape), full(mod.shape), full(w_b.shape), full(w_u.shape),
        full(w_d.shape),
    ]
    args = [after, cot, loss, mod, w_b, w_u, w_d]
    body = functools.partial(middle_kernel, clip)
    aliases = {}
    if earlier is not None:
        in_specs += [pl.BlockSpec(memory_space=pl.ANY)] * len(earlier)
        args += list(earlier)
        aliases = {7 + number: 2 + number for number in range(len(earlier))}
        body = functools.partial(middle_kernel_next, len(earlier), clip)
    return pl.pallas_call(
        body,
        grid=(tiles,),
        in_specs=in_specs,
        out_specs=[block, block] + [own(columns) for columns in widths]
        + [pl.BlockSpec((16, width), lambda t: (0, 0))],
        out_shape=[
            jax.ShapeDtypeStruct(after.shape, bf16), jax.ShapeDtypeStruct(after.shape, bf16),
        ]
        + [jax.ShapeDtypeStruct((clip_count * rows, columns), bf16) for columns in widths]
        + [jax.ShapeDtypeStruct((16, width), f32)],
        scratch_shapes=[
            VMEM((tokens, 3 * width), bf16),
            VMEM((16, tokens), f32),
            VMEM((tokens, tokens), f32),
            VMEM((tokens, width), bf16),
        ],
        input_output_aliases=aliases,
        compiler_params=pltpu.CompilerParams(vmem_limit_bytes=VMEM_LIMIT),
        cost_estimate=pl.CostEstimate(
            flops=rows * 100_000_000, bytes_accessed=rows * 40_000, transcendentals=0
        ),
    )(*args)


def space_back_kernel(
    clip, grad_ref, x_ref, mod, w_c, qkv, branch, totals,
    out_ref, gb_ref, gqkv_ref, sums, gmix,
):
    width = x_ref.shape[-1]
    tokens = x_ref.shape[-2]
    row = clip * 9
    piece = lambda number: mod[row + number : row + number + 1, :]

    @pl.when(pl.program_id(0) == 0)
    def _():
        sums[...] = jnp.zeros_like(sums)

    grad = grad_ref[...].reshape(tokens, width).astype(f32)
    grad_branch = (grad * piece(2)).astype(bf16)
    gb_ref[...] = grad_branch
    sums[2:3, :] += column_sum(grad * branch[...].astype(f32))
    sums[3:4, :] += column_sum(grad_branch.astype(f32))
    gmix[...] = dot(grad_branch, w_c[:, 3 * width :], 1, 1).astype(bf16)
    attend_back(qkv, gmix, totals, gqkv_ref, width, None)
    grad_hidden = dot(gqkv_ref[...], w_c[:, : 3 * width], 1, 1)
    norm, scale = normed(x_ref[...].reshape(tokens, width).astype(f32))
    sums[0:1, :] += column_sum(grad_hidden)
    sums[1:2, :] += column_sum(grad_hidden * norm)
    result = grad + norm_back(grad_hidden, 1.0 + piece(1), norm, scale)
    out_ref[...] = result.reshape(out_ref.shape)


def space_back_next(count, clip, *refs):
    space_back_kernel(clip, *refs[:7], *refs[7 + count :])


def space_back_call(clip, grad, x, mod, w_c, qkv, branch, totals, earlier):
    clip_count, frame_count, tokens, width = x.shape
    frames = grad.shape[0]
    part = grad.shape[2]
    rows = frame_count * tokens
    by_frame = lambda columns: pl.BlockSpec(
        (None, tokens, columns), lambda f: (clip * frame_count + f, 0, 0)
    )
    own = lambda columns: pl.BlockSpec((tokens, columns), lambda f: (clip * frame_count + f, 0))
    in_specs = [
        pl.BlockSpec((frames, 1, part, width), lambda f: (0, f, 0, 0)),
        pl.BlockSpec((1, 1, tokens, width), lambda f: (clip, f, 0, 0)),
        full(mod.shape),
        full(w_c.shape),
        by_frame(3 * width),
        by_frame(width),
        pl.BlockSpec((None, 16, tokens), lambda f: (clip * frame_count + f, 0, 0)),
    ]
    args = [grad, x, mod, w_c, qkv, branch, totals]
    body = functools.partial(space_back_kernel, clip)
    aliases = {}
    if earlier is not None:
        in_specs += [pl.BlockSpec(memory_space=pl.ANY)] * len(earlier)
        args += list(earlier)
        aliases = {7 + number: number for number in range(len(earlier))}
        body = functools.partial(space_back_next, len(earlier), clip)
    return pl.pallas_call(
        body,
        grid=(frame_count,),
        in_specs=in_specs,
        out_specs=[
            pl.BlockSpec((1, 1, tokens, width), lambda f: (clip, f, 0, 0)),
            own(width),
            own(3 * width),
            pl.BlockSpec((8, width), lambda f: (0, 0)),
        ],
        out_shape=[
            jax.ShapeDtypeStruct(x.shape, f32),
            jax.ShapeDtypeStruct((clip_count * rows, width), bf16),
            jax.ShapeDtypeStruct((clip_count * rows, 3 * width), bf16),
            jax.ShapeDtypeStruct((8, width), f32),
        ],
        scratch_shapes=[VMEM((tokens, width), bf16)],
        input_output_aliases=aliases,
        compiler_params=pltpu.CompilerParams(vmem_limit_bytes=VMEM_LIMIT),
        cost_estimate=pl.CostEstimate(
            flops=rows * 20_000_000, bytes_accessed=rows * width * 20, transcendentals=0
        ),
    )(*args)


def shards(
    inputs, cotangent, time_steps, weight_index, ada_weight, ada_bias, space_qkv, space_out,
    space_out_bias, time_qkv, time_out, time_out_bias, up_weight, up_bias, down_weight, down_bias,
):
    clip_count, frame_count, patch_count, width = inputs.shape
    clips, frames = lax.axis_size("clip"), lax.axis_size("frame")
    owners = clips * frames
    owner = lax.axis_index("clip") * frames + lax.axis_index("frame")
    part = patch_count // frames
    rows = ada_weight.shape[0]

    embed = jax.nn.silu(embed_steps(time_steps, width)).astype(bf16)
    embed = jnp.pad(embed, ((0, 16 - clip_count), (0, 0)))
    place = lax.broadcasted_iota(jnp.int32, (width, 128), 0) - owner * rows
    lane = lax.broadcasted_iota(jnp.int32, (width, 128), 1)
    select = ((place == lane) & (lane < rows)).astype(bf16)
    ada = jnp.pad(ada_weight, ((0, 128 - rows), (0, 0)))

    def spread_bias(vector):
        length = vector.shape[0]
        empty = jnp.zeros((owners * length,), f32)
        return lax.dynamic_update_slice(empty, vector.astype(f32), (owner * length,)).reshape(
            -1, width
        )

    bias = jnp.concatenate(
        [
            spread_bias(vector)
            for vector in (ada_bias, space_out_bias, time_out_bias, up_bias, down_bias)
        ],
        axis=0,
    )
    sh_c = jnp.concatenate([space_qkv, space_out], axis=1)
    sh_b = jnp.concatenate([time_qkv, time_out], axis=1)
    (
        w_c, w_b, w_u, w_d, mod, chosen, totals, hidden_one, qkv_one, mixed_one, branch_one,
        after_first, after_later, cot_first,
    ) = start_call(
        clips, frames, inputs, cotangent, sh_c, sh_b, up_weight, down_weight, embed, select, ada,
        bias,
    )

    def exchange(values):
        return lax.all_to_all(values, "frame", split_axis=0, concat_axis=0, tiled=True)

    loss = jnp.exp2(weight_index.astype(f32) * 0.5 - 1.0)
    loss = jnp.broadcast_to(loss[:, None], (clip_count, width))
    cots, afters = [cot_first], [after_first]
    for clip in range(1, clip_count):
        patches = cotangent[clip].reshape(frame_count, frames, part, width)
        cots.append(exchange(jnp.swapaxes(patches, 0, 1)))
        place = (clip - 1) * frame_count
        patches = after_later[place : place + frame_count]
        patches = patches.reshape(frame_count, frames, part, width)
        afters.append(exchange(jnp.swapaxes(patches, 0, 1)))

    earlier = None
    outs, grads, mid_sums = [], [], []
    for clip in range(clip_count):
        out, grad, *rest = middle_call(
            clip, clip_count, afters[clip], cots[clip], loss, mod, w_b, w_u, w_d, earlier
        )
        earlier = rest[:-1]
        mid_sums.append(rest[-1])
        outs.append(exchange(out))
        grads.append(exchange(grad))
    act, gup, h3, gb3, mixed_two, gb2, h2, gqkv_two = earlier

    earlier = None
    space_sums = []
    for clip in range(clip_count):
        *earlier, sums = space_back_call(
            clip, grads[clip], inputs, mod, w_c, qkv_one, branch_one, totals, earlier
        )
        space_sums.append(sums)
    input_grad, gb1, gqkv_one = earlier
    pieces = []
    for clip in range(clip_count):
        pieces += [space_sums[clip][0:3], mid_sums[clip][0:6]]
    pieces.append(sum(entry[3:4] for entry in space_sums))
    pieces.append(sum(entry[6:12] for entry in mid_sums))
    small = jnp.concatenate(pieces, axis=0)
    small = jnp.pad(small, ((0, ROWS - small.shape[0]), (0, 0)))
    gathered, own_u, own_d, own_b, own_c = grad_call(
        clips, frames, small, h3, gup, act, gb3, h2, gqkv_two, mixed_two, gb2,
        hidden_one.reshape(-1, width), gqkv_one, mixed_one.reshape(-1, width), gb1,
    )
    cut = 3 * width
    count = clip_count * 9
    grad_modulation = gathered[:, :count].reshape(clips * clip_count, 9 * width)
    picked = chosen.reshape(clips, 16, 128)[:, :clip_count, :rows].reshape(-1, rows)
    grad_ada = lax.dot_general(
        picked.astype(f32), grad_modulation, (((0,), (0,)), ((), ())), precision=highest
    )
    grad_ada_bias = jnp.sum(grad_modulation, axis=0)
    biases = jnp.sum(gathered[:, count : count + 7], axis=0)

    def own_slice(vector):
        length = vector.shape[0] // owners
        return lax.dynamic_slice_in_dim(vector, owner * length, length, 0)

    outputs = jnp.stack(
        [
            jnp.swapaxes(out, 0, 1).reshape(frame_count, patch_count, width)
            for out in outs
        ]
    )
    return (
        outputs,
        input_grad,
        grad_ada,
        own_slice(grad_ada_bias),
        own_c[:, :cut],
        own_c[:, cut:],
        own_slice(biases[0]),
        own_b[:, :cut],
        own_b[:, cut:],
        own_slice(biases[1]),
        own_u,
        own_slice(biases[2:6].reshape(-1)),
        own_d,
        own_slice(biases[6]),
    )


def solution(mesh):
    tokens = P("clip", "frame", None, None)
    matrix = P(("clip", "frame"), None)
    vector = P(("clip", "frame"))
    in_specs = (
        tokens, tokens, P("clip"), P("clip"), matrix, vector, matrix, matrix, vector, matrix,
        matrix, vector, matrix, vector, matrix, vector,
    )
    out_specs = (
        tokens, tokens, matrix, vector, matrix, matrix, vector, matrix, matrix, vector, matrix,
        vector, matrix, vector,
    )
    return jax.shard_map(shards, mesh=mesh, in_specs=in_specs, out_specs=out_specs, check_vma=False)
```

```python
import functools
import math

import jax
import jax.numpy as jnp
from jax import lax
from jax.experimental import pallas as pl
from jax.experimental.pallas import tpu as pltpu
from jax.sharding import PartitionSpec as P

HEADS = 12
HEAD = 64
PAIRS = HEADS // 2
ROWS = 32
GELU_C = math.sqrt(2.0 / math.pi)
GELU_A = 0.044715
VMEM_LIMIT = 58 << 20

f32 = jnp.float32
bf16 = jnp.bfloat16
highest = lax.Precision.HIGHEST
MESH = pl.DeviceIdType.MESH
VMEM = pltpu.VMEM
DMA = pltpu.SemaphoreType.DMA


def embed_steps(time_steps, model_width):
    half_width = model_width // 2
    frequencies = jnp.exp(
        -math.log(10000.0) * jnp.arange(half_width, dtype=f32) / half_width
    )
    angles = time_steps.astype(f32)[:, None] * frequencies[None, :]
    return jnp.concatenate([jnp.cos(angles), jnp.sin(angles)], axis=1)


def dot(left, right, left_dim, right_dim):
    return lax.dot_general(
        left, right, (((left_dim,), (right_dim,)), ((), ())), preferred_element_type=f32
    )


def flip(index, mask):
    bit = 1
    while bit <= mask:
        if mask & bit:
            index = index + bit * (1 - 2 * ((index // bit) % 2))
        bit *= 2
    return index


def span(masks):
    out = [0]
    for mask in masks:
        out = out + [entry ^ mask for entry in out]
    return out


def frame_masks(frames):
    masks, bit = [], 1
    while bit < frames:
        masks.append(bit)
        bit *= 2
    if len(masks) > 1:
        masks = [frames - 1] + masks[:-1]
    return masks


def clip_tail_masks(clips):
    masks, bit = [], 2
    while bit < clips:
        masks.append(bit)
        bit *= 2
    return masks


def greet(clips, frames):
    clip, frame = lax.axis_index("clip"), lax.axis_index("frame")
    barrier = pltpu.get_barrier_semaphore()
    for step in range(1, clips):
        pl.semaphore_signal(
            barrier, inc=1, device_id={"clip": lax.rem(clip + step, clips)}, device_id_type=MESH
        )
    for step in range(1, frames):
        pl.semaphore_signal(
            barrier, inc=1, device_id={"frame": lax.rem(frame + step, frames)}, device_id_type=MESH
        )
    pl.semaphore_wait(barrier, clips + frames - 2)


def spread(axis, size, source_of, target, send_sems, recv_sems):
    me = lax.axis_index(axis)
    copies = []
    for step in range(1, size):
        peer = lax.rem(me + step, size)
        copy = pltpu.make_async_remote_copy(
            src_ref=source_of(peer),
            dst_ref=target.at[me],
            send_sem=send_sems.at[step - 1],
            recv_sem=recv_sems.at[step - 1],
            device_id={axis: peer},
            device_id_type=MESH,
        )
        copy.start()
        copies.append(copy)
    return copies


def start_kernel(
    clips, frames, clip_count,
    x_ref, cotangent, sh_c, sh_b, sh_u, sh_d, embed, select, ada, bias,
    w_c, w_b, w_u, w_d, mod, chosen, totals, hidden_out, qkv_out, mixed_out, branch_out,
    after_first, after_later, cot_first,
    v_c, z_c, z_b, z_u, z_d, st_w, b_c, b_b, b_u, b_d,
    embeds, parts, terms, arrived, held, lined, hidden, qkv, mixed, branch, after,
    zs, zr, cs, cr, xs, xr, ls, es, er, ps, pr, fs, fr, ts, tr, hs, hr, os, ws,
):
    clip, frame = lax.axis_index("clip"), lax.axis_index("frame")
    shards_in = (sh_c, sh_b, sh_u, sh_d)
    zoned = (z_c, z_b, z_u, z_d)
    blocks = (b_c, b_b, b_u, b_d)
    wholes = (v_c, w_b, w_u, w_d)
    width = mod.shape[1]
    frame_count, tokens = x_ref.shape[1], x_ref.shape[2]
    part = tokens // frames
    greet(clips, frames)
    masks = frame_masks(frames)
    sends = []
    stage = {}

    def frame_step(group, step):
        number = (1 << step) - 1
        copies = []
        for offset in span(masks[:step]):
            slot = flip(frame, offset)
            source = shards_in[group] if offset == 0 else zoned[group].at[slot]
            copy = pltpu.make_async_remote_copy(
                src_ref=source,
                dst_ref=zoned[group].at[slot],
                send_sem=zs.at[group, number],
                recv_sem=zr.at[group, number],
                device_id={"frame": flip(frame, masks[step])},
                device_id_type=MESH,
            )
            copy.start()
            copies.append(copy)
            number += 1
        sends.extend(copies)
        stage[group] = copies

    def frame_rest(group):
        for step in range(1, len(masks)):
            for copy in stage[group]:
                copy.wait_recv()
            frame_step(group, step)

    tail = clip_tail_masks(clips)
    steps = len(tail)
    orders = (tail, tail[::-1])
    moving = {}

    def block_send(group, half, step, position, offset):
        whole = wholes[group]
        block_rows = whole.shape[0] // clips
        columns = whole.shape[1] // 2
        rows = pl.ds(pl.multiple_of(flip(clip, offset) * block_rows, block_rows), block_rows)
        lanes = pl.ds(half * columns, columns)
        target = whole.at[rows, lanes]
        number = (1 << step) - 1 + position
        copy = pltpu.make_async_remote_copy(
            src_ref=blocks[group].at[:, lanes] if offset == 0 else target,
            dst_ref=target,
            send_sem=xs.at[group, half, number],
            recv_sem=xr.at[group, half, number],
            device_id={"clip": flip(clip, orders[half][step])},
            device_id_type=MESH,
        )
        copy.start()
        moving[group, half, number] = copy

    core_copies = {group: [] for group in range(4)}

    def core_send(group, offset):
        whole = wholes[group]
        block_rows = whole.shape[0] // clips
        rows = pl.ds(pl.multiple_of(flip(clip, offset) * block_rows, block_rows), block_rows)
        number = len(core_copies[group])
        copy = pltpu.make_async_remote_copy(
            src_ref=blocks[group] if offset == 0 else whole.at[rows, :],
            dst_ref=whole.at[rows, :],
            send_sem=cs.at[group, number],
            recv_sem=cr.at[group, number],
            device_id={"clip": flip(clip, 1)},
            device_id_type=MESH,
        )
        copy.start()
        core_copies[group].append(copy)

    local_copies = []

    def block_ready(group):
        for copy in stage[group]:
            copy.wait_recv()
        rows, columns = shards_in[group].shape
        block_rows = frames * rows
        if rows % 16:
            for slot in range(frames):
                st_w[slot * rows : (slot + 1) * rows, :columns] = zoned[group][slot].astype(f32)
            blocks[group][...] = st_w[:block_rows, :columns].astype(bf16)
        else:
            for slot in range(frames):
                blocks[group][slot * rows : (slot + 1) * rows, :] = zoned[group][slot]
        for step in range(steps):
            for half in range(2):
                block_send(group, half, step, 0, 0)
        core_send(group, 0)
        place = pl.ds(pl.multiple_of(clip * block_rows, block_rows), block_rows)
        keep = pltpu.make_async_copy(blocks[group], wholes[group].at[place, :], ls.at[group])
        keep.start()
        local_copies.append(keep)

    def block_forward(group):
        for step in range(1, steps):
            for half in range(2):
                for position in range(1 << (step - 1), 1 << step):
                    moving[group, half, position - 1].wait_recv()
                for later in range(step, steps):
                    for position, offset in enumerate(span(orders[half][:later])):
                        if (1 << (step - 1)) <= position < (1 << step):
                            block_send(group, half, later, position, offset)

    def block_finish(group):
        last = (1 << (steps - 1)) - 1
        for half in range(2):
            for number in range(last, (1 << steps) - 1):
                moving[group, half, number].wait_recv()
        for offset in span(tail)[1:]:
            core_send(group, offset)

    def core_finish(group):
        for copy in core_copies[group]:
            copy.wait_recv()

    for group in range(4):
        frame_step(group, 0)
    own = spread("clip", clips, lambda peer: embed, embeds, es, er)
    sends.extend(own)
    embeds[clip] = embed[...]
    for group in range(4):
        zoned[group][frame] = shards_in[group][...]
    for copy in own:
        copy.wait_recv()
    picked = dot(embeds[...].reshape(clips * 16, width), select[...], 1, 0).astype(bf16)
    chosen[...] = picked
    parts[...] = dot(picked, ada[...], 1, 0)
    for peer in range(clips):
        for local in range(clip_count):
            row = peer * 16 + local
            for piece in range(9):
                terms[peer, local * 9 + piece : local * 9 + piece + 1, :] = (
                    parts[row : row + 1, piece * width : (piece + 1) * width]
                    + bias[piece : piece + 1, :]
                )
        base = clip_count * 9
        terms[peer, base : base + 7, :] = bias[9:16, :]
        if base + 7 < ROWS:
            terms[peer, base + 7 : ROWS, :] = jnp.zeros((ROWS - base - 7, width), f32)
    own = spread("clip", clips, lambda peer: terms.at[peer], arrived, ps, pr)
    sends.extend(own)
    arrived[clip] = terms[clip]
    frame_rest(0)
    for copy in own:
        copy.wait_recv()
    total = arrived[0]
    for peer in range(1, clips):
        total = total + arrived[peer]
    held[...] = total
    own = spread("frame", frames, lambda peer: held, lined, fs, fr)
    sends.extend(own)
    lined[frame] = total
    block_ready(0)
    for group in range(1, 4):
        frame_rest(group)

    cot_copies = []
    for step in range(1, frames):
        peer = lax.rem(frame + step, frames)
        copy = pltpu.make_async_remote_copy(
            src_ref=cotangent.at[0, :, pl.ds(pl.multiple_of(peer * part, part), part), :],
            dst_ref=cot_first.at[frame],
            send_sem=ts.at[step - 1],
            recv_sem=tr.at[step - 1],
            device_id={"frame": peer},
            device_id_type=MESH,
        )
        copy.start()
        cot_copies.append(copy)
    keep = pltpu.make_async_copy(
        cotangent.at[0, :, pl.ds(pl.multiple_of(frame * part, part), part), :],
        cot_first.at[frame],
        ls.at[4],
    )
    keep.start()
    local_copies.append(keep)

    for copy in own:
        copy.wait_recv()
    total = lined[0]
    for peer in range(1, frames):
        total = total + lined[peer]
    mod[...] = total
    block_forward(0)
    for group in range(1, 4):
        block_ready(group)
    block_finish(0)
    core_finish(0)
    local_copies[0].wait()

    keep = pltpu.make_async_copy(v_c, w_c, ls.at[5])
    keep.start()
    local_copies.append(keep)

    def after_copy(f, step):
        peer = lax.rem(frame + step, frames)
        return pltpu.make_async_remote_copy(
            src_ref=after.at[f, pl.ds(pl.multiple_of(peer * part, part), part), :],
            dst_ref=after_first.at[frame, f],
            send_sem=hs.at[f, step - 1],
            recv_sem=hr.at[f, step - 1],
            device_id={"frame": peer},
            device_id_type=MESH,
        )

    def own_after(f):
        return pltpu.make_async_copy(
            after.at[f, pl.ds(pl.multiple_of(frame * part, part), part), :],
            after_first.at[frame, f],
            os.at[f],
        )

    def later_after(f):
        return pltpu.make_async_copy(after.at[f], after_later.at[f - frame_count], os.at[f])

    kept = ((hidden, hidden_out), (qkv, qkv_out), (mixed, mixed_out), (branch, branch_out))

    def write_back(f):
        return [
            pltpu.make_async_copy(source.at[f], target.at[f], ws.at[number, f])
            for number, (source, target) in enumerate(kept)
        ]

    for local in range(clip_count):
        row = local * 9

        def one_frame(index, carry):
            f = local * frame_count + index
            values = x_ref[local, index].astype(f32)
            norm, _ = normed(values)
            scaled = norm * (1.0 + mod[row + 1 : row + 2, :]) + mod[row : row + 1, :]
            lowered = scaled.astype(bf16)
            hidden[f] = lowered
            qkv[f] = dot(lowered, v_c[:, : 3 * width], 1, 0).astype(bf16)
            attend(qkv.at[f], mixed.at[f], totals.at[f], width, None)
            grown = dot(mixed[f], v_c[:, 3 * width :], 1, 0) + mod[18:19, :]
            branch[f] = grown.astype(bf16)
            after[f] = (values + mod[row + 2 : row + 3, :] * grown).astype(bf16)
            if local == 0:
                for step in range(1, frames):
                    after_copy(f, step).start()
                own_after(f).start()
            else:
                later_after(f).start()
            for copy in write_back(f):
                copy.start()
            return carry

        lax.fori_loop(0, frame_count, one_frame, 0)
        if local == 0:
            block_forward(1)
    for group in range(2, 4):
        block_forward(group)
    for group in range(1, 4):
        block_finish(group)
    for group in range(1, 4):
        core_finish(group)

    def settle(f, carry):
        for step in range(1, frames):
            copy = after_copy(f, step)
            copy.wait_recv()
            copy.wait_send()
        own_after(f).wait()
        return carry

    lax.fori_loop(0, frame_count, settle, 0)

    def settle_later(f, carry):
        later_after(f).wait()
        return carry

    lax.fori_loop(frame_count, clip_count * frame_count, settle_later, 0)

    def settle_kept(f, carry):
        for copy in write_back(f):
            copy.wait()
        return carry

    lax.fori_loop(0, clip_count * frame_count, settle_kept, 0)
    for copy in cot_copies:
        copy.wait_recv()
        copy.wait_send()
    for copy in local_copies[1:]:
        copy.wait()
    for copy in moving.values():
        copy.wait_send()
    for group in range(4):
        for copy in core_copies[group]:
            copy.wait_send()
    for copy in sends:
        copy.wait_send()


def start_call(
    clips, frames, inputs, cotangent, sh_c, sh_b, sh_u, sh_d, embed, select, ada, bias
):
    clip_count, frame_count, tokens, width = inputs.shape
    rows, columns = sh_c.shape
    rows_d = sh_d.shape[0]
    block = frames * rows
    block_d = frames * rows_d
    peers = max(clips // 2 - 1, 1)
    total = clip_count * frame_count
    part = tokens // frames
    whole = jax.ShapeDtypeStruct((clips * block, columns), bf16)
    vmem = pl.BlockSpec(memory_space=VMEM)
    hbm = pl.BlockSpec(memory_space=pl.ANY)
    zoned = lambda height, lanes: VMEM((frames, height, lanes), bf16)
    saved = lambda lanes: jax.ShapeDtypeStruct((total, tokens, lanes), bf16)
    lent = lambda lanes: VMEM((total, tokens, lanes), bf16)
    traded = jax.ShapeDtypeStruct((frames, frame_count, part, width), bf16)
    return pl.pallas_call(
        functools.partial(start_kernel, clips, frames, clip_count),
        out_shape=(
            whole, whole, whole,
            jax.ShapeDtypeStruct((clips * block_d, width), bf16),
            jax.ShapeDtypeStruct((ROWS, width), f32),
            jax.ShapeDtypeStruct((clips * 16, 128), bf16),
            jax.ShapeDtypeStruct((total, 16, tokens), f32),
            saved(width), saved(3 * width), saved(width), saved(width),
            traded,
            jax.ShapeDtypeStruct(((clip_count - 1) * frame_count, tokens, width), bf16),
            traded,
        ),
        in_specs=[vmem, hbm] + [vmem] * 8,
        out_specs=(hbm, hbm, hbm, hbm, vmem, vmem, vmem) + (hbm,) * 7,
        scratch_shapes=[
            VMEM((clips * block, columns), bf16),
            zoned(rows, columns), zoned(rows, columns), zoned(rows, columns), zoned(rows_d, width),
            VMEM((max(block, block_d), columns), f32),
            VMEM((block, columns), bf16),
            VMEM((block, columns), bf16),
            VMEM((block, columns), bf16),
            VMEM((block_d, width), bf16),
            VMEM((clips, 16, width), bf16),
            VMEM((clips * 16, 9 * width), f32),
            VMEM((clips, ROWS, width), f32),
            VMEM((clips, ROWS, width), f32),
            VMEM((ROWS, width), f32),
            VMEM((frames, ROWS, width), f32),
            lent(width), lent(3 * width), lent(width), lent(width), lent(width),
            DMA((4, frames - 1)), DMA((4, frames - 1)),
            DMA((4, clips // 2)), DMA((4, clips // 2)),
            DMA((4, 2, peers)), DMA((4, 2, peers)),
            DMA((6,)),
            DMA((clips - 1,)), DMA((clips - 1,)),
            DMA((clips - 1,)), DMA((clips - 1,)),
            DMA((frames - 1,)), DMA((frames - 1,)),
            DMA((frames - 1,)), DMA((frames - 1,)),
            DMA((frame_count, frames - 1)), DMA((frame_count, frames - 1)),
            DMA((total,)),
            DMA((4, total)),
        ],
        compiler_params=pltpu.CompilerParams(
            collective_id=0, has_side_effects=True, vmem_limit_bytes=VMEM_LIMIT
        ),
    )(inputs, cotangent, sh_c, sh_b, sh_u, sh_d, embed, select, ada, bias)


STEP = 512
SLOTS = 3


def grad_kernel(
    clips, frames,
    small, h3, gup, act, gb3, h2, gqkv2, mix2, gb2, h1, gqkv1, mix1, gb1,
    gathered, out_u, out_d, out_b, out_c,
    sum_w, sum_d, core_w, core_d, side_w, side_d, line_w, line_d, last_w, last_d,
    left, right, total, lined, held,
    lsem, rsem, cs, cr, xs, xr, zs, zr, fs, fr, ps, pr,
):
    clip, frame = lax.axis_index("clip"), lax.axis_index("frame")
    tokens = h3.shape[0]
    width = small.shape[1]
    wide = sum_w.shape[-1]
    narrow = sum_d.shape[-1]
    tail = clip_tail_masks(clips)
    orders = (tail, tail[::-1])
    masks = frame_masks(frames)
    greet(clips, frames)
    first = spread("frame", frames, lambda peer: small, lined, fs, fr)
    lined[frame] = small[...]

    chunks = [
        (1, 0, [(act, gb3, 0, 0, narrow)], out_d, 0),
        (1, 1, [(act, gb3, narrow, 0, narrow)], out_d, narrow),
        (0, 0, [(h3, gup, 0, 0, wide)], out_u, 0),
        (0, 1, [(h3, gup, wide, 0, wide)], out_u, wide),
        (0, 2, [(h2, gqkv2, 0, 0, wide)], out_b, 0),
        (0, 3, [(h2, gqkv2, wide, 0, width), (mix2, gb2, 0, width, width)], out_b, wide),
        (0, 4, [(h1, gqkv1, 0, 0, wide)], out_c, 0),
        (0, 5, [(h1, gqkv1, wide, 0, width), (mix1, gb1, 0, width, width)], out_c, wide),
    ]
    sums, cores, sides = (sum_w, sum_d), (core_w, core_d), (side_w, side_d)
    lines, lasts = (line_w, line_d), (last_w, last_d)
    flights = {}

    steps = tokens // STEP
    line_up = []
    for kind, _, parts, _, _ in chunks:
        for part in parts:
            for group in range(part[0].shape[1] // width):
                line_up.append(part[:3] + (part[3] + group * part[4], part[4], group))
    begins = [0]
    for kind, _, parts, _, _ in chunks:
        begins.append(begins[-1] + sum(part[0].shape[1] // width for part in parts))

    def load(entry, step, slot):
        one, other, begin, _, lanes, group = line_up[entry]
        rows = pl.ds(pl.multiple_of(step * STEP, STEP), STEP)
        return (
            pltpu.make_async_copy(
                one.at[rows, pl.ds(group * width, width)], left.at[slot], lsem.at[slot]
            ),
            pltpu.make_async_copy(
                other.at[rows, pl.ds(begin, lanes)],
                right.at[slot, :, pl.ds(0, lanes)],
                rsem.at[slot],
            ),
        )

    def place_of(entry, step):
        return lax.rem(entry * steps + step, SLOTS)

    def multiply(number):
        kind, place = chunks[number][:2]
        for entry in range(begins[number], begins[number + 1]):
            at, lanes = line_up[entry][3:5]

            def body(step, carry):
                ahead = step + SLOTS - 1

                @pl.when(ahead < steps)
                def _():
                    for copy in load(entry, ahead, place_of(entry, ahead)):
                        copy.start()

                if entry + 1 < len(line_up):

                    @pl.when(ahead >= steps)
                    def _():
                        for copy in load(entry + 1, ahead - steps, place_of(entry, ahead)):
                            copy.start()

                slot = place_of(entry, step)
                for copy in load(entry, step, slot):
                    copy.wait()
                product = dot(left[slot], right[slot, :, :lanes], 0, 0)
                columns = slice(at, at + lanes)

                @pl.when(step == 0)
                def _():
                    total[:, columns] = product

                @pl.when(step > 0)
                def _():
                    total[:, columns] += product

                return carry

            lax.fori_loop(0, steps, body, 0)
        rows, lanes = sums[kind].shape[2:]
        for block in range(clips):
            begin = block * rows
            column = begin // width * lanes
            begin = begin % width
            sums[kind][place, block] = total[begin : begin + rows, column : column + lanes].astype(
                bf16
            )

    def core_start(number):
        kind, place = chunks[number][:2]
        copies = []
        for position, offset in enumerate(span(tail)):
            copy = pltpu.make_async_remote_copy(
                src_ref=sums[kind].at[place, flip(clip, offset ^ 1)],
                dst_ref=cores[kind].at[place, position],
                send_sem=cs.at[number, position],
                recv_sem=cr.at[number, position],
                device_id={"clip": flip(clip, 1)},
                device_id_type=MESH,
            )
            copy.start()
            copies.append(copy)
        flights[number, "core"] = copies

    def half_of(kind, half):
        if kind:
            rows = sums[kind].shape[2] // 2
            return (slice(half * rows, (half + 1) * rows), slice(None))
        lanes = sums[kind].shape[3] // 2
        return (slice(None), slice(half * lanes, (half + 1) * lanes))

    def side_start(number, step):
        kind, place = chunks[number][:2]
        copies = []
        for half in range(2):
            mask = orders[half][step]
            for position, offset in enumerate(span(orders[half][:step])):
                entry = (1 << step) - 1 + position
                copy = pltpu.make_async_remote_copy(
                    src_ref=sums[kind].at[(place, flip(clip, offset ^ mask)) + half_of(kind, half)],
                    dst_ref=sides[kind].at[place, half, entry],
                    send_sem=xs.at[number, half, entry],
                    recv_sem=xr.at[number, half, entry],
                    device_id={"clip": flip(clip, mask)},
                    device_id_type=MESH,
                )
                copy.start()
                copies.append(copy)
        flights[number, "side", step] = copies

    def core_add(number):
        kind, place = chunks[number][:2]
        for copy in flights[number, "core"]:
            copy.wait_recv()
        for position, offset in enumerate(span(tail)):
            block = flip(clip, offset)
            sums[kind][place, block] = (
                sums[kind][place, block].astype(f32) + cores[kind][place, position].astype(f32)
            ).astype(bf16)
        side_start(number, len(tail) - 1)

    def side_add(number, step):
        kind, place = chunks[number][:2]
        for copy in flights[number, "side", step]:
            copy.wait_recv()
        for half in range(2):
            for position, offset in enumerate(span(orders[half][:step])):
                entry = (1 << step) - 1 + position
                block = flip(clip, offset)
                where = (place, block) + half_of(kind, half)
                sums[kind][where] = (
                    sums[kind][where].astype(f32) + sides[kind][place, half, entry].astype(f32)
                ).astype(bf16)
        if step:
            side_start(number, step - 1)
        else:
            rows = lines[kind].shape[2]
            block = sums[kind][place, clip].astype(f32)
            for slot in range(frames):
                lines[kind][place, slot] = block[slot * rows : (slot + 1) * rows, :].astype(bf16)
            line_start(number, len(masks) - 1)

    def line_start(number, step):
        kind, place = chunks[number][:2]
        copies = []
        for position, offset in enumerate(span(masks[:step])):
            entry = (1 << step) - 1 + position
            copy = pltpu.make_async_remote_copy(
                src_ref=lines[kind].at[place, flip(frame, offset ^ masks[step])],
                dst_ref=lasts[kind].at[place, entry],
                send_sem=zs.at[number, entry],
                recv_sem=zr.at[number, entry],
                device_id={"frame": flip(frame, masks[step])},
                device_id_type=MESH,
            )
            copy.start()
            copies.append(copy)
        flights[number, "line", step] = copies

    def line_add(number, step):
        kind, place, _, target, begin = chunks[number]
        for copy in flights[number, "line", step]:
            copy.wait_recv()
        for position, offset in enumerate(span(masks[:step])):
            entry = (1 << step) - 1 + position
            slot = flip(frame, offset)
            value = lines[kind][place, slot].astype(f32) + lasts[kind][place, entry].astype(f32)
            if step:
                lines[kind][place, slot] = value.astype(bf16)
            else:
                target[:, begin : begin + value.shape[1]] = value
        if step:
            line_start(number, step - 1)

    stages = [core_start, core_add]
    for step in range(len(tail))[::-1]:
        stages.append(functools.partial(side_add, step=step))
    for step in range(len(masks))[::-1]:
        stages.append(functools.partial(line_add, step=step))

    for step in range(SLOTS - 1):
        for copy in load(0, step, step):
            copy.start()
    second = None
    lags = [0, 1, 3]
    while len(lags) < len(stages):
        lags.append(lags[-1] + 1)
    for turn in range(len(chunks) + lags[-1]):
        for depth in range(len(stages))[::-1]:
            if depth > 0 and 0 <= turn - lags[depth] < len(chunks):
                stages[depth](turn - lags[depth])
        if turn < len(chunks):
            multiply(turn)
            core_start(turn)
        if turn == 0:
            for copy in first:
                copy.wait_recv()
            summed = lined[0]
            for peer in range(1, frames):
                summed = summed + lined[peer]
            held[...] = summed
            second = spread("clip", clips, lambda peer: held, gathered, ps, pr)
            gathered[clip] = summed
    for copy in second:
        copy.wait_recv()
    for copy in first + second:
        copy.wait_send()
    for copies in flights.values():
        for copy in copies:
            copy.wait_send()


def grad_call(clips, frames, small, *operands):
    h3, gup, act = operands[:3]
    width, hidden = h3.shape[1], act.shape[1]
    owners = clips * frames
    wide, narrow = hidden // 2, width // 2
    rows_w, rows_d = width // owners, hidden // owners
    peers = max(clips // 2 - 1, 1)
    vmem = pl.BlockSpec(memory_space=VMEM)
    hbm = pl.BlockSpec(memory_space=pl.ANY)

    return pl.pallas_call(
        functools.partial(grad_kernel, clips, frames),
        out_shape=(
            jax.ShapeDtypeStruct((clips,) + small.shape, f32),
            jax.ShapeDtypeStruct((rows_w, hidden), f32),
            jax.ShapeDtypeStruct((rows_d, width), f32),
            jax.ShapeDtypeStruct((rows_w, hidden), f32),
            jax.ShapeDtypeStruct((rows_w, hidden), f32),
        ),
        in_specs=[vmem] + [hbm] * len(operands),
        out_specs=(vmem,) * 5,
        scratch_shapes=[
            VMEM((6, clips, rows_w * frames, wide), bf16),
            VMEM((2, clips, rows_d * frames, narrow), bf16),
            VMEM((6, clips // 2, rows_w * frames, wide), bf16),
            VMEM((2, clips // 2, rows_d * frames, narrow), bf16),
            VMEM((6, 2, peers, rows_w * frames, wide // 2), bf16),
            VMEM((2, 2, peers, rows_d * frames // 2, narrow), bf16),
            VMEM((6, frames, rows_w, wide), bf16),
            VMEM((2, frames, rows_d, narrow), bf16),
            VMEM((6, frames - 1, rows_w, wide), bf16),
            VMEM((2, frames - 1, rows_d, narrow), bf16),
            VMEM((SLOTS, STEP, width), bf16),
            VMEM((SLOTS, STEP, wide), bf16),
            VMEM((width, wide), f32),
            VMEM((frames,) + small.shape, f32),
            VMEM(small.shape, f32),
            DMA((SLOTS,)), DMA((SLOTS,)),
            DMA((8, clips // 2)), DMA((8, clips // 2)),
            DMA((8, 2, peers)), DMA((8, 2, peers)),
            DMA((8, frames - 1)), DMA((8, frames - 1)),
            DMA((frames - 1,)), DMA((frames - 1,)),
            DMA((clips - 1,)), DMA((clips - 1,)),
        ],
        compiler_params=pltpu.CompilerParams(
            collective_id=1, has_side_effects=True, vmem_limit_bytes=VMEM_LIMIT
        ),
    )(small, *operands)


def normed(values):
    centred = values - jnp.mean(values, axis=-1, keepdims=True)
    scale = lax.rsqrt(jnp.mean(centred * centred, axis=-1, keepdims=True) + 1e-06)
    return centred * scale, scale


def norm_back(grad, scaled, norm, scale):
    inner = grad * scaled
    return scale * (
        inner
        - jnp.mean(inner, axis=-1, keepdims=True)
        - norm * jnp.mean(inner * norm, axis=-1, keepdims=True)
    )


def column_sum(values):
    return jnp.sum(values, axis=0, keepdims=True)


def attend(qkv, mixed, totals, width, mask):
    tokens = qkv.shape[0]
    low = lax.broadcasted_iota(jnp.int32, (tokens, 128), 1) < HEAD
    for pair in range(PAIRS):
        at = pair * 128
        queries = qkv[:, at : at + 128] * bf16(0.125)
        keys = qkv[:, width + at : width + at + 128]
        values = qkv[:, 2 * width + at : 2 * width + at + 128]
        halves = []
        for half in range(2):
            own = jnp.where(low if half == 0 else ~low, queries, bf16(0))
            scores = dot(keys, own, 1, 1)
            if mask is not None:
                scores = scores + mask[...]
            peak = jnp.max(scores, axis=0, keepdims=True)
            terms = jnp.exp(scores - peak)
            total = jnp.sum(terms, axis=0, keepdims=True)
            weights = (terms * (1.0 / total)).astype(bf16)
            totals[2 * pair + half : 2 * pair + half + 1, :] = peak + jnp.log(total)
            halves.append(dot(weights, values, 0, 0))
        mixed[:, at : at + 128] = jnp.where(low, halves[0], halves[1]).astype(bf16)


def attend_back(qkv, grad_mixed, totals, grad_qkv, width, mask):
    tokens = qkv.shape[0]
    low = lax.broadcasted_iota(jnp.int32, (tokens, 128), 1) < HEAD
    for pair in range(PAIRS):
        at = pair * 128
        queries = qkv[:, at : at + 128]
        keys = qkv[:, width + at : width + at + 128]
        values = qkv[:, 2 * width + at : 2 * width + at + 128]
        grads = grad_mixed[:, at : at + 128]
        halves = []
        for half in range(2):
            pick = low if half == 0 else ~low
            own = jnp.where(pick, queries * bf16(0.125), bf16(0))
            own_grads = jnp.where(pick, grads, bf16(0))
            scores = dot(keys, own, 1, 1)
            if mask is not None:
                scores = scores + mask[...]
            weights = jnp.exp(scores - totals[2 * pair + half : 2 * pair + half + 1, :])
            grad_weights = dot(values, own_grads, 1, 1)
            inner = jnp.sum(weights * grad_weights, axis=0, keepdims=True)
            grad_scores = (weights * (grad_weights - inner)).astype(bf16)
            halves.append(
                (
                    dot(grad_scores, keys, 0, 0),
                    dot(grad_scores, queries, 1, 0),
                    dot(weights.astype(bf16), grads, 1, 0),
                )
            )
        for part, factor in ((0, 0.125), (1, 0.125), (2, 1.0)):
            joined = jnp.where(low, halves[0][part], halves[1][part]) * factor
            start = part * width + at
            grad_qkv[:, start : start + 128] = joined.astype(bf16)


def full(shape):
    return pl.BlockSpec(shape, lambda *_: (0,) * len(shape), pipeline_mode=pl.Buffered(1))


def middle_kernel(
    clips, frames, tiles,
    after_first, cot_first, after_later, cotangent, loss, mod, w_b, w_u, w_d,
    act_ref, gup_ref, h3_ref, gb3_ref, mixed_ref, gb2_ref, h2_ref, gqkv_ref, sums,
    after_second, cot_second, grad_first, out_first, grad_later, out_later,
    qkv, totals, mask, gmix, after_tile, cot_tile, grad_stage, out_stage,
    ts, tr, us, ur, gs, gr, os, orr, ls, ks, ws,
):
    frame = lax.axis_index("frame")
    step = pl.program_id(0)
    last = pl.num_programs(0) - 1
    clip = lax.div(step, tiles)
    tile = lax.rem(step, tiles)
    slot = lax.rem(step, 2)
    width = mod.shape[1]
    frame_count, group = after_tile.shape[2], after_tile.shape[3]
    part = tiles * group
    tokens = frames * frame_count * group
    row = clip * 9
    piece = lambda number: mod[pl.ds(row + number, 1), :]

    def own_part(index):
        return pl.ds(pl.multiple_of(index * part, part), part)

    def later_copies():
        copies = []
        for hop in range(1, frames):
            peer = lax.rem(frame + hop, frames)
            for source, target, send, recv in (
                (after_later.at[:, own_part(peer), :], after_second, ts, tr),
                (cotangent.at[1, :, own_part(peer), :], cot_second, us, ur),
            ):
                copies.append(
                    pltpu.make_async_remote_copy(
                        src_ref=source,
                        dst_ref=target.at[frame],
                        send_sem=send.at[hop - 1],
                        recv_sem=recv.at[hop - 1],
                        device_id={"frame": peer},
                        device_id_type=MESH,
                    )
                )
        return copies[0::2] + copies[1::2]

    def own_copies():
        return (
            pltpu.make_async_copy(
                after_later.at[:, own_part(frame), :], after_second.at[frame], ks.at[0]
            ),
            pltpu.make_async_copy(
                cotangent.at[1, :, own_part(frame), :], cot_second.at[frame], ks.at[1]
            ),
        )

    def load(source, other, index, place):
        rows = pl.ds(pl.multiple_of(index * group, group), group)
        return (
            pltpu.make_async_copy(source.at[:, :, rows, :], after_tile.at[place], ls.at[place, 0]),
            pltpu.make_async_copy(other.at[:, :, rows, :], cot_tile.at[place], ls.at[place, 1]),
        )

    def tile_copies(index):
        rows = pl.ds(pl.multiple_of(index * group, group), group)
        far = pl.ds(pl.multiple_of(frame * part + index * group, group), group)
        copies = []
        for hop in range(1, frames):
            peer = lax.rem(frame + hop, frames)
            for source, target, send, recv in (
                (grad_stage, grad_first.at[frame, :, rows, :], gs, gr),
                (out_stage, out_first.at[:, far, :], os, orr),
            ):
                copies.append(
                    pltpu.make_async_remote_copy(
                        src_ref=source.at[index, peer],
                        dst_ref=target,
                        send_sem=send.at[index, hop - 1],
                        recv_sem=recv.at[index, hop - 1],
                        device_id={"frame": peer},
                        device_id_type=MESH,
                    )
                )
        return copies

    def tile_own(index):
        rows = pl.ds(pl.multiple_of(index * group, group), group)
        far = pl.ds(pl.multiple_of(frame * part + index * group, group), group)
        return (
            pltpu.make_async_copy(
                grad_stage.at[index, frame], grad_first.at[frame, :, rows, :], ws.at[0, index]
            ),
            pltpu.make_async_copy(
                out_stage.at[index, frame], out_first.at[:, far, :], ws.at[1, index]
            ),
        )

    def tile_later(index):
        place = index + tiles
        rows = pl.ds(pl.multiple_of(index * group, group), group)
        return (
            pltpu.make_async_copy(
                grad_stage.at[place], grad_later.at[:, :, rows, :], ws.at[0, place]
            ),
            pltpu.make_async_copy(
                out_stage.at[place], out_later.at[:, :, rows, :], ws.at[1, place]
            ),
        )

    @pl.when(step == 0)
    def _():
        barrier = pltpu.get_barrier_semaphore()
        for hop in range(1, frames):
            pl.semaphore_signal(
                barrier,
                inc=1,
                device_id={"frame": lax.rem(frame + hop, frames)},
                device_id_type=MESH,
            )
        pl.semaphore_wait(barrier, frames - 1)
        for copy in load(after_first, cot_first, 0, 0):
            copy.start()
        for copy in later_copies():
            copy.start()
        for copy in own_copies():
            copy.start()
        first = lax.broadcasted_iota(jnp.int32, (tokens, tokens), 0)
        second = lax.broadcasted_iota(jnp.int32, (tokens, tokens), 1)
        mask[...] = jnp.where(lax.rem(first, group) == lax.rem(second, group), 0.0, -1e30)

    @pl.when(step == tiles)
    def _():
        for copy in later_copies():
            copy.wait_recv()
        for copy in own_copies():
            copy.wait()
        for copy in load(after_second, cot_second, 0, slot):
            copy.start()

    for copy in load(after_first, cot_first, 0, slot):
        copy.wait()

    @pl.when(step + 1 < tiles)
    def _():
        for copy in load(after_first, cot_first, step + 1, 1 - slot):
            copy.start()

    @pl.when((step >= tiles) & (step < last))
    def _():
        for copy in load(after_second, cot_second, tile + 1, 1 - slot):
            copy.start()

    @pl.when(tile == 0)
    def _():
        sums[...] = jnp.zeros_like(sums)

    def add(place, values):
        sums[place : place + 1, :] += values

    after = after_tile[slot].reshape(tokens, width).astype(f32)
    norm, scale = normed(after)
    hidden = (norm * (1.0 + piece(4)) + piece(3)).astype(bf16)
    h2_ref[...] = hidden
    qkv[...] = dot(hidden, w_b[:, : 3 * width], 1, 0).astype(bf16)
    attend(qkv, mixed_ref, totals, width, mask)
    branch_two = dot(mixed_ref[...], w_b[:, 3 * width :], 1, 0) + mod[19:20, :]
    after_two = after + piece(5) * branch_two
    norm_three, scale_three = normed(after_two)
    hidden = (norm_three * (1.0 + piece(7)) + piece(6)).astype(bf16)
    h3_ref[...] = hidden
    grad_out = cot_tile[slot].reshape(tokens, width).astype(f32) * loss[pl.ds(clip, 1), :]
    grad_branch = (grad_out * piece(8)).astype(bf16)
    gb3_ref[...] = grad_branch
    add(11, column_sum(grad_branch.astype(f32)))
    branch_three = jnp.zeros((tokens, width), f32)
    grad_hidden = jnp.zeros((tokens, width), f32)
    for chunk in range(w_u.shape[1] // width):
        cut = slice(chunk * width, (chunk + 1) * width)
        upper = dot(hidden, w_u[:, cut], 1, 0) + mod[20 + chunk : 21 + chunk, :]
        square = upper * upper
        bend = jnp.tanh(upper * (GELU_C + (GELU_C * GELU_A) * square))
        half = 0.5 + 0.5 * bend
        act = (upper * half).astype(bf16)
        slope = half + (0.5 * upper) * (1.0 - bend * bend) * (
            GELU_C + (3.0 * GELU_C * GELU_A) * square
        )
        act_ref[:, cut] = act
        branch_three += dot(act, w_d[cut, :], 1, 0)
        grad_upper = (dot(grad_branch, w_d[cut, :], 1, 1) * slope).astype(bf16)
        gup_ref[:, cut] = grad_upper
        add(7 + chunk, column_sum(grad_upper.astype(f32)))
        grad_hidden += dot(grad_upper, w_u[:, cut], 1, 1)
    branch_three += mod[24:25, :]
    out = (after_two + piece(8) * branch_three).astype(bf16)
    out_stage[step] = out.reshape(out_stage.shape[1:])
    add(5, column_sum(grad_out * branch_three))
    add(3, column_sum(grad_hidden))
    add(4, column_sum(grad_hidden * norm_three))
    grad_two = grad_out + norm_back(grad_hidden, 1.0 + piece(7), norm_three, scale_three)
    add(2, column_sum(grad_two * branch_two))
    grad_branch = (grad_two * piece(5)).astype(bf16)
    gb2_ref[...] = grad_branch
    add(6, column_sum(grad_branch.astype(f32)))
    gmix[...] = dot(grad_branch, w_b[:, 3 * width :], 1, 1).astype(bf16)
    attend_back(qkv, gmix, totals, gqkv_ref, width, mask)
    grad_hidden = dot(gqkv_ref[...], w_b[:, : 3 * width], 1, 1).astype(bf16).astype(f32)
    add(0, column_sum(grad_hidden))
    add(1, column_sum(grad_hidden * norm))
    grad_one = grad_two + norm_back(grad_hidden, 1.0 + piece(4), norm, scale)
    grad_stage[step] = grad_one.astype(bf16).reshape(grad_stage.shape[1:])

    @pl.when(step < tiles)
    def _():
        for copy in tile_copies(tile):
            copy.start()
        for copy in tile_own(tile):
            copy.start()

    @pl.when(step >= tiles)
    def _():
        for copy in tile_later(tile):
            copy.start()

    @pl.when(step == last)
    def _():
        for copy in later_copies():
            copy.wait_send()

        def settle(index, carry):
            for copy in tile_copies(index):
                copy.wait_send()
                copy.wait_recv()
            for copy in tile_own(index) + tile_later(index):
                copy.wait()
            return carry

        lax.fori_loop(0, tiles, settle, 0)


def middle_call(
    clips, frames, after_first, cot_first, after_later, cotangent, loss, mod, w_b, w_u, w_d
):
    _, frame_count, part, width = after_first.shape
    group = min(16, part)
    tiles = part // group
    tokens = frames * frame_count * group
    hidden_width = w_u.shape[1]
    widths = (hidden_width, hidden_width, width, width, width, width, width, 3 * width)
    own = lambda columns: pl.BlockSpec((tokens, columns), lambda t: (t, 0))
    hbm = pl.BlockSpec(memory_space=pl.ANY)
    rows = 2 * tiles * tokens
    traded = jax.ShapeDtypeStruct(after_first.shape, bf16)
    slab = (frames, frame_count, group, width)
    return pl.pallas_call(
        functools.partial(middle_kernel, clips, frames, tiles),
        grid=(2 * tiles,),
        in_specs=[
            hbm, hbm, hbm, hbm, full(loss.shape), full(mod.shape), full(w_b.shape),
            full(w_u.shape), full(w_d.shape),
        ],
        out_specs=[own(columns) for columns in widths]
        + [pl.BlockSpec((None, 16, width), lambda t: (t // tiles, 0, 0))]
        + [hbm] * 6,
        out_shape=[jax.ShapeDtypeStruct((rows, columns), bf16) for columns in widths]
        + [
            jax.ShapeDtypeStruct((2, 16, width), f32),
            traded, traded, traded,
            jax.ShapeDtypeStruct((frame_count, frames * part, width), bf16),
            traded, traded,
        ],
        scratch_shapes=[
            VMEM((tokens, 3 * width), bf16),
            VMEM((16, tokens), f32),
            VMEM((tokens, tokens), f32),
            VMEM((tokens, width), bf16),
            VMEM((2,) + slab, bf16),
            VMEM((2,) + slab, bf16),
            VMEM((2 * tiles,) + slab, bf16),
            VMEM((2 * tiles,) + slab, bf16),
            DMA((frames - 1,)), DMA((frames - 1,)),
            DMA((frames - 1,)), DMA((frames - 1,)),
            DMA((tiles, frames - 1)), DMA((tiles, frames - 1)),
            DMA((tiles, frames - 1)), DMA((tiles, frames - 1)),
            DMA((2, 2)), DMA((2,)), DMA((2, 2 * tiles)),
        ],
        compiler_params=pltpu.CompilerParams(
            collective_id=2, has_side_effects=True, vmem_limit_bytes=VMEM_LIMIT
        ),
    )(after_first, cot_first, after_later, cotangent, loss, mod, w_b, w_u, w_d)


def space_back_kernel(
    clip, grad_ref, x_ref, mod, w_c, qkv, branch, totals,
    out_ref, gb_ref, gqkv_ref, sums, gmix,
):
    width = x_ref.shape[-1]
    tokens = x_ref.shape[-2]
    row = clip * 9
    piece = lambda number: mod[row + number : row + number + 1, :]

    @pl.when(pl.program_id(0) == 0)
    def _():
        sums[...] = jnp.zeros_like(sums)

    grad = grad_ref[...].reshape(tokens, width).astype(f32)
    grad_branch = (grad * piece(2)).astype(bf16)
    gb_ref[...] = grad_branch
    sums[2:3, :] += column_sum(grad * branch[...].astype(f32))
    sums[3:4, :] += column_sum(grad_branch.astype(f32))
    gmix[...] = dot(grad_branch, w_c[:, 3 * width :], 1, 1).astype(bf16)
    attend_back(qkv, gmix, totals, gqkv_ref, width, None)
    grad_hidden = dot(gqkv_ref[...], w_c[:, : 3 * width], 1, 1)
    norm, scale = normed(x_ref[...].reshape(tokens, width).astype(f32))
    sums[0:1, :] += column_sum(grad_hidden)
    sums[1:2, :] += column_sum(grad_hidden * norm)
    result = grad + norm_back(grad_hidden, 1.0 + piece(1), norm, scale)
    out_ref[...] = result.reshape(out_ref.shape)


def space_back_next(count, clip, *refs):
    space_back_kernel(clip, *refs[:7], *refs[7 + count :])


def space_back_call(clip, grad, x, mod, w_c, qkv, branch, totals, earlier):
    clip_count, frame_count, tokens, width = x.shape
    frames = grad.shape[0]
    part = grad.shape[2]
    rows = frame_count * tokens
    by_frame = lambda columns: pl.BlockSpec(
        (None, tokens, columns), lambda f: (clip * frame_count + f, 0, 0)
    )
    own = lambda columns: pl.BlockSpec((tokens, columns), lambda f: (clip * frame_count + f, 0))
    in_specs = [
        pl.BlockSpec((frames, 1, part, width), lambda f: (0, f, 0, 0)),
        pl.BlockSpec((1, 1, tokens, width), lambda f: (clip, f, 0, 0)),
        full(mod.shape),
        full(w_c.shape),
        by_frame(3 * width),
        by_frame(width),
        pl.BlockSpec((None, 16, tokens), lambda f: (clip * frame_count + f, 0, 0)),
    ]
    args = [grad, x, mod, w_c, qkv, branch, totals]
    body = functools.partial(space_back_kernel, clip)
    aliases = {}
    if earlier is not None:
        in_specs += [pl.BlockSpec(memory_space=pl.ANY)] * len(earlier)
        args += list(earlier)
        aliases = {7 + number: number for number in range(len(earlier))}
        body = functools.partial(space_back_next, len(earlier), clip)
    return pl.pallas_call(
        body,
        grid=(frame_count,),
        in_specs=in_specs,
        out_specs=[
            pl.BlockSpec((1, 1, tokens, width), lambda f: (clip, f, 0, 0)),
            own(width),
            own(3 * width),
            pl.BlockSpec((8, width), lambda f: (0, 0)),
        ],
        out_shape=[
            jax.ShapeDtypeStruct(x.shape, f32),
            jax.ShapeDtypeStruct((clip_count * rows, width), bf16),
            jax.ShapeDtypeStruct((clip_count * rows, 3 * width), bf16),
            jax.ShapeDtypeStruct((8, width), f32),
        ],
        scratch_shapes=[VMEM((tokens, width), bf16)],
        input_output_aliases=aliases,
        compiler_params=pltpu.CompilerParams(vmem_limit_bytes=VMEM_LIMIT),
        cost_estimate=pl.CostEstimate(
            flops=rows * 20_000_000, bytes_accessed=rows * width * 20, transcendentals=0
        ),
    )(*args)


def shards(
    inputs, cotangent, time_steps, weight_index, ada_weight, ada_bias, space_qkv, space_out,
    space_out_bias, time_qkv, time_out, time_out_bias, up_weight, up_bias, down_weight, down_bias,
):
    clip_count, frame_count, patch_count, width = inputs.shape
    clips, frames = lax.axis_size("clip"), lax.axis_size("frame")
    owners = clips * frames
    owner = lax.axis_index("clip") * frames + lax.axis_index("frame")
    part = patch_count // frames
    rows = ada_weight.shape[0]

    embed = jax.nn.silu(embed_steps(time_steps, width)).astype(bf16)
    embed = jnp.pad(embed, ((0, 16 - clip_count), (0, 0)))
    place = lax.broadcasted_iota(jnp.int32, (width, 128), 0) - owner * rows
    lane = lax.broadcasted_iota(jnp.int32, (width, 128), 1)
    select = ((place == lane) & (lane < rows)).astype(bf16)
    ada = jnp.pad(ada_weight, ((0, 128 - rows), (0, 0)))

    def spread_bias(vector):
        length = vector.shape[0]
        empty = jnp.zeros((owners * length,), f32)
        return lax.dynamic_update_slice(empty, vector.astype(f32), (owner * length,)).reshape(
            -1, width
        )

    bias = jnp.concatenate(
        [
            spread_bias(vector)
            for vector in (ada_bias, space_out_bias, time_out_bias, up_bias, down_bias)
        ],
        axis=0,
    )
    sh_c = jnp.concatenate([space_qkv, space_out], axis=1)
    sh_b = jnp.concatenate([time_qkv, time_out], axis=1)
    (
        w_c, w_b, w_u, w_d, mod, chosen, totals, hidden_one, qkv_one, mixed_one, branch_one,
        after_first, after_later, cot_first,
    ) = start_call(
        clips, frames, inputs, cotangent, sh_c, sh_b, up_weight, down_weight, embed, select, ada,
        bias,
    )

    def exchange(values):
        return lax.all_to_all(values, "frame", split_axis=0, concat_axis=0, tiled=True)

    loss = jnp.exp2(weight_index.astype(f32) * 0.5 - 1.0)
    loss = jnp.broadcast_to(loss[:, None], (clip_count, width))
    (
        act, gup, h3, gb3, mixed_two, gb2, h2, gqkv_two, mid_sums, _, _, grad_first, out_first,
        grad_later, out_later,
    ) = middle_call(
        clips, frames, after_first, cot_first, after_later, cotangent, loss, mod, w_b, w_u, w_d
    )
    grads = [grad_first, exchange(grad_later)]
    out_second = jnp.swapaxes(exchange(out_later), 0, 1).reshape(out_first.shape)

    earlier = None
    space_sums = []
    for clip in range(clip_count):
        *earlier, sums = space_back_call(
            clip, grads[clip], inputs, mod, w_c, qkv_one, branch_one, totals, earlier
        )
        space_sums.append(sums)
    input_grad, gb1, gqkv_one = earlier
    pieces = []
    for clip in range(clip_count):
        pieces += [space_sums[clip][0:3], mid_sums[clip][0:6]]
    pieces.append(sum(entry[3:4] for entry in space_sums))
    pieces.append(sum(entry[6:12] for entry in mid_sums))
    small = jnp.concatenate(pieces, axis=0)
    small = jnp.pad(small, ((0, ROWS - small.shape[0]), (0, 0)))
    gathered, own_u, own_d, own_b, own_c = grad_call(
        clips, frames, small, h3, gup, act, gb3, h2, gqkv_two, mixed_two, gb2,
        hidden_one.reshape(-1, width), gqkv_one, mixed_one.reshape(-1, width), gb1,
    )
    cut = 3 * width
    count = clip_count * 9
    grad_modulation = gathered[:, :count].reshape(clips * clip_count, 9 * width)
    picked = chosen.reshape(clips, 16, 128)[:, :clip_count, :rows].reshape(-1, rows)
    grad_ada = lax.dot_general(
        picked.astype(f32), grad_modulation, (((0,), (0,)), ((), ())), precision=highest
    )
    grad_ada_bias = jnp.sum(grad_modulation, axis=0)
    biases = jnp.sum(gathered[:, count : count + 7], axis=0)

    def own_slice(vector):
        length = vector.shape[0] // owners
        return lax.dynamic_slice_in_dim(vector, owner * length, length, 0)

    outputs = jnp.stack([out_first, out_second])
    return (
        outputs,
        input_grad,
        grad_ada,
        own_slice(grad_ada_bias),
        own_c[:, :cut],
        own_c[:, cut:],
        own_slice(biases[0]),
        own_b[:, :cut],
        own_b[:, cut:],
        own_slice(biases[1]),
        own_u,
        own_slice(biases[2:6].reshape(-1)),
        own_d,
        own_slice(biases[6]),
    )


def solution(mesh):
    tokens = P("clip", "frame", None, None)
    matrix = P(("clip", "frame"), None)
    vector = P(("clip", "frame"))
    in_specs = (
        tokens, tokens, P("clip"), P("clip"), matrix, vector, matrix, matrix, vector, matrix,
        matrix, vector, matrix, vector, matrix, vector,
    )
    out_specs = (
        tokens, tokens, matrix, vector, matrix, matrix, vector, matrix, matrix, vector, matrix,
        vector, matrix, vector,
    )
    return jax.shard_map(shards, mesh=mesh, in_specs=in_specs, out_specs=out_specs, check_vma=False)
```

```python
import functools
import math

import jax
import jax.numpy as jnp
from jax import lax
from jax.experimental import pallas as pl
from jax.experimental.pallas import tpu as pltpu
from jax.sharding import PartitionSpec as P

HEADS = 12
HEAD = 64
PAIRS = HEADS // 2
ROWS = 32
GELU_C = math.sqrt(2.0 / math.pi)
GELU_A = 0.044715
VMEM_LIMIT = 58 << 20

f32 = jnp.float32
bf16 = jnp.bfloat16
highest = lax.Precision.HIGHEST
MESH = pl.DeviceIdType.MESH
VMEM = pltpu.VMEM
DMA = pltpu.SemaphoreType.DMA


def embed_steps(time_steps, model_width):
    half_width = model_width // 2
    frequencies = jnp.exp(
        -math.log(10000.0) * jnp.arange(half_width, dtype=f32) / half_width
    )
    angles = time_steps.astype(f32)[:, None] * frequencies[None, :]
    return jnp.concatenate([jnp.cos(angles), jnp.sin(angles)], axis=1)


def dot(left, right, left_dim, right_dim):
    return lax.dot_general(
        left, right, (((left_dim,), (right_dim,)), ((), ())), preferred_element_type=f32
    )


def flip(index, mask):
    bit = 1
    while bit <= mask:
        if mask & bit:
            index = index + bit * (1 - 2 * ((index // bit) % 2))
        bit *= 2
    return index


def span(masks):
    out = [0]
    for mask in masks:
        out = out + [entry ^ mask for entry in out]
    return out


def frame_masks(frames):
    masks, bit = [], 1
    while bit < frames:
        masks.append(bit)
        bit *= 2
    if len(masks) > 1:
        masks = [frames - 1] + masks[:-1]
    return masks


def clip_tail_masks(clips):
    masks, bit = [], 2
    while bit < clips:
        masks.append(bit)
        bit *= 2
    return masks


def greet(clips, frames):
    clip, frame = lax.axis_index("clip"), lax.axis_index("frame")
    barrier = pltpu.get_barrier_semaphore()
    for step in range(1, clips):
        pl.semaphore_signal(
            barrier, inc=1, device_id={"clip": lax.rem(clip + step, clips)}, device_id_type=MESH
        )
    for step in range(1, frames):
        pl.semaphore_signal(
            barrier, inc=1, device_id={"frame": lax.rem(frame + step, frames)}, device_id_type=MESH
        )
    pl.semaphore_wait(barrier, clips + frames - 2)


def spread(axis, size, source_of, target, send_sems, recv_sems):
    me = lax.axis_index(axis)
    copies = []
    for step in range(1, size):
        peer = lax.rem(me + step, size)
        copy = pltpu.make_async_remote_copy(
            src_ref=source_of(peer),
            dst_ref=target.at[me],
            send_sem=send_sems.at[step - 1],
            recv_sem=recv_sems.at[step - 1],
            device_id={axis: peer},
            device_id_type=MESH,
        )
        copy.start()
        copies.append(copy)
    return copies


def start_kernel(
    clips, frames, clip_count,
    x_ref, cotangent, sh_c, sh_b, sh_u, sh_d, embed, select, ada, bias,
    w_c, w_b, w_u, w_d, mod, chosen, totals, hidden_out, qkv_out, mixed_out, branch_out,
    after_first, after_later, cot_first,
    v_c, z_c, z_b, z_u, z_d, st_w, b_c, b_b, b_u, b_d,
    embeds, parts, terms, arrived, held, lined, hidden, qkv, mixed, branch, after,
    zs, zr, cs, cr, xs, xr, ls, es, er, ps, pr, fs, fr, ts, tr, hs, hr, os, ws,
):
    clip, frame = lax.axis_index("clip"), lax.axis_index("frame")
    shards_in = (sh_c, sh_b, sh_u, sh_d)
    zoned = (z_c, z_b, z_u, z_d)
    blocks = (b_c, b_b, b_u, b_d)
    wholes = (v_c, w_b, w_u, w_d)
    width = mod.shape[1]
    frame_count, tokens = x_ref.shape[1], x_ref.shape[2]
    part = tokens // frames
    greet(clips, frames)
    masks = frame_masks(frames)
    sends = []
    stage = {}

    def frame_step(group, step):
        number = (1 << step) - 1
        copies = []
        for offset in span(masks[:step]):
            slot = flip(frame, offset)
            source = shards_in[group] if offset == 0 else zoned[group].at[slot]
            copy = pltpu.make_async_remote_copy(
                src_ref=source,
                dst_ref=zoned[group].at[slot],
                send_sem=zs.at[group, number],
                recv_sem=zr.at[group, number],
                device_id={"frame": flip(frame, masks[step])},
                device_id_type=MESH,
            )
            copy.start()
            copies.append(copy)
            number += 1
        sends.extend(copies)
        stage[group] = copies

    def frame_rest(group):
        for step in range(1, len(masks)):
            for copy in stage[group]:
                copy.wait_recv()
            frame_step(group, step)

    tail = clip_tail_masks(clips)
    steps = len(tail)
    orders = (tail, tail[::-1])
    moving = {}

    def block_send(group, half, step, position, offset):
        whole = wholes[group]
        block_rows = whole.shape[0] // clips
        columns = whole.shape[1] // 2
        rows = pl.ds(pl.multiple_of(flip(clip, offset) * block_rows, block_rows), block_rows)
        lanes = pl.ds(half * columns, columns)
        target = whole.at[rows, lanes]
        number = (1 << step) - 1 + position
        copy = pltpu.make_async_remote_copy(
            src_ref=blocks[group].at[:, lanes] if offset == 0 else target,
            dst_ref=target,
            send_sem=xs.at[group, half, number],
            recv_sem=xr.at[group, half, number],
            device_id={"clip": flip(clip, orders[half][step])},
            device_id_type=MESH,
        )
        copy.start()
        moving[group, half, number] = copy

    core_copies = {group: [] for group in range(4)}

    def core_send(group, offset):
        whole = wholes[group]
        block_rows = whole.shape[0] // clips
        rows = pl.ds(pl.multiple_of(flip(clip, offset) * block_rows, block_rows), block_rows)
        number = len(core_copies[group])
        copy = pltpu.make_async_remote_copy(
            src_ref=blocks[group] if offset == 0 else whole.at[rows, :],
            dst_ref=whole.at[rows, :],
            send_sem=cs.at[group, number],
            recv_sem=cr.at[group, number],
            device_id={"clip": flip(clip, 1)},
            device_id_type=MESH,
        )
        copy.start()
        core_copies[group].append(copy)

    local_copies = []

    def block_ready(group):
        for copy in stage[group]:
            copy.wait_recv()
        rows, columns = shards_in[group].shape
        block_rows = frames * rows
        if rows % 16:
            for slot in range(frames):
                st_w[slot * rows : (slot + 1) * rows, :columns] = zoned[group][slot].astype(f32)
            blocks[group][...] = st_w[:block_rows, :columns].astype(bf16)
        else:
            for slot in range(frames):
                blocks[group][slot * rows : (slot + 1) * rows, :] = zoned[group][slot]
        for step in range(steps):
            for half in range(2):
                block_send(group, half, step, 0, 0)
        core_send(group, 0)
        place = pl.ds(pl.multiple_of(clip * block_rows, block_rows), block_rows)
        keep = pltpu.make_async_copy(blocks[group], wholes[group].at[place, :], ls.at[group])
        keep.start()
        local_copies.append(keep)

    def block_forward(group):
        for step in range(1, steps):
            for half in range(2):
                for position in range(1 << (step - 1), 1 << step):
                    moving[group, half, position - 1].wait_recv()
                for later in range(step, steps):
                    for position, offset in enumerate(span(orders[half][:later])):
                        if (1 << (step - 1)) <= position < (1 << step):
                            block_send(group, half, later, position, offset)

    def block_finish(group):
        last = (1 << (steps - 1)) - 1
        for half in range(2):
            for number in range(last, (1 << steps) - 1):
                moving[group, half, number].wait_recv()
        for offset in span(tail)[1:]:
            core_send(group, offset)

    def core_finish(group):
        for copy in core_copies[group]:
            copy.wait_recv()

    for group in range(4):
        frame_step(group, 0)
    own = spread("clip", clips, lambda peer: embed, embeds, es, er)
    sends.extend(own)
    embeds[clip] = embed[...]
    for group in range(4):
        zoned[group][frame] = shards_in[group][...]
    for copy in own:
        copy.wait_recv()
    picked = dot(embeds[...].reshape(clips * 16, width), select[...], 1, 0).astype(bf16)
    chosen[...] = picked
    parts[...] = dot(picked, ada[...], 1, 0)
    for peer in range(clips):
        for local in range(clip_count):
            row = peer * 16 + local
            for piece in range(9):
                terms[peer, local * 9 + piece : local * 9 + piece + 1, :] = (
                    parts[row : row + 1, piece * width : (piece + 1) * width]
                    + bias[piece : piece + 1, :]
                )
        base = clip_count * 9
        terms[peer, base : base + 7, :] = bias[9:16, :]
        if base + 7 < ROWS:
            terms[peer, base + 7 : ROWS, :] = jnp.zeros((ROWS - base - 7, width), f32)
    own = spread("clip", clips, lambda peer: terms.at[peer], arrived, ps, pr)
    sends.extend(own)
    arrived[clip] = terms[clip]
    frame_rest(0)
    for copy in own:
        copy.wait_recv()
    total = arrived[0]
    for peer in range(1, clips):
        total = total + arrived[peer]
    held[...] = total
    own = spread("frame", frames, lambda peer: held, lined, fs, fr)
    sends.extend(own)
    lined[frame] = total
    block_ready(0)
    for group in range(1, 4):
        frame_rest(group)

    cot_copies = []
    for step in range(1, frames):
        peer = lax.rem(frame + step, frames)
        copy = pltpu.make_async_remote_copy(
            src_ref=cotangent.at[0, :, pl.ds(pl.multiple_of(peer * part, part), part), :],
            dst_ref=cot_first.at[frame],
            send_sem=ts.at[step - 1],
            recv_sem=tr.at[step - 1],
            device_id={"frame": peer},
            device_id_type=MESH,
        )
        copy.start()
        cot_copies.append(copy)
    keep = pltpu.make_async_copy(
        cotangent.at[0, :, pl.ds(pl.multiple_of(frame * part, part), part), :],
        cot_first.at[frame],
        ls.at[4],
    )
    keep.start()
    local_copies.append(keep)

    for copy in own:
        copy.wait_recv()
    total = lined[0]
    for peer in range(1, frames):
        total = total + lined[peer]
    mod[...] = total
    block_forward(0)
    for group in range(1, 4):
        block_ready(group)
    block_finish(0)
    core_finish(0)
    local_copies[0].wait()

    keep = pltpu.make_async_copy(v_c, w_c, ls.at[5])
    keep.start()
    local_copies.append(keep)

    def after_copy(f, step):
        peer = lax.rem(frame + step, frames)
        return pltpu.make_async_remote_copy(
            src_ref=after.at[f, pl.ds(pl.multiple_of(peer * part, part), part), :],
            dst_ref=after_first.at[frame, f],
            send_sem=hs.at[f, step - 1],
            recv_sem=hr.at[f, step - 1],
            device_id={"frame": peer},
            device_id_type=MESH,
        )

    def own_after(f):
        return pltpu.make_async_copy(
            after.at[f, pl.ds(pl.multiple_of(frame * part, part), part), :],
            after_first.at[frame, f],
            os.at[f],
        )

    def later_after(f):
        return pltpu.make_async_copy(after.at[f], after_later.at[f - frame_count], os.at[f])

    kept = ((hidden, hidden_out), (qkv, qkv_out), (mixed, mixed_out), (branch, branch_out))

    def write_back(f):
        return [
            pltpu.make_async_copy(source.at[f], target.at[f], ws.at[number, f])
            for number, (source, target) in enumerate(kept)
        ]

    for local in range(clip_count):
        row = local * 9

        def one_frame(index, carry):
            f = local * frame_count + index
            values = x_ref[local, index].astype(f32)
            norm, _ = normed(values)
            scaled = norm * (1.0 + mod[row + 1 : row + 2, :]) + mod[row : row + 1, :]
            lowered = scaled.astype(bf16)
            hidden[f] = lowered
            qkv[f] = dot(lowered, v_c[:, : 3 * width], 1, 0).astype(bf16)
            attend(qkv.at[f], mixed.at[f], totals.at[f], width, None)
            grown = dot(mixed[f], v_c[:, 3 * width :], 1, 0) + mod[18:19, :]
            branch[f] = grown.astype(bf16)
            after[f] = (values + mod[row + 2 : row + 3, :] * grown).astype(bf16)
            if local == 0:
                for step in range(1, frames):
                    after_copy(f, step).start()
                own_after(f).start()
            else:
                later_after(f).start()
            for copy in write_back(f):
                copy.start()
            return carry

        lax.fori_loop(0, frame_count, one_frame, 0)
        if local == 0:
            block_forward(1)
    for group in range(2, 4):
        block_forward(group)
    for group in range(1, 4):
        block_finish(group)
    for group in range(1, 4):
        core_finish(group)

    def settle(f, carry):
        for step in range(1, frames):
            copy = after_copy(f, step)
            copy.wait_recv()
            copy.wait_send()
        own_after(f).wait()
        return carry

    lax.fori_loop(0, frame_count, settle, 0)

    def settle_later(f, carry):
        later_after(f).wait()
        return carry

    lax.fori_loop(frame_count, clip_count * frame_count, settle_later, 0)

    def settle_kept(f, carry):
        for copy in write_back(f):
            copy.wait()
        return carry

    lax.fori_loop(0, clip_count * frame_count, settle_kept, 0)
    for copy in cot_copies:
        copy.wait_recv()
        copy.wait_send()
    for copy in local_copies[1:]:
        copy.wait()
    for copy in moving.values():
        copy.wait_send()
    for group in range(4):
        for copy in core_copies[group]:
            copy.wait_send()
    for copy in sends:
        copy.wait_send()


def start_call(
    clips, frames, inputs, cotangent, sh_c, sh_b, sh_u, sh_d, embed, select, ada, bias
):
    clip_count, frame_count, tokens, width = inputs.shape
    rows, columns = sh_c.shape
    rows_d = sh_d.shape[0]
    block = frames * rows
    block_d = frames * rows_d
    peers = max(clips // 2 - 1, 1)
    total = clip_count * frame_count
    part = tokens // frames
    whole = jax.ShapeDtypeStruct((clips * block, columns), bf16)
    vmem = pl.BlockSpec(memory_space=VMEM)
    hbm = pl.BlockSpec(memory_space=pl.ANY)
    zoned = lambda height, lanes: VMEM((frames, height, lanes), bf16)
    saved = lambda lanes: jax.ShapeDtypeStruct((total, tokens, lanes), bf16)
    lent = lambda lanes: VMEM((total, tokens, lanes), bf16)
    traded = jax.ShapeDtypeStruct((frames, frame_count, part, width), bf16)
    return pl.pallas_call(
        functools.partial(start_kernel, clips, frames, clip_count),
        out_shape=(
            whole, whole, whole,
            jax.ShapeDtypeStruct((clips * block_d, width), bf16),
            jax.ShapeDtypeStruct((ROWS, width), f32),
            jax.ShapeDtypeStruct((clips * 16, 128), bf16),
            jax.ShapeDtypeStruct((total, 16, tokens), f32),
            saved(width), saved(3 * width), saved(width), saved(width),
            traded,
            jax.ShapeDtypeStruct(((clip_count - 1) * frame_count, tokens, width), bf16),
            traded,
        ),
        in_specs=[vmem, hbm] + [vmem] * 8,
        out_specs=(hbm, hbm, hbm, hbm, vmem, vmem, vmem) + (hbm,) * 7,
        scratch_shapes=[
            VMEM((clips * block, columns), bf16),
            zoned(rows, columns), zoned(rows, columns), zoned(rows, columns), zoned(rows_d, width),
            VMEM((max(block, block_d), columns), f32),
            VMEM((block, columns), bf16),
            VMEM((block, columns), bf16),
            VMEM((block, columns), bf16),
            VMEM((block_d, width), bf16),
            VMEM((clips, 16, width), bf16),
            VMEM((clips * 16, 9 * width), f32),
            VMEM((clips, ROWS, width), f32),
            VMEM((clips, ROWS, width), f32),
            VMEM((ROWS, width), f32),
            VMEM((frames, ROWS, width), f32),
            lent(width), lent(3 * width), lent(width), lent(width), lent(width),
            DMA((4, frames - 1)), DMA((4, frames - 1)),
            DMA((4, clips // 2)), DMA((4, clips // 2)),
            DMA((4, 2, peers)), DMA((4, 2, peers)),
            DMA((6,)),
            DMA((clips - 1,)), DMA((clips - 1,)),
            DMA((clips - 1,)), DMA((clips - 1,)),
            DMA((frames - 1,)), DMA((frames - 1,)),
            DMA((frames - 1,)), DMA((frames - 1,)),
            DMA((frame_count, frames - 1)), DMA((frame_count, frames - 1)),
            DMA((total,)),
            DMA((4, total)),
        ],
        compiler_params=pltpu.CompilerParams(
            collective_id=0, has_side_effects=True, vmem_limit_bytes=VMEM_LIMIT
        ),
    )(inputs, cotangent, sh_c, sh_b, sh_u, sh_d, embed, select, ada, bias)


STEP = 512
SLOTS = 3


def grad_kernel(
    clips, frames, clip_count,
    small, chosen, out_later, h3, gup, act, gb3, h2, gqkv2, mix2, gb2, h1, gqkv1, mix1, gb1,
    out_second, grad_ada, bias_sums, out_u, out_d, out_b, out_bo, out_c, out_co,
    sum_w, sum_d, core_w, core_d, side_w, side_d, line_w, line_d, last_w, last_d,
    left, right, total, gathered, lined, held,
    lsem, rsem, cs, cr, xs, xr, zs, zr, fs, fr, ps, pr, os, orr, ks,
):
    clip, frame = lax.axis_index("clip"), lax.axis_index("frame")
    tokens = h3.shape[0]
    width = small.shape[1]
    wide = sum_w.shape[-1]
    narrow = sum_d.shape[-1]
    tail = clip_tail_masks(clips)
    orders = (tail, tail[::-1])
    masks = frame_masks(frames)
    greet(clips, frames)
    first = spread("frame", frames, lambda peer: small, lined, fs, fr)
    lined[frame] = small[...]
    part = out_later.shape[2]
    out_copies = []
    mine = pl.ds(pl.multiple_of(frame * part, part), part)
    for hop in range(1, frames):
        peer = lax.rem(frame + hop, frames)
        copy = pltpu.make_async_remote_copy(
            src_ref=out_later.at[peer],
            dst_ref=out_second.at[:, mine, :],
            send_sem=os.at[hop - 1],
            recv_sem=orr.at[hop - 1],
            device_id={"frame": peer},
            device_id_type=MESH,
        )
        copy.start()
        out_copies.append(copy)
    own_out = pltpu.make_async_copy(out_later.at[frame], out_second.at[:, mine, :], ks)
    own_out.start()

    chunks = [
        (1, 0, [(act, gb3, 0, 0, narrow)], out_d, 0),
        (1, 1, [(act, gb3, narrow, 0, narrow)], out_d, narrow),
        (0, 0, [(h3, gup, 0, 0, wide)], out_u, 0),
        (0, 1, [(h3, gup, wide, 0, wide)], out_u, wide),
        (0, 2, [(h2, gqkv2, 0, 0, wide)], out_b, 0),
        (0, 3, [(h2, gqkv2, wide, 0, width), (mix2, gb2, 0, width, width)], out_b, wide),
        (0, 4, [(h1, gqkv1, 0, 0, wide)], out_c, 0),
        (0, 5, [(h1, gqkv1, wide, 0, width), (mix1, gb1, 0, width, width)], out_c, wide),
    ]
    sums, cores, sides = (sum_w, sum_d), (core_w, core_d), (side_w, side_d)
    lines, lasts = (line_w, line_d), (last_w, last_d)
    flights = {}

    steps = tokens // STEP
    line_up = []
    for kind, _, parts, _, _ in chunks:
        for part in parts:
            for group in range(part[0].shape[1] // width):
                line_up.append(part[:3] + (part[3] + group * part[4], part[4], group))
    begins = [0]
    for kind, _, parts, _, _ in chunks:
        begins.append(begins[-1] + sum(part[0].shape[1] // width for part in parts))

    def load(entry, step, slot):
        one, other, begin, _, lanes, group = line_up[entry]
        rows = pl.ds(pl.multiple_of(step * STEP, STEP), STEP)
        return (
            pltpu.make_async_copy(
                one.at[rows, pl.ds(group * width, width)], left.at[slot], lsem.at[slot]
            ),
            pltpu.make_async_copy(
                other.at[rows, pl.ds(begin, lanes)],
                right.at[slot, :, pl.ds(0, lanes)],
                rsem.at[slot],
            ),
        )

    def place_of(entry, step):
        return lax.rem(entry * steps + step, SLOTS)

    def multiply(number):
        kind, place = chunks[number][:2]
        for entry in range(begins[number], begins[number + 1]):
            at, lanes = line_up[entry][3:5]

            def body(step, carry):
                ahead = step + SLOTS - 1

                @pl.when(ahead < steps)
                def _():
                    for copy in load(entry, ahead, place_of(entry, ahead)):
                        copy.start()

                if entry + 1 < len(line_up):

                    @pl.when(ahead >= steps)
                    def _():
                        for copy in load(entry + 1, ahead - steps, place_of(entry, ahead)):
                            copy.start()

                slot = place_of(entry, step)
                for copy in load(entry, step, slot):
                    copy.wait()
                product = dot(left[slot], right[slot, :, :lanes], 0, 0)
                columns = slice(at, at + lanes)

                @pl.when(step == 0)
                def _():
                    total[:, columns] = product

                @pl.when(step > 0)
                def _():
                    total[:, columns] += product

                return carry

            lax.fori_loop(0, steps, body, 0)
        rows, lanes = sums[kind].shape[2:]
        for block in range(clips):
            begin = block * rows
            column = begin // width * lanes
            begin = begin % width
            sums[kind][place, block] = total[begin : begin + rows, column : column + lanes].astype(
                bf16
            )

    def core_start(number):
        kind, place = chunks[number][:2]
        copies = []
        for position, offset in enumerate(span(tail)):
            copy = pltpu.make_async_remote_copy(
                src_ref=sums[kind].at[place, flip(clip, offset ^ 1)],
                dst_ref=cores[kind].at[place, position],
                send_sem=cs.at[number, position],
                recv_sem=cr.at[number, position],
                device_id={"clip": flip(clip, 1)},
                device_id_type=MESH,
            )
            copy.start()
            copies.append(copy)
        flights[number, "core"] = copies

    def half_of(kind, half):
        if kind:
            rows = sums[kind].shape[2] // 2
            return (slice(half * rows, (half + 1) * rows), slice(None))
        lanes = sums[kind].shape[3] // 2
        return (slice(None), slice(half * lanes, (half + 1) * lanes))

    def side_start(number, step):
        kind, place = chunks[number][:2]
        copies = []
        for half in range(2):
            mask = orders[half][step]
            for position, offset in enumerate(span(orders[half][:step])):
                entry = (1 << step) - 1 + position
                copy = pltpu.make_async_remote_copy(
                    src_ref=sums[kind].at[(place, flip(clip, offset ^ mask)) + half_of(kind, half)],
                    dst_ref=sides[kind].at[place, half, entry],
                    send_sem=xs.at[number, half, entry],
                    recv_sem=xr.at[number, half, entry],
                    device_id={"clip": flip(clip, mask)},
                    device_id_type=MESH,
                )
                copy.start()
                copies.append(copy)
        flights[number, "side", step] = copies

    def core_add(number):
        kind, place = chunks[number][:2]
        for copy in flights[number, "core"]:
            copy.wait_recv()
        for position, offset in enumerate(span(tail)):
            block = flip(clip, offset)
            sums[kind][place, block] = (
                sums[kind][place, block].astype(f32) + cores[kind][place, position].astype(f32)
            ).astype(bf16)
        side_start(number, len(tail) - 1)

    def side_add(number, step):
        kind, place = chunks[number][:2]
        for copy in flights[number, "side", step]:
            copy.wait_recv()
        for half in range(2):
            for position, offset in enumerate(span(orders[half][:step])):
                entry = (1 << step) - 1 + position
                block = flip(clip, offset)
                where = (place, block) + half_of(kind, half)
                sums[kind][where] = (
                    sums[kind][where].astype(f32) + sides[kind][place, half, entry].astype(f32)
                ).astype(bf16)
        if step:
            side_start(number, step - 1)
        else:
            rows = lines[kind].shape[2]
            block = sums[kind][place, clip].astype(f32)
            for slot in range(frames):
                lines[kind][place, slot] = block[slot * rows : (slot + 1) * rows, :].astype(bf16)
            line_start(number, len(masks) - 1)

    def line_start(number, step):
        kind, place = chunks[number][:2]
        copies = []
        for position, offset in enumerate(span(masks[:step])):
            entry = (1 << step) - 1 + position
            copy = pltpu.make_async_remote_copy(
                src_ref=lines[kind].at[place, flip(frame, offset ^ masks[step])],
                dst_ref=lasts[kind].at[place, entry],
                send_sem=zs.at[number, entry],
                recv_sem=zr.at[number, entry],
                device_id={"frame": flip(frame, masks[step])},
                device_id_type=MESH,
            )
            copy.start()
            copies.append(copy)
        flights[number, "line", step] = copies

    def line_add(number, step):
        kind, place, _, target, begin = chunks[number]
        for copy in flights[number, "line", step]:
            copy.wait_recv()
        for position, offset in enumerate(span(masks[:step])):
            entry = (1 << step) - 1 + position
            slot = flip(frame, offset)
            value = lines[kind][place, slot].astype(f32) + lasts[kind][place, entry].astype(f32)
            if step:
                lines[kind][place, slot] = value.astype(bf16)
            elif begin + value.shape[1] > target.shape[1]:
                cut = target.shape[1] - begin
                target[:, begin:] = value[:, :cut]
                (out_bo if target is out_b else out_co)[...] = value[:, cut:]
            else:
                target[:, begin : begin + value.shape[1]] = value
        if step:
            line_start(number, step - 1)

    stages = [core_start, core_add]
    for step in range(len(tail))[::-1]:
        stages.append(functools.partial(side_add, step=step))
    for step in range(len(masks))[::-1]:
        stages.append(functools.partial(line_add, step=step))

    def finish_small():
        for copy in second:
            copy.wait_recv()
        rows = grad_ada.shape[0]
        for number in range(9):
            terms = [
                gathered[peer, local * 9 + number : local * 9 + number + 1, :]
                for peer in range(clips)
                for local in range(clip_count)
            ]
            terms = jnp.concatenate(terms, axis=0)
            grad_ada[:, number * width : (number + 1) * width] = lax.dot_general(
                chosen[...], terms, (((1,), (0,)), ((), ())), precision=highest,
                preferred_element_type=f32,
            )[:rows, :]
            bias_sums[number : number + 1, :] = column_sum(terms)
        base = clip_count * 9
        summed = gathered[0, base : base + 7, :]
        for peer in range(1, clips):
            summed = summed + gathered[peer, base : base + 7, :]
        bias_sums[9:16, :] = summed

    for step in range(SLOTS - 1):
        for copy in load(0, step, step):
            copy.start()
    second = None
    lags = [0, 1, 3]
    while len(lags) < len(stages):
        lags.append(lags[-1] + 1)
    for turn in range(len(chunks) + lags[-1]):
        for depth in range(len(stages))[::-1]:
            if depth > 0 and 0 <= turn - lags[depth] < len(chunks):
                stages[depth](turn - lags[depth])
        if turn < len(chunks):
            multiply(turn)
            core_start(turn)
        if turn == len(chunks):
            finish_small()
        if turn == 0:
            for copy in first:
                copy.wait_recv()
            summed = lined[0]
            for peer in range(1, frames):
                summed = summed + lined[peer]
            held[...] = summed
            second = spread("clip", clips, lambda peer: held, gathered, ps, pr)
            gathered[clip] = summed
    own_out.wait()
    for copy in out_copies:
        copy.wait_recv()
        copy.wait_send()
    for copy in first + second:
        copy.wait_send()
    for copies in flights.values():
        for copy in copies:
            copy.wait_send()


def grad_call(clips, frames, clip_count, small, chosen, out_later, *operands):
    h3, gup, act = operands[:3]
    _, frame_count, part, _ = out_later.shape
    width, hidden = h3.shape[1], act.shape[1]
    owners = clips * frames
    wide, narrow = hidden // 2, width // 2
    rows_w, rows_d = width // owners, hidden // owners
    peers = max(clips // 2 - 1, 1)
    vmem = pl.BlockSpec(memory_space=VMEM)
    hbm = pl.BlockSpec(memory_space=pl.ANY)

    return pl.pallas_call(
        functools.partial(grad_kernel, clips, frames, clip_count),
        out_shape=(
            jax.ShapeDtypeStruct((frame_count, frames * part, width), bf16),
            jax.ShapeDtypeStruct((rows_w, 9 * width), f32),
            jax.ShapeDtypeStruct((16, width), f32),
            jax.ShapeDtypeStruct((rows_w, hidden), f32),
            jax.ShapeDtypeStruct((rows_d, width), f32),
            jax.ShapeDtypeStruct((rows_w, 3 * width), f32),
            jax.ShapeDtypeStruct((rows_w, width), f32),
            jax.ShapeDtypeStruct((rows_w, 3 * width), f32),
            jax.ShapeDtypeStruct((rows_w, width), f32),
        ),
        in_specs=[vmem, vmem] + [hbm] * (1 + len(operands)),
        out_specs=(hbm,) + (vmem,) * 8,
        scratch_shapes=[
            VMEM((6, clips, rows_w * frames, wide), bf16),
            VMEM((2, clips, rows_d * frames, narrow), bf16),
            VMEM((6, clips // 2, rows_w * frames, wide), bf16),
            VMEM((2, clips // 2, rows_d * frames, narrow), bf16),
            VMEM((6, 2, peers, rows_w * frames, wide // 2), bf16),
            VMEM((2, 2, peers, rows_d * frames // 2, narrow), bf16),
            VMEM((6, frames, rows_w, wide), bf16),
            VMEM((2, frames, rows_d, narrow), bf16),
            VMEM((6, frames - 1, rows_w, wide), bf16),
            VMEM((2, frames - 1, rows_d, narrow), bf16),
            VMEM((SLOTS, STEP, width), bf16),
            VMEM((SLOTS, STEP, wide), bf16),
            VMEM((width, wide), f32),
            VMEM((clips,) + small.shape, f32),
            VMEM((frames,) + small.shape, f32),
            VMEM(small.shape, f32),
            DMA((SLOTS,)), DMA((SLOTS,)),
            DMA((8, clips // 2)), DMA((8, clips // 2)),
            DMA((8, 2, peers)), DMA((8, 2, peers)),
            DMA((8, frames - 1)), DMA((8, frames - 1)),
            DMA((frames - 1,)), DMA((frames - 1,)),
            DMA((clips - 1,)), DMA((clips - 1,)),
            DMA((frames - 1,)), DMA((frames - 1,)),
            DMA,
        ],
        compiler_params=pltpu.CompilerParams(
            collective_id=1, has_side_effects=True, vmem_limit_bytes=VMEM_LIMIT
        ),
    )(small, chosen, out_later, *operands)


def normed(values):
    centred = values - jnp.mean(values, axis=-1, keepdims=True)
    scale = lax.rsqrt(jnp.mean(centred * centred, axis=-1, keepdims=True) + 1e-06)
    return centred * scale, scale


def norm_back(grad, scaled, norm, scale):
    inner = grad * scaled
    return scale * (
        inner
        - jnp.mean(inner, axis=-1, keepdims=True)
        - norm * jnp.mean(inner * norm, axis=-1, keepdims=True)
    )


def column_sum(values):
    return jnp.sum(values, axis=0, keepdims=True)


def attend(qkv, mixed, totals, width, mask):
    tokens = qkv.shape[0]
    low = lax.broadcasted_iota(jnp.int32, (tokens, 128), 1) < HEAD
    for pair in range(PAIRS):
        at = pair * 128
        queries = qkv[:, at : at + 128] * bf16(0.125)
        keys = qkv[:, width + at : width + at + 128]
        values = qkv[:, 2 * width + at : 2 * width + at + 128]
        halves = []
        for half in range(2):
            own = jnp.where(low if half == 0 else ~low, queries, bf16(0))
            scores = dot(keys, own, 1, 1)
            if mask is not None:
                scores = scores + mask[...]
            peak = jnp.max(scores, axis=0, keepdims=True)
            terms = jnp.exp(scores - peak)
            total = jnp.sum(terms, axis=0, keepdims=True)
            weights = (terms * (1.0 / total)).astype(bf16)
            totals[2 * pair + half : 2 * pair + half + 1, :] = peak + jnp.log(total)
            halves.append(dot(weights, values, 0, 0))
        mixed[:, at : at + 128] = jnp.where(low, halves[0], halves[1]).astype(bf16)


def attend_back(qkv, grad_mixed, totals, grad_qkv, width, mask):
    tokens = qkv.shape[0]
    low = lax.broadcasted_iota(jnp.int32, (tokens, 128), 1) < HEAD
    for pair in range(PAIRS):
        at = pair * 128
        queries = qkv[:, at : at + 128]
        keys = qkv[:, width + at : width + at + 128]
        values = qkv[:, 2 * width + at : 2 * width + at + 128]
        grads = grad_mixed[:, at : at + 128]
        halves = []
        for half in range(2):
            pick = low if half == 0 else ~low
            own = jnp.where(pick, queries * bf16(0.125), bf16(0))
            own_grads = jnp.where(pick, grads, bf16(0))
            scores = dot(keys, own, 1, 1)
            if mask is not None:
                scores = scores + mask[...]
            weights = jnp.exp(scores - totals[2 * pair + half : 2 * pair + half + 1, :])
            grad_weights = dot(values, own_grads, 1, 1)
            inner = jnp.sum(weights * grad_weights, axis=0, keepdims=True)
            grad_scores = (weights * (grad_weights - inner)).astype(bf16)
            halves.append(
                (
                    dot(grad_scores, keys, 0, 0),
                    dot(grad_scores, queries, 1, 0),
                    dot(weights.astype(bf16), grads, 1, 0),
                )
            )
        for part, factor in ((0, 0.125), (1, 0.125), (2, 1.0)):
            joined = jnp.where(low, halves[0][part], halves[1][part]) * factor
            start = part * width + at
            grad_qkv[:, start : start + 128] = joined.astype(bf16)


def full(shape):
    return pl.BlockSpec(shape, lambda *_: (0,) * len(shape), pipeline_mode=pl.Buffered(1))


def middle_kernel(
    clips, frames, tiles,
    after_first, cot_first, after_later, cotangent, loss, mod, w_b, w_u, w_d,
    act_ref, gup_ref, h3_ref, gb3_ref, mixed_ref, gb2_ref, h2_ref, gqkv_ref, sums,
    after_second, cot_second, grad_first, grad_later, out_first, out_later,
    qkv, totals, mask, gmix, after_tile, cot_tile, grad_stage, out_stage,
    ts, tr, us, ur, gs, gr, os, orr, ls, ks, ws,
):
    frame = lax.axis_index("frame")
    step = pl.program_id(0)
    last = pl.num_programs(0) - 1
    clip = lax.div(step, tiles)
    tile = lax.rem(step, tiles)
    slot = lax.rem(step, 2)
    width = mod.shape[1]
    frame_count, group = after_tile.shape[2], after_tile.shape[3]
    part = tiles * group
    tokens = frames * frame_count * group
    row = clip * 9
    piece = lambda number: mod[pl.ds(row + number, 1), :]

    def own_part(index):
        return pl.ds(pl.multiple_of(index * part, part), part)

    def later_copies(number):
        copies = []
        for hop in range(1, frames):
            peer = lax.rem(frame + hop, frames)
            if number:
                source, target, send, recv = cotangent.at[1, :, own_part(peer), :], cot_second, us, ur
            else:
                source, target, send, recv = after_later.at[:, own_part(peer), :], after_second, ts, tr
            copies.append(
                pltpu.make_async_remote_copy(
                    src_ref=source,
                    dst_ref=target.at[frame],
                    send_sem=send.at[hop - 1],
                    recv_sem=recv.at[hop - 1],
                    device_id={"frame": peer},
                    device_id_type=MESH,
                )
            )
        return copies

    def own_copy(number):
        source = cotangent.at[1] if number else after_later
        target = cot_second if number else after_second
        return pltpu.make_async_copy(
            source.at[:, own_part(frame), :], target.at[frame], ks.at[number]
        )

    def load(source, number, index, place):
        rows = pl.ds(pl.multiple_of(index * group, group), group)
        target = (after_tile, cot_tile)[number].at[place]
        return pltpu.make_async_copy(source.at[:, :, rows, :], target, ls.at[place, number])

    def grad_copies(index):
        rows = pl.ds(pl.multiple_of(index * group, group), group)
        copies = []
        for hop in range(1, frames):
            peer = lax.rem(frame + hop, frames)
            copies.append(
                pltpu.make_async_remote_copy(
                    src_ref=grad_stage.at[index, peer],
                    dst_ref=grad_first.at[frame, :, rows, :],
                    send_sem=gs.at[index, hop - 1],
                    recv_sem=gr.at[index, hop - 1],
                    device_id={"frame": peer},
                    device_id_type=MESH,
                )
            )
        return copies

    def out_rows(index):
        return pl.ds(pl.multiple_of(frame * part + index * group, group), group)

    def out_copies(index):
        copies = []
        for hop in range(1, frames):
            peer = lax.rem(frame + hop, frames)
            copies.append(
                pltpu.make_async_remote_copy(
                    src_ref=out_stage.at[index, peer],
                    dst_ref=out_first.at[:, out_rows(index), :],
                    send_sem=os.at[index, hop - 1],
                    recv_sem=orr.at[index, hop - 1],
                    device_id={"frame": peer},
                    device_id_type=MESH,
                )
            )
        return copies

    def own_stages(index):
        rows = pl.ds(pl.multiple_of(index * group, group), group)
        return (
            pltpu.make_async_copy(
                grad_stage.at[index, frame], grad_first.at[frame, :, rows, :], ws.at[0, index]
            ),
            pltpu.make_async_copy(
                out_stage.at[index, frame], out_first.at[:, out_rows(index), :], ws.at[1, index]
            ),
        )

    def later_stages(index):
        place = index + tiles
        rows = pl.ds(pl.multiple_of(index * group, group), group)
        return (
            pltpu.make_async_copy(
                grad_stage.at[place], grad_later.at[:, :, rows, :], ws.at[0, place]
            ),
            pltpu.make_async_copy(
                out_stage.at[place], out_later.at[:, :, rows, :], ws.at[1, place]
            ),
        )

    @pl.when(step == 0)
    def _():
        barrier = pltpu.get_barrier_semaphore()
        for hop in range(1, frames):
            pl.semaphore_signal(
                barrier,
                inc=1,
                device_id={"frame": lax.rem(frame + hop, frames)},
                device_id_type=MESH,
            )
        pl.semaphore_wait(barrier, frames - 1)
        load(after_first, 0, 0, 0).start()
        load(cot_first, 1, 0, 0).start()
        for number in range(2):
            for copy in later_copies(number):
                copy.start()
            own_copy(number).start()
        first = lax.broadcasted_iota(jnp.int32, (tokens, tokens), 0)
        second = lax.broadcasted_iota(jnp.int32, (tokens, tokens), 1)
        mask[...] = jnp.where(lax.rem(first, group) == lax.rem(second, group), 0.0, -1e30)

    @pl.when(step == tiles)
    def _():
        for copy in later_copies(0):
            copy.wait_recv()
        own_copy(0).wait()
        load(after_second, 0, 0, slot).start()

    load(after_first, 0, 0, slot).wait()

    @pl.when(step + 1 < tiles)
    def _():
        load(after_first, 0, step + 1, 1 - slot).start()
        load(cot_first, 1, step + 1, 1 - slot).start()

    @pl.when((step >= tiles) & (step < last))
    def _():
        load(after_second, 0, tile + 1, 1 - slot).start()

    @pl.when((step > tiles) & (step < last))
    def _():
        load(cot_second, 1, tile + 1, 1 - slot).start()

    @pl.when(tile == 0)
    def _():
        sums[...] = jnp.zeros_like(sums)

    def add(place, values):
        sums[place : place + 1, :] += values

    after = after_tile[slot].reshape(tokens, width).astype(f32)
    norm, scale = normed(after)
    hidden = (norm * (1.0 + piece(4)) + piece(3)).astype(bf16)
    h2_ref[...] = hidden
    qkv[...] = dot(hidden, w_b[:, : 3 * width], 1, 0).astype(bf16)
    attend(qkv, mixed_ref, totals, width, mask)
    branch_two = dot(mixed_ref[...], w_b[:, 3 * width :], 1, 0) + mod[19:20, :]
    after_two = after + piece(5) * branch_two
    norm_three, scale_three = normed(after_two)
    hidden = (norm_three * (1.0 + piece(7)) + piece(6)).astype(bf16)
    h3_ref[...] = hidden

    @pl.when(step == tiles)
    def _():
        for copy in later_copies(1):
            copy.wait_recv()
        own_copy(1).wait()
        load(cot_second, 1, 0, slot).start()
        if tiles > 1:
            load(cot_second, 1, 1, 1 - slot).start()

        def send(index, carry):
            for copy in grad_copies(index):
                copy.start()
            return carry

        lax.fori_loop(0, tiles, send, 0)

        def send_out(index, carry):
            for copy in out_copies(index):
                copy.start()
            return carry

        lax.fori_loop(0, tiles, send_out, 0)

    load(cot_first, 1, 0, slot).wait()
    grad_out = cot_tile[slot].reshape(tokens, width).astype(f32) * loss[pl.ds(clip, 1), :]
    grad_branch = (grad_out * piece(8)).astype(bf16)
    gb3_ref[...] = grad_branch
    add(11, column_sum(grad_branch.astype(f32)))
    branch_three = jnp.zeros((tokens, width), f32)
    grad_hidden = jnp.zeros((tokens, width), f32)
    for chunk in range(w_u.shape[1] // width):
        cut = slice(chunk * width, (chunk + 1) * width)
        upper = dot(hidden, w_u[:, cut], 1, 0) + mod[20 + chunk : 21 + chunk, :]
        square = upper * upper
        bend = jnp.tanh(upper * (GELU_C + (GELU_C * GELU_A) * square))
        half = 0.5 + 0.5 * bend
        act = (upper * half).astype(bf16)
        slope = half + (0.5 * upper) * (1.0 - bend * bend) * (
            GELU_C + (3.0 * GELU_C * GELU_A) * square
        )
        act_ref[:, cut] = act
        branch_three += dot(act, w_d[cut, :], 1, 0)
        grad_upper = (dot(grad_branch, w_d[cut, :], 1, 1) * slope).astype(bf16)
        gup_ref[:, cut] = grad_upper
        add(7 + chunk, column_sum(grad_upper.astype(f32)))
        grad_hidden += dot(grad_upper, w_u[:, cut], 1, 1)
    branch_three += mod[24:25, :]
    out = (after_two + piece(8) * branch_three).astype(bf16)
    out_stage[step] = out.reshape(out_stage.shape[1:])
    add(5, column_sum(grad_out * branch_three))
    add(3, column_sum(grad_hidden))
    add(4, column_sum(grad_hidden * norm_three))
    grad_two = grad_out + norm_back(grad_hidden, 1.0 + piece(7), norm_three, scale_three)
    add(2, column_sum(grad_two * branch_two))
    grad_branch = (grad_two * piece(5)).astype(bf16)
    gb2_ref[...] = grad_branch
    add(6, column_sum(grad_branch.astype(f32)))
    gmix[...] = dot(grad_branch, w_b[:, 3 * width :], 1, 1).astype(bf16)
    attend_back(qkv, gmix, totals, gqkv_ref, width, mask)
    grad_hidden = dot(gqkv_ref[...], w_b[:, : 3 * width], 1, 1).astype(bf16).astype(f32)
    add(0, column_sum(grad_hidden))
    add(1, column_sum(grad_hidden * norm))
    grad_one = grad_two + norm_back(grad_hidden, 1.0 + piece(4), norm, scale)
    grad_stage[step] = grad_one.astype(bf16).reshape(grad_stage.shape[1:])

    @pl.when(step < tiles)
    def _():
        for copy in own_stages(tile):
            copy.start()

    @pl.when(step >= tiles)
    def _():
        for copy in later_stages(tile):
            copy.start()

    @pl.when(step == last)
    def _():
        for copy in later_copies(0) + later_copies(1):
            copy.wait_send()

        def settle(index, carry):
            for copy in grad_copies(index) + out_copies(index):
                copy.wait_send()
                copy.wait_recv()
            for copy in own_stages(index) + later_stages(index):
                copy.wait()
            return carry

        lax.fori_loop(0, tiles, settle, 0)


def middle_call(
    clips, frames, after_first, cot_first, after_later, cotangent, loss, mod, w_b, w_u, w_d
):
    _, frame_count, part, width = after_first.shape
    group = min(16, part)
    tiles = part // group
    tokens = frames * frame_count * group
    hidden_width = w_u.shape[1]
    widths = (hidden_width, hidden_width, width, width, width, width, width, 3 * width)
    own = lambda columns: pl.BlockSpec((tokens, columns), lambda t: (t, 0))
    hbm = pl.BlockSpec(memory_space=pl.ANY)
    rows = 2 * tiles * tokens
    traded = jax.ShapeDtypeStruct(after_first.shape, bf16)
    slab = (frames, frame_count, group, width)
    return pl.pallas_call(
        functools.partial(middle_kernel, clips, frames, tiles),
        grid=(2 * tiles,),
        in_specs=[
            hbm, hbm, hbm, hbm, full(loss.shape), full(mod.shape), full(w_b.shape),
            full(w_u.shape), full(w_d.shape),
        ],
        out_specs=[own(columns) for columns in widths]
        + [pl.BlockSpec((None, 16, width), lambda t: (t // tiles, 0, 0))]
        + [hbm] * 6,
        out_shape=[jax.ShapeDtypeStruct((rows, columns), bf16) for columns in widths]
        + [
            jax.ShapeDtypeStruct((2, 16, width), f32),
            traded, traded, traded, traded,
            jax.ShapeDtypeStruct((frame_count, frames * part, width), bf16),
            traded,
        ],
        scratch_shapes=[
            VMEM((tokens, 3 * width), bf16),
            VMEM((16, tokens), f32),
            VMEM((tokens, tokens), f32),
            VMEM((tokens, width), bf16),
            VMEM((2,) + slab, bf16),
            VMEM((2,) + slab, bf16),
            VMEM((2 * tiles,) + slab, bf16),
            VMEM((2 * tiles,) + slab, bf16),
            DMA((frames - 1,)), DMA((frames - 1,)),
            DMA((frames - 1,)), DMA((frames - 1,)),
            DMA((tiles, frames - 1)), DMA((tiles, frames - 1)),
            DMA((tiles, frames - 1)), DMA((tiles, frames - 1)),
            DMA((2, 2)), DMA((2,)), DMA((2, 2 * tiles)),
        ],
        compiler_params=pltpu.CompilerParams(
            collective_id=2, has_side_effects=True, vmem_limit_bytes=VMEM_LIMIT
        ),
    )(after_first, cot_first, after_later, cotangent, loss, mod, w_b, w_u, w_d)


def space_back_kernel(
    clip, grad_ref, x_ref, mod, w_c, qkv, branch, totals,
    out_ref, gb_ref, gqkv_ref, sums, gmix,
):
    width = x_ref.shape[-1]
    tokens = x_ref.shape[-2]
    row = clip * 9
    piece = lambda number: mod[row + number : row + number + 1, :]

    @pl.when(pl.program_id(0) == 0)
    def _():
        sums[...] = jnp.zeros_like(sums)

    grad = grad_ref[...].reshape(tokens, width).astype(f32)
    grad_branch = (grad * piece(2)).astype(bf16)
    gb_ref[...] = grad_branch
    sums[2:3, :] += column_sum(grad * branch[...].astype(f32))
    sums[3:4, :] += column_sum(grad_branch.astype(f32))
    gmix[...] = dot(grad_branch, w_c[:, 3 * width :], 1, 1).astype(bf16)
    attend_back(qkv, gmix, totals, gqkv_ref, width, None)
    grad_hidden = dot(gqkv_ref[...], w_c[:, : 3 * width], 1, 1)
    norm, scale = normed(x_ref[...].reshape(tokens, width).astype(f32))
    sums[0:1, :] += column_sum(grad_hidden)
    sums[1:2, :] += column_sum(grad_hidden * norm)
    result = grad + norm_back(grad_hidden, 1.0 + piece(1), norm, scale)
    out_ref[...] = result.reshape(out_ref.shape)


def space_back_next(count, clip, *refs):
    space_back_kernel(clip, *refs[:7], *refs[7 + count :])


def space_back_call(clip, grad, x, mod, w_c, qkv, branch, totals, earlier):
    clip_count, frame_count, tokens, width = x.shape
    frames = grad.shape[0]
    part = grad.shape[2]
    rows = frame_count * tokens
    by_frame = lambda columns: pl.BlockSpec(
        (None, tokens, columns), lambda f: (clip * frame_count + f, 0, 0)
    )
    own = lambda columns: pl.BlockSpec((tokens, columns), lambda f: (clip * frame_count + f, 0))
    in_specs = [
        pl.BlockSpec((frames, 1, part, width), lambda f: (0, f, 0, 0)),
        pl.BlockSpec((1, 1, tokens, width), lambda f: (clip, f, 0, 0)),
        full(mod.shape),
        full(w_c.shape),
        by_frame(3 * width),
        by_frame(width),
        pl.BlockSpec((None, 16, tokens), lambda f: (clip * frame_count + f, 0, 0)),
    ]
    args = [grad, x, mod, w_c, qkv, branch, totals]
    body = functools.partial(space_back_kernel, clip)
    aliases = {}
    if earlier is not None:
        in_specs += [pl.BlockSpec(memory_space=pl.ANY)] * len(earlier)
        args += list(earlier)
        aliases = {7 + number: number for number in range(len(earlier))}
        body = functools.partial(space_back_next, len(earlier), clip)
    return pl.pallas_call(
        body,
        grid=(frame_count,),
        in_specs=in_specs,
        out_specs=[
            pl.BlockSpec((1, 1, tokens, width), lambda f: (clip, f, 0, 0)),
            own(width),
            own(3 * width),
            pl.BlockSpec((8, width), lambda f: (0, 0)),
        ],
        out_shape=[
            jax.ShapeDtypeStruct(x.shape, f32),
            jax.ShapeDtypeStruct((clip_count * rows, width), bf16),
            jax.ShapeDtypeStruct((clip_count * rows, 3 * width), bf16),
            jax.ShapeDtypeStruct((8, width), f32),
        ],
        scratch_shapes=[VMEM((tokens, width), bf16)],
        input_output_aliases=aliases,
        compiler_params=pltpu.CompilerParams(vmem_limit_bytes=VMEM_LIMIT),
        cost_estimate=pl.CostEstimate(
            flops=rows * 20_000_000, bytes_accessed=rows * width * 20, transcendentals=0
        ),
    )(*args)


def shards(
    inputs, cotangent, time_steps, weight_index, ada_weight, ada_bias, space_qkv, space_out,
    space_out_bias, time_qkv, time_out, time_out_bias, up_weight, up_bias, down_weight, down_bias,
):
    clip_count, frame_count, patch_count, width = inputs.shape
    clips, frames = lax.axis_size("clip"), lax.axis_size("frame")
    owners = clips * frames
    owner = lax.axis_index("clip") * frames + lax.axis_index("frame")
    part = patch_count // frames
    rows = ada_weight.shape[0]

    embed = jax.nn.silu(embed_steps(time_steps, width)).astype(bf16)
    embed = jnp.pad(embed, ((0, 16 - clip_count), (0, 0)))
    place = lax.broadcasted_iota(jnp.int32, (width, 128), 0) - owner * rows
    lane = lax.broadcasted_iota(jnp.int32, (width, 128), 1)
    select = ((place == lane) & (lane < rows)).astype(bf16)
    ada = jnp.pad(ada_weight, ((0, 128 - rows), (0, 0)))

    def spread_bias(vector):
        length = vector.shape[0]
        empty = jnp.zeros((owners * length,), f32)
        return lax.dynamic_update_slice(empty, vector.astype(f32), (owner * length,)).reshape(
            -1, width
        )

    bias = jnp.concatenate(
        [
            spread_bias(vector)
            for vector in (ada_bias, space_out_bias, time_out_bias, up_bias, down_bias)
        ],
        axis=0,
    )
    sh_c = jnp.concatenate([space_qkv, space_out], axis=1)
    sh_b = jnp.concatenate([time_qkv, time_out], axis=1)
    (
        w_c, w_b, w_u, w_d, mod, chosen, totals, hidden_one, qkv_one, mixed_one, branch_one,
        after_first, after_later, cot_first,
    ) = start_call(
        clips, frames, inputs, cotangent, sh_c, sh_b, up_weight, down_weight, embed, select, ada,
        bias,
    )

    def exchange(values):
        return lax.all_to_all(values, "frame", split_axis=0, concat_axis=0, tiled=True)

    loss = jnp.exp2(weight_index.astype(f32) * 0.5 - 1.0)
    loss = jnp.broadcast_to(loss[:, None], (clip_count, width))
    (
        act, gup, h3, gb3, mixed_two, gb2, h2, gqkv_two, mid_sums, _, _, grad_first,
        grad_later, out_first, out_later,
    ) = middle_call(
        clips, frames, after_first, cot_first, after_later, cotangent, loss, mod, w_b, w_u, w_d
    )
    grads = [grad_first, exchange(grad_later)]

    earlier = None
    space_sums = []
    for clip in range(clip_count):
        *earlier, sums = space_back_call(
            clip, grads[clip], inputs, mod, w_c, qkv_one, branch_one, totals, earlier
        )
        space_sums.append(sums)
    input_grad, gb1, gqkv_one = earlier
    pieces = []
    for clip in range(clip_count):
        pieces += [space_sums[clip][0:3], mid_sums[clip][0:6]]
    pieces.append(sum(entry[3:4] for entry in space_sums))
    pieces.append(sum(entry[6:12] for entry in mid_sums))
    small = jnp.concatenate(pieces, axis=0)
    small = jnp.pad(small, ((0, ROWS - small.shape[0]), (0, 0)))
    picked = chosen.reshape(clips, 16, 128)[:, :clip_count].reshape(clips * clip_count, 128)
    out_second, grad_ada, sums, own_u, own_d, own_b, own_bo, own_c, own_co = grad_call(
        clips, frames, clip_count, small, picked.astype(f32).T, out_later, h3, gup, act, gb3, h2, gqkv_two,
        mixed_two, gb2, hidden_one.reshape(-1, width), gqkv_one, mixed_one.reshape(-1, width), gb1,
    )
    biases = sums[9:]
    outputs = jnp.stack([out_first, out_second])

    def own_slice(vector):
        length = vector.shape[0] // owners
        return lax.dynamic_slice_in_dim(vector, owner * length, length, 0)

    return (
        outputs,
        input_grad,
        grad_ada,
        own_slice(sums[:9].reshape(-1)),
        own_c,
        own_co,
        own_slice(biases[0]),
        own_b,
        own_bo,
        own_slice(biases[1]),
        own_u,
        own_slice(biases[2:6].reshape(-1)),
        own_d,
        own_slice(biases[6]),
    )


def solution(mesh):
    tokens = P("clip", "frame", None, None)
    matrix = P(("clip", "frame"), None)
    vector = P(("clip", "frame"))
    in_specs = (
        tokens, tokens, P("clip"), P("clip"), matrix, vector, matrix, matrix, vector, matrix,
        matrix, vector, matrix, vector, matrix, vector,
    )
    out_specs = (
        tokens, tokens, matrix, vector, matrix, matrix, vector, matrix, matrix, vector, matrix,
        vector, matrix, vector,
    )
    return jax.shard_map(shards, mesh=mesh, in_specs=in_specs, out_specs=out_specs, check_vma=False)
```

```python
import functools
import math

import jax
import jax.numpy as jnp
from jax import lax
from jax.experimental import pallas as pl
from jax.experimental.pallas import tpu as pltpu
from jax.sharding import PartitionSpec as P

HEADS = 12
HEAD = 64
PAIRS = HEADS // 2
ROWS = 32
GELU_C = math.sqrt(2.0 / math.pi)
GELU_A = 0.044715
VMEM_LIMIT = 58 << 20

f32 = jnp.float32
bf16 = jnp.bfloat16
highest = lax.Precision.HIGHEST
MESH = pl.DeviceIdType.MESH
VMEM = pltpu.VMEM
DMA = pltpu.SemaphoreType.DMA


def embed_steps(time_steps, model_width):
    half_width = model_width // 2
    frequencies = jnp.exp(
        -math.log(10000.0) * jnp.arange(half_width, dtype=f32) / half_width
    )
    angles = time_steps.astype(f32)[:, None] * frequencies[None, :]
    return jnp.concatenate([jnp.cos(angles), jnp.sin(angles)], axis=1)


def dot(left, right, left_dim, right_dim):
    return lax.dot_general(
        left, right, (((left_dim,), (right_dim,)), ((), ())), preferred_element_type=f32
    )


def flip(index, mask):
    bit = 1
    while bit <= mask:
        if mask & bit:
            index = index + bit * (1 - 2 * ((index // bit) % 2))
        bit *= 2
    return index


def span(masks):
    out = [0]
    for mask in masks:
        out = out + [entry ^ mask for entry in out]
    return out


def frame_masks(frames):
    masks, bit = [], 1
    while bit < frames:
        masks.append(bit)
        bit *= 2
    if len(masks) > 1:
        masks = [frames - 1] + masks[:-1]
    return masks


def clip_tail_masks(clips):
    masks, bit = [], 2
    while bit < clips:
        masks.append(bit)
        bit *= 2
    return masks


def greet(clips, frames):
    clip, frame = lax.axis_index("clip"), lax.axis_index("frame")
    barrier = pltpu.get_barrier_semaphore()
    for step in range(1, clips):
        pl.semaphore_signal(
            barrier, inc=1, device_id={"clip": lax.rem(clip + step, clips)}, device_id_type=MESH
        )
    for step in range(1, frames):
        pl.semaphore_signal(
            barrier, inc=1, device_id={"frame": lax.rem(frame + step, frames)}, device_id_type=MESH
        )
    pl.semaphore_wait(barrier, clips + frames - 2)


def spread(axis, size, source_of, target, send_sems, recv_sems):
    me = lax.axis_index(axis)
    copies = []
    for step in range(1, size):
        peer = lax.rem(me + step, size)
        copy = pltpu.make_async_remote_copy(
            src_ref=source_of(peer),
            dst_ref=target.at[me],
            send_sem=send_sems.at[step - 1],
            recv_sem=recv_sems.at[step - 1],
            device_id={axis: peer},
            device_id_type=MESH,
        )
        copy.start()
        copies.append(copy)
    return copies


def start_kernel(
    clips, frames, clip_count,
    x_ref, cotangent, sh_c, sh_b, sh_u, sh_d, embed, select, ada, bias,
    w_c, w_b, w_u, w_d, mod, chosen, totals, hidden_out, qkv_out, mixed_out, branch_out,
    after_first, after_later, cot_first,
    v_c, z_c, z_b, z_u, z_d, st_w, b_c, b_b, b_u, b_d,
    embeds, parts, terms, arrived, held, lined, hidden, qkv, mixed, branch, after,
    zs, zr, cs, cr, xs, xr, ls, es, er, ps, pr, fs, fr, ts, tr, hs, hr, os, ws,
):
    clip, frame = lax.axis_index("clip"), lax.axis_index("frame")
    shards_in = (sh_c, sh_b, sh_u, sh_d)
    zoned = (z_c, z_b, z_u, z_d)
    blocks = (b_c, b_b, b_u, b_d)
    wholes = (v_c, w_b, w_u, w_d)
    width = mod.shape[1]
    frame_count, tokens = x_ref.shape[1], x_ref.shape[2]
    part = tokens // frames
    greet(clips, frames)
    masks = frame_masks(frames)
    sends = []
    stage = {}

    def frame_step(group, step):
        number = (1 << step) - 1
        copies = []
        for offset in span(masks[:step]):
            slot = flip(frame, offset)
            source = shards_in[group] if offset == 0 else zoned[group].at[slot]
            copy = pltpu.make_async_remote_copy(
                src_ref=source,
                dst_ref=zoned[group].at[slot],
                send_sem=zs.at[group, number],
                recv_sem=zr.at[group, number],
                device_id={"frame": flip(frame, masks[step])},
                device_id_type=MESH,
            )
            copy.start()
            copies.append(copy)
            number += 1
        sends.extend(copies)
        stage[group] = copies

    def frame_rest(group):
        for step in range(1, len(masks)):
            for copy in stage[group]:
                copy.wait_recv()
            frame_step(group, step)

    tail = clip_tail_masks(clips)
    steps = len(tail)
    orders = (tail, tail[::-1])
    moving = {}

    def block_send(group, half, step, position, offset):
        whole = wholes[group]
        block_rows = whole.shape[0] // clips
        columns = whole.shape[1] // 2
        rows = pl.ds(pl.multiple_of(flip(clip, offset) * block_rows, block_rows), block_rows)
        lanes = pl.ds(half * columns, columns)
        target = whole.at[rows, lanes]
        number = (1 << step) - 1 + position
        copy = pltpu.make_async_remote_copy(
            src_ref=blocks[group].at[:, lanes] if offset == 0 else target,
            dst_ref=target,
            send_sem=xs.at[group, half, number],
            recv_sem=xr.at[group, half, number],
            device_id={"clip": flip(clip, orders[half][step])},
            device_id_type=MESH,
        )
        copy.start()
        moving[group, half, number] = copy

    core_copies = {group: [] for group in range(4)}

    def core_send(group, offset):
        whole = wholes[group]
        block_rows = whole.shape[0] // clips
        rows = pl.ds(pl.multiple_of(flip(clip, offset) * block_rows, block_rows), block_rows)
        number = len(core_copies[group])
        copy = pltpu.make_async_remote_copy(
            src_ref=blocks[group] if offset == 0 else whole.at[rows, :],
            dst_ref=whole.at[rows, :],
            send_sem=cs.at[group, number],
            recv_sem=cr.at[group, number],
            device_id={"clip": flip(clip, 1)},
            device_id_type=MESH,
        )
        copy.start()
        core_copies[group].append(copy)

    local_copies = []

    def block_ready(group):
        for copy in stage[group]:
            copy.wait_recv()
        rows, columns = shards_in[group].shape
        block_rows = frames * rows
        if rows % 16:
            for slot in range(frames):
                st_w[slot * rows : (slot + 1) * rows, :columns] = zoned[group][slot].astype(f32)
            blocks[group][...] = st_w[:block_rows, :columns].astype(bf16)
        else:
            for slot in range(frames):
                blocks[group][slot * rows : (slot + 1) * rows, :] = zoned[group][slot]
        for step in range(steps):
            for half in range(2):
                block_send(group, half, step, 0, 0)
        core_send(group, 0)
        place = pl.ds(pl.multiple_of(clip * block_rows, block_rows), block_rows)
        keep = pltpu.make_async_copy(blocks[group], wholes[group].at[place, :], ls.at[group])
        keep.start()
        local_copies.append(keep)

    def block_forward(group):
        for step in range(1, steps):
            for half in range(2):
                for position in range(1 << (step - 1), 1 << step):
                    moving[group, half, position - 1].wait_recv()
                for later in range(step, steps):
                    for position, offset in enumerate(span(orders[half][:later])):
                        if (1 << (step - 1)) <= position < (1 << step):
                            block_send(group, half, later, position, offset)

    def block_finish(group):
        last = (1 << (steps - 1)) - 1
        for half in range(2):
            for number in range(last, (1 << steps) - 1):
                moving[group, half, number].wait_recv()
        for offset in span(tail)[1:]:
            core_send(group, offset)

    def core_finish(group):
        for copy in core_copies[group]:
            copy.wait_recv()

    frame_step(0, 0)
    own = spread("clip", clips, lambda peer: embed, embeds, es, er)
    sends.extend(own)
    embeds[clip] = embed[...]
    for group in range(4):
        zoned[group][frame] = shards_in[group][...]
    frame_rest(0)
    for copy in own:
        copy.wait_recv()
    picked = dot(embeds[...].reshape(clips * 16, width), select[...], 1, 0).astype(bf16)
    chosen[...] = picked
    parts[...] = dot(picked, ada[...], 1, 0)
    for peer in range(clips):
        for local in range(clip_count):
            row = peer * 16 + local
            for piece in range(9):
                terms[peer, local * 9 + piece : local * 9 + piece + 1, :] = (
                    parts[row : row + 1, piece * width : (piece + 1) * width]
                    + bias[piece : piece + 1, :]
                )
        base = clip_count * 9
        terms[peer, base : base + 7, :] = bias[9:16, :]
        if base + 7 < ROWS:
            terms[peer, base + 7 : ROWS, :] = jnp.zeros((ROWS - base - 7, width), f32)
    own = spread("clip", clips, lambda peer: terms.at[peer], arrived, ps, pr)
    sends.extend(own)
    arrived[clip] = terms[clip]
    block_ready(0)
    for group in range(1, 4):
        frame_step(group, 0)
    for copy in own:
        copy.wait_recv()
    total = arrived[0]
    for peer in range(1, clips):
        total = total + arrived[peer]
    held[...] = total
    own = spread("frame", frames, lambda peer: held, lined, fs, fr)
    sends.extend(own)
    lined[frame] = total
    for group in range(1, 4):
        frame_rest(group)

    cot_copies = []
    for step in range(1, frames):
        peer = lax.rem(frame + step, frames)
        copy = pltpu.make_async_remote_copy(
            src_ref=cotangent.at[0, :, pl.ds(pl.multiple_of(peer * part, part), part), :],
            dst_ref=cot_first.at[frame],
            send_sem=ts.at[step - 1],
            recv_sem=tr.at[step - 1],
            device_id={"frame": peer},
            device_id_type=MESH,
        )
        copy.start()
        cot_copies.append(copy)
    keep = pltpu.make_async_copy(
        cotangent.at[0, :, pl.ds(pl.multiple_of(frame * part, part), part), :],
        cot_first.at[frame],
        ls.at[4],
    )
    keep.start()
    local_copies.append(keep)

    for copy in own:
        copy.wait_recv()
    total = lined[0]
    for peer in range(1, frames):
        total = total + lined[peer]
    mod[...] = total
    block_forward(0)
    for group in range(1, 4):
        block_ready(group)
    block_finish(0)
    core_finish(0)
    local_copies[0].wait()

    keep = pltpu.make_async_copy(v_c, w_c, ls.at[5])
    keep.start()
    local_copies.append(keep)

    def after_copy(f, step):
        peer = lax.rem(frame + step, frames)
        return pltpu.make_async_remote_copy(
            src_ref=after.at[f, pl.ds(pl.multiple_of(peer * part, part), part), :],
            dst_ref=after_first.at[frame, f],
            send_sem=hs.at[f, step - 1],
            recv_sem=hr.at[f, step - 1],
            device_id={"frame": peer},
            device_id_type=MESH,
        )

    def own_after(f):
        return pltpu.make_async_copy(
            after.at[f, pl.ds(pl.multiple_of(frame * part, part), part), :],
            after_first.at[frame, f],
            os.at[f],
        )

    def later_after(f):
        return pltpu.make_async_copy(after.at[f], after_later.at[f - frame_count], os.at[f])

    kept = ((hidden, hidden_out), (qkv, qkv_out), (mixed, mixed_out), (branch, branch_out))

    def write_back(f):
        return [
            pltpu.make_async_copy(source.at[f], target.at[f], ws.at[number, f])
            for number, (source, target) in enumerate(kept)
        ]

    for local in range(clip_count):
        row = local * 9

        def one_frame(index, carry):
            f = local * frame_count + index
            values = x_ref[local, index].astype(f32)
            norm, _ = normed(values)
            scaled = norm * (1.0 + mod[row + 1 : row + 2, :]) + mod[row : row + 1, :]
            lowered = scaled.astype(bf16)
            hidden[f] = lowered
            qkv[f] = dot(lowered, v_c[:, : 3 * width], 1, 0).astype(bf16)
            attend(qkv.at[f], mixed.at[f], totals.at[f], width, None)
            grown = dot(mixed[f], v_c[:, 3 * width :], 1, 0) + mod[18:19, :]
            branch[f] = grown.astype(bf16)
            after[f] = (values + mod[row + 2 : row + 3, :] * grown).astype(bf16)
            if local == 0:
                for step in range(1, frames):
                    after_copy(f, step).start()
                own_after(f).start()
            else:
                later_after(f).start()
            for copy in write_back(f):
                copy.start()
            return carry

        lax.fori_loop(0, frame_count, one_frame, 0)
        if local == 0:
            block_forward(1)
    for group in range(2, 4):
        block_forward(group)
    for group in range(1, 4):
        block_finish(group)
    for group in range(1, 4):
        core_finish(group)

    def settle(f, carry):
        for step in range(1, frames):
            copy = after_copy(f, step)
            copy.wait_recv()
            copy.wait_send()
        own_after(f).wait()
        return carry

    lax.fori_loop(0, frame_count, settle, 0)

    def settle_later(f, carry):
        later_after(f).wait()
        return carry

    lax.fori_loop(frame_count, clip_count * frame_count, settle_later, 0)

    def settle_kept(f, carry):
        for copy in write_back(f):
            copy.wait()
        return carry

    lax.fori_loop(0, clip_count * frame_count, settle_kept, 0)
    for copy in cot_copies:
        copy.wait_recv()
        copy.wait_send()
    for copy in local_copies[1:]:
        copy.wait()
    for copy in moving.values():
        copy.wait_send()
    for group in range(4):
        for copy in core_copies[group]:
            copy.wait_send()
    for copy in sends:
        copy.wait_send()


def start_call(
    clips, frames, inputs, cotangent, sh_c, sh_b, sh_u, sh_d, embed, select, ada, bias
):
    clip_count, frame_count, tokens, width = inputs.shape
    rows, columns = sh_c.shape
    rows_d = sh_d.shape[0]
    block = frames * rows
    block_d = frames * rows_d
    peers = max(clips // 2 - 1, 1)
    total = clip_count * frame_count
    part = tokens // frames
    whole = jax.ShapeDtypeStruct((clips * block, columns), bf16)
    vmem = pl.BlockSpec(memory_space=VMEM)
    hbm = pl.BlockSpec(memory_space=pl.ANY)
    zoned = lambda height, lanes: VMEM((frames, height, lanes), bf16)
    saved = lambda lanes: jax.ShapeDtypeStruct((total, tokens, lanes), bf16)
    lent = lambda lanes: VMEM((total, tokens, lanes), bf16)
    traded = jax.ShapeDtypeStruct((frames, frame_count, part, width), bf16)
    return pl.pallas_call(
        functools.partial(start_kernel, clips, frames, clip_count),
        out_shape=(
            whole, whole, whole,
            jax.ShapeDtypeStruct((clips * block_d, width), bf16),
            jax.ShapeDtypeStruct((ROWS, width), f32),
            jax.ShapeDtypeStruct((clips * 16, 128), bf16),
            jax.ShapeDtypeStruct((total, 16, tokens), f32),
            saved(width), saved(3 * width), saved(width), saved(width),
            traded,
            jax.ShapeDtypeStruct(((clip_count - 1) * frame_count, tokens, width), bf16),
            traded,
        ),
        in_specs=[vmem, hbm] + [vmem] * 8,
        out_specs=(hbm, hbm, hbm, hbm, vmem, vmem, vmem) + (hbm,) * 7,
        scratch_shapes=[
            VMEM((clips * block, columns), bf16),
            zoned(rows, columns), zoned(rows, columns), zoned(rows, columns), zoned(rows_d, width),
            VMEM((max(block, block_d), columns), f32),
            VMEM((block, columns), bf16),
            VMEM((block, columns), bf16),
            VMEM((block, columns), bf16),
            VMEM((block_d, width), bf16),
            VMEM((clips, 16, width), bf16),
            VMEM((clips * 16, 9 * width), f32),
            VMEM((clips, ROWS, width), f32),
            VMEM((clips, ROWS, width), f32),
            VMEM((ROWS, width), f32),
            VMEM((frames, ROWS, width), f32),
            lent(width), lent(3 * width), lent(width), lent(width), lent(width),
            DMA((4, frames - 1)), DMA((4, frames - 1)),
            DMA((4, clips // 2)), DMA((4, clips // 2)),
            DMA((4, 2, peers)), DMA((4, 2, peers)),
            DMA((6,)),
            DMA((clips - 1,)), DMA((clips - 1,)),
            DMA((clips - 1,)), DMA((clips - 1,)),
            DMA((frames - 1,)), DMA((frames - 1,)),
            DMA((frames - 1,)), DMA((frames - 1,)),
            DMA((frame_count, frames - 1)), DMA((frame_count, frames - 1)),
            DMA((total,)),
            DMA((4, total)),
        ],
        compiler_params=pltpu.CompilerParams(
            collective_id=0, has_side_effects=True, vmem_limit_bytes=VMEM_LIMIT
        ),
    )(inputs, cotangent, sh_c, sh_b, sh_u, sh_d, embed, select, ada, bias)


STEP = 512
SLOTS = 3


def grad_kernel(
    clips, frames, clip_count,
    small, chosen, out_all, h3, gup, act, gb3, h2, gqkv2, mix2, gb2, h1, gqkv1, mix1, gb1,
    outputs, grad_ada, bias_sums, out_u, out_d, out_b, out_bo, out_c, out_co,
    sum_w, sum_d, core_w, core_d, side_w, side_d, line_w, line_d, last_w, last_d,
    left, right, total, gathered, lined, held,
    lsem, rsem, cs, cr, xs, xr, zs, zr, fs, fr, ps, pr, os, orr, ks,
):
    clip, frame = lax.axis_index("clip"), lax.axis_index("frame")
    tokens = h3.shape[0]
    width = small.shape[1]
    wide = sum_w.shape[-1]
    narrow = sum_d.shape[-1]
    tail = clip_tail_masks(clips)
    orders = (tail, tail[::-1])
    masks = frame_masks(frames)
    greet(clips, frames)
    first = spread("frame", frames, lambda peer: small, lined, fs, fr)
    lined[frame] = small[...]
    part = out_all.shape[3]
    frame_count = out_all.shape[2]
    out_copies = []
    mine = pl.ds(pl.multiple_of(frame * part, part), part)

    def send_output(number):
        local, index = divmod(number, frame_count)
        for hop in range(1, frames):
            peer = lax.rem(frame + hop, frames)
            copy = pltpu.make_async_remote_copy(
                src_ref=out_all.at[local, peer, index],
                dst_ref=outputs.at[local, index, mine, :],
                send_sem=os.at[number, hop - 1],
                recv_sem=orr.at[number, hop - 1],
                device_id={"frame": peer},
                device_id_type=MESH,
            )
            copy.start()
            out_copies.append(copy)

    own_outs = []
    for local in range(clip_count):
        copy = pltpu.make_async_copy(
            out_all.at[local, frame], outputs.at[local, :, mine, :], ks.at[local]
        )
        copy.start()
        own_outs.append(copy)

    chunks = [
        (1, 0, [(act, gb3, 0, 0, narrow)], out_d, 0),
        (1, 1, [(act, gb3, narrow, 0, narrow)], out_d, narrow),
        (0, 0, [(h3, gup, 0, 0, wide)], out_u, 0),
        (0, 1, [(h3, gup, wide, 0, wide)], out_u, wide),
        (0, 2, [(h2, gqkv2, 0, 0, wide)], out_b, 0),
        (0, 3, [(h2, gqkv2, wide, 0, width), (mix2, gb2, 0, width, width)], out_b, wide),
        (0, 4, [(h1, gqkv1, 0, 0, wide)], out_c, 0),
        (0, 5, [(h1, gqkv1, wide, 0, width), (mix1, gb1, 0, width, width)], out_c, wide),
    ]
    sums, cores, sides = (sum_w, sum_d), (core_w, core_d), (side_w, side_d)
    lines, lasts = (line_w, line_d), (last_w, last_d)
    flights = {}

    steps = tokens // STEP
    line_up = []
    for kind, _, parts, _, _ in chunks:
        for part in parts:
            for group in range(part[0].shape[1] // width):
                line_up.append(part[:3] + (part[3] + group * part[4], part[4], group))
    begins = [0]
    for kind, _, parts, _, _ in chunks:
        begins.append(begins[-1] + sum(part[0].shape[1] // width for part in parts))

    def load(entry, step, slot):
        one, other, begin, _, lanes, group = line_up[entry]
        rows = pl.ds(pl.multiple_of(step * STEP, STEP), STEP)
        return (
            pltpu.make_async_copy(
                one.at[rows, pl.ds(group * width, width)], left.at[slot], lsem.at[slot]
            ),
            pltpu.make_async_copy(
                other.at[rows, pl.ds(begin, lanes)],
                right.at[slot, :, pl.ds(0, lanes)],
                rsem.at[slot],
            ),
        )

    def place_of(entry, step):
        return lax.rem(entry * steps + step, SLOTS)

    def multiply(number):
        kind, place = chunks[number][:2]
        for entry in range(begins[number], begins[number + 1]):
            at, lanes = line_up[entry][3:5]

            def body(step, carry):
                ahead = step + SLOTS - 1

                @pl.when(ahead < steps)
                def _():
                    for copy in load(entry, ahead, place_of(entry, ahead)):
                        copy.start()

                if entry + 1 < len(line_up):

                    @pl.when(ahead >= steps)
                    def _():
                        for copy in load(entry + 1, ahead - steps, place_of(entry, ahead)):
                            copy.start()

                slot = place_of(entry, step)
                for copy in load(entry, step, slot):
                    copy.wait()
                columns = slice(at, at + lanes)
                before = jnp.where(step > 0, total[:, columns], 0.0)
                total[:, columns] = before + dot(left[slot], right[slot, :, :lanes], 0, 0)
                return carry

            lax.fori_loop(0, steps, body, 0)
        rows, lanes = sums[kind].shape[2:]
        for block in range(clips):
            begin = block * rows
            column = begin // width * lanes
            begin = begin % width
            sums[kind][place, block] = total[begin : begin + rows, column : column + lanes].astype(
                bf16
            )

    def core_start(number):
        kind, place = chunks[number][:2]
        copies = []
        for position, offset in enumerate(span(tail)):
            copy = pltpu.make_async_remote_copy(
                src_ref=sums[kind].at[place, flip(clip, offset ^ 1)],
                dst_ref=cores[kind].at[place, position],
                send_sem=cs.at[number, position],
                recv_sem=cr.at[number, position],
                device_id={"clip": flip(clip, 1)},
                device_id_type=MESH,
            )
            copy.start()
            copies.append(copy)
        flights[number, "core"] = copies

    def half_of(kind, half):
        if kind:
            rows = sums[kind].shape[2] // 2
            return (slice(half * rows, (half + 1) * rows), slice(None))
        lanes = sums[kind].shape[3] // 2
        return (slice(None), slice(half * lanes, (half + 1) * lanes))

    def side_start(number, step):
        kind, place = chunks[number][:2]
        copies = []
        for half in range(2):
            mask = orders[half][step]
            for position, offset in enumerate(span(orders[half][:step])):
                entry = (1 << step) - 1 + position
                copy = pltpu.make_async_remote_copy(
                    src_ref=sums[kind].at[(place, flip(clip, offset ^ mask)) + half_of(kind, half)],
                    dst_ref=sides[kind].at[place, half, entry],
                    send_sem=xs.at[number, half, entry],
                    recv_sem=xr.at[number, half, entry],
                    device_id={"clip": flip(clip, mask)},
                    device_id_type=MESH,
                )
                copy.start()
                copies.append(copy)
        flights[number, "side", step] = copies

    def core_add(number):
        kind, place = chunks[number][:2]
        for copy in flights[number, "core"]:
            copy.wait_recv()
        for position, offset in enumerate(span(tail)):
            block = flip(clip, offset)
            sums[kind][place, block] = (
                sums[kind][place, block].astype(f32) + cores[kind][place, position].astype(f32)
            ).astype(bf16)
        side_start(number, len(tail) - 1)

    def side_add(number, step):
        kind, place = chunks[number][:2]
        for copy in flights[number, "side", step]:
            copy.wait_recv()
        for half in range(2):
            for position, offset in enumerate(span(orders[half][:step])):
                entry = (1 << step) - 1 + position
                block = flip(clip, offset)
                where = (place, block) + half_of(kind, half)
                sums[kind][where] = (
                    sums[kind][where].astype(f32) + sides[kind][place, half, entry].astype(f32)
                ).astype(bf16)
        if step:
            side_start(number, step - 1)
        else:
            rows = lines[kind].shape[2]
            block = sums[kind][place, clip].astype(f32)
            for slot in range(frames):
                lines[kind][place, slot] = block[slot * rows : (slot + 1) * rows, :].astype(bf16)
            line_start(number, len(masks) - 1)

    def line_start(number, step):
        kind, place = chunks[number][:2]
        copies = []
        for position, offset in enumerate(span(masks[:step])):
            entry = (1 << step) - 1 + position
            copy = pltpu.make_async_remote_copy(
                src_ref=lines[kind].at[place, flip(frame, offset ^ masks[step])],
                dst_ref=lasts[kind].at[place, entry],
                send_sem=zs.at[number, entry],
                recv_sem=zr.at[number, entry],
                device_id={"frame": flip(frame, masks[step])},
                device_id_type=MESH,
            )
            copy.start()
            copies.append(copy)
        flights[number, "line", step] = copies

    def line_add(number, step):
        kind, place, _, target, begin = chunks[number]
        for copy in flights[number, "line", step]:
            copy.wait_recv()
        for position, offset in enumerate(span(masks[:step])):
            entry = (1 << step) - 1 + position
            slot = flip(frame, offset)
            value = lines[kind][place, slot].astype(f32) + lasts[kind][place, entry].astype(f32)
            if step:
                lines[kind][place, slot] = value.astype(bf16)
            elif begin + value.shape[1] > target.shape[1]:
                cut = target.shape[1] - begin
                target[:, begin:] = value[:, :cut]
                (out_bo if target is out_b else out_co)[...] = value[:, cut:]
            else:
                target[:, begin : begin + value.shape[1]] = value
        if step:
            line_start(number, step - 1)

    stages = [core_start, core_add]
    for step in range(len(tail))[::-1]:
        stages.append(functools.partial(side_add, step=step))
    for step in range(len(masks))[::-1]:
        stages.append(functools.partial(line_add, step=step))

    def finish_small():
        for copy in second:
            copy.wait_recv()
        rows = grad_ada.shape[0]
        for number in range(9):
            terms = [
                gathered[peer, local * 9 + number : local * 9 + number + 1, :]
                for peer in range(clips)
                for local in range(clip_count)
            ]
            terms = jnp.concatenate(terms, axis=0)
            grad_ada[:, number * width : (number + 1) * width] = lax.dot_general(
                chosen[...], terms, (((1,), (0,)), ((), ())), precision=highest,
                preferred_element_type=f32,
            )[:rows, :]
            bias_sums[number : number + 1, :] = column_sum(terms)
        base = clip_count * 9
        summed = gathered[0, base : base + 7, :]
        for peer in range(1, clips):
            summed = summed + gathered[peer, base : base + 7, :]
        bias_sums[9:16, :] = summed

    for step in range(SLOTS - 1):
        for copy in load(0, step, step):
            copy.start()
    second = None
    lags = [0, 1, 3]
    while len(lags) < len(stages):
        lags.append(lags[-1] + 1)
    for turn in range(len(chunks) + lags[-1]):
        for depth in range(len(stages))[::-1]:
            if depth > 0 and 0 <= turn - lags[depth] < len(chunks):
                stages[depth](turn - lags[depth])
        if turn < clip_count * frame_count:
            send_output(turn)
        if turn < len(chunks):
            multiply(turn)
            core_start(turn)
        if turn == len(chunks):
            finish_small()
        if turn == 0:
            for copy in first:
                copy.wait_recv()
            summed = lined[0]
            for peer in range(1, frames):
                summed = summed + lined[peer]
            held[...] = summed
            second = spread("clip", clips, lambda peer: held, gathered, ps, pr)
            gathered[clip] = summed
    for copy in own_outs:
        copy.wait()
    for copy in out_copies:
        copy.wait_recv()
        copy.wait_send()
    for copy in first + second:
        copy.wait_send()
    for copies in flights.values():
        for copy in copies:
            copy.wait_send()


def grad_call(clips, frames, clip_count, small, chosen, out_all, *operands):
    h3, gup, act = operands[:3]
    _, _, frame_count, part, _ = out_all.shape
    width, hidden = h3.shape[1], act.shape[1]
    owners = clips * frames
    wide, narrow = hidden // 2, width // 2
    rows_w, rows_d = width // owners, hidden // owners
    peers = max(clips // 2 - 1, 1)
    vmem = pl.BlockSpec(memory_space=VMEM)
    hbm = pl.BlockSpec(memory_space=pl.ANY)

    return pl.pallas_call(
        functools.partial(grad_kernel, clips, frames, clip_count),
        out_shape=(
            jax.ShapeDtypeStruct((clip_count, frame_count, frames * part, width), bf16),
            jax.ShapeDtypeStruct((rows_w, 9 * width), f32),
            jax.ShapeDtypeStruct((16, width), f32),
            jax.ShapeDtypeStruct((rows_w, hidden), f32),
            jax.ShapeDtypeStruct((rows_d, width), f32),
            jax.ShapeDtypeStruct((rows_w, 3 * width), f32),
            jax.ShapeDtypeStruct((rows_w, width), f32),
            jax.ShapeDtypeStruct((rows_w, 3 * width), f32),
            jax.ShapeDtypeStruct((rows_w, width), f32),
        ),
        in_specs=[vmem, vmem] + [hbm] * (1 + len(operands)),
        out_specs=(hbm,) + (vmem,) * 8,
        scratch_shapes=[
            VMEM((6, clips, rows_w * frames, wide), bf16),
            VMEM((2, clips, rows_d * frames, narrow), bf16),
            VMEM((6, clips // 2, rows_w * frames, wide), bf16),
            VMEM((2, clips // 2, rows_d * frames, narrow), bf16),
            VMEM((6, 2, peers, rows_w * frames, wide // 2), bf16),
            VMEM((2, 2, peers, rows_d * frames // 2, narrow), bf16),
            VMEM((6, frames, rows_w, wide), bf16),
            VMEM((2, frames, rows_d, narrow), bf16),
            VMEM((6, frames - 1, rows_w, wide), bf16),
            VMEM((2, frames - 1, rows_d, narrow), bf16),
            VMEM((SLOTS, STEP, width), bf16),
            VMEM((SLOTS, STEP, wide), bf16),
            VMEM((width, wide), f32),
            VMEM((clips,) + small.shape, f32),
            VMEM((frames,) + small.shape, f32),
            VMEM(small.shape, f32),
            DMA((SLOTS,)), DMA((SLOTS,)),
            DMA((8, clips // 2)), DMA((8, clips // 2)),
            DMA((8, 2, peers)), DMA((8, 2, peers)),
            DMA((8, frames - 1)), DMA((8, frames - 1)),
            DMA((frames - 1,)), DMA((frames - 1,)),
            DMA((clips - 1,)), DMA((clips - 1,)),
            DMA((clip_count * frame_count, frames - 1)),
            DMA((clip_count * frame_count, frames - 1)),
            DMA((clip_count,)),
        ],
        compiler_params=pltpu.CompilerParams(
            collective_id=1, has_side_effects=True, vmem_limit_bytes=VMEM_LIMIT
        ),
    )(small, chosen, out_all, *operands)


def normed(values):
    centred = values - jnp.mean(values, axis=-1, keepdims=True)
    scale = lax.rsqrt(jnp.mean(centred * centred, axis=-1, keepdims=True) + 1e-06)
    return centred * scale, scale


def norm_back(grad, scaled, norm, scale):
    inner = grad * scaled
    return scale * (
        inner
        - jnp.mean(inner, axis=-1, keepdims=True)
        - norm * jnp.mean(inner * norm, axis=-1, keepdims=True)
    )


def column_sum(values):
    return jnp.sum(values, axis=0, keepdims=True)


def attend(qkv, mixed, totals, width, mask):
    tokens = qkv.shape[0]
    low = lax.broadcasted_iota(jnp.int32, (tokens, 128), 1) < HEAD
    for pair in range(PAIRS):
        at = pair * 128
        queries = qkv[:, at : at + 128] * bf16(0.125)
        keys = qkv[:, width + at : width + at + 128]
        values = qkv[:, 2 * width + at : 2 * width + at + 128]
        halves = []
        for half in range(2):
            own = jnp.where(low if half == 0 else ~low, queries, bf16(0))
            scores = dot(keys, own, 1, 1)
            if mask is not None:
                scores = scores + mask[...]
            peak = jnp.max(scores, axis=0, keepdims=True)
            terms = jnp.exp(scores - peak)
            total = jnp.sum(terms, axis=0, keepdims=True)
            weights = (terms * (1.0 / total)).astype(bf16)
            totals[2 * pair + half : 2 * pair + half + 1, :] = peak + jnp.log(total)
            halves.append(dot(weights, values, 0, 0))
        mixed[:, at : at + 128] = jnp.where(low, halves[0], halves[1]).astype(bf16)


def attend_back(qkv, grad_mixed, totals, grad_qkv, width, mask):
    tokens = qkv.shape[0]
    low = lax.broadcasted_iota(jnp.int32, (tokens, 128), 1) < HEAD
    for pair in range(PAIRS):
        at = pair * 128
        queries = qkv[:, at : at + 128]
        keys = qkv[:, width + at : width + at + 128]
        values = qkv[:, 2 * width + at : 2 * width + at + 128]
        grads = grad_mixed[:, at : at + 128]
        halves = []
        for half in range(2):
            pick = low if half == 0 else ~low
            own = jnp.where(pick, queries * bf16(0.125), bf16(0))
            own_grads = jnp.where(pick, grads, bf16(0))
            scores = dot(keys, own, 1, 1)
            if mask is not None:
                scores = scores + mask[...]
            weights = jnp.exp(scores - totals[2 * pair + half : 2 * pair + half + 1, :])
            grad_weights = dot(values, own_grads, 1, 1)
            inner = jnp.sum(weights * grad_weights, axis=0, keepdims=True)
            grad_scores = (weights * (grad_weights - inner)).astype(bf16)
            halves.append(
                (
                    dot(grad_scores, keys, 0, 0),
                    dot(grad_scores, queries, 1, 0),
                    dot(weights.astype(bf16), grads, 1, 0),
                )
            )
        for part, factor in ((0, 0.125), (1, 0.125), (2, 1.0)):
            joined = jnp.where(low, halves[0][part], halves[1][part]) * factor
            start = part * width + at
            grad_qkv[:, start : start + 128] = joined.astype(bf16)


def full(shape):
    return pl.BlockSpec(shape, lambda *_: (0,) * len(shape), pipeline_mode=pl.Buffered(1))


def middle_kernel(
    clips, frames, tiles,
    after_first, cot_first, after_later, cotangent, loss, mod, w_b, w_u, w_d,
    act_ref, gup_ref, h3_ref, gb3_ref, mixed_ref, gb2_ref, h2_ref, gqkv_ref, sums,
    after_second, cot_second, grad_first, grad_later, out_all,
    qkv, totals, mask, gmix, after_tile, cot_tile, grad_stage, out_stage,
    ts, tr, us, ur, gs, gr, ls, ks, ws,
):
    frame = lax.axis_index("frame")
    step = pl.program_id(0)
    last = pl.num_programs(0) - 1
    clip = lax.div(step, tiles)
    tile = lax.rem(step, tiles)
    slot = lax.rem(step, 2)
    width = mod.shape[1]
    frame_count, group = after_tile.shape[2], after_tile.shape[3]
    part = tiles * group
    tokens = frames * frame_count * group
    row = clip * 9
    piece = lambda number: mod[pl.ds(row + number, 1), :]

    def own_part(index):
        return pl.ds(pl.multiple_of(index * part, part), part)

    def later_copies(number):
        copies = []
        for hop in range(1, frames):
            peer = lax.rem(frame + hop, frames)
            if number:
                source, target, send, recv = cotangent.at[1, :, own_part(peer), :], cot_second, us, ur
            else:
                source, target, send, recv = after_later.at[:, own_part(peer), :], after_second, ts, tr
            copies.append(
                pltpu.make_async_remote_copy(
                    src_ref=source,
                    dst_ref=target.at[frame],
                    send_sem=send.at[hop - 1],
                    recv_sem=recv.at[hop - 1],
                    device_id={"frame": peer},
                    device_id_type=MESH,
                )
            )
        return copies

    def own_copy(number):
        source = cotangent.at[1] if number else after_later
        target = cot_second if number else after_second
        return pltpu.make_async_copy(
            source.at[:, own_part(frame), :], target.at[frame], ks.at[number]
        )

    def load(source, number, index, place):
        rows = pl.ds(pl.multiple_of(index * group, group), group)
        target = (after_tile, cot_tile)[number].at[place]
        return pltpu.make_async_copy(source.at[:, :, rows, :], target, ls.at[place, number])

    def grad_copies(index):
        rows = pl.ds(pl.multiple_of(index * group, group), group)
        copies = []
        for hop in range(1, frames):
            peer = lax.rem(frame + hop, frames)
            copies.append(
                pltpu.make_async_remote_copy(
                    src_ref=grad_stage.at[index, peer],
                    dst_ref=grad_first.at[frame, :, rows, :],
                    send_sem=gs.at[index, hop - 1],
                    recv_sem=gr.at[index, hop - 1],
                    device_id={"frame": peer},
                    device_id_type=MESH,
                )
            )
        return copies

    def grad_own(index):
        rows = pl.ds(pl.multiple_of(index * group, group), group)
        return pltpu.make_async_copy(
            grad_stage.at[index, frame], grad_first.at[frame, :, rows, :], ws.at[0, index]
        )

    def grad_keep(index):
        place = index + tiles
        rows = pl.ds(pl.multiple_of(index * group, group), group)
        return pltpu.make_async_copy(
            grad_stage.at[place], grad_later.at[:, :, rows, :], ws.at[0, place]
        )

    def out_keep(number):
        rows = pl.ds(pl.multiple_of(lax.rem(number, tiles) * group, group), group)
        return pltpu.make_async_copy(
            out_stage.at[number], out_all.at[lax.div(number, tiles), :, :, rows, :], ws.at[1, number]
        )

    @pl.when(step == 0)
    def _():
        barrier = pltpu.get_barrier_semaphore()
        for hop in range(1, frames):
            pl.semaphore_signal(
                barrier,
                inc=1,
                device_id={"frame": lax.rem(frame + hop, frames)},
                device_id_type=MESH,
            )
        pl.semaphore_wait(barrier, frames - 1)
        load(after_first, 0, 0, 0).start()
        load(cot_first, 1, 0, 0).start()
        for number in range(2):
            for copy in later_copies(number):
                copy.start()
            own_copy(number).start()
        first = lax.broadcasted_iota(jnp.int32, (tokens, tokens), 0)
        second = lax.broadcasted_iota(jnp.int32, (tokens, tokens), 1)
        mask[...] = jnp.where(lax.rem(first, group) == lax.rem(second, group), 0.0, -1e30)

    @pl.when(step == tiles)
    def _():
        for copy in later_copies(0):
            copy.wait_recv()
        own_copy(0).wait()
        load(after_second, 0, 0, slot).start()

    load(after_first, 0, 0, slot).wait()

    @pl.when(step + 1 < tiles)
    def _():
        load(after_first, 0, step + 1, 1 - slot).start()
        load(cot_first, 1, step + 1, 1 - slot).start()

    @pl.when((step >= tiles) & (step < last))
    def _():
        load(after_second, 0, tile + 1, 1 - slot).start()

    @pl.when((step > tiles) & (step < last))
    def _():
        load(cot_second, 1, tile + 1, 1 - slot).start()

    @pl.when(tile == 0)
    def _():
        sums[...] = jnp.zeros_like(sums)

    def add(place, values):
        sums[place : place + 1, :] += values

    after = after_tile[slot].reshape(tokens, width).astype(f32)
    norm, scale = normed(after)
    hidden = (norm * (1.0 + piece(4)) + piece(3)).astype(bf16)
    h2_ref[...] = hidden
    qkv[...] = dot(hidden, w_b[:, : 3 * width], 1, 0).astype(bf16)
    attend(qkv, mixed_ref, totals, width, mask)
    branch_two = dot(mixed_ref[...], w_b[:, 3 * width :], 1, 0) + mod[19:20, :]
    after_two = after + piece(5) * branch_two
    norm_three, scale_three = normed(after_two)
    hidden = (norm_three * (1.0 + piece(7)) + piece(6)).astype(bf16)
    h3_ref[...] = hidden

    @pl.when(step == tiles)
    def _():
        for copy in later_copies(1):
            copy.wait_recv()
        own_copy(1).wait()
        load(cot_second, 1, 0, slot).start()
        if tiles > 1:
            load(cot_second, 1, 1, 1 - slot).start()

        def send(index, carry):
            for copy in grad_copies(index):
                copy.start()
            return carry

        lax.fori_loop(0, tiles, send, 0)

    load(cot_first, 1, 0, slot).wait()
    grad_out = cot_tile[slot].reshape(tokens, width).astype(f32) * loss[pl.ds(clip, 1), :]
    grad_branch = (grad_out * piece(8)).astype(bf16)
    gb3_ref[...] = grad_branch
    add(11, column_sum(grad_branch.astype(f32)))
    branch_three = jnp.zeros((tokens, width), f32)
    grad_hidden = jnp.zeros((tokens, width), f32)
    for chunk in range(w_u.shape[1] // width):
        cut = slice(chunk * width, (chunk + 1) * width)
        upper = dot(hidden, w_u[:, cut], 1, 0) + mod[20 + chunk : 21 + chunk, :]
        square = upper * upper
        bend = jnp.tanh(upper * (GELU_C + (GELU_C * GELU_A) * square))
        half = 0.5 + 0.5 * bend
        act = (upper * half).astype(bf16)
        slope = half + (0.5 * upper) * (1.0 - bend * bend) * (
            GELU_C + (3.0 * GELU_C * GELU_A) * square
        )
        act_ref[:, cut] = act
        branch_three += dot(act, w_d[cut, :], 1, 0)
        grad_upper = (dot(grad_branch, w_d[cut, :], 1, 1) * slope).astype(bf16)
        gup_ref[:, cut] = grad_upper
        add(7 + chunk, column_sum(grad_upper.astype(f32)))
        grad_hidden += dot(grad_upper, w_u[:, cut], 1, 1)
    branch_three += mod[24:25, :]
    out = (after_two + piece(8) * branch_three).astype(bf16)
    out_stage[step] = out.reshape(out_stage.shape[1:])
    add(5, column_sum(grad_out * branch_three))
    add(3, column_sum(grad_hidden))
    add(4, column_sum(grad_hidden * norm_three))
    grad_two = grad_out + norm_back(grad_hidden, 1.0 + piece(7), norm_three, scale_three)
    add(2, column_sum(grad_two * branch_two))
    grad_branch = (grad_two * piece(5)).astype(bf16)
    gb2_ref[...] = grad_branch
    add(6, column_sum(grad_branch.astype(f32)))
    gmix[...] = dot(grad_branch, w_b[:, 3 * width :], 1, 1).astype(bf16)
    attend_back(qkv, gmix, totals, gqkv_ref, width, mask)
    grad_hidden = dot(gqkv_ref[...], w_b[:, : 3 * width], 1, 1).astype(bf16).astype(f32)
    add(0, column_sum(grad_hidden))
    add(1, column_sum(grad_hidden * norm))
    grad_one = grad_two + norm_back(grad_hidden, 1.0 + piece(4), norm, scale)
    grad_stage[step] = grad_one.astype(bf16).reshape(grad_stage.shape[1:])

    out_keep(step).start()

    @pl.when(step < tiles)
    def _():
        grad_own(tile).start()

    @pl.when(step >= tiles)
    def _():
        grad_keep(tile).start()

    @pl.when(step == last)
    def _():
        for copy in later_copies(0) + later_copies(1):
            copy.wait_send()

        def settle(index, carry):
            for copy in grad_copies(index):
                copy.wait_send()
                copy.wait_recv()
            grad_own(index).wait()
            grad_keep(index).wait()
            out_keep(index).wait()
            out_keep(index + tiles).wait()
            return carry

        lax.fori_loop(0, tiles, settle, 0)


def middle_call(
    clips, frames, after_first, cot_first, after_later, cotangent, loss, mod, w_b, w_u, w_d
):
    _, frame_count, part, width = after_first.shape
    group = min(16, part)
    tiles = part // group
    tokens = frames * frame_count * group
    hidden_width = w_u.shape[1]
    widths = (hidden_width, hidden_width, width, width, width, width, width, 3 * width)
    own = lambda columns: pl.BlockSpec((tokens, columns), lambda t: (t, 0))
    hbm = pl.BlockSpec(memory_space=pl.ANY)
    rows = 2 * tiles * tokens
    traded = jax.ShapeDtypeStruct(after_first.shape, bf16)
    slab = (frames, frame_count, group, width)
    return pl.pallas_call(
        functools.partial(middle_kernel, clips, frames, tiles),
        grid=(2 * tiles,),
        in_specs=[
            hbm, hbm, hbm, hbm, full(loss.shape), full(mod.shape), full(w_b.shape),
            full(w_u.shape), full(w_d.shape),
        ],
        out_specs=[own(columns) for columns in widths]
        + [pl.BlockSpec((None, 16, width), lambda t: (t // tiles, 0, 0))]
        + [hbm] * 5,
        out_shape=[jax.ShapeDtypeStruct((rows, columns), bf16) for columns in widths]
        + [
            jax.ShapeDtypeStruct((2, 16, width), f32),
            traded, traded, traded, traded,
            jax.ShapeDtypeStruct((2,) + after_first.shape, bf16),
        ],
        scratch_shapes=[
            VMEM((tokens, 3 * width), bf16),
            VMEM((16, tokens), f32),
            VMEM((tokens, tokens), f32),
            VMEM((tokens, width), bf16),
            VMEM((2,) + slab, bf16),
            VMEM((2,) + slab, bf16),
            VMEM((2 * tiles,) + slab, bf16),
            VMEM((2 * tiles,) + slab, bf16),
            DMA((frames - 1,)), DMA((frames - 1,)),
            DMA((frames - 1,)), DMA((frames - 1,)),
            DMA((tiles, frames - 1)), DMA((tiles, frames - 1)),
            DMA((2, 2)), DMA((2,)), DMA((2, 2 * tiles)),
        ],
        compiler_params=pltpu.CompilerParams(
            collective_id=2, has_side_effects=True, vmem_limit_bytes=VMEM_LIMIT
        ),
    )(after_first, cot_first, after_later, cotangent, loss, mod, w_b, w_u, w_d)


def space_back_kernel(
    clip, grad_ref, x_ref, mod, w_c, qkv, branch, totals,
    out_ref, gb_ref, gqkv_ref, sums, gmix,
):
    width = x_ref.shape[-1]
    tokens = x_ref.shape[-2]
    row = clip * 9
    piece = lambda number: mod[row + number : row + number + 1, :]

    @pl.when(pl.program_id(0) == 0)
    def _():
        sums[...] = jnp.zeros_like(sums)

    grad = grad_ref[...].reshape(tokens, width).astype(f32)
    grad_branch = (grad * piece(2)).astype(bf16)
    gb_ref[...] = grad_branch
    sums[2:3, :] += column_sum(grad * branch[...].astype(f32))
    sums[3:4, :] += column_sum(grad_branch.astype(f32))
    gmix[...] = dot(grad_branch, w_c[:, 3 * width :], 1, 1).astype(bf16)
    attend_back(qkv, gmix, totals, gqkv_ref, width, None)
    grad_hidden = dot(gqkv_ref[...], w_c[:, : 3 * width], 1, 1)
    norm, scale = normed(x_ref[...].reshape(tokens, width).astype(f32))
    sums[0:1, :] += column_sum(grad_hidden)
    sums[1:2, :] += column_sum(grad_hidden * norm)
    result = grad + norm_back(grad_hidden, 1.0 + piece(1), norm, scale)
    out_ref[...] = result.reshape(out_ref.shape)


def space_back_next(count, clip, *refs):
    space_back_kernel(clip, *refs[:7], *refs[7 + count :])


def space_back_call(clip, grad, x, mod, w_c, qkv, branch, totals, earlier):
    clip_count, frame_count, tokens, width = x.shape
    frames = grad.shape[0]
    part = grad.shape[2]
    rows = frame_count * tokens
    by_frame = lambda columns: pl.BlockSpec(
        (None, tokens, columns), lambda f: (clip * frame_count + f, 0, 0)
    )
    own = lambda columns: pl.BlockSpec((tokens, columns), lambda f: (clip * frame_count + f, 0))
    in_specs = [
        pl.BlockSpec((frames, 1, part, width), lambda f: (0, f, 0, 0)),
        pl.BlockSpec((1, 1, tokens, width), lambda f: (clip, f, 0, 0)),
        full(mod.shape),
        full(w_c.shape),
        by_frame(3 * width),
        by_frame(width),
        pl.BlockSpec((None, 16, tokens), lambda f: (clip * frame_count + f, 0, 0)),
    ]
    args = [grad, x, mod, w_c, qkv, branch, totals]
    body = functools.partial(space_back_kernel, clip)
    aliases = {}
    if earlier is not None:
        in_specs += [pl.BlockSpec(memory_space=pl.ANY)] * len(earlier)
        args += list(earlier)
        aliases = {7 + number: number for number in range(len(earlier))}
        body = functools.partial(space_back_next, len(earlier), clip)
    return pl.pallas_call(
        body,
        grid=(frame_count,),
        in_specs=in_specs,
        out_specs=[
            pl.BlockSpec((1, 1, tokens, width), lambda f: (clip, f, 0, 0)),
            own(width),
            own(3 * width),
            pl.BlockSpec((8, width), lambda f: (0, 0)),
        ],
        out_shape=[
            jax.ShapeDtypeStruct(x.shape, f32),
            jax.ShapeDtypeStruct((clip_count * rows, width), bf16),
            jax.ShapeDtypeStruct((clip_count * rows, 3 * width), bf16),
            jax.ShapeDtypeStruct((8, width), f32),
        ],
        scratch_shapes=[VMEM((tokens, width), bf16)],
        input_output_aliases=aliases,
        compiler_params=pltpu.CompilerParams(vmem_limit_bytes=VMEM_LIMIT),
        cost_estimate=pl.CostEstimate(
            flops=rows * 20_000_000, bytes_accessed=rows * width * 20, transcendentals=0
        ),
    )(*args)


def shards(
    inputs, cotangent, time_steps, weight_index, ada_weight, ada_bias, space_qkv, space_out,
    space_out_bias, time_qkv, time_out, time_out_bias, up_weight, up_bias, down_weight, down_bias,
):
    clip_count, frame_count, patch_count, width = inputs.shape
    clips, frames = lax.axis_size("clip"), lax.axis_size("frame")
    owners = clips * frames
    owner = lax.axis_index("clip") * frames + lax.axis_index("frame")
    part = patch_count // frames
    rows = ada_weight.shape[0]

    embed = jax.nn.silu(embed_steps(time_steps, width)).astype(bf16)
    embed = jnp.pad(embed, ((0, 16 - clip_count), (0, 0)))
    place = lax.broadcasted_iota(jnp.int32, (width, 128), 0) - owner * rows
    lane = lax.broadcasted_iota(jnp.int32, (width, 128), 1)
    select = ((place == lane) & (lane < rows)).astype(bf16)
    ada = jnp.pad(ada_weight, ((0, 128 - rows), (0, 0)))

    def spread_bias(vector):
        length = vector.shape[0]
        empty = jnp.zeros((owners * length,), f32)
        return lax.dynamic_update_slice(empty, vector.astype(f32), (owner * length,)).reshape(
            -1, width
        )

    bias = jnp.concatenate(
        [
            spread_bias(vector)
            for vector in (ada_bias, space_out_bias, time_out_bias, up_bias, down_bias)
        ],
        axis=0,
    )
    sh_c = jnp.concatenate([space_qkv, space_out], axis=1)
    sh_b = jnp.concatenate([time_qkv, time_out], axis=1)
    (
        w_c, w_b, w_u, w_d, mod, chosen, totals, hidden_one, qkv_one, mixed_one, branch_one,
        after_first, after_later, cot_first,
    ) = start_call(
        clips, frames, inputs, cotangent, sh_c, sh_b, up_weight, down_weight, embed, select, ada,
        bias,
    )

    def exchange(values):
        return lax.all_to_all(values, "frame", split_axis=0, concat_axis=0, tiled=True)

    loss = jnp.exp2(weight_index.astype(f32) * 0.5 - 1.0)
    loss = jnp.broadcast_to(loss[:, None], (clip_count, width))
    (
        act, gup, h3, gb3, mixed_two, gb2, h2, gqkv_two, mid_sums, _, _, grad_first,
        grad_later, out_all,
    ) = middle_call(
        clips, frames, after_first, cot_first, after_later, cotangent, loss, mod, w_b, w_u, w_d
    )
    grads = [grad_first, exchange(grad_later)]

    earlier = None
    space_sums = []
    for clip in range(clip_count):
        *earlier, sums = space_back_call(
            clip, grads[clip], inputs, mod, w_c, qkv_one, branch_one, totals, earlier
        )
        space_sums.append(sums)
    input_grad, gb1, gqkv_one = earlier
    pieces = []
    for clip in range(clip_count):
        pieces += [space_sums[clip][0:3], mid_sums[clip][0:6]]
    pieces.append(sum(entry[3:4] for entry in space_sums))
    pieces.append(sum(entry[6:12] for entry in mid_sums))
    small = jnp.concatenate(pieces, axis=0)
    small = jnp.pad(small, ((0, ROWS - small.shape[0]), (0, 0)))
    picked = chosen.reshape(clips, 16, 128)[:, :clip_count].reshape(clips * clip_count, 128)
    outputs, grad_ada, sums, own_u, own_d, own_b, own_bo, own_c, own_co = grad_call(
        clips, frames, clip_count, small, picked.astype(f32).T, out_all, h3, gup, act, gb3, h2, gqkv_two,
        mixed_two, gb2, hidden_one.reshape(-1, width), gqkv_one, mixed_one.reshape(-1, width), gb1,
    )
    biases = sums[9:]

    def own_slice(vector):
        length = vector.shape[0] // owners
        return lax.dynamic_slice_in_dim(vector, owner * length, length, 0)

    return (
        outputs,
        input_grad,
        grad_ada,
        own_slice(sums[:9].reshape(-1)),
        own_c,
        own_co,
        own_slice(biases[0]),
        own_b,
        own_bo,
        own_slice(biases[1]),
        own_u,
        own_slice(biases[2:6].reshape(-1)),
        own_d,
        own_slice(biases[6]),
    )


def solution(mesh):
    tokens = P("clip", "frame", None, None)
    matrix = P(("clip", "frame"), None)
    vector = P(("clip", "frame"))
    in_specs = (
        tokens, tokens, P("clip"), P("clip"), matrix, vector, matrix, matrix, vector, matrix,
        matrix, vector, matrix, vector, matrix, vector,
    )
    out_specs = (
        tokens, tokens, matrix, vector, matrix, matrix, vector, matrix, matrix, vector, matrix,
        vector, matrix, vector,
    )
    return jax.shard_map(shards, mesh=mesh, in_specs=in_specs, out_specs=out_specs, check_vma=False)
```

```python
import functools
import math

import jax
import jax.numpy as jnp
from jax import lax
from jax.experimental import pallas as pl
from jax.experimental.pallas import tpu as pltpu
from jax.sharding import PartitionSpec as P

HEADS = 12
HEAD = 64
GROUP = 4
ROWS = 32
GELU_C = math.sqrt(2.0 / math.pi)
GELU_A = 0.044715
VMEM_LIMIT = 58 << 20

f32 = jnp.float32
bf16 = jnp.bfloat16
highest = lax.Precision.HIGHEST
MESH = pl.DeviceIdType.MESH
VMEM = pltpu.VMEM
DMA = pltpu.SemaphoreType.DMA


def embed_steps(time_steps, model_width):
    half_width = model_width // 2
    frequencies = jnp.exp(
        -math.log(10000.0) * jnp.arange(half_width, dtype=f32) / half_width
    )
    angles = time_steps.astype(f32)[:, None] * frequencies[None, :]
    return jnp.concatenate([jnp.cos(angles), jnp.sin(angles)], axis=1)


def dot(left, right, left_dim, right_dim):
    return lax.dot_general(
        left, right, (((left_dim,), (right_dim,)), ((), ())), preferred_element_type=f32
    )


def flip(index, mask):
    bit = 1
    while bit <= mask:
        if mask & bit:
            index = index + bit * (1 - 2 * ((index // bit) % 2))
        bit *= 2
    return index


def span(masks):
    out = [0]
    for mask in masks:
        out = out + [entry ^ mask for entry in out]
    return out


def frame_masks(frames):
    masks, bit = [], 1
    while bit < frames:
        masks.append(bit)
        bit *= 2
    if len(masks) > 1:
        masks = [frames - 1] + masks[:-1]
    return masks


def clip_tail_masks(clips):
    masks, bit = [], 2
    while bit < clips:
        masks.append(bit)
        bit *= 2
    return masks


def greet(clips, frames):
    clip, frame = lax.axis_index("clip"), lax.axis_index("frame")
    barrier = pltpu.get_barrier_semaphore()
    for step in range(1, clips):
        pl.semaphore_signal(
            barrier, inc=1, device_id={"clip": lax.rem(clip + step, clips)}, device_id_type=MESH
        )
    for step in range(1, frames):
        pl.semaphore_signal(
            barrier, inc=1, device_id={"frame": lax.rem(frame + step, frames)}, device_id_type=MESH
        )
    pl.semaphore_wait(barrier, clips + frames - 2)


def spread(axis, size, source_of, target, send_sems, recv_sems):
    me = lax.axis_index(axis)
    copies = []
    for step in range(1, size):
        peer = lax.rem(me + step, size)
        copy = pltpu.make_async_remote_copy(
            src_ref=source_of(peer),
            dst_ref=target.at[me],
            send_sem=send_sems.at[step - 1],
            recv_sem=recv_sems.at[step - 1],
            device_id={axis: peer},
            device_id_type=MESH,
        )
        copy.start()
        copies.append(copy)
    return copies


def start_kernel(
    clips, frames, clip_count,
    x_ref, cotangent, sh_c, sh_b, sh_u, sh_d, embed, select, ada, bias,
    w_c, w_b, w_u, w_d, mod, chosen, totals, hidden_out, qkv_out, mixed_out, branch_out,
    after_first, after_later, cot_first,
    v_c, z_c, z_b, z_u, z_d, st_w, b_c, b_b, b_u, b_d,
    embeds, parts, terms, arrived, held, lined, hidden, qkv, mixed, branch, after,
    zs, zr, cs, cr, xs, xr, ls, es, er, ps, pr, fs, fr, ts, tr, hs, hr, os, ws,
):
    clip, frame = lax.axis_index("clip"), lax.axis_index("frame")
    shards_in = (sh_c, sh_b, sh_u, sh_d)
    zoned = (z_c, z_b, z_u, z_d)
    blocks = (b_c, b_b, b_u, b_d)
    wholes = (v_c, w_b, w_u, w_d)
    width = mod.shape[1]
    frame_count, tokens = x_ref.shape[1], x_ref.shape[2]
    part = tokens // frames
    greet(clips, frames)
    masks = frame_masks(frames)
    sends = []
    stage = {}

    def frame_step(group, step):
        number = (1 << step) - 1
        copies = []
        for offset in span(masks[:step]):
            slot = flip(frame, offset)
            source = shards_in[group] if offset == 0 else zoned[group].at[slot]
            copy = pltpu.make_async_remote_copy(
                src_ref=source,
                dst_ref=zoned[group].at[slot],
                send_sem=zs.at[group, number],
                recv_sem=zr.at[group, number],
                device_id={"frame": flip(frame, masks[step])},
                device_id_type=MESH,
            )
            copy.start()
            copies.append(copy)
            number += 1
        sends.extend(copies)
        stage[group] = copies

    def frame_rest(group):
        for step in range(1, len(masks)):
            for copy in stage[group]:
                copy.wait_recv()
            frame_step(group, step)

    tail = clip_tail_masks(clips)
    steps = len(tail)
    orders = (tail, tail[::-1])
    moving = {}

    def block_send(group, half, step, position, offset):
        whole = wholes[group]
        block_rows = whole.shape[0] // clips
        columns = whole.shape[1] // 2
        rows = pl.ds(pl.multiple_of(flip(clip, offset) * block_rows, block_rows), block_rows)
        lanes = pl.ds(half * columns, columns)
        target = whole.at[rows, lanes]
        number = (1 << step) - 1 + position
        copy = pltpu.make_async_remote_copy(
            src_ref=blocks[group].at[:, lanes] if offset == 0 else target,
            dst_ref=target,
            send_sem=xs.at[group, half, number],
            recv_sem=xr.at[group, half, number],
            device_id={"clip": flip(clip, orders[half][step])},
            device_id_type=MESH,
        )
        copy.start()
        moving[group, half, number] = copy

    core_copies = {group: [] for group in range(4)}

    def core_send(group, offset):
        whole = wholes[group]
        block_rows = whole.shape[0] // clips
        rows = pl.ds(pl.multiple_of(flip(clip, offset) * block_rows, block_rows), block_rows)
        number = len(core_copies[group])
        copy = pltpu.make_async_remote_copy(
            src_ref=blocks[group] if offset == 0 else whole.at[rows, :],
            dst_ref=whole.at[rows, :],
            send_sem=cs.at[group, number],
            recv_sem=cr.at[group, number],
            device_id={"clip": flip(clip, 1)},
            device_id_type=MESH,
        )
        copy.start()
        core_copies[group].append(copy)

    local_copies = []

    def block_ready(group):
        for copy in stage[group]:
            copy.wait_recv()
        rows, columns = shards_in[group].shape
        block_rows = frames * rows
        if rows % 16:
            for slot in range(frames):
                st_w[slot * rows : (slot + 1) * rows, :columns] = zoned[group][slot].astype(f32)
            blocks[group][...] = st_w[:block_rows, :columns].astype(bf16)
        else:
            for slot in range(frames):
                blocks[group][slot * rows : (slot + 1) * rows, :] = zoned[group][slot]
        for step in range(steps):
            for half in range(2):
                block_send(group, half, step, 0, 0)
        core_send(group, 0)
        place = pl.ds(pl.multiple_of(clip * block_rows, block_rows), block_rows)
        keep = pltpu.make_async_copy(blocks[group], wholes[group].at[place, :], ls.at[group])
        keep.start()
        local_copies.append(keep)

    def block_forward(group):
        for step in range(1, steps):
            for half in range(2):
                for position in range(1 << (step - 1), 1 << step):
                    moving[group, half, position - 1].wait_recv()
                for later in range(step, steps):
                    for position, offset in enumerate(span(orders[half][:later])):
                        if (1 << (step - 1)) <= position < (1 << step):
                            block_send(group, half, later, position, offset)

    def block_finish(group):
        last = (1 << (steps - 1)) - 1
        for half in range(2):
            for number in range(last, (1 << steps) - 1):
                moving[group, half, number].wait_recv()
        for offset in span(tail)[1:]:
            core_send(group, offset)

    def core_finish(group):
        for copy in core_copies[group]:
            copy.wait_recv()

    frame_step(0, 0)
    own = spread("clip", clips, lambda peer: embed, embeds, es, er)
    sends.extend(own)
    embeds[clip] = embed[...]
    for group in range(4):
        zoned[group][frame] = shards_in[group][...]
    frame_rest(0)
    for copy in own:
        copy.wait_recv()
    picked = dot(embeds[...].reshape(clips * 16, width), select[...], 1, 0).astype(bf16)
    chosen[...] = picked
    parts[...] = dot(picked, ada[...], 1, 0)
    for peer in range(clips):
        for local in range(clip_count):
            row = peer * 16 + local
            for piece in range(9):
                terms[peer, local * 9 + piece : local * 9 + piece + 1, :] = (
                    parts[row : row + 1, piece * width : (piece + 1) * width]
                    + bias[piece : piece + 1, :]
                )
        base = clip_count * 9
        terms[peer, base : base + 7, :] = bias[9:16, :]
        if base + 7 < ROWS:
            terms[peer, base + 7 : ROWS, :] = jnp.zeros((ROWS - base - 7, width), f32)
    own = spread("clip", clips, lambda peer: terms.at[peer], arrived, ps, pr)
    sends.extend(own)
    arrived[clip] = terms[clip]
    block_ready(0)
    for group in range(1, 4):
        frame_step(group, 0)
    for copy in own:
        copy.wait_recv()
    total = arrived[0]
    for peer in range(1, clips):
        total = total + arrived[peer]
    held[...] = total
    own = spread("frame", frames, lambda peer: held, lined, fs, fr)
    sends.extend(own)
    lined[frame] = total
    for group in range(1, 4):
        frame_rest(group)

    cot_copies = []
    for step in range(1, frames):
        peer = lax.rem(frame + step, frames)
        copy = pltpu.make_async_remote_copy(
            src_ref=cotangent.at[0, :, pl.ds(pl.multiple_of(peer * part, part), part), :],
            dst_ref=cot_first.at[frame],
            send_sem=ts.at[step - 1],
            recv_sem=tr.at[step - 1],
            device_id={"frame": peer},
            device_id_type=MESH,
        )
        copy.start()
        cot_copies.append(copy)
    keep = pltpu.make_async_copy(
        cotangent.at[0, :, pl.ds(pl.multiple_of(frame * part, part), part), :],
        cot_first.at[frame],
        ls.at[4],
    )
    keep.start()
    local_copies.append(keep)

    for copy in own:
        copy.wait_recv()
    total = lined[0]
    for peer in range(1, frames):
        total = total + lined[peer]
    mod[...] = total
    block_forward(0)
    for group in range(1, 4):
        block_ready(group)
    block_finish(0)
    core_finish(0)
    local_copies[0].wait()

    keep = pltpu.make_async_copy(v_c, w_c, ls.at[5])
    keep.start()
    local_copies.append(keep)

    def after_copy(f, step):
        peer = lax.rem(frame + step, frames)
        return pltpu.make_async_remote_copy(
            src_ref=after.at[f, pl.ds(pl.multiple_of(peer * part, part), part), :],
            dst_ref=after_first.at[frame, f],
            send_sem=hs.at[f, step - 1],
            recv_sem=hr.at[f, step - 1],
            device_id={"frame": peer},
            device_id_type=MESH,
        )

    def own_after(f):
        return pltpu.make_async_copy(
            after.at[f, pl.ds(pl.multiple_of(frame * part, part), part), :],
            after_first.at[frame, f],
            os.at[f],
        )

    def later_after(f):
        return pltpu.make_async_copy(after.at[f], after_later.at[f - frame_count], os.at[f])

    kept = ((hidden, hidden_out), (qkv, qkv_out), (mixed, mixed_out), (branch, branch_out))

    def write_back(f):
        return [
            pltpu.make_async_copy(source.at[f], target.at[f], ws.at[number, f])
            for number, (source, target) in enumerate(kept)
        ]

    for local in range(clip_count):
        row = local * 9

        def one_frame(index, carry):
            f = local * frame_count + index
            values = x_ref[local, index].astype(f32)
            norm, _ = normed(values)
            scaled = norm * (1.0 + mod[row + 1 : row + 2, :]) + mod[row : row + 1, :]
            lowered = scaled.astype(bf16)
            hidden[f] = lowered
            qkv[f] = dot(lowered, v_c[:, : 3 * width], 1, 0).astype(bf16)
            attend(qkv.at[f], mixed.at[f], totals.at[f], width, None)
            grown = dot(mixed[f], v_c[:, 3 * width :], 1, 0) + mod[18:19, :]
            branch[f] = grown.astype(bf16)
            after[f] = (values + mod[row + 2 : row + 3, :] * grown).astype(bf16)
            if local == 0:
                for step in range(1, frames):
                    after_copy(f, step).start()
                own_after(f).start()
            else:
                later_after(f).start()
            for copy in write_back(f):
                copy.start()
            return carry

        lax.fori_loop(0, frame_count, one_frame, 0)
        if local == 0:
            block_forward(1)
    for group in range(2, 4):
        block_forward(group)
    for group in range(1, 4):
        block_finish(group)
    for group in range(1, 4):
        core_finish(group)

    def settle(f, carry):
        for step in range(1, frames):
            copy = after_copy(f, step)
            copy.wait_recv()
            copy.wait_send()
        own_after(f).wait()
        return carry

    lax.fori_loop(0, frame_count, settle, 0)

    def settle_later(f, carry):
        later_after(f).wait()
        return carry

    lax.fori_loop(frame_count, clip_count * frame_count, settle_later, 0)

    def settle_kept(f, carry):
        for copy in write_back(f):
            copy.wait()
        return carry

    lax.fori_loop(0, clip_count * frame_count, settle_kept, 0)
    for copy in cot_copies:
        copy.wait_recv()
        copy.wait_send()
    for copy in local_copies[1:]:
        copy.wait()
    for copy in moving.values():
        copy.wait_send()
    for group in range(4):
        for copy in core_copies[group]:
            copy.wait_send()
    for copy in sends:
        copy.wait_send()


def start_call(
    clips, frames, inputs, cotangent, sh_c, sh_b, sh_u, sh_d, embed, select, ada, bias
):
    clip_count, frame_count, tokens, width = inputs.shape
    rows, columns = sh_c.shape
    rows_d = sh_d.shape[0]
    block = frames * rows
    block_d = frames * rows_d
    peers = max(clips // 2 - 1, 1)
    total = clip_count * frame_count
    part = tokens // frames
    whole = jax.ShapeDtypeStruct((clips * block, columns), bf16)
    vmem = pl.BlockSpec(memory_space=VMEM)
    hbm = pl.BlockSpec(memory_space=pl.ANY)
    zoned = lambda height, lanes: VMEM((frames, height, lanes), bf16)
    saved = lambda lanes: jax.ShapeDtypeStruct((total, tokens, lanes), bf16)
    lent = lambda lanes: VMEM((total, tokens, lanes), bf16)
    traded = jax.ShapeDtypeStruct((frames, frame_count, part, width), bf16)
    return pl.pallas_call(
        functools.partial(start_kernel, clips, frames, clip_count),
        out_shape=(
            whole, whole, whole,
            jax.ShapeDtypeStruct((clips * block_d, width), bf16),
            jax.ShapeDtypeStruct((ROWS, width), f32),
            jax.ShapeDtypeStruct((clips * 16, 128), bf16),
            jax.ShapeDtypeStruct((total, 16, tokens), f32),
            saved(width), saved(3 * width), saved(width), saved(width),
            traded,
            jax.ShapeDtypeStruct(((clip_count - 1) * frame_count, tokens, width), bf16),
            traded,
        ),
        in_specs=[vmem, hbm] + [vmem] * 8,
        out_specs=(hbm, hbm, hbm, hbm, vmem, vmem, vmem) + (hbm,) * 7,
        scratch_shapes=[
            VMEM((clips * block, columns), bf16),
            zoned(rows, columns), zoned(rows, columns), zoned(rows, columns), zoned(rows_d, width),
            VMEM((max(block, block_d), columns), f32),
            VMEM((block, columns), bf16),
            VMEM((block, columns), bf16),
            VMEM((block, columns), bf16),
            VMEM((block_d, width), bf16),
            VMEM((clips, 16, width), bf16),
            VMEM((clips * 16, 9 * width), f32),
            VMEM((clips, ROWS, width), f32),
            VMEM((clips, ROWS, width), f32),
            VMEM((ROWS, width), f32),
            VMEM((frames, ROWS, width), f32),
            lent(width), lent(3 * width), lent(width), lent(width), lent(width),
            DMA((4, frames - 1)), DMA((4, frames - 1)),
            DMA((4, clips // 2)), DMA((4, clips // 2)),
            DMA((4, 2, peers)), DMA((4, 2, peers)),
            DMA((6,)),
            DMA((clips - 1,)), DMA((clips - 1,)),
            DMA((clips - 1,)), DMA((clips - 1,)),
            DMA((frames - 1,)), DMA((frames - 1,)),
            DMA((frames - 1,)), DMA((frames - 1,)),
            DMA((frame_count, frames - 1)), DMA((frame_count, frames - 1)),
            DMA((total,)),
            DMA((4, total)),
        ],
        compiler_params=pltpu.CompilerParams(
            collective_id=0, has_side_effects=True, vmem_limit_bytes=VMEM_LIMIT
        ),
    )(inputs, cotangent, sh_c, sh_b, sh_u, sh_d, embed, select, ada, bias)


STEP = 512
SLOTS = 3


def grad_kernel(
    clips, frames, clip_count,
    small, chosen, out_all, h3, gup, act, gb3, h2, gqkv2, mix2, gb2, h1, gqkv1, mix1, gb1,
    outputs, grad_ada, bias_sums, out_u, out_d, out_b, out_bo, out_c, out_co,
    sum_w, sum_d, core_w, core_d, side_w, side_d, line_w, line_d, last_w, last_d,
    left, right, total, gathered, lined, held,
    lsem, rsem, cs, cr, xs, xr, zs, zr, fs, fr, ps, pr, os, orr, ks,
):
    clip, frame = lax.axis_index("clip"), lax.axis_index("frame")
    tokens = h3.shape[0]
    width = small.shape[1]
    wide = sum_w.shape[-1]
    narrow = sum_d.shape[-1]
    tail = clip_tail_masks(clips)
    orders = (tail, tail[::-1])
    masks = frame_masks(frames)
    greet(clips, frames)
    first = spread("frame", frames, lambda peer: small, lined, fs, fr)
    lined[frame] = small[...]
    part = out_all.shape[3]
    frame_count = out_all.shape[2]
    out_copies = []
    mine = pl.ds(pl.multiple_of(frame * part, part), part)

    def send_output(number):
        local, index = divmod(number, frame_count)
        for hop in range(1, frames):
            peer = lax.rem(frame + hop, frames)
            copy = pltpu.make_async_remote_copy(
                src_ref=out_all.at[local, peer, index],
                dst_ref=outputs.at[local, index, mine, :],
                send_sem=os.at[number, hop - 1],
                recv_sem=orr.at[number, hop - 1],
                device_id={"frame": peer},
                device_id_type=MESH,
            )
            copy.start()
            out_copies.append(copy)

    own_outs = []
    for local in range(clip_count):
        copy = pltpu.make_async_copy(
            out_all.at[local, frame], outputs.at[local, :, mine, :], ks.at[local]
        )
        copy.start()
        own_outs.append(copy)

    chunks = [
        (1, 0, [(act, gb3, 0, 0, narrow)], out_d, 0),
        (1, 1, [(act, gb3, narrow, 0, narrow)], out_d, narrow),
        (0, 0, [(h3, gup, 0, 0, wide)], out_u, 0),
        (0, 1, [(h3, gup, wide, 0, wide)], out_u, wide),
        (0, 2, [(h2, gqkv2, 0, 0, wide)], out_b, 0),
        (0, 3, [(h2, gqkv2, wide, 0, width), (mix2, gb2, 0, width, width)], out_b, wide),
        (0, 4, [(h1, gqkv1, 0, 0, wide)], out_c, 0),
        (0, 5, [(h1, gqkv1, wide, 0, width), (mix1, gb1, 0, width, width)], out_c, wide),
    ]
    sums, cores, sides = (sum_w, sum_d), (core_w, core_d), (side_w, side_d)
    lines, lasts = (line_w, line_d), (last_w, last_d)
    flights = {}

    steps = tokens // STEP
    line_up = []
    for kind, _, parts, _, _ in chunks:
        for part in parts:
            for group in range(part[0].shape[1] // width):
                line_up.append(part[:3] + (part[3] + group * part[4], part[4], group))
    begins = [0]
    for kind, _, parts, _, _ in chunks:
        begins.append(begins[-1] + sum(part[0].shape[1] // width for part in parts))

    def load(entry, step, slot):
        one, other, begin, _, lanes, group = line_up[entry]
        rows = pl.ds(pl.multiple_of(step * STEP, STEP), STEP)
        return (
            pltpu.make_async_copy(
                one.at[rows, pl.ds(group * width, width)], left.at[slot], lsem.at[slot]
            ),
            pltpu.make_async_copy(
                other.at[rows, pl.ds(begin, lanes)],
                right.at[slot, :, pl.ds(0, lanes)],
                rsem.at[slot],
            ),
        )

    def place_of(entry, step):
        return lax.rem(entry * steps + step, SLOTS)

    def multiply(number):
        kind, place = chunks[number][:2]
        for entry in range(begins[number], begins[number + 1]):
            at, lanes = line_up[entry][3:5]

            def body(step, carry):
                ahead = step + SLOTS - 1

                @pl.when(ahead < steps)
                def _():
                    for copy in load(entry, ahead, place_of(entry, ahead)):
                        copy.start()

                if entry + 1 < len(line_up):

                    @pl.when(ahead >= steps)
                    def _():
                        for copy in load(entry + 1, ahead - steps, place_of(entry, ahead)):
                            copy.start()

                slot = place_of(entry, step)
                for copy in load(entry, step, slot):
                    copy.wait()
                columns = slice(at, at + lanes)
                before = jnp.where(step > 0, total[:, columns], 0.0)
                total[:, columns] = before + dot(left[slot], right[slot, :, :lanes], 0, 0)
                return carry

            lax.fori_loop(0, steps, body, 0)
        rows, lanes = sums[kind].shape[2:]
        for block in range(clips):
            begin = block * rows
            column = begin // width * lanes
            begin = begin % width
            sums[kind][place, block] = total[begin : begin + rows, column : column + lanes].astype(
                bf16
            )

    def core_start(number):
        kind, place = chunks[number][:2]
        copies = []
        for position, offset in enumerate(span(tail)):
            copy = pltpu.make_async_remote_copy(
                src_ref=sums[kind].at[place, flip(clip, offset ^ 1)],
                dst_ref=cores[kind].at[place, position],
                send_sem=cs.at[number, position],
                recv_sem=cr.at[number, position],
                device_id={"clip": flip(clip, 1)},
                device_id_type=MESH,
            )
            copy.start()
            copies.append(copy)
        flights[number, "core"] = copies

    def half_of(kind, half):
        if kind:
            rows = sums[kind].shape[2] // 2
            return (slice(half * rows, (half + 1) * rows), slice(None))
        lanes = sums[kind].shape[3] // 2
        return (slice(None), slice(half * lanes, (half + 1) * lanes))

    def side_start(number, step):
        kind, place = chunks[number][:2]
        copies = []
        for half in range(2):
            mask = orders[half][step]
            for position, offset in enumerate(span(orders[half][:step])):
                entry = (1 << step) - 1 + position
                copy = pltpu.make_async_remote_copy(
                    src_ref=sums[kind].at[(place, flip(clip, offset ^ mask)) + half_of(kind, half)],
                    dst_ref=sides[kind].at[place, half, entry],
                    send_sem=xs.at[number, half, entry],
                    recv_sem=xr.at[number, half, entry],
                    device_id={"clip": flip(clip, mask)},
                    device_id_type=MESH,
                )
                copy.start()
                copies.append(copy)
        flights[number, "side", step] = copies

    def core_add(number):
        kind, place = chunks[number][:2]
        for copy in flights[number, "core"]:
            copy.wait_recv()
        for position, offset in enumerate(span(tail)):
            block = flip(clip, offset)
            sums[kind][place, block] = (
                sums[kind][place, block].astype(f32) + cores[kind][place, position].astype(f32)
            ).astype(bf16)
        side_start(number, len(tail) - 1)

    def side_add(number, step):
        kind, place = chunks[number][:2]
        for copy in flights[number, "side", step]:
            copy.wait_recv()
        for half in range(2):
            for position, offset in enumerate(span(orders[half][:step])):
                entry = (1 << step) - 1 + position
                block = flip(clip, offset)
                where = (place, block) + half_of(kind, half)
                sums[kind][where] = (
                    sums[kind][where].astype(f32) + sides[kind][place, half, entry].astype(f32)
                ).astype(bf16)
        if step:
            side_start(number, step - 1)
        else:
            rows = lines[kind].shape[2]
            block = sums[kind][place, clip].astype(f32)
            for slot in range(frames):
                lines[kind][place, slot] = block[slot * rows : (slot + 1) * rows, :].astype(bf16)
            line_start(number, len(masks) - 1)

    def line_start(number, step):
        kind, place = chunks[number][:2]
        copies = []
        for position, offset in enumerate(span(masks[:step])):
            entry = (1 << step) - 1 + position
            copy = pltpu.make_async_remote_copy(
                src_ref=lines[kind].at[place, flip(frame, offset ^ masks[step])],
                dst_ref=lasts[kind].at[place, entry],
                send_sem=zs.at[number, entry],
                recv_sem=zr.at[number, entry],
                device_id={"frame": flip(frame, masks[step])},
                device_id_type=MESH,
            )
            copy.start()
            copies.append(copy)
        flights[number, "line", step] = copies

    def line_add(number, step):
        kind, place, _, target, begin = chunks[number]
        for copy in flights[number, "line", step]:
            copy.wait_recv()
        for position, offset in enumerate(span(masks[:step])):
            entry = (1 << step) - 1 + position
            slot = flip(frame, offset)
            value = lines[kind][place, slot].astype(f32) + lasts[kind][place, entry].astype(f32)
            if step:
                lines[kind][place, slot] = value.astype(bf16)
            elif begin + value.shape[1] > target.shape[1]:
                cut = target.shape[1] - begin
                target[:, begin:] = value[:, :cut]
                (out_bo if target is out_b else out_co)[...] = value[:, cut:]
            else:
                target[:, begin : begin + value.shape[1]] = value
        if step:
            line_start(number, step - 1)

    stages = [core_start, core_add]
    for step in range(len(tail))[::-1]:
        stages.append(functools.partial(side_add, step=step))
    for step in range(len(masks))[::-1]:
        stages.append(functools.partial(line_add, step=step))

    def finish_small():
        for copy in second:
            copy.wait_recv()
        rows = grad_ada.shape[0]
        for number in range(9):
            terms = [
                gathered[peer, local * 9 + number : local * 9 + number + 1, :]
                for peer in range(clips)
                for local in range(clip_count)
            ]
            terms = jnp.concatenate(terms, axis=0)
            grad_ada[:, number * width : (number + 1) * width] = lax.dot_general(
                chosen[...], terms, (((1,), (0,)), ((), ())), precision=highest,
                preferred_element_type=f32,
            )[:rows, :]
            bias_sums[number : number + 1, :] = column_sum(terms)
        base = clip_count * 9
        summed = gathered[0, base : base + 7, :]
        for peer in range(1, clips):
            summed = summed + gathered[peer, base : base + 7, :]
        bias_sums[9:16, :] = summed

    for step in range(SLOTS - 1):
        for copy in load(0, step, step):
            copy.start()
    second = None
    lags = [0, 1, 3]
    while len(lags) < len(stages):
        lags.append(lags[-1] + 1)
    for turn in range(len(chunks) + lags[-1]):
        for depth in range(len(stages))[::-1]:
            if depth > 0 and 0 <= turn - lags[depth] < len(chunks):
                stages[depth](turn - lags[depth])
        if turn < clip_count * frame_count:
            send_output(turn)
        if turn < len(chunks):
            multiply(turn)
            core_start(turn)
        if turn == len(chunks):
            finish_small()
        if turn == 0:
            for copy in first:
                copy.wait_recv()
            summed = lined[0]
            for peer in range(1, frames):
                summed = summed + lined[peer]
            held[...] = summed
            second = spread("clip", clips, lambda peer: held, gathered, ps, pr)
            gathered[clip] = summed
    for copy in own_outs:
        copy.wait()
    for copy in out_copies:
        copy.wait_recv()
        copy.wait_send()
    for copy in first + second:
        copy.wait_send()
    for copies in flights.values():
        for copy in copies:
            copy.wait_send()


def grad_call(clips, frames, clip_count, small, chosen, out_all, *operands):
    h3, gup, act = operands[:3]
    _, _, frame_count, part, _ = out_all.shape
    width, hidden = h3.shape[1], act.shape[1]
    owners = clips * frames
    wide, narrow = hidden // 2, width // 2
    rows_w, rows_d = width // owners, hidden // owners
    peers = max(clips // 2 - 1, 1)
    vmem = pl.BlockSpec(memory_space=VMEM)
    hbm = pl.BlockSpec(memory_space=pl.ANY)

    return pl.pallas_call(
        functools.partial(grad_kernel, clips, frames, clip_count),
        out_shape=(
            jax.ShapeDtypeStruct((clip_count, frame_count, frames * part, width), bf16),
            jax.ShapeDtypeStruct((rows_w, 9 * width), f32),
            jax.ShapeDtypeStruct((16, width), f32),
            jax.ShapeDtypeStruct((rows_w, hidden), f32),
            jax.ShapeDtypeStruct((rows_d, width), f32),
            jax.ShapeDtypeStruct((rows_w, 3 * width), f32),
            jax.ShapeDtypeStruct((rows_w, width), f32),
            jax.ShapeDtypeStruct((rows_w, 3 * width), f32),
            jax.ShapeDtypeStruct((rows_w, width), f32),
        ),
        in_specs=[vmem, vmem] + [hbm] * (1 + len(operands)),
        out_specs=(hbm,) + (vmem,) * 8,
        scratch_shapes=[
            VMEM((6, clips, rows_w * frames, wide), bf16),
            VMEM((2, clips, rows_d * frames, narrow), bf16),
            VMEM((6, clips // 2, rows_w * frames, wide), bf16),
            VMEM((2, clips // 2, rows_d * frames, narrow), bf16),
            VMEM((6, 2, peers, rows_w * frames, wide // 2), bf16),
            VMEM((2, 2, peers, rows_d * frames // 2, narrow), bf16),
            VMEM((6, frames, rows_w, wide), bf16),
            VMEM((2, frames, rows_d, narrow), bf16),
            VMEM((6, frames - 1, rows_w, wide), bf16),
            VMEM((2, frames - 1, rows_d, narrow), bf16),
            VMEM((SLOTS, STEP, width), bf16),
            VMEM((SLOTS, STEP, wide), bf16),
            VMEM((width, wide), f32),
            VMEM((clips,) + small.shape, f32),
            VMEM((frames,) + small.shape, f32),
            VMEM(small.shape, f32),
            DMA((SLOTS,)), DMA((SLOTS,)),
            DMA((8, clips // 2)), DMA((8, clips // 2)),
            DMA((8, 2, peers)), DMA((8, 2, peers)),
            DMA((8, frames - 1)), DMA((8, frames - 1)),
            DMA((frames - 1,)), DMA((frames - 1,)),
            DMA((clips - 1,)), DMA((clips - 1,)),
            DMA((clip_count * frame_count, frames - 1)),
            DMA((clip_count * frame_count, frames - 1)),
            DMA((clip_count,)),
        ],
        compiler_params=pltpu.CompilerParams(
            collective_id=1, has_side_effects=True, vmem_limit_bytes=VMEM_LIMIT
        ),
    )(small, chosen, out_all, *operands)


def normed(values):
    centred = values - jnp.mean(values, axis=-1, keepdims=True)
    scale = lax.rsqrt(jnp.mean(centred * centred, axis=-1, keepdims=True) + 1e-06)
    return centred * scale, scale


def norm_back(grad, scaled, norm, scale):
    inner = grad * scaled
    return scale * (
        inner
        - jnp.mean(inner, axis=-1, keepdims=True)
        - norm * jnp.mean(inner * norm, axis=-1, keepdims=True)
    )


def column_sum(values):
    return jnp.sum(values, axis=0, keepdims=True)


def head_lanes(tokens):
    lane = lax.broadcasted_iota(jnp.int32, (tokens, GROUP * HEAD), 1)
    return [(lane >= HEAD * head) & (lane < HEAD * (head + 1)) for head in range(GROUP)]


def stacked(values, picks):
    return jnp.concatenate([jnp.where(pick, values, bf16(0)) for pick in picks], axis=0)


def unstacked(values, picks, tokens):
    result = values[(GROUP - 1) * tokens :]
    for head in range(GROUP - 1):
        result = jnp.where(picks[head], values[head * tokens : (head + 1) * tokens], result)
    return result


def masked_scores(keys, own, mask):
    scores = dot(keys, own, 1, 1)
    if mask is not None:
        scores = scores + jnp.concatenate([mask[...]] * GROUP, axis=1)
    return scores


def attend(qkv, mixed, totals, width, mask):
    tokens = qkv.shape[0]
    lanes = GROUP * HEAD
    picks = head_lanes(tokens)
    for group in range(HEADS // GROUP):
        at = group * lanes
        own = stacked(qkv[:, at : at + lanes] * bf16(0.125), picks)
        keys = qkv[:, width + at : width + at + lanes]
        values = qkv[:, 2 * width + at : 2 * width + at + lanes]
        scores = masked_scores(keys, own, mask)
        peak = jnp.max(scores, axis=0, keepdims=True)
        terms = jnp.exp(scores - peak)
        total = jnp.sum(terms, axis=0, keepdims=True)
        weights = (terms * (1.0 / total)).astype(bf16)
        logs = peak + jnp.log(total)
        for head in range(GROUP):
            row = group * GROUP + head
            totals[row : row + 1, :] = logs[:, head * tokens : (head + 1) * tokens]
        result = unstacked(dot(weights, values, 0, 0), picks, tokens)
        mixed[:, at : at + lanes] = result.astype(bf16)


def attend_back(qkv, grad_mixed, totals, grad_qkv, width, mask):
    tokens = qkv.shape[0]
    lanes = GROUP * HEAD
    picks = head_lanes(tokens)
    for group in range(HEADS // GROUP):
        at = group * lanes
        own = stacked(qkv[:, at : at + lanes] * bf16(0.125), picks)
        keys = qkv[:, width + at : width + at + lanes]
        values = qkv[:, 2 * width + at : 2 * width + at + lanes]
        own_grads = stacked(grad_mixed[:, at : at + lanes], picks)
        logs = jnp.concatenate(
            [totals[group * GROUP + head : group * GROUP + head + 1, :] for head in range(GROUP)],
            axis=1,
        )
        weights = jnp.exp(masked_scores(keys, own, mask) - logs)
        grad_weights = dot(values, own_grads, 1, 1)
        inner = jnp.sum(weights * grad_weights, axis=0, keepdims=True)
        grad_scores = (weights * (grad_weights - inner)).astype(bf16)
        grad_queries = unstacked(dot(grad_scores, keys, 0, 0), picks, tokens) * 0.125
        grad_keys = dot(grad_scores, own, 1, 0)
        grad_values = dot(weights.astype(bf16), own_grads, 1, 0)
        for part, grad in enumerate((grad_queries, grad_keys, grad_values)):
            start = part * width + at
            grad_qkv[:, start : start + lanes] = grad.astype(bf16)


def full(shape):
    return pl.BlockSpec(shape, lambda *_: (0,) * len(shape), pipeline_mode=pl.Buffered(1))


def middle_kernel(
    clips, frames, tiles,
    after_first, cot_first, after_later, cotangent, loss, mod, w_b, w_u, w_d,
    act_ref, gup_ref, h3_ref, gb3_ref, mixed_ref, gb2_ref, h2_ref, gqkv_ref, sums,
    after_second, cot_second, grad_first, grad_later, out_all,
    qkv, totals, mask, gmix, after_tile, cot_tile, grad_stage, out_stage,
    ts, tr, us, ur, gs, gr, ls, ks, ws,
):
    frame = lax.axis_index("frame")
    step = pl.program_id(0)
    last = pl.num_programs(0) - 1
    clip = lax.div(step, tiles)
    tile = lax.rem(step, tiles)
    slot = lax.rem(step, 2)
    width = mod.shape[1]
    frame_count, group = after_tile.shape[2], after_tile.shape[3]
    part = tiles * group
    tokens = frames * frame_count * group
    row = clip * 9
    piece = lambda number: mod[pl.ds(row + number, 1), :]

    def own_part(index):
        return pl.ds(pl.multiple_of(index * part, part), part)

    def later_copies(number):
        copies = []
        for hop in range(1, frames):
            peer = lax.rem(frame + hop, frames)
            if number:
                source, target, send, recv = cotangent.at[1, :, own_part(peer), :], cot_second, us, ur
            else:
                source, target, send, recv = after_later.at[:, own_part(peer), :], after_second, ts, tr
            copies.append(
                pltpu.make_async_remote_copy(
                    src_ref=source,
                    dst_ref=target.at[frame],
                    send_sem=send.at[hop - 1],
                    recv_sem=recv.at[hop - 1],
                    device_id={"frame": peer},
                    device_id_type=MESH,
                )
            )
        return copies

    def own_copy(number):
        source = cotangent.at[1] if number else after_later
        target = cot_second if number else after_second
        return pltpu.make_async_copy(
            source.at[:, own_part(frame), :], target.at[frame], ks.at[number]
        )

    def load(source, number, index, place):
        rows = pl.ds(pl.multiple_of(index * group, group), group)
        target = (after_tile, cot_tile)[number].at[place]
        return pltpu.make_async_copy(source.at[:, :, rows, :], target, ls.at[place, number])

    def grad_copies(index):
        rows = pl.ds(pl.multiple_of(index * group, group), group)
        copies = []
        for hop in range(1, frames):
            peer = lax.rem(frame + hop, frames)
            copies.append(
                pltpu.make_async_remote_copy(
                    src_ref=grad_stage.at[index, peer],
                    dst_ref=grad_first.at[frame, :, rows, :],
                    send_sem=gs.at[index, hop - 1],
                    recv_sem=gr.at[index, hop - 1],
                    device_id={"frame": peer},
                    device_id_type=MESH,
                )
            )
        return copies

    def grad_own(index):
        rows = pl.ds(pl.multiple_of(index * group, group), group)
        return pltpu.make_async_copy(
            grad_stage.at[index, frame], grad_first.at[frame, :, rows, :], ws.at[0, index]
        )

    def grad_keep(index):
        place = index + tiles
        rows = pl.ds(pl.multiple_of(index * group, group), group)
        return pltpu.make_async_copy(
            grad_stage.at[place], grad_later.at[:, :, rows, :], ws.at[0, place]
        )

    def out_keep(number):
        rows = pl.ds(pl.multiple_of(lax.rem(number, tiles) * group, group), group)
        return pltpu.make_async_copy(
            out_stage.at[number], out_all.at[lax.div(number, tiles), :, :, rows, :], ws.at[1, number]
        )

    @pl.when(step == 0)
    def _():
        barrier = pltpu.get_barrier_semaphore()
        for hop in range(1, frames):
            pl.semaphore_signal(
                barrier,
                inc=1,
                device_id={"frame": lax.rem(frame + hop, frames)},
                device_id_type=MESH,
            )
        pl.semaphore_wait(barrier, frames - 1)
        load(after_first, 0, 0, 0).start()
        load(cot_first, 1, 0, 0).start()
        for number in range(2):
            for copy in later_copies(number):
                copy.start()
            own_copy(number).start()
        first = lax.broadcasted_iota(jnp.int32, (tokens, tokens), 0)
        second = lax.broadcasted_iota(jnp.int32, (tokens, tokens), 1)
        mask[...] = jnp.where(lax.rem(first, group) == lax.rem(second, group), 0.0, -1e30)

    @pl.when(step == tiles)
    def _():
        for copy in later_copies(0):
            copy.wait_recv()
        own_copy(0).wait()
        load(after_second, 0, 0, slot).start()

    load(after_first, 0, 0, slot).wait()

    @pl.when(step + 1 < tiles)
    def _():
        load(after_first, 0, step + 1, 1 - slot).start()
        load(cot_first, 1, step + 1, 1 - slot).start()

    @pl.when((step >= tiles) & (step < last))
    def _():
        load(after_second, 0, tile + 1, 1 - slot).start()

    @pl.when((step > tiles) & (step < last))
    def _():
        load(cot_second, 1, tile + 1, 1 - slot).start()

    @pl.when(tile == 0)
    def _():
        sums[...] = jnp.zeros_like(sums)

    def add(place, values):
        sums[place : place + 1, :] += values

    after = after_tile[slot].reshape(tokens, width).astype(f32)
    norm, scale = normed(after)
    hidden = (norm * (1.0 + piece(4)) + piece(3)).astype(bf16)
    h2_ref[...] = hidden
    qkv[...] = dot(hidden, w_b[:, : 3 * width], 1, 0).astype(bf16)
    attend(qkv, mixed_ref, totals, width, mask)
    branch_two = dot(mixed_ref[...], w_b[:, 3 * width :], 1, 0) + mod[19:20, :]
    after_two = after + piece(5) * branch_two
    norm_three, scale_three = normed(after_two)
    hidden = (norm_three * (1.0 + piece(7)) + piece(6)).astype(bf16)
    h3_ref[...] = hidden

    @pl.when(step == tiles)
    def _():
        for copy in later_copies(1):
            copy.wait_recv()
        own_copy(1).wait()
        load(cot_second, 1, 0, slot).start()
        if tiles > 1:
            load(cot_second, 1, 1, 1 - slot).start()

        def send(index, carry):
            for copy in grad_copies(index):
                copy.start()
            return carry

        lax.fori_loop(0, tiles, send, 0)

    load(cot_first, 1, 0, slot).wait()
    grad_out = cot_tile[slot].reshape(tokens, width).astype(f32) * loss[pl.ds(clip, 1), :]
    grad_branch = (grad_out * piece(8)).astype(bf16)
    gb3_ref[...] = grad_branch
    add(11, column_sum(grad_branch.astype(f32)))
    branch_three = jnp.zeros((tokens, width), f32)
    grad_hidden = jnp.zeros((tokens, width), f32)
    for chunk in range(w_u.shape[1] // width):
        cut = slice(chunk * width, (chunk + 1) * width)
        upper = dot(hidden, w_u[:, cut], 1, 0) + mod[20 + chunk : 21 + chunk, :]
        square = upper * upper
        bend = jnp.tanh(upper * (GELU_C + (GELU_C * GELU_A) * square))
        half = 0.5 + 0.5 * bend
        act = (upper * half).astype(bf16)
        slope = half + (0.5 * upper) * (1.0 - bend * bend) * (
            GELU_C + (3.0 * GELU_C * GELU_A) * square
        )
        act_ref[:, cut] = act
        branch_three += dot(act, w_d[cut, :], 1, 0)
        grad_upper = (dot(grad_branch, w_d[cut, :], 1, 1) * slope).astype(bf16)
        gup_ref[:, cut] = grad_upper
        add(7 + chunk, column_sum(grad_upper.astype(f32)))
        grad_hidden += dot(grad_upper, w_u[:, cut], 1, 1)
    branch_three += mod[24:25, :]
    out = (after_two + piece(8) * branch_three).astype(bf16)
    out_stage[step] = out.reshape(out_stage.shape[1:])
    add(5, column_sum(grad_out * branch_three))
    add(3, column_sum(grad_hidden))
    add(4, column_sum(grad_hidden * norm_three))
    grad_two = grad_out + norm_back(grad_hidden, 1.0 + piece(7), norm_three, scale_three)
    add(2, column_sum(grad_two * branch_two))
    grad_branch = (grad_two * piece(5)).astype(bf16)
    gb2_ref[...] = grad_branch
    add(6, column_sum(grad_branch.astype(f32)))
    gmix[...] = dot(grad_branch, w_b[:, 3 * width :], 1, 1).astype(bf16)
    attend_back(qkv, gmix, totals, gqkv_ref, width, mask)
    grad_hidden = dot(gqkv_ref[...], w_b[:, : 3 * width], 1, 1).astype(bf16).astype(f32)
    add(0, column_sum(grad_hidden))
    add(1, column_sum(grad_hidden * norm))
    grad_one = grad_two + norm_back(grad_hidden, 1.0 + piece(4), norm, scale)
    grad_stage[step] = grad_one.astype(bf16).reshape(grad_stage.shape[1:])

    out_keep(step).start()

    @pl.when(step < tiles)
    def _():
        grad_own(tile).start()

    @pl.when(step >= tiles)
    def _():
        grad_keep(tile).start()

    @pl.when(step == last)
    def _():
        for copy in later_copies(0) + later_copies(1):
            copy.wait_send()

        def settle(index, carry):
            for copy in grad_copies(index):
                copy.wait_send()
                copy.wait_recv()
            grad_own(index).wait()
            grad_keep(index).wait()
            out_keep(index).wait()
            out_keep(index + tiles).wait()
            return carry

        lax.fori_loop(0, tiles, settle, 0)


def middle_call(
    clips, frames, after_first, cot_first, after_later, cotangent, loss, mod, w_b, w_u, w_d
):
    _, frame_count, part, width = after_first.shape
    group = min(16, part)
    tiles = part // group
    tokens = frames * frame_count * group
    hidden_width = w_u.shape[1]
    widths = (hidden_width, hidden_width, width, width, width, width, width, 3 * width)
    own = lambda columns: pl.BlockSpec((tokens, columns), lambda t: (t, 0))
    hbm = pl.BlockSpec(memory_space=pl.ANY)
    rows = 2 * tiles * tokens
    traded = jax.ShapeDtypeStruct(after_first.shape, bf16)
    slab = (frames, frame_count, group, width)
    return pl.pallas_call(
        functools.partial(middle_kernel, clips, frames, tiles),
        grid=(2 * tiles,),
        in_specs=[
            hbm, hbm, hbm, hbm, full(loss.shape), full(mod.shape), full(w_b.shape),
            full(w_u.shape), full(w_d.shape),
        ],
        out_specs=[own(columns) for columns in widths]
        + [pl.BlockSpec((None, 16, width), lambda t: (t // tiles, 0, 0))]
        + [hbm] * 5,
        out_shape=[jax.ShapeDtypeStruct((rows, columns), bf16) for columns in widths]
        + [
            jax.ShapeDtypeStruct((2, 16, width), f32),
            traded, traded, traded, traded,
            jax.ShapeDtypeStruct((2,) + after_first.shape, bf16),
        ],
        scratch_shapes=[
            VMEM((tokens, 3 * width), bf16),
            VMEM((16, tokens), f32),
            VMEM((tokens, tokens), f32),
            VMEM((tokens, width), bf16),
            VMEM((2,) + slab, bf16),
            VMEM((2,) + slab, bf16),
            VMEM((2 * tiles,) + slab, bf16),
            VMEM((2 * tiles,) + slab, bf16),
            DMA((frames - 1,)), DMA((frames - 1,)),
            DMA((frames - 1,)), DMA((frames - 1,)),
            DMA((tiles, frames - 1)), DMA((tiles, frames - 1)),
            DMA((2, 2)), DMA((2,)), DMA((2, 2 * tiles)),
        ],
        compiler_params=pltpu.CompilerParams(
            collective_id=2, has_side_effects=True, vmem_limit_bytes=VMEM_LIMIT
        ),
    )(after_first, cot_first, after_later, cotangent, loss, mod, w_b, w_u, w_d)


def space_back_kernel(
    clip, grad_ref, x_ref, mod, w_c, qkv, branch, totals,
    out_ref, gb_ref, gqkv_ref, sums, gmix,
):
    width = x_ref.shape[-1]
    tokens = x_ref.shape[-2]
    row = clip * 9
    piece = lambda number: mod[row + number : row + number + 1, :]

    @pl.when(pl.program_id(0) == 0)
    def _():
        sums[...] = jnp.zeros_like(sums)

    grad = grad_ref[...].reshape(tokens, width).astype(f32)
    grad_branch = (grad * piece(2)).astype(bf16)
    gb_ref[...] = grad_branch
    sums[2:3, :] += column_sum(grad * branch[...].astype(f32))
    sums[3:4, :] += column_sum(grad_branch.astype(f32))
    gmix[...] = dot(grad_branch, w_c[:, 3 * width :], 1, 1).astype(bf16)
    attend_back(qkv, gmix, totals, gqkv_ref, width, None)
    grad_hidden = dot(gqkv_ref[...], w_c[:, : 3 * width], 1, 1)
    norm, scale = normed(x_ref[...].reshape(tokens, width).astype(f32))
    sums[0:1, :] += column_sum(grad_hidden)
    sums[1:2, :] += column_sum(grad_hidden * norm)
    result = grad + norm_back(grad_hidden, 1.0 + piece(1), norm, scale)
    out_ref[...] = result.reshape(out_ref.shape)


def space_back_next(count, clip, *refs):
    space_back_kernel(clip, *refs[:7], *refs[7 + count :])


def space_back_call(clip, grad, x, mod, w_c, qkv, branch, totals, earlier):
    clip_count, frame_count, tokens, width = x.shape
    frames = grad.shape[0]
    part = grad.shape[2]
    rows = frame_count * tokens
    by_frame = lambda columns: pl.BlockSpec(
        (None, tokens, columns), lambda f: (clip * frame_count + f, 0, 0)
    )
    own = lambda columns: pl.BlockSpec((tokens, columns), lambda f: (clip * frame_count + f, 0))
    in_specs = [
        pl.BlockSpec((frames, 1, part, width), lambda f: (0, f, 0, 0)),
        pl.BlockSpec((1, 1, tokens, width), lambda f: (clip, f, 0, 0)),
        full(mod.shape),
        full(w_c.shape),
        by_frame(3 * width),
        by_frame(width),
        pl.BlockSpec((None, 16, tokens), lambda f: (clip * frame_count + f, 0, 0)),
    ]
    args = [grad, x, mod, w_c, qkv, branch, totals]
    body = functools.partial(space_back_kernel, clip)
    aliases = {}
    if earlier is not None:
        in_specs += [pl.BlockSpec(memory_space=pl.ANY)] * len(earlier)
        args += list(earlier)
        aliases = {7 + number: number for number in range(len(earlier))}
        body = functools.partial(space_back_next, len(earlier), clip)
    return pl.pallas_call(
        body,
        grid=(frame_count,),
        in_specs=in_specs,
        out_specs=[
            pl.BlockSpec((1, 1, tokens, width), lambda f: (clip, f, 0, 0)),
            own(width),
            own(3 * width),
            pl.BlockSpec((8, width), lambda f: (0, 0)),
        ],
        out_shape=[
            jax.ShapeDtypeStruct(x.shape, f32),
            jax.ShapeDtypeStruct((clip_count * rows, width), bf16),
            jax.ShapeDtypeStruct((clip_count * rows, 3 * width), bf16),
            jax.ShapeDtypeStruct((8, width), f32),
        ],
        scratch_shapes=[VMEM((tokens, width), bf16)],
        input_output_aliases=aliases,
        compiler_params=pltpu.CompilerParams(vmem_limit_bytes=VMEM_LIMIT),
        cost_estimate=pl.CostEstimate(
            flops=rows * 20_000_000, bytes_accessed=rows * width * 20, transcendentals=0
        ),
    )(*args)


def shards(
    inputs, cotangent, time_steps, weight_index, ada_weight, ada_bias, space_qkv, space_out,
    space_out_bias, time_qkv, time_out, time_out_bias, up_weight, up_bias, down_weight, down_bias,
):
    clip_count, frame_count, patch_count, width = inputs.shape
    clips, frames = lax.axis_size("clip"), lax.axis_size("frame")
    owners = clips * frames
    owner = lax.axis_index("clip") * frames + lax.axis_index("frame")
    part = patch_count // frames
    rows = ada_weight.shape[0]

    embed = jax.nn.silu(embed_steps(time_steps, width)).astype(bf16)
    embed = jnp.pad(embed, ((0, 16 - clip_count), (0, 0)))
    place = lax.broadcasted_iota(jnp.int32, (width, 128), 0) - owner * rows
    lane = lax.broadcasted_iota(jnp.int32, (width, 128), 1)
    select = ((place == lane) & (lane < rows)).astype(bf16)
    ada = jnp.pad(ada_weight, ((0, 128 - rows), (0, 0)))

    def spread_bias(vector):
        length = vector.shape[0]
        empty = jnp.zeros((owners * length,), f32)
        return lax.dynamic_update_slice(empty, vector.astype(f32), (owner * length,)).reshape(
            -1, width
        )

    bias = jnp.concatenate(
        [
            spread_bias(vector)
            for vector in (ada_bias, space_out_bias, time_out_bias, up_bias, down_bias)
        ],
        axis=0,
    )
    sh_c = jnp.concatenate([space_qkv, space_out], axis=1)
    sh_b = jnp.concatenate([time_qkv, time_out], axis=1)
    (
        w_c, w_b, w_u, w_d, mod, chosen, totals, hidden_one, qkv_one, mixed_one, branch_one,
        after_first, after_later, cot_first,
    ) = start_call(
        clips, frames, inputs, cotangent, sh_c, sh_b, up_weight, down_weight, embed, select, ada,
        bias,
    )

    def exchange(values):
        return lax.all_to_all(values, "frame", split_axis=0, concat_axis=0, tiled=True)

    loss = jnp.exp2(weight_index.astype(f32) * 0.5 - 1.0)
    loss = jnp.broadcast_to(loss[:, None], (clip_count, width))
    (
        act, gup, h3, gb3, mixed_two, gb2, h2, gqkv_two, mid_sums, _, _, grad_first,
        grad_later, out_all,
    ) = middle_call(
        clips, frames, after_first, cot_first, after_later, cotangent, loss, mod, w_b, w_u, w_d
    )
    grads = [grad_first, exchange(grad_later)]

    earlier = None
    space_sums = []
    for clip in range(clip_count):
        *earlier, sums = space_back_call(
            clip, grads[clip], inputs, mod, w_c, qkv_one, branch_one, totals, earlier
        )
        space_sums.append(sums)
    input_grad, gb1, gqkv_one = earlier
    pieces = []
    for clip in range(clip_count):
        pieces += [space_sums[clip][0:3], mid_sums[clip][0:6]]
    pieces.append(sum(entry[3:4] for entry in space_sums))
    pieces.append(sum(entry[6:12] for entry in mid_sums))
    small = jnp.concatenate(pieces, axis=0)
    small = jnp.pad(small, ((0, ROWS - small.shape[0]), (0, 0)))
    picked = chosen.reshape(clips, 16, 128)[:, :clip_count].reshape(clips * clip_count, 128)
    outputs, grad_ada, sums, own_u, own_d, own_b, own_bo, own_c, own_co = grad_call(
        clips, frames, clip_count, small, picked.astype(f32).T, out_all, h3, gup, act, gb3, h2, gqkv_two,
        mixed_two, gb2, hidden_one.reshape(-1, width), gqkv_one, mixed_one.reshape(-1, width), gb1,
    )
    biases = sums[9:]

    def own_slice(vector):
        length = vector.shape[0] // owners
        return lax.dynamic_slice_in_dim(vector, owner * length, length, 0)

    return (
        outputs,
        input_grad,
        grad_ada,
        own_slice(sums[:9].reshape(-1)),
        own_c,
        own_co,
        own_slice(biases[0]),
        own_b,
        own_bo,
        own_slice(biases[1]),
        own_u,
        own_slice(biases[2:6].reshape(-1)),
        own_d,
        own_slice(biases[6]),
    )


def solution(mesh):
    tokens = P("clip", "frame", None, None)
    matrix = P(("clip", "frame"), None)
    vector = P(("clip", "frame"))
    in_specs = (
        tokens, tokens, P("clip"), P("clip"), matrix, vector, matrix, matrix, vector, matrix,
        matrix, vector, matrix, vector, matrix, vector,
    )
    out_specs = (
        tokens, tokens, matrix, vector, matrix, matrix, vector, matrix, matrix, vector, matrix,
        vector, matrix, vector,
    )
    return jax.shard_map(shards, mesh=mesh, in_specs=in_specs, out_specs=out_specs, check_vma=False)
```

```python
import functools
import math

import jax
import jax.numpy as jnp
from jax import lax
from jax.experimental import pallas as pl
from jax.experimental.pallas import tpu as pltpu
from jax.sharding import PartitionSpec as P

HEADS = 12
HEAD = 64
GROUP = 4
ROWS = 32
GELU_C = math.sqrt(2.0 / math.pi)
GELU_A = 0.044715
VMEM_LIMIT = 58 << 20

f32 = jnp.float32
bf16 = jnp.bfloat16
highest = lax.Precision.HIGHEST
MESH = pl.DeviceIdType.MESH
VMEM = pltpu.VMEM
DMA = pltpu.SemaphoreType.DMA


def embed_steps(time_steps, model_width):
    half_width = model_width // 2
    frequencies = jnp.exp(
        -math.log(10000.0) * jnp.arange(half_width, dtype=f32) / half_width
    )
    angles = time_steps.astype(f32)[:, None] * frequencies[None, :]
    return jnp.concatenate([jnp.cos(angles), jnp.sin(angles)], axis=1)


def dot(left, right, left_dim, right_dim):
    return lax.dot_general(
        left, right, (((left_dim,), (right_dim,)), ((), ())), preferred_element_type=f32
    )


def flip(index, mask):
    bit = 1
    while bit <= mask:
        if mask & bit:
            index = index + bit * (1 - 2 * ((index // bit) % 2))
        bit *= 2
    return index


def span(masks):
    out = [0]
    for mask in masks:
        out = out + [entry ^ mask for entry in out]
    return out


def frame_masks(frames):
    masks, bit = [], 1
    while bit < frames:
        masks.append(bit)
        bit *= 2
    if len(masks) > 1:
        masks = [frames - 1] + masks[:-1]
    return masks


def clip_tail_masks(clips):
    masks, bit = [], 2
    while bit < clips:
        masks.append(bit)
        bit *= 2
    return masks


def greet(clips, frames):
    clip, frame = lax.axis_index("clip"), lax.axis_index("frame")
    barrier = pltpu.get_barrier_semaphore()
    for step in range(1, clips):
        pl.semaphore_signal(
            barrier, inc=1, device_id={"clip": lax.rem(clip + step, clips)}, device_id_type=MESH
        )
    for step in range(1, frames):
        pl.semaphore_signal(
            barrier, inc=1, device_id={"frame": lax.rem(frame + step, frames)}, device_id_type=MESH
        )
    pl.semaphore_wait(barrier, clips + frames - 2)


def spread(axis, size, source_of, target, send_sems, recv_sems):
    me = lax.axis_index(axis)
    copies = []
    for step in range(1, size):
        peer = lax.rem(me + step, size)
        copy = pltpu.make_async_remote_copy(
            src_ref=source_of(peer),
            dst_ref=target.at[me],
            send_sem=send_sems.at[step - 1],
            recv_sem=recv_sems.at[step - 1],
            device_id={axis: peer},
            device_id_type=MESH,
        )
        copy.start()
        copies.append(copy)
    return copies


def start_kernel(
    clips, frames, clip_count,
    x_ref, cotangent, sh_c, sh_b, sh_u, sh_d, embed, select, ada, bias,
    w_c, w_b, w_u, w_d, mod, chosen, totals, hidden_out, qkv_out, mixed_out, branch_out,
    after_first, after_later, cot_first,
    v_c, z_c, z_b, z_u, z_d, st_w, b_c, b_b, b_u, b_d,
    embeds, parts, terms, arrived, held, lined, hidden, qkv, mixed, branch, after,
    zs, zr, cs, cr, xs, xr, ls, es, er, ps, pr, fs, fr, ts, tr, hs, hr, os, ws,
):
    clip, frame = lax.axis_index("clip"), lax.axis_index("frame")
    shards_in = (sh_c, sh_b, sh_u, sh_d)
    zoned = (z_c, z_b, z_u, z_d)
    blocks = (b_c, b_b, b_u, b_d)
    wholes = (v_c, w_b, w_u, w_d)
    width = mod.shape[1]
    frame_count, tokens = x_ref.shape[1], x_ref.shape[2]
    part = tokens // frames
    greet(clips, frames)
    masks = frame_masks(frames)
    sends = []
    stage = {}

    def frame_step(group, step):
        number = (1 << step) - 1
        copies = []
        for offset in span(masks[:step]):
            slot = flip(frame, offset)
            source = shards_in[group] if offset == 0 else zoned[group].at[slot]
            copy = pltpu.make_async_remote_copy(
                src_ref=source,
                dst_ref=zoned[group].at[slot],
                send_sem=zs.at[group, number],
                recv_sem=zr.at[group, number],
                device_id={"frame": flip(frame, masks[step])},
                device_id_type=MESH,
            )
            copy.start()
            copies.append(copy)
            number += 1
        sends.extend(copies)
        stage[group] = copies

    def frame_rest(group):
        for step in range(1, len(masks)):
            for copy in stage[group]:
                copy.wait_recv()
            frame_step(group, step)

    tail = clip_tail_masks(clips)
    steps = len(tail)
    orders = (tail, tail[::-1])
    moving = {}

    def block_send(group, half, step, position, offset):
        whole = wholes[group]
        block_rows = whole.shape[0] // clips
        columns = whole.shape[1] // 2
        rows = pl.ds(pl.multiple_of(flip(clip, offset) * block_rows, block_rows), block_rows)
        lanes = pl.ds(half * columns, columns)
        target = whole.at[rows, lanes]
        number = (1 << step) - 1 + position
        copy = pltpu.make_async_remote_copy(
            src_ref=blocks[group].at[:, lanes] if offset == 0 else target,
            dst_ref=target,
            send_sem=xs.at[group, half, number],
            recv_sem=xr.at[group, half, number],
            device_id={"clip": flip(clip, orders[half][step])},
            device_id_type=MESH,
        )
        copy.start()
        moving[group, half, number] = copy

    core_copies = {group: [] for group in range(4)}

    def core_send(group, offset):
        whole = wholes[group]
        block_rows = whole.shape[0] // clips
        rows = pl.ds(pl.multiple_of(flip(clip, offset) * block_rows, block_rows), block_rows)
        number = len(core_copies[group])
        copy = pltpu.make_async_remote_copy(
            src_ref=blocks[group] if offset == 0 else whole.at[rows, :],
            dst_ref=whole.at[rows, :],
            send_sem=cs.at[group, number],
            recv_sem=cr.at[group, number],
            device_id={"clip": flip(clip, 1)},
            device_id_type=MESH,
        )
        copy.start()
        core_copies[group].append(copy)

    local_copies = []

    def block_ready(group):
        for copy in stage[group]:
            copy.wait_recv()
        rows, columns = shards_in[group].shape
        block_rows = frames * rows
        if rows % 16:
            for slot in range(frames):
                st_w[slot * rows : (slot + 1) * rows, :columns] = zoned[group][slot].astype(f32)
            blocks[group][...] = st_w[:block_rows, :columns].astype(bf16)
        else:
            for slot in range(frames):
                blocks[group][slot * rows : (slot + 1) * rows, :] = zoned[group][slot]
        for step in range(steps):
            for half in range(2):
                block_send(group, half, step, 0, 0)
        core_send(group, 0)
        place = pl.ds(pl.multiple_of(clip * block_rows, block_rows), block_rows)
        keep = pltpu.make_async_copy(blocks[group], wholes[group].at[place, :], ls.at[group])
        keep.start()
        local_copies.append(keep)

    def block_forward(group):
        for step in range(1, steps):
            for half in range(2):
                for position in range(1 << (step - 1), 1 << step):
                    moving[group, half, position - 1].wait_recv()
                for later in range(step, steps):
                    for position, offset in enumerate(span(orders[half][:later])):
                        if (1 << (step - 1)) <= position < (1 << step):
                            block_send(group, half, later, position, offset)

    def block_finish(group):
        last = (1 << (steps - 1)) - 1
        for half in range(2):
            for number in range(last, (1 << steps) - 1):
                moving[group, half, number].wait_recv()
        for offset in span(tail)[1:]:
            core_send(group, offset)

    def core_finish(group):
        for copy in core_copies[group]:
            copy.wait_recv()

    frame_step(0, 0)
    own = spread("clip", clips, lambda peer: embed, embeds, es, er)
    sends.extend(own)
    embeds[clip] = embed[...]
    for group in range(4):
        zoned[group][frame] = shards_in[group][...]
    frame_rest(0)
    for copy in own:
        copy.wait_recv()
    picked = dot(embeds[...].reshape(clips * 16, width), select[...], 1, 0).astype(bf16)
    chosen[...] = picked
    parts[...] = dot(picked, ada[...], 1, 0)
    for peer in range(clips):
        for local in range(clip_count):
            row = peer * 16 + local
            for piece in range(9):
                terms[peer, local * 9 + piece : local * 9 + piece + 1, :] = (
                    parts[row : row + 1, piece * width : (piece + 1) * width]
                    + bias[piece : piece + 1, :]
                )
        base = clip_count * 9
        terms[peer, base : base + 7, :] = bias[9:16, :]
        if base + 7 < ROWS:
            terms[peer, base + 7 : ROWS, :] = jnp.zeros((ROWS - base - 7, width), f32)
    own = spread("clip", clips, lambda peer: terms.at[peer], arrived, ps, pr)
    sends.extend(own)
    arrived[clip] = terms[clip]
    block_ready(0)
    for group in range(1, 4):
        frame_step(group, 0)
    for copy in own:
        copy.wait_recv()
    total = arrived[0]
    for peer in range(1, clips):
        total = total + arrived[peer]
    held[...] = total
    own = spread("frame", frames, lambda peer: held, lined, fs, fr)
    sends.extend(own)
    lined[frame] = total
    for group in range(1, 4):
        frame_rest(group)

    cot_copies = []
    for step in range(frames - 1, 0, -1):
        peer = flip(frame, step)
        copy = pltpu.make_async_remote_copy(
            src_ref=cotangent.at[0, :, pl.ds(pl.multiple_of(peer * part, part), part), :],
            dst_ref=cot_first.at[frame],
            send_sem=ts.at[step - 1],
            recv_sem=tr.at[step - 1],
            device_id={"frame": peer},
            device_id_type=MESH,
        )
        copy.start()
        cot_copies.append(copy)
    keep = pltpu.make_async_copy(
        cotangent.at[0, :, pl.ds(pl.multiple_of(frame * part, part), part), :],
        cot_first.at[frame],
        ls.at[4],
    )
    keep.start()
    local_copies.append(keep)

    for copy in own:
        copy.wait_recv()
    total = lined[0]
    for peer in range(1, frames):
        total = total + lined[peer]
    mod[...] = total
    block_forward(0)
    for group in range(1, 4):
        block_ready(group)
    block_finish(0)
    core_finish(0)
    local_copies[0].wait()

    keep = pltpu.make_async_copy(v_c, w_c, ls.at[5])
    keep.start()
    local_copies.append(keep)

    def after_copy(f, step):
        peer = flip(frame, step)
        return pltpu.make_async_remote_copy(
            src_ref=after.at[f, pl.ds(pl.multiple_of(peer * part, part), part), :],
            dst_ref=after_first.at[frame, f],
            send_sem=hs.at[f, step - 1],
            recv_sem=hr.at[f, step - 1],
            device_id={"frame": peer},
            device_id_type=MESH,
        )

    def own_after(f):
        return pltpu.make_async_copy(
            after.at[f, pl.ds(pl.multiple_of(frame * part, part), part), :],
            after_first.at[frame, f],
            os.at[f],
        )

    def later_after(f):
        return pltpu.make_async_copy(after.at[f], after_later.at[f - frame_count], os.at[f])

    kept = ((hidden, hidden_out), (qkv, qkv_out), (mixed, mixed_out), (branch, branch_out))

    def write_back(f):
        return [
            pltpu.make_async_copy(source.at[f], target.at[f], ws.at[number, f])
            for number, (source, target) in enumerate(kept)
        ]

    for local in range(clip_count):
        row = local * 9

        def one_frame(index, carry):
            f = local * frame_count + index
            values = x_ref[local, index].astype(f32)
            norm, _ = normed(values)
            scaled = norm * (1.0 + mod[row + 1 : row + 2, :]) + mod[row : row + 1, :]
            lowered = scaled.astype(bf16)
            hidden[f] = lowered
            qkv[f] = dot(lowered, v_c[:, : 3 * width], 1, 0).astype(bf16)
            attend(qkv.at[f], mixed.at[f], totals.at[f], width, None)
            grown = dot(mixed[f], v_c[:, 3 * width :], 1, 0) + mod[18:19, :]
            branch[f] = grown.astype(bf16)
            after[f] = (values + mod[row + 2 : row + 3, :] * grown).astype(bf16)
            if local == 0:
                for step in range(frames - 1, 0, -1):
                    after_copy(f, step).start()
                own_after(f).start()
            else:
                later_after(f).start()
            for copy in write_back(f):
                copy.start()
            return carry

        lax.fori_loop(0, frame_count, one_frame, 0)
        if local == 0:
            block_forward(1)
    for group in range(2, 4):
        block_forward(group)
    for group in range(1, 4):
        block_finish(group)
    for group in range(1, 4):
        core_finish(group)

    def settle(f, carry):
        for step in range(1, frames):
            copy = after_copy(f, step)
            copy.wait_recv()
            copy.wait_send()
        own_after(f).wait()
        return carry

    lax.fori_loop(0, frame_count, settle, 0)

    def settle_later(f, carry):
        later_after(f).wait()
        return carry

    lax.fori_loop(frame_count, clip_count * frame_count, settle_later, 0)

    def settle_kept(f, carry):
        for copy in write_back(f):
            copy.wait()
        return carry

    lax.fori_loop(0, clip_count * frame_count, settle_kept, 0)
    for copy in cot_copies:
        copy.wait_recv()
        copy.wait_send()
    for copy in local_copies[1:]:
        copy.wait()
    for copy in moving.values():
        copy.wait_send()
    for group in range(4):
        for copy in core_copies[group]:
            copy.wait_send()
    for copy in sends:
        copy.wait_send()


def start_call(
    clips, frames, inputs, cotangent, sh_c, sh_b, sh_u, sh_d, embed, select, ada, bias
):
    clip_count, frame_count, tokens, width = inputs.shape
    rows, columns = sh_c.shape
    rows_d = sh_d.shape[0]
    block = frames * rows
    block_d = frames * rows_d
    peers = max(clips // 2 - 1, 1)
    total = clip_count * frame_count
    part = tokens // frames
    whole = jax.ShapeDtypeStruct((clips * block, columns), bf16)
    vmem = pl.BlockSpec(memory_space=VMEM)
    hbm = pl.BlockSpec(memory_space=pl.ANY)
    zoned = lambda height, lanes: VMEM((frames, height, lanes), bf16)
    saved = lambda lanes: jax.ShapeDtypeStruct((total, tokens, lanes), bf16)
    lent = lambda lanes: VMEM((total, tokens, lanes), bf16)
    traded = jax.ShapeDtypeStruct((frames, frame_count, part, width), bf16)
    return pl.pallas_call(
        functools.partial(start_kernel, clips, frames, clip_count),
        out_shape=(
            whole, whole, whole,
            jax.ShapeDtypeStruct((clips * block_d, width), bf16),
            jax.ShapeDtypeStruct((ROWS, width), f32),
            jax.ShapeDtypeStruct((clips * 16, 128), bf16),
            jax.ShapeDtypeStruct((total, 16, tokens), f32),
            saved(width), saved(3 * width), saved(width), saved(width),
            traded,
            jax.ShapeDtypeStruct(((clip_count - 1) * frame_count, tokens, width), bf16),
            traded,
        ),
        in_specs=[vmem, hbm] + [vmem] * 8,
        out_specs=(hbm, hbm, hbm, hbm, vmem, vmem, vmem) + (hbm,) * 7,
        scratch_shapes=[
            VMEM((clips * block, columns), bf16),
            zoned(rows, columns), zoned(rows, columns), zoned(rows, columns), zoned(rows_d, width),
            VMEM((max(block, block_d), columns), f32),
            VMEM((block, columns), bf16),
            VMEM((block, columns), bf16),
            VMEM((block, columns), bf16),
            VMEM((block_d, width), bf16),
            VMEM((clips, 16, width), bf16),
            VMEM((clips * 16, 9 * width), f32),
            VMEM((clips, ROWS, width), f32),
            VMEM((clips, ROWS, width), f32),
            VMEM((ROWS, width), f32),
            VMEM((frames, ROWS, width), f32),
            lent(width), lent(3 * width), lent(width), lent(width), lent(width),
            DMA((4, frames - 1)), DMA((4, frames - 1)),
            DMA((4, clips // 2)), DMA((4, clips // 2)),
            DMA((4, 2, peers)), DMA((4, 2, peers)),
            DMA((6,)),
            DMA((clips - 1,)), DMA((clips - 1,)),
            DMA((clips - 1,)), DMA((clips - 1,)),
            DMA((frames - 1,)), DMA((frames - 1,)),
            DMA((frames - 1,)), DMA((frames - 1,)),
            DMA((frame_count, frames - 1)), DMA((frame_count, frames - 1)),
            DMA((total,)),
            DMA((4, total)),
        ],
        compiler_params=pltpu.CompilerParams(
            collective_id=0, has_side_effects=True, vmem_limit_bytes=VMEM_LIMIT
        ),
    )(inputs, cotangent, sh_c, sh_b, sh_u, sh_d, embed, select, ada, bias)


STEP = 512
SLOTS = 3


def grad_kernel(
    clips, frames, clip_count,
    small, chosen, out_all, h3, gup, act, gb3, h2, gqkv2, mix2, gb2, h1, gqkv1, mix1, gb1,
    outputs, grad_ada, bias_sums, out_u, out_d, out_b, out_bo, out_c, out_co,
    sum_w, sum_d, core_w, core_d, side_w, side_d, line_w, line_d, last_w, last_d,
    left, right, total, gathered, lined, held,
    lsem, rsem, cs, cr, xs, xr, zs, zr, fs, fr, ps, pr, os, orr, ks,
):
    clip, frame = lax.axis_index("clip"), lax.axis_index("frame")
    tokens = h3.shape[0]
    width = small.shape[1]
    wide = sum_w.shape[-1]
    narrow = sum_d.shape[-1]
    tail = clip_tail_masks(clips)
    orders = (tail, tail[::-1])
    masks = frame_masks(frames)
    greet(clips, frames)
    first = spread("frame", frames, lambda peer: small, lined, fs, fr)
    lined[frame] = small[...]
    part = out_all.shape[3]
    frame_count = out_all.shape[2]
    out_copies = []
    mine = pl.ds(pl.multiple_of(frame * part, part), part)

    def send_output(number):
        local, index = divmod(number, frame_count)
        for hop in range(frames - 1, 0, -1):
            peer = flip(frame, hop)
            copy = pltpu.make_async_remote_copy(
                src_ref=out_all.at[local, peer, index],
                dst_ref=outputs.at[local, index, mine, :],
                send_sem=os.at[number, hop - 1],
                recv_sem=orr.at[number, hop - 1],
                device_id={"frame": peer},
                device_id_type=MESH,
            )
            copy.start()
            out_copies.append(copy)

    own_outs = []
    for local in range(clip_count):
        copy = pltpu.make_async_copy(
            out_all.at[local, frame], outputs.at[local, :, mine, :], ks.at[local]
        )
        copy.start()
        own_outs.append(copy)

    chunks = [
        (1, 0, [(act, gb3, 0, 0, narrow)], out_d, 0),
        (1, 1, [(act, gb3, narrow, 0, narrow)], out_d, narrow),
        (0, 0, [(h3, gup, 0, 0, wide)], out_u, 0),
        (0, 1, [(h3, gup, wide, 0, wide)], out_u, wide),
        (0, 2, [(h2, gqkv2, 0, 0, wide)], out_b, 0),
        (0, 3, [(h2, gqkv2, wide, 0, width), (mix2, gb2, 0, width, width)], out_b, wide),
        (0, 4, [(h1, gqkv1, 0, 0, wide)], out_c, 0),
        (0, 5, [(h1, gqkv1, wide, 0, width), (mix1, gb1, 0, width, width)], out_c, wide),
    ]
    sums, cores, sides = (sum_w, sum_d), (core_w, core_d), (side_w, side_d)
    lines, lasts = (line_w, line_d), (last_w, last_d)
    flights = {}

    steps = tokens // STEP
    line_up = []
    for kind, _, parts, _, _ in chunks:
        for part in parts:
            for group in range(part[0].shape[1] // width):
                line_up.append(part[:3] + (part[3] + group * part[4], part[4], group))
    begins = [0]
    for kind, _, parts, _, _ in chunks:
        begins.append(begins[-1] + sum(part[0].shape[1] // width for part in parts))

    def load(entry, step, slot):
        one, other, begin, _, lanes, group = line_up[entry]
        rows = pl.ds(pl.multiple_of(step * STEP, STEP), STEP)
        return (
            pltpu.make_async_copy(
                one.at[rows, pl.ds(group * width, width)], left.at[slot], lsem.at[slot]
            ),
            pltpu.make_async_copy(
                other.at[rows, pl.ds(begin, lanes)],
                right.at[slot, :, pl.ds(0, lanes)],
                rsem.at[slot],
            ),
        )

    def place_of(entry, step):
        return lax.rem(entry * steps + step, SLOTS)

    def multiply(number):
        kind, place = chunks[number][:2]
        for entry in range(begins[number], begins[number + 1]):
            at, lanes = line_up[entry][3:5]

            def body(step, carry):
                ahead = step + SLOTS - 1

                @pl.when(ahead < steps)
                def _():
                    for copy in load(entry, ahead, place_of(entry, ahead)):
                        copy.start()

                if entry + 1 < len(line_up):

                    @pl.when(ahead >= steps)
                    def _():
                        for copy in load(entry + 1, ahead - steps, place_of(entry, ahead)):
                            copy.start()

                slot = place_of(entry, step)
                for copy in load(entry, step, slot):
                    copy.wait()
                columns = slice(at, at + lanes)
                before = jnp.where(step > 0, total[:, columns], 0.0)
                total[:, columns] = before + dot(left[slot], right[slot, :, :lanes], 0, 0)
                return carry

            lax.fori_loop(0, steps, body, 0)
        rows, lanes = sums[kind].shape[2:]
        for block in range(clips):
            begin = block * rows
            column = begin // width * lanes
            begin = begin % width
            sums[kind][place, block] = total[begin : begin + rows, column : column + lanes].astype(
                bf16
            )

    def core_start(number):
        kind, place = chunks[number][:2]
        copies = []
        for position, offset in enumerate(span(tail)):
            copy = pltpu.make_async_remote_copy(
                src_ref=sums[kind].at[place, flip(clip, offset ^ 1)],
                dst_ref=cores[kind].at[place, position],
                send_sem=cs.at[number, position],
                recv_sem=cr.at[number, position],
                device_id={"clip": flip(clip, 1)},
                device_id_type=MESH,
            )
            copy.start()
            copies.append(copy)
        flights[number, "core"] = copies

    def half_of(kind, half):
        if kind:
            rows = sums[kind].shape[2] // 2
            return (slice(half * rows, (half + 1) * rows), slice(None))
        lanes = sums[kind].shape[3] // 2
        return (slice(None), slice(half * lanes, (half + 1) * lanes))

    def side_start(number, step):
        kind, place = chunks[number][:2]
        copies = []
        for half in range(2):
            mask = orders[half][step]
            for position, offset in enumerate(span(orders[half][:step])):
                entry = (1 << step) - 1 + position
                copy = pltpu.make_async_remote_copy(
                    src_ref=sums[kind].at[(place, flip(clip, offset ^ mask)) + half_of(kind, half)],
                    dst_ref=sides[kind].at[place, half, entry],
                    send_sem=xs.at[number, half, entry],
                    recv_sem=xr.at[number, half, entry],
                    device_id={"clip": flip(clip, mask)},
                    device_id_type=MESH,
                )
                copy.start()
                copies.append(copy)
        flights[number, "side", step] = copies

    def core_add(number):
        kind, place = chunks[number][:2]
        for copy in flights[number, "core"]:
            copy.wait_recv()
        for position, offset in enumerate(span(tail)):
            block = flip(clip, offset)
            sums[kind][place, block] = (
                sums[kind][place, block].astype(f32) + cores[kind][place, position].astype(f32)
            ).astype(bf16)
        side_start(number, len(tail) - 1)

    def side_add(number, step):
        kind, place = chunks[number][:2]
        for copy in flights[number, "side", step]:
            copy.wait_recv()
        for half in range(2):
            for position, offset in enumerate(span(orders[half][:step])):
                entry = (1 << step) - 1 + position
                block = flip(clip, offset)
                where = (place, block) + half_of(kind, half)
                sums[kind][where] = (
                    sums[kind][where].astype(f32) + sides[kind][place, half, entry].astype(f32)
                ).astype(bf16)
        if step:
            side_start(number, step - 1)
        else:
            rows = lines[kind].shape[2]
            block = sums[kind][place, clip].astype(f32)
            for slot in range(frames):
                lines[kind][place, slot] = block[slot * rows : (slot + 1) * rows, :].astype(bf16)
            line_start(number, len(masks) - 1)

    def line_start(number, step):
        kind, place = chunks[number][:2]
        copies = []
        for position, offset in enumerate(span(masks[:step])):
            entry = (1 << step) - 1 + position
            copy = pltpu.make_async_remote_copy(
                src_ref=lines[kind].at[place, flip(frame, offset ^ masks[step])],
                dst_ref=lasts[kind].at[place, entry],
                send_sem=zs.at[number, entry],
                recv_sem=zr.at[number, entry],
                device_id={"frame": flip(frame, masks[step])},
                device_id_type=MESH,
            )
            copy.start()
            copies.append(copy)
        flights[number, "line", step] = copies

    def line_add(number, step):
        kind, place, _, target, begin = chunks[number]
        for copy in flights[number, "line", step]:
            copy.wait_recv()
        for position, offset in enumerate(span(masks[:step])):
            entry = (1 << step) - 1 + position
            slot = flip(frame, offset)
            value = lines[kind][place, slot].astype(f32) + lasts[kind][place, entry].astype(f32)
            if step:
                lines[kind][place, slot] = value.astype(bf16)
            elif begin + value.shape[1] > target.shape[1]:
                cut = target.shape[1] - begin
                target[:, begin:] = value[:, :cut]
                (out_bo if target is out_b else out_co)[...] = value[:, cut:]
            else:
                target[:, begin : begin + value.shape[1]] = value
        if step:
            line_start(number, step - 1)

    stages = [core_start, core_add]
    for step in range(len(tail))[::-1]:
        stages.append(functools.partial(side_add, step=step))
    for step in range(len(masks))[::-1]:
        stages.append(functools.partial(line_add, step=step))

    def finish_small():
        for copy in second:
            copy.wait_recv()
        rows = grad_ada.shape[0]
        for number in range(9):
            terms = [
                gathered[peer, local * 9 + number : local * 9 + number + 1, :]
                for peer in range(clips)
                for local in range(clip_count)
            ]
            terms = jnp.concatenate(terms, axis=0)
            grad_ada[:, number * width : (number + 1) * width] = lax.dot_general(
                chosen[...], terms, (((1,), (0,)), ((), ())), precision=highest,
                preferred_element_type=f32,
            )[:rows, :]
            bias_sums[number : number + 1, :] = column_sum(terms)
        base = clip_count * 9
        summed = gathered[0, base : base + 7, :]
        for peer in range(1, clips):
            summed = summed + gathered[peer, base : base + 7, :]
        bias_sums[9:16, :] = summed

    for step in range(SLOTS - 1):
        for copy in load(0, step, step):
            copy.start()
    second = None
    lags = [0, 1, 3]
    while len(lags) < len(stages):
        lags.append(lags[-1] + 1)
    for turn in range(len(chunks) + lags[-1]):
        for depth in range(len(stages))[::-1]:
            if depth > 0 and 0 <= turn - lags[depth] < len(chunks):
                stages[depth](turn - lags[depth])
        if turn < clip_count * frame_count:
            send_output(turn)
        if turn < len(chunks):
            multiply(turn)
            core_start(turn)
        if turn == len(chunks):
            finish_small()
        if turn == 0:
            for copy in first:
                copy.wait_recv()
            summed = lined[0]
            for peer in range(1, frames):
                summed = summed + lined[peer]
            held[...] = summed
            second = spread("clip", clips, lambda peer: held, gathered, ps, pr)
            gathered[clip] = summed
    for copy in own_outs:
        copy.wait()
    for copy in out_copies:
        copy.wait_recv()
        copy.wait_send()
    for copy in first + second:
        copy.wait_send()
    for copies in flights.values():
        for copy in copies:
            copy.wait_send()


def grad_call(clips, frames, clip_count, small, chosen, out_all, *operands):
    h3, gup, act = operands[:3]
    _, _, frame_count, part, _ = out_all.shape
    width, hidden = h3.shape[1], act.shape[1]
    owners = clips * frames
    wide, narrow = hidden // 2, width // 2
    rows_w, rows_d = width // owners, hidden // owners
    peers = max(clips // 2 - 1, 1)
    vmem = pl.BlockSpec(memory_space=VMEM)
    hbm = pl.BlockSpec(memory_space=pl.ANY)

    return pl.pallas_call(
        functools.partial(grad_kernel, clips, frames, clip_count),
        out_shape=(
            jax.ShapeDtypeStruct((clip_count, frame_count, frames * part, width), bf16),
            jax.ShapeDtypeStruct((rows_w, 9 * width), f32),
            jax.ShapeDtypeStruct((16, width), f32),
            jax.ShapeDtypeStruct((rows_w, hidden), f32),
            jax.ShapeDtypeStruct((rows_d, width), f32),
            jax.ShapeDtypeStruct((rows_w, 3 * width), f32),
            jax.ShapeDtypeStruct((rows_w, width), f32),
            jax.ShapeDtypeStruct((rows_w, 3 * width), f32),
            jax.ShapeDtypeStruct((rows_w, width), f32),
        ),
        in_specs=[vmem, vmem] + [hbm] * (1 + len(operands)),
        out_specs=(hbm,) + (vmem,) * 8,
        scratch_shapes=[
            VMEM((6, clips, rows_w * frames, wide), bf16),
            VMEM((2, clips, rows_d * frames, narrow), bf16),
            VMEM((6, clips // 2, rows_w * frames, wide), bf16),
            VMEM((2, clips // 2, rows_d * frames, narrow), bf16),
            VMEM((6, 2, peers, rows_w * frames, wide // 2), bf16),
            VMEM((2, 2, peers, rows_d * frames // 2, narrow), bf16),
            VMEM((6, frames, rows_w, wide), bf16),
            VMEM((2, frames, rows_d, narrow), bf16),
            VMEM((6, frames - 1, rows_w, wide), bf16),
            VMEM((2, frames - 1, rows_d, narrow), bf16),
            VMEM((SLOTS, STEP, width), bf16),
            VMEM((SLOTS, STEP, wide), bf16),
            VMEM((width, wide), f32),
            VMEM((clips,) + small.shape, f32),
            VMEM((frames,) + small.shape, f32),
            VMEM(small.shape, f32),
            DMA((SLOTS,)), DMA((SLOTS,)),
            DMA((8, clips // 2)), DMA((8, clips // 2)),
            DMA((8, 2, peers)), DMA((8, 2, peers)),
            DMA((8, frames - 1)), DMA((8, frames - 1)),
            DMA((frames - 1,)), DMA((frames - 1,)),
            DMA((clips - 1,)), DMA((clips - 1,)),
            DMA((clip_count * frame_count, frames - 1)),
            DMA((clip_count * frame_count, frames - 1)),
            DMA((clip_count,)),
        ],
        compiler_params=pltpu.CompilerParams(
            collective_id=1, has_side_effects=True, vmem_limit_bytes=VMEM_LIMIT
        ),
    )(small, chosen, out_all, *operands)


def normed(values):
    centred = values - jnp.mean(values, axis=-1, keepdims=True)
    scale = lax.rsqrt(jnp.mean(centred * centred, axis=-1, keepdims=True) + 1e-06)
    return centred * scale, scale


def norm_back(grad, scaled, norm, scale):
    inner = grad * scaled
    return scale * (
        inner
        - jnp.mean(inner, axis=-1, keepdims=True)
        - norm * jnp.mean(inner * norm, axis=-1, keepdims=True)
    )


def column_sum(values):
    return jnp.sum(values, axis=0, keepdims=True)


def head_lanes(tokens):
    lane = lax.broadcasted_iota(jnp.int32, (tokens, GROUP * HEAD), 1)
    return [(lane >= HEAD * head) & (lane < HEAD * (head + 1)) for head in range(GROUP)]


def stacked(values, picks):
    return jnp.concatenate([jnp.where(pick, values, bf16(0)) for pick in picks], axis=0)


def unstacked(values, picks, tokens):
    result = values[(GROUP - 1) * tokens :]
    for head in range(GROUP - 1):
        result = jnp.where(picks[head], values[head * tokens : (head + 1) * tokens], result)
    return result


def masked_scores(keys, own, mask):
    scores = dot(keys, own, 1, 1)
    if mask is not None:
        scores = scores + jnp.concatenate([mask[...]] * GROUP, axis=1)
    return scores


def attend(qkv, mixed, totals, width, mask):
    tokens = qkv.shape[0]
    lanes = GROUP * HEAD
    picks = head_lanes(tokens)
    for group in range(HEADS // GROUP):
        at = group * lanes
        own = stacked(qkv[:, at : at + lanes] * bf16(0.125), picks)
        keys = qkv[:, width + at : width + at + lanes]
        values = qkv[:, 2 * width + at : 2 * width + at + lanes]
        scores = masked_scores(keys, own, mask)
        peak = jnp.max(scores, axis=0, keepdims=True)
        terms = jnp.exp(scores - peak)
        total = jnp.sum(terms, axis=0, keepdims=True)
        weights = (terms * (1.0 / total)).astype(bf16)
        logs = peak + jnp.log(total)
        for head in range(GROUP):
            row = group * GROUP + head
            totals[row : row + 1, :] = logs[:, head * tokens : (head + 1) * tokens]
        result = unstacked(dot(weights, values, 0, 0), picks, tokens)
        mixed[:, at : at + lanes] = result.astype(bf16)


def attend_back(qkv, grad_mixed, totals, grad_qkv, width, mask):
    tokens = qkv.shape[0]
    lanes = GROUP * HEAD
    picks = head_lanes(tokens)
    for group in range(HEADS // GROUP):
        at = group * lanes
        own = stacked(qkv[:, at : at + lanes] * bf16(0.125), picks)
        keys = qkv[:, width + at : width + at + lanes]
        values = qkv[:, 2 * width + at : 2 * width + at + lanes]
        own_grads = stacked(grad_mixed[:, at : at + lanes], picks)
        logs = jnp.concatenate(
            [totals[group * GROUP + head : group * GROUP + head + 1, :] for head in range(GROUP)],
            axis=1,
        )
        weights = jnp.exp(masked_scores(keys, own, mask) - logs)
        grad_weights = dot(values, own_grads, 1, 1)
        inner = jnp.sum(weights * grad_weights, axis=0, keepdims=True)
        grad_scores = (weights * (grad_weights - inner)).astype(bf16)
        grad_queries = unstacked(dot(grad_scores, keys, 0, 0), picks, tokens) * 0.125
        grad_keys = dot(grad_scores, own, 1, 0)
        grad_values = dot(weights.astype(bf16), own_grads, 1, 0)
        for part, grad in enumerate((grad_queries, grad_keys, grad_values)):
            start = part * width + at
            grad_qkv[:, start : start + lanes] = grad.astype(bf16)


def full(shape):
    return pl.BlockSpec(shape, lambda *_: (0,) * len(shape), pipeline_mode=pl.Buffered(1))


def middle_kernel(
    clips, frames, tiles,
    after_first, cot_first, after_later, cotangent, loss, mod, w_b, w_u, w_d,
    act_ref, gup_ref, h3_ref, gb3_ref, mixed_ref, gb2_ref, h2_ref, gqkv_ref, sums,
    after_second, cot_second, grad_first, grad_second, grad_later, out_all,
    qkv, totals, mask, gmix, after_tile, cot_tile, grad_stage, out_stage,
    ts, tr, us, ur, gs, gr, hs, hr, ls, ks, ws,
):
    frame = lax.axis_index("frame")
    step = pl.program_id(0)
    last = pl.num_programs(0) - 1
    clip = lax.div(step, tiles)
    tile = lax.rem(step, tiles)
    slot = lax.rem(step, 2)
    width = mod.shape[1]
    frame_count, group = after_tile.shape[2], after_tile.shape[3]
    part = tiles * group
    tokens = frames * frame_count * group
    row = clip * 9
    piece = lambda number: mod[pl.ds(row + number, 1), :]

    def own_part(index):
        return pl.ds(pl.multiple_of(index * part, part), part)

    def later_copies(number):
        copies = []
        for hop in range(frames - 1, 0, -1):
            peer = flip(frame, hop)
            if number:
                source, target, send, recv = cotangent.at[1, :, own_part(peer), :], cot_second, us, ur
            else:
                source, target, send, recv = after_later.at[:, own_part(peer), :], after_second, ts, tr
            copies.append(
                pltpu.make_async_remote_copy(
                    src_ref=source,
                    dst_ref=target.at[frame],
                    send_sem=send.at[hop - 1],
                    recv_sem=recv.at[hop - 1],
                    device_id={"frame": peer},
                    device_id_type=MESH,
                )
            )
        return copies

    def own_copy(number):
        source = cotangent.at[1] if number else after_later
        target = cot_second if number else after_second
        return pltpu.make_async_copy(
            source.at[:, own_part(frame), :], target.at[frame], ks.at[number]
        )

    def load(source, number, index, place):
        rows = pl.ds(pl.multiple_of(index * group, group), group)
        target = (after_tile, cot_tile)[number].at[place]
        return pltpu.make_async_copy(source.at[:, :, rows, :], target, ls.at[place, number])

    early = tiles // 2

    def grad_copies(index, later=False):
        place = index + tiles if later else index
        target, send, recv = (grad_second, hs, hr) if later else (grad_first, gs, gr)
        rows = pl.ds(pl.multiple_of(index * group, group), group)
        copies = []
        for hop in range(frames - 1, 0, -1):
            peer = flip(frame, hop)
            copies.append(
                pltpu.make_async_remote_copy(
                    src_ref=grad_stage.at[place, peer],
                    dst_ref=target.at[frame, :, rows, :],
                    send_sem=send.at[index, hop - 1],
                    recv_sem=recv.at[index, hop - 1],
                    device_id={"frame": peer},
                    device_id_type=MESH,
                )
            )
        return copies

    def grad_own(index, later=False):
        place = index + tiles if later else index
        target = grad_second if later else grad_first
        rows = pl.ds(pl.multiple_of(index * group, group), group)
        return pltpu.make_async_copy(
            grad_stage.at[place, frame], target.at[frame, :, rows, :], ws.at[0, place]
        )

    def grad_keep(index):
        place = index + tiles
        rows = pl.ds(pl.multiple_of((index - early) * group, group), group)
        return pltpu.make_async_copy(
            grad_stage.at[place], grad_later.at[:, :, rows, :], ws.at[0, place]
        )

    def out_keep(number):
        rows = pl.ds(pl.multiple_of(lax.rem(number, tiles) * group, group), group)
        return pltpu.make_async_copy(
            out_stage.at[number], out_all.at[lax.div(number, tiles), :, :, rows, :], ws.at[1, number]
        )

    @pl.when(step == 0)
    def _():
        barrier = pltpu.get_barrier_semaphore()
        for hop in range(1, frames):
            pl.semaphore_signal(
                barrier,
                inc=1,
                device_id={"frame": lax.rem(frame + hop, frames)},
                device_id_type=MESH,
            )
        pl.semaphore_wait(barrier, frames - 1)
        load(after_first, 0, 0, 0).start()
        load(cot_first, 1, 0, 0).start()
        for number in range(2):
            for copy in later_copies(number):
                copy.start()
            own_copy(number).start()
        first = lax.broadcasted_iota(jnp.int32, (tokens, tokens), 0)
        second = lax.broadcasted_iota(jnp.int32, (tokens, tokens), 1)
        mask[...] = jnp.where(lax.rem(first, group) == lax.rem(second, group), 0.0, -1e30)

    @pl.when(step == tiles)
    def _():
        for copy in later_copies(0):
            copy.wait_recv()
        own_copy(0).wait()
        load(after_second, 0, 0, slot).start()

    load(after_first, 0, 0, slot).wait()

    @pl.when(step + 1 < tiles)
    def _():
        load(after_first, 0, step + 1, 1 - slot).start()
        load(cot_first, 1, step + 1, 1 - slot).start()

    @pl.when((step >= tiles) & (step < last))
    def _():
        load(after_second, 0, tile + 1, 1 - slot).start()

    @pl.when((step > tiles) & (step < last))
    def _():
        load(cot_second, 1, tile + 1, 1 - slot).start()

    @pl.when(tile == 0)
    def _():
        sums[...] = jnp.zeros_like(sums)

    def add(place, values):
        sums[place : place + 1, :] += values

    after = after_tile[slot].reshape(tokens, width).astype(f32)
    norm, scale = normed(after)
    hidden = (norm * (1.0 + piece(4)) + piece(3)).astype(bf16)
    h2_ref[...] = hidden
    qkv[...] = dot(hidden, w_b[:, : 3 * width], 1, 0).astype(bf16)
    attend(qkv, mixed_ref, totals, width, mask)
    branch_two = dot(mixed_ref[...], w_b[:, 3 * width :], 1, 0) + mod[19:20, :]
    after_two = after + piece(5) * branch_two
    norm_three, scale_three = normed(after_two)
    hidden = (norm_three * (1.0 + piece(7)) + piece(6)).astype(bf16)
    h3_ref[...] = hidden

    @pl.when(step == tiles)
    def _():
        for copy in later_copies(1):
            copy.wait_recv()
        own_copy(1).wait()
        load(cot_second, 1, 0, slot).start()
        if tiles > 1:
            load(cot_second, 1, 1, 1 - slot).start()

        def send(index, carry):
            for copy in grad_copies(index):
                copy.start()
            return carry

        lax.fori_loop(0, tiles, send, 0)

    load(cot_first, 1, 0, slot).wait()
    grad_out = cot_tile[slot].reshape(tokens, width).astype(f32) * loss[pl.ds(clip, 1), :]
    grad_branch = (grad_out * piece(8)).astype(bf16)
    gb3_ref[...] = grad_branch
    add(11, column_sum(grad_branch.astype(f32)))
    branch_three = jnp.zeros((tokens, width), f32)
    grad_hidden = jnp.zeros((tokens, width), f32)
    for chunk in range(w_u.shape[1] // width):
        cut = slice(chunk * width, (chunk + 1) * width)
        upper = dot(hidden, w_u[:, cut], 1, 0) + mod[20 + chunk : 21 + chunk, :]
        square = upper * upper
        bend = jnp.tanh(upper * (GELU_C + (GELU_C * GELU_A) * square))
        half = 0.5 + 0.5 * bend
        act = (upper * half).astype(bf16)
        slope = half + (0.5 * upper) * (1.0 - bend * bend) * (
            GELU_C + (3.0 * GELU_C * GELU_A) * square
        )
        act_ref[:, cut] = act
        branch_three += dot(act, w_d[cut, :], 1, 0)
        grad_upper = (dot(grad_branch, w_d[cut, :], 1, 1) * slope).astype(bf16)
        gup_ref[:, cut] = grad_upper
        add(7 + chunk, column_sum(grad_upper.astype(f32)))
        grad_hidden += dot(grad_upper, w_u[:, cut], 1, 1)
    branch_three += mod[24:25, :]
    out = (after_two + piece(8) * branch_three).astype(bf16)
    out_stage[step] = out.reshape(out_stage.shape[1:])
    add(5, column_sum(grad_out * branch_three))
    add(3, column_sum(grad_hidden))
    add(4, column_sum(grad_hidden * norm_three))
    grad_two = grad_out + norm_back(grad_hidden, 1.0 + piece(7), norm_three, scale_three)
    add(2, column_sum(grad_two * branch_two))
    grad_branch = (grad_two * piece(5)).astype(bf16)
    gb2_ref[...] = grad_branch
    add(6, column_sum(grad_branch.astype(f32)))
    gmix[...] = dot(grad_branch, w_b[:, 3 * width :], 1, 1).astype(bf16)
    attend_back(qkv, gmix, totals, gqkv_ref, width, mask)
    grad_hidden = dot(gqkv_ref[...], w_b[:, : 3 * width], 1, 1).astype(bf16).astype(f32)
    add(0, column_sum(grad_hidden))
    add(1, column_sum(grad_hidden * norm))
    grad_one = grad_two + norm_back(grad_hidden, 1.0 + piece(4), norm, scale)
    grad_stage[step] = grad_one.astype(bf16).reshape(grad_stage.shape[1:])

    out_keep(step).start()

    @pl.when(step < tiles)
    def _():
        grad_own(tile).start()

    if early:

        @pl.when((step >= tiles) & (tile < early))
        def _():
            for copy in grad_copies(tile, True):
                copy.start()
            grad_own(tile, True).start()

    @pl.when((step >= tiles) & (tile >= early))
    def _():
        grad_keep(tile).start()

    @pl.when(step == last)
    def _():
        for copy in later_copies(0) + later_copies(1):
            copy.wait_send()

        def settle(index, carry):
            for copy in grad_copies(index):
                copy.wait_send()
                copy.wait_recv()
            grad_own(index).wait()
            out_keep(index).wait()
            out_keep(index + tiles).wait()
            return carry

        lax.fori_loop(0, tiles, settle, 0)

        def settle_early(index, carry):
            for copy in grad_copies(index, True):
                copy.wait_send()
                copy.wait_recv()
            grad_own(index, True).wait()
            return carry

        if early:
            lax.fori_loop(0, early, settle_early, 0)

        def settle_kept(index, carry):
            grad_keep(index).wait()
            return carry

        lax.fori_loop(early, tiles, settle_kept, 0)


def middle_call(
    clips, frames, after_first, cot_first, after_later, cotangent, loss, mod, w_b, w_u, w_d
):
    _, frame_count, part, width = after_first.shape
    group = min(16, part)
    tiles = part // group
    tokens = frames * frame_count * group
    hidden_width = w_u.shape[1]
    widths = (hidden_width, hidden_width, width, width, width, width, width, 3 * width)
    own = lambda columns: pl.BlockSpec((tokens, columns), lambda t: (t, 0))
    hbm = pl.BlockSpec(memory_space=pl.ANY)
    rows = 2 * tiles * tokens
    traded = jax.ShapeDtypeStruct(after_first.shape, bf16)
    slab = (frames, frame_count, group, width)
    return pl.pallas_call(
        functools.partial(middle_kernel, clips, frames, tiles),
        grid=(2 * tiles,),
        in_specs=[
            hbm, hbm, hbm, hbm, full(loss.shape), full(mod.shape), full(w_b.shape),
            full(w_u.shape), full(w_d.shape),
        ],
        out_specs=[own(columns) for columns in widths]
        + [pl.BlockSpec((None, 16, width), lambda t: (t // tiles, 0, 0))]
        + [hbm] * 6,
        out_shape=[jax.ShapeDtypeStruct((rows, columns), bf16) for columns in widths]
        + [
            jax.ShapeDtypeStruct((2, 16, width), f32),
            traded, traded, traded, traded,
            jax.ShapeDtypeStruct(
                (frames, frame_count, part - tiles // 2 * group, width), bf16
            ),
            jax.ShapeDtypeStruct((2,) + after_first.shape, bf16),
        ],
        scratch_shapes=[
            VMEM((tokens, 3 * width), bf16),
            VMEM((16, tokens), f32),
            VMEM((tokens, tokens), f32),
            VMEM((tokens, width), bf16),
            VMEM((2,) + slab, bf16),
            VMEM((2,) + slab, bf16),
            VMEM((2 * tiles,) + slab, bf16),
            VMEM((2 * tiles,) + slab, bf16),
            DMA((frames - 1,)), DMA((frames - 1,)),
            DMA((frames - 1,)), DMA((frames - 1,)),
            DMA((tiles, frames - 1)), DMA((tiles, frames - 1)),
            DMA((max(tiles // 2, 1), frames - 1)), DMA((max(tiles // 2, 1), frames - 1)),
            DMA((2, 2)), DMA((2,)), DMA((2, 2 * tiles)),
        ],
        compiler_params=pltpu.CompilerParams(
            collective_id=2, has_side_effects=True, vmem_limit_bytes=VMEM_LIMIT
        ),
    )(after_first, cot_first, after_later, cotangent, loss, mod, w_b, w_u, w_d)


def space_back_kernel(
    clip, grad_refs, x_ref, mod, w_c, qkv, branch, totals,
    out_ref, gb_ref, gqkv_ref, sums, gmix,
):
    width = x_ref.shape[-1]
    tokens = x_ref.shape[-2]
    row = clip * 9
    piece = lambda number: mod[row + number : row + number + 1, :]

    @pl.when(pl.program_id(0) == 0)
    def _():
        sums[...] = jnp.zeros_like(sums)

    joined = [grad_ref[...] for grad_ref in grad_refs]
    joined = joined[0] if len(joined) == 1 else jnp.concatenate(joined, axis=2)
    grad = joined.reshape(tokens, width).astype(f32)
    grad_branch = (grad * piece(2)).astype(bf16)
    gb_ref[...] = grad_branch
    sums[2:3, :] += column_sum(grad * branch[...].astype(f32))
    sums[3:4, :] += column_sum(grad_branch.astype(f32))
    gmix[...] = dot(grad_branch, w_c[:, 3 * width :], 1, 1).astype(bf16)
    attend_back(qkv, gmix, totals, gqkv_ref, width, None)
    grad_hidden = dot(gqkv_ref[...], w_c[:, : 3 * width], 1, 1)
    norm, scale = normed(x_ref[...].reshape(tokens, width).astype(f32))
    sums[0:1, :] += column_sum(grad_hidden)
    sums[1:2, :] += column_sum(grad_hidden * norm)
    result = grad + norm_back(grad_hidden, 1.0 + piece(1), norm, scale)
    out_ref[...] = result.reshape(out_ref.shape)


def space_back_entry(count, parts, clip, *refs):
    base = 6 + parts
    space_back_kernel(clip, refs[:parts], *refs[parts:base], *refs[base + count :])


def space_back_call(clip, grad, x, mod, w_c, qkv, branch, totals, earlier):
    clip_count, frame_count, tokens, width = x.shape
    frames = grad[0].shape[0]
    part = tokens // frames
    rest = [entry.shape[2] for entry in grad[1:]]
    heights = [part - sum(rest)] + rest
    if heights[0] == 0:
        grad, heights = grad[1:], heights[1:]
    rows = frame_count * tokens
    by_frame = lambda columns: pl.BlockSpec(
        (None, tokens, columns), lambda f: (clip * frame_count + f, 0, 0)
    )
    own = lambda columns: pl.BlockSpec((tokens, columns), lambda f: (clip * frame_count + f, 0))
    in_specs = [
        pl.BlockSpec((frames, 1, height, width), lambda f: (0, f, 0, 0)) for height in heights
    ] + [
        pl.BlockSpec((1, 1, tokens, width), lambda f: (clip, f, 0, 0)),
        full(mod.shape),
        full(w_c.shape),
        by_frame(3 * width),
        by_frame(width),
        pl.BlockSpec((None, 16, tokens), lambda f: (clip * frame_count + f, 0, 0)),
    ]
    args = list(grad) + [x, mod, w_c, qkv, branch, totals]
    begin = len(args)
    body = functools.partial(space_back_entry, len(earlier or ()), len(grad), clip)
    aliases = {}
    if earlier is not None:
        in_specs += [pl.BlockSpec(memory_space=pl.ANY)] * len(earlier)
        args += list(earlier)
        aliases = {begin + number: number for number in range(len(earlier))}
    return pl.pallas_call(
        body,
        grid=(frame_count,),
        in_specs=in_specs,
        out_specs=[
            pl.BlockSpec((1, 1, tokens, width), lambda f: (clip, f, 0, 0)),
            own(width),
            own(3 * width),
            pl.BlockSpec((8, width), lambda f: (0, 0)),
        ],
        out_shape=[
            jax.ShapeDtypeStruct(x.shape, f32),
            jax.ShapeDtypeStruct((clip_count * rows, width), bf16),
            jax.ShapeDtypeStruct((clip_count * rows, 3 * width), bf16),
            jax.ShapeDtypeStruct((8, width), f32),
        ],
        scratch_shapes=[VMEM((tokens, width), bf16)],
        input_output_aliases=aliases,
        compiler_params=pltpu.CompilerParams(vmem_limit_bytes=VMEM_LIMIT),
        cost_estimate=pl.CostEstimate(
            flops=rows * 20_000_000, bytes_accessed=rows * width * 20, transcendentals=0
        ),
    )(*args)


def shards(
    inputs, cotangent, time_steps, weight_index, ada_weight, ada_bias, space_qkv, space_out,
    space_out_bias, time_qkv, time_out, time_out_bias, up_weight, up_bias, down_weight, down_bias,
):
    clip_count, frame_count, patch_count, width = inputs.shape
    clips, frames = lax.axis_size("clip"), lax.axis_size("frame")
    owners = clips * frames
    owner = lax.axis_index("clip") * frames + lax.axis_index("frame")
    part = patch_count // frames
    rows = ada_weight.shape[0]

    embed = jax.nn.silu(embed_steps(time_steps, width)).astype(bf16)
    embed = jnp.pad(embed, ((0, 16 - clip_count), (0, 0)))
    place = lax.broadcasted_iota(jnp.int32, (width, 128), 0) - owner * rows
    lane = lax.broadcasted_iota(jnp.int32, (width, 128), 1)
    select = ((place == lane) & (lane < rows)).astype(bf16)
    ada = jnp.pad(ada_weight, ((0, 128 - rows), (0, 0)))

    def spread_bias(vector):
        length = vector.shape[0]
        empty = jnp.zeros((owners * length,), f32)
        return lax.dynamic_update_slice(empty, vector.astype(f32), (owner * length,)).reshape(
            -1, width
        )

    bias = jnp.concatenate(
        [
            spread_bias(vector)
            for vector in (ada_bias, space_out_bias, time_out_bias, up_bias, down_bias)
        ],
        axis=0,
    )
    sh_c = jnp.concatenate([space_qkv, space_out], axis=1)
    sh_b = jnp.concatenate([time_qkv, time_out], axis=1)
    (
        w_c, w_b, w_u, w_d, mod, chosen, totals, hidden_one, qkv_one, mixed_one, branch_one,
        after_first, after_later, cot_first,
    ) = start_call(
        clips, frames, inputs, cotangent, sh_c, sh_b, up_weight, down_weight, embed, select, ada,
        bias,
    )

    def exchange(values):
        return lax.all_to_all(values, "frame", split_axis=0, concat_axis=0, tiled=True)

    loss = jnp.exp2(weight_index.astype(f32) * 0.5 - 1.0)
    loss = jnp.broadcast_to(loss[:, None], (clip_count, width))
    (
        act, gup, h3, gb3, mixed_two, gb2, h2, gqkv_two, mid_sums, _, _, grad_first,
        grad_second, grad_later, out_all,
    ) = middle_call(
        clips, frames, after_first, cot_first, after_later, cotangent, loss, mod, w_b, w_u, w_d
    )
    grads = [(grad_first,), (grad_second, exchange(grad_later))]

    earlier = None
    space_sums = []
    for clip in range(clip_count):
        *earlier, sums = space_back_call(
            clip, grads[clip], inputs, mod, w_c, qkv_one, branch_one, totals, earlier
        )
        space_sums.append(sums)
    input_grad, gb1, gqkv_one = earlier
    pieces = []
    for clip in range(clip_count):
        pieces += [space_sums[clip][0:3], mid_sums[clip][0:6]]
    pieces.append(sum(entry[3:4] for entry in space_sums))
    pieces.append(sum(entry[6:12] for entry in mid_sums))
    small = jnp.concatenate(pieces, axis=0)
    small = jnp.pad(small, ((0, ROWS - small.shape[0]), (0, 0)))
    picked = chosen.reshape(clips, 16, 128)[:, :clip_count].reshape(clips * clip_count, 128)
    outputs, grad_ada, sums, own_u, own_d, own_b, own_bo, own_c, own_co = grad_call(
        clips, frames, clip_count, small, picked.astype(f32).T, out_all, h3, gup, act, gb3, h2, gqkv_two,
        mixed_two, gb2, hidden_one.reshape(-1, width), gqkv_one, mixed_one.reshape(-1, width), gb1,
    )
    biases = sums[9:]

    def own_slice(vector):
        length = vector.shape[0] // owners
        return lax.dynamic_slice_in_dim(vector, owner * length, length, 0)

    return (
        outputs,
        input_grad,
        grad_ada,
        own_slice(sums[:9].reshape(-1)),
        own_c,
        own_co,
        own_slice(biases[0]),
        own_b,
        own_bo,
        own_slice(biases[1]),
        own_u,
        own_slice(biases[2:6].reshape(-1)),
        own_d,
        own_slice(biases[6]),
    )


def solution(mesh):
    tokens = P("clip", "frame", None, None)
    matrix = P(("clip", "frame"), None)
    vector = P(("clip", "frame"))
    in_specs = (
        tokens, tokens, P("clip"), P("clip"), matrix, vector, matrix, matrix, vector, matrix,
        matrix, vector, matrix, vector, matrix, vector,
    )
    out_specs = (
        tokens, tokens, matrix, vector, matrix, matrix, vector, matrix, matrix, vector, matrix,
        vector, matrix, vector,
    )
    return jax.shard_map(shards, mesh=mesh, in_specs=in_specs, out_specs=out_specs, check_vma=False)
```

```python
import functools
import math

import jax
import jax.numpy as jnp
from jax import lax
from jax.experimental import pallas as pl
from jax.experimental.pallas import tpu as pltpu
from jax.sharding import PartitionSpec as P

HEADS = 12
HEAD = 64
GROUP = 4
ROWS = 32
GELU_C = math.sqrt(2.0 / math.pi)
GELU_A = 0.044715
VMEM_LIMIT = 58 << 20

f32 = jnp.float32
bf16 = jnp.bfloat16
highest = lax.Precision.HIGHEST
MESH = pl.DeviceIdType.MESH
VMEM = pltpu.VMEM
DMA = pltpu.SemaphoreType.DMA


def embed_steps(time_steps, model_width):
    half_width = model_width // 2
    frequencies = jnp.exp(
        -math.log(10000.0) * jnp.arange(half_width, dtype=f32) / half_width
    )
    angles = time_steps.astype(f32)[:, None] * frequencies[None, :]
    return jnp.concatenate([jnp.cos(angles), jnp.sin(angles)], axis=1)


def dot(left, right, left_dim, right_dim):
    return lax.dot_general(
        left, right, (((left_dim,), (right_dim,)), ((), ())), preferred_element_type=f32
    )


def flip(index, mask):
    bit = 1
    while bit <= mask:
        if mask & bit:
            index = index + bit * (1 - 2 * ((index // bit) % 2))
        bit *= 2
    return index


def span(masks):
    out = [0]
    for mask in masks:
        out = out + [entry ^ mask for entry in out]
    return out


def frame_masks(frames):
    masks, bit = [], 1
    while bit < frames:
        masks.append(bit)
        bit *= 2
    if len(masks) > 1:
        masks = [frames - 1] + masks[:-1]
    return masks


def clip_tail_masks(clips):
    masks, bit = [], 2
    while bit < clips:
        masks.append(bit)
        bit *= 2
    return masks


def greet(clips, frames):
    clip, frame = lax.axis_index("clip"), lax.axis_index("frame")
    barrier = pltpu.get_barrier_semaphore()
    for step in range(1, clips):
        pl.semaphore_signal(
            barrier, inc=1, device_id={"clip": lax.rem(clip + step, clips)}, device_id_type=MESH
        )
    for step in range(1, frames):
        pl.semaphore_signal(
            barrier, inc=1, device_id={"frame": lax.rem(frame + step, frames)}, device_id_type=MESH
        )
    pl.semaphore_wait(barrier, clips + frames - 2)


def spread(axis, size, source_of, target, send_sems, recv_sems):
    me = lax.axis_index(axis)
    copies = []
    for step in range(1, size):
        peer = lax.rem(me + step, size)
        copy = pltpu.make_async_remote_copy(
            src_ref=source_of(peer),
            dst_ref=target.at[me],
            send_sem=send_sems.at[step - 1],
            recv_sem=recv_sems.at[step - 1],
            device_id={axis: peer},
            device_id_type=MESH,
        )
        copy.start()
        copies.append(copy)
    return copies


def start_kernel(
    clips, frames, clip_count,
    x_ref, cotangent, sq, so, tq, to, sh_u, sh_d, embed, select, ada, bias,
    w_c, w_b, w_u, w_d, mod, chosen, totals, hidden_out, qkv_out, mixed_out, branch_out,
    after_first, after_later, cot_first,
    v_c, z_c, z_b, z_u, z_d, st_w, b_c, b_b, b_u, b_d,
    ada_full, embeds, parts, terms, arrived, held, lined, hidden, qkv, mixed, branch, after,
    zs, zr, cs, cr, xs, xr, ls, es, er, ps, pr, fs, fr, ts, tr, hs, hr, os, ws,
):
    clip, frame = lax.axis_index("clip"), lax.axis_index("frame")
    zoned = (z_c, z_b, z_u, z_d)
    blocks = (b_c, b_b, b_u, b_d)
    wholes = (v_c, w_b, w_u, w_d)
    width = mod.shape[1]
    frame_count, tokens = x_ref.shape[1], x_ref.shape[2]
    part = tokens // frames
    greet(clips, frames)
    masks = frame_masks(frames)
    sends = []
    stage = {}

    def frame_step(group, step):
        number = (1 << step) - 1
        copies = []
        for offset in span(masks[:step]):
            slot = flip(frame, offset)
            copy = pltpu.make_async_remote_copy(
                src_ref=zoned[group].at[slot],
                dst_ref=zoned[group].at[slot],
                send_sem=zs.at[group, number],
                recv_sem=zr.at[group, number],
                device_id={"frame": flip(frame, masks[step])},
                device_id_type=MESH,
            )
            copy.start()
            copies.append(copy)
            number += 1
        sends.extend(copies)
        stage[group] = copies

    def frame_rest(group):
        for step in range(1, len(masks)):
            for copy in stage[group]:
                copy.wait_recv()
            frame_step(group, step)

    tail = clip_tail_masks(clips)
    steps = len(tail)
    orders = (tail, tail[::-1])
    moving = {}

    def block_send(group, half, step, position, offset):
        whole = wholes[group]
        block_rows = whole.shape[0] // clips
        columns = whole.shape[1] // 2
        rows = pl.ds(pl.multiple_of(flip(clip, offset) * block_rows, block_rows), block_rows)
        lanes = pl.ds(half * columns, columns)
        target = whole.at[rows, lanes]
        number = (1 << step) - 1 + position
        copy = pltpu.make_async_remote_copy(
            src_ref=blocks[group].at[:, lanes] if offset == 0 else target,
            dst_ref=target,
            send_sem=xs.at[group, half, number],
            recv_sem=xr.at[group, half, number],
            device_id={"clip": flip(clip, orders[half][step])},
            device_id_type=MESH,
        )
        copy.start()
        moving[group, half, number] = copy

    core_copies = {group: [] for group in range(4)}

    def core_send(group, offset):
        whole = wholes[group]
        block_rows = whole.shape[0] // clips
        rows = pl.ds(pl.multiple_of(flip(clip, offset) * block_rows, block_rows), block_rows)
        number = len(core_copies[group])
        copy = pltpu.make_async_remote_copy(
            src_ref=blocks[group] if offset == 0 else whole.at[rows, :],
            dst_ref=whole.at[rows, :],
            send_sem=cs.at[group, number],
            recv_sem=cr.at[group, number],
            device_id={"clip": flip(clip, 1)},
            device_id_type=MESH,
        )
        copy.start()
        core_copies[group].append(copy)

    local_copies = []

    def block_ready(group):
        for copy in stage[group]:
            copy.wait_recv()
        rows, columns = zoned[group].shape[1:]
        block_rows = frames * rows
        if rows % 16:
            for slot in range(frames):
                st_w[slot * rows : (slot + 1) * rows, :columns] = zoned[group][slot].astype(f32)
            blocks[group][...] = st_w[:block_rows, :columns].astype(bf16)
        else:
            for slot in range(frames):
                blocks[group][slot * rows : (slot + 1) * rows, :] = zoned[group][slot]
        for step in range(steps):
            for half in range(2):
                block_send(group, half, step, 0, 0)
        core_send(group, 0)
        place = pl.ds(pl.multiple_of(clip * block_rows, block_rows), block_rows)
        keep = pltpu.make_async_copy(blocks[group], wholes[group].at[place, :], ls.at[group])
        keep.start()
        local_copies.append(keep)

    def block_forward(group):
        for step in range(1, steps):
            for half in range(2):
                for position in range(1 << (step - 1), 1 << step):
                    moving[group, half, position - 1].wait_recv()
                for later in range(step, steps):
                    for position, offset in enumerate(span(orders[half][:later])):
                        if (1 << (step - 1)) <= position < (1 << step):
                            block_send(group, half, later, position, offset)

    def block_finish(group):
        last = (1 << (steps - 1)) - 1
        for half in range(2):
            for number in range(last, (1 << steps) - 1):
                moving[group, half, number].wait_recv()
        for offset in span(tail)[1:]:
            core_send(group, offset)

    def core_finish(group):
        for copy in core_copies[group]:
            copy.wait_recv()

    for group, first, second in ((0, sq, so), (1, tq, to)):
        zoned[group][frame, :, : 3 * width] = first[...]
        zoned[group][frame, :, 3 * width :] = second[...]
    frame_step(0, 0)
    own = spread("clip", clips, lambda peer: embed, embeds, es, er)
    sends.extend(own)
    embeds[clip] = embed[...]
    z_u[frame] = sh_u[...]
    z_d[frame] = sh_d[...]
    ada_full[...] = jnp.zeros_like(ada_full)
    ada_full[: ada.shape[0], :] = ada[...]
    frame_rest(0)
    for group in range(1, 4):
        frame_step(group, 0)
    cot_copies = []

    def cot_send(index):
        for step in range(frames - 1, 0, -1):
            peer = flip(frame, step)
            copy = pltpu.make_async_remote_copy(
                src_ref=cotangent.at[0, index, pl.ds(pl.multiple_of(peer * part, part), part), :],
                dst_ref=cot_first.at[frame, index],
                send_sem=ts.at[index, step - 1],
                recv_sem=tr.at[index, step - 1],
                device_id={"frame": peer},
                device_id_type=MESH,
            )
            copy.start()
            cot_copies.append(copy)

    cot_send(0)
    for copy in own:
        copy.wait_recv()
    picked = dot(embeds[...].reshape(clips * 16, width), select[...], 1, 0).astype(bf16)
    chosen[...] = picked
    parts[...] = dot(picked, ada_full[...], 1, 0)
    for peer in range(clips):
        for local in range(clip_count):
            row = peer * 16 + local
            for piece in range(9):
                terms[peer, local * 9 + piece : local * 9 + piece + 1, :] = (
                    parts[row : row + 1, piece * width : (piece + 1) * width]
                    + bias[piece : piece + 1, :]
                )
        base = clip_count * 9
        terms[peer, base : base + 7, :] = bias[9:16, :]
        if base + 7 < ROWS:
            terms[peer, base + 7 : ROWS, :] = jnp.zeros((ROWS - base - 7, width), f32)
    own = spread("clip", clips, lambda peer: terms.at[peer], arrived, ps, pr)
    sends.extend(own)
    arrived[clip] = terms[clip]
    block_ready(0)
    for copy in own:
        copy.wait_recv()
    total = arrived[0]
    for peer in range(1, clips):
        total = total + arrived[peer]
    held[...] = total
    own = spread("frame", frames, lambda peer: held, lined, fs, fr)
    sends.extend(own)
    lined[frame] = total
    for group in range(1, 4):
        frame_rest(group)

    for index in range(1, frame_count):
        cot_send(index)
    keep = pltpu.make_async_copy(
        cotangent.at[0, :, pl.ds(pl.multiple_of(frame * part, part), part), :],
        cot_first.at[frame],
        ls.at[4],
    )
    keep.start()
    local_copies.append(keep)

    for copy in own:
        copy.wait_recv()
    total = lined[0]
    for peer in range(1, frames):
        total = total + lined[peer]
    mod[...] = total
    block_forward(0)
    for group in range(1, 4):
        block_ready(group)
    block_finish(0)
    core_finish(0)
    local_copies[0].wait()

    keep = pltpu.make_async_copy(v_c, w_c, ls.at[5])
    keep.start()
    local_copies.append(keep)

    def after_copy(f, step):
        peer = flip(frame, step)
        return pltpu.make_async_remote_copy(
            src_ref=after.at[f, pl.ds(pl.multiple_of(peer * part, part), part), :],
            dst_ref=after_first.at[frame, f],
            send_sem=hs.at[f, step - 1],
            recv_sem=hr.at[f, step - 1],
            device_id={"frame": peer},
            device_id_type=MESH,
        )

    def own_after(f):
        return pltpu.make_async_copy(
            after.at[f, pl.ds(pl.multiple_of(frame * part, part), part), :],
            after_first.at[frame, f],
            os.at[f],
        )

    def later_after(f):
        return pltpu.make_async_copy(after.at[f], after_later.at[f - frame_count], os.at[f])

    kept = ((hidden, hidden_out), (qkv, qkv_out), (mixed, mixed_out), (branch, branch_out))

    def write_back(f):
        return [
            pltpu.make_async_copy(source.at[f], target.at[f], ws.at[number, f])
            for number, (source, target) in enumerate(kept)
        ]

    for local in range(clip_count):
        row = local * 9

        def one_frame(index, carry):
            f = local * frame_count + index
            values = x_ref[local, index].astype(f32)
            norm, _ = normed(values)
            scaled = norm * (1.0 + mod[row + 1 : row + 2, :]) + mod[row : row + 1, :]
            lowered = scaled.astype(bf16)
            hidden[f] = lowered
            qkv[f] = dot(lowered, v_c[:, : 3 * width], 1, 0).astype(bf16)
            attend(qkv.at[f], mixed.at[f], totals.at[f], width, None)
            grown = dot(mixed[f], v_c[:, 3 * width :], 1, 0) + mod[18:19, :]
            branch[f] = grown.astype(bf16)
            after[f] = (values + mod[row + 2 : row + 3, :] * grown).astype(bf16)
            if local == 0:
                for step in range(frames - 1, 0, -1):
                    after_copy(f, step).start()
                own_after(f).start()
            else:
                later_after(f).start()
            for copy in write_back(f):
                copy.start()
            return carry

        lax.fori_loop(0, frame_count, one_frame, 0)
        if local == 0:
            block_forward(1)
    for group in range(2, 4):
        block_forward(group)
    for group in range(1, 4):
        block_finish(group)
    for group in range(1, 4):
        core_finish(group)

    def settle(f, carry):
        for step in range(1, frames):
            copy = after_copy(f, step)
            copy.wait_recv()
            copy.wait_send()
        own_after(f).wait()
        return carry

    lax.fori_loop(0, frame_count, settle, 0)

    def settle_later(f, carry):
        later_after(f).wait()
        return carry

    lax.fori_loop(frame_count, clip_count * frame_count, settle_later, 0)

    def settle_kept(f, carry):
        for copy in write_back(f):
            copy.wait()
        return carry

    lax.fori_loop(0, clip_count * frame_count, settle_kept, 0)
    for copy in cot_copies:
        copy.wait_recv()
        copy.wait_send()
    for copy in local_copies[1:]:
        copy.wait()
    for copy in moving.values():
        copy.wait_send()
    for group in range(4):
        for copy in core_copies[group]:
            copy.wait_send()
    for copy in sends:
        copy.wait_send()


def start_call(
    clips, frames, inputs, cotangent, sq, so, tq, to, sh_u, sh_d, embed, select, ada, bias
):
    clip_count, frame_count, tokens, width = inputs.shape
    rows, columns = sh_u.shape
    rows_d = sh_d.shape[0]
    block = frames * rows
    block_d = frames * rows_d
    peers = max(clips // 2 - 1, 1)
    total = clip_count * frame_count
    part = tokens // frames
    whole = jax.ShapeDtypeStruct((clips * block, columns), bf16)
    vmem = pl.BlockSpec(memory_space=VMEM)
    hbm = pl.BlockSpec(memory_space=pl.ANY)
    zoned = lambda height, lanes: VMEM((frames, height, lanes), bf16)
    saved = lambda lanes: jax.ShapeDtypeStruct((total, tokens, lanes), bf16)
    lent = lambda lanes: VMEM((total, tokens, lanes), bf16)
    traded = jax.ShapeDtypeStruct((frames, frame_count, part, width), bf16)
    return pl.pallas_call(
        functools.partial(start_kernel, clips, frames, clip_count),
        out_shape=(
            whole, whole, whole,
            jax.ShapeDtypeStruct((clips * block_d, width), bf16),
            jax.ShapeDtypeStruct((ROWS, width), f32),
            jax.ShapeDtypeStruct((clips * 16, 128), bf16),
            jax.ShapeDtypeStruct((total, 16, tokens), f32),
            saved(width), saved(3 * width), saved(width), saved(width),
            traded,
            jax.ShapeDtypeStruct(((clip_count - 1) * frame_count, tokens, width), bf16),
            traded,
        ),
        in_specs=[vmem, hbm] + [vmem] * 10,
        out_specs=(hbm, hbm, hbm, hbm, vmem, vmem, vmem) + (hbm,) * 7,
        scratch_shapes=[
            VMEM((clips * block, columns), bf16),
            zoned(rows, columns), zoned(rows, columns), zoned(rows, columns), zoned(rows_d, width),
            VMEM((max(block, block_d), columns), f32),
            VMEM((block, columns), bf16),
            VMEM((block, columns), bf16),
            VMEM((block, columns), bf16),
            VMEM((block_d, width), bf16),
            VMEM((128, 9 * width), bf16),
            VMEM((clips, 16, width), bf16),
            VMEM((clips * 16, 9 * width), f32),
            VMEM((clips, ROWS, width), f32),
            VMEM((clips, ROWS, width), f32),
            VMEM((ROWS, width), f32),
            VMEM((frames, ROWS, width), f32),
            lent(width), lent(3 * width), lent(width), lent(width), lent(width),
            DMA((4, frames - 1)), DMA((4, frames - 1)),
            DMA((4, clips // 2)), DMA((4, clips // 2)),
            DMA((4, 2, peers)), DMA((4, 2, peers)),
            DMA((6,)),
            DMA((clips - 1,)), DMA((clips - 1,)),
            DMA((clips - 1,)), DMA((clips - 1,)),
            DMA((frames - 1,)), DMA((frames - 1,)),
            DMA((frame_count, frames - 1)), DMA((frame_count, frames - 1)),
            DMA((frame_count, frames - 1)), DMA((frame_count, frames - 1)),
            DMA((total,)),
            DMA((4, total)),
        ],
        compiler_params=pltpu.CompilerParams(
            collective_id=0, has_side_effects=True, vmem_limit_bytes=VMEM_LIMIT
        ),
    )(inputs, cotangent, sq, so, tq, to, sh_u, sh_d, embed, select, ada, bias)


STEP = 512
SLOTS = 3


def grad_kernel(
    clips, frames, clip_count,
    small, chosen, out_all, h3, gup, act, gb3, h2, gqkv2, mix2, gb2, h1, gqkv1, mix1, gb1,
    outputs, grad_ada, bias_sums, out_u, out_d, out_b, out_bo, out_c, out_co,
    sum_w, sum_d, sum_s, core_w, core_d, core_s, side_w, side_d, side_s,
    line_w, line_d, line_s, last_w, last_d, last_s,
    left, right, total, gathered, lined, held,
    lsem, rsem, cs, cr, xs, xr, zs, zr, fs, fr, ps, pr, os, orr, ks,
):
    clip, frame = lax.axis_index("clip"), lax.axis_index("frame")
    tokens = h3.shape[0]
    width = small.shape[1]
    wide = sum_w.shape[-1]
    narrow = sum_d.shape[-1]
    tail = clip_tail_masks(clips)
    orders = (tail, tail[::-1])
    masks = frame_masks(frames)
    greet(clips, frames)
    first = spread("frame", frames, lambda peer: small, lined, fs, fr)
    lined[frame] = small[...]
    part = out_all.shape[3]
    frame_count = out_all.shape[2]
    out_copies = []
    mine = pl.ds(pl.multiple_of(frame * part, part), part)

    def send_output(number):
        local, index = divmod(number, frame_count)
        for hop in range(frames - 1, 0, -1):
            peer = flip(frame, hop)
            copy = pltpu.make_async_remote_copy(
                src_ref=out_all.at[local, peer, index],
                dst_ref=outputs.at[local, index, mine, :],
                send_sem=os.at[number, hop - 1],
                recv_sem=orr.at[number, hop - 1],
                device_id={"frame": peer},
                device_id_type=MESH,
            )
            copy.start()
            out_copies.append(copy)

    own_outs = []
    for local in range(clip_count):
        copy = pltpu.make_async_copy(
            out_all.at[local, frame], outputs.at[local, :, mine, :], ks.at[local]
        )
        copy.start()
        own_outs.append(copy)

    chunks = [
        (1, 0, [(act, gb3, 0, 0, narrow)], out_d, 0),
        (1, 1, [(act, gb3, narrow, 0, narrow)], out_d, narrow),
        (0, 0, [(h3, gup, 0, 0, wide)], out_u, 0),
        (0, 1, [(h3, gup, wide, 0, wide)], out_u, wide),
        (0, 2, [(h2, gqkv2, 0, 0, wide)], out_b, 0),
        (0, 3, [(h2, gqkv2, wide, 0, width), (mix2, gb2, 0, width, width)], out_b, wide),
        (0, 4, [(h1, gqkv1, 0, 0, wide)], out_c, 0),
        (2, 0, [(h1, gqkv1, wide, 0, width)], out_c, wide),
        (2, 1, [(mix1, gb1, 0, 0, width)], out_co, 0),
    ]
    sums, cores = (sum_w, sum_d, sum_s), (core_w, core_d, core_s)
    sides = (side_w, side_d, side_s)
    lines, lasts = (line_w, line_d, line_s), (last_w, last_d, last_s)
    flights = {}

    steps = tokens // STEP
    line_up = []
    for kind, _, parts, _, _ in chunks:
        for part in parts:
            for group in range(part[0].shape[1] // width):
                line_up.append(part[:3] + (part[3] + group * part[4], part[4], group))
    begins = [0]
    for kind, _, parts, _, _ in chunks:
        begins.append(begins[-1] + sum(part[0].shape[1] // width for part in parts))

    def load(entry, step, slot):
        one, other, begin, _, lanes, group = line_up[entry]
        rows = pl.ds(pl.multiple_of(step * STEP, STEP), STEP)
        return (
            pltpu.make_async_copy(
                one.at[rows, pl.ds(group * width, width)], left.at[slot], lsem.at[slot]
            ),
            pltpu.make_async_copy(
                other.at[rows, pl.ds(begin, lanes)],
                right.at[slot, :, pl.ds(0, lanes)],
                rsem.at[slot],
            ),
        )

    def place_of(entry, step):
        return lax.rem(entry * steps + step, SLOTS)

    def multiply(number):
        kind, place = chunks[number][:2]
        for entry in range(begins[number], begins[number + 1]):
            at, lanes = line_up[entry][3:5]

            def body(step, carry):
                ahead = step + SLOTS - 1

                @pl.when(ahead < steps)
                def _():
                    for copy in load(entry, ahead, place_of(entry, ahead)):
                        copy.start()

                if entry + 1 < len(line_up):

                    @pl.when(ahead >= steps)
                    def _():
                        for copy in load(entry + 1, ahead - steps, place_of(entry, ahead)):
                            copy.start()

                slot = place_of(entry, step)
                for copy in load(entry, step, slot):
                    copy.wait()
                columns = slice(at, at + lanes)
                before = jnp.where(step > 0, total[:, columns], 0.0)
                total[:, columns] = before + dot(left[slot], right[slot, :, :lanes], 0, 0)
                return carry

            lax.fori_loop(0, steps, body, 0)
        rows, lanes = sums[kind].shape[2:]
        for block in range(clips):
            begin = block * rows
            column = begin // width * lanes
            begin = begin % width
            sums[kind][place, block] = total[begin : begin + rows, column : column + lanes].astype(
                bf16
            )

    def core_start(number):
        kind, place = chunks[number][:2]
        copies = []
        for position, offset in enumerate(span(tail)):
            copy = pltpu.make_async_remote_copy(
                src_ref=sums[kind].at[place, flip(clip, offset ^ 1)],
                dst_ref=cores[kind].at[place, position],
                send_sem=cs.at[number, position],
                recv_sem=cr.at[number, position],
                device_id={"clip": flip(clip, 1)},
                device_id_type=MESH,
            )
            copy.start()
            copies.append(copy)
        flights[number, "core"] = copies

    def half_of(kind, half):
        if kind == 1:
            rows = sums[kind].shape[2] // 2
            return (slice(half * rows, (half + 1) * rows), slice(None))
        lanes = sums[kind].shape[3] // 2
        return (slice(None), slice(half * lanes, (half + 1) * lanes))

    def side_start(number, step):
        kind, place = chunks[number][:2]
        copies = []
        for half in range(2):
            mask = orders[half][step]
            for position, offset in enumerate(span(orders[half][:step])):
                entry = (1 << step) - 1 + position
                copy = pltpu.make_async_remote_copy(
                    src_ref=sums[kind].at[(place, flip(clip, offset ^ mask)) + half_of(kind, half)],
                    dst_ref=sides[kind].at[place, half, entry],
                    send_sem=xs.at[number, half, entry],
                    recv_sem=xr.at[number, half, entry],
                    device_id={"clip": flip(clip, mask)},
                    device_id_type=MESH,
                )
                copy.start()
                copies.append(copy)
        flights[number, "side", step] = copies

    def core_add(number):
        kind, place = chunks[number][:2]
        for copy in flights[number, "core"]:
            copy.wait_recv()
        for position, offset in enumerate(span(tail)):
            block = flip(clip, offset)
            sums[kind][place, block] = (
                sums[kind][place, block].astype(f32) + cores[kind][place, position].astype(f32)
            ).astype(bf16)
        side_start(number, len(tail) - 1)

    def side_add(number, step):
        kind, place = chunks[number][:2]
        for copy in flights[number, "side", step]:
            copy.wait_recv()
        for half in range(2):
            for position, offset in enumerate(span(orders[half][:step])):
                entry = (1 << step) - 1 + position
                block = flip(clip, offset)
                where = (place, block) + half_of(kind, half)
                sums[kind][where] = (
                    sums[kind][where].astype(f32) + sides[kind][place, half, entry].astype(f32)
                ).astype(bf16)
        if step:
            side_start(number, step - 1)
        else:
            rows = lines[kind].shape[2]
            block = sums[kind][place, clip].astype(f32)
            for slot in range(frames):
                lines[kind][place, slot] = block[slot * rows : (slot + 1) * rows, :].astype(bf16)
            line_start(number, len(masks) - 1)

    def line_start(number, step):
        kind, place = chunks[number][:2]
        copies = []
        for position, offset in enumerate(span(masks[:step])):
            entry = (1 << step) - 1 + position
            copy = pltpu.make_async_remote_copy(
                src_ref=lines[kind].at[place, flip(frame, offset ^ masks[step])],
                dst_ref=lasts[kind].at[place, entry],
                send_sem=zs.at[number, entry],
                recv_sem=zr.at[number, entry],
                device_id={"frame": flip(frame, masks[step])},
                device_id_type=MESH,
            )
            copy.start()
            copies.append(copy)
        flights[number, "line", step] = copies

    def line_add(number, step):
        kind, place, _, target, begin = chunks[number]
        for copy in flights[number, "line", step]:
            copy.wait_recv()
        for position, offset in enumerate(span(masks[:step])):
            entry = (1 << step) - 1 + position
            slot = flip(frame, offset)
            value = lines[kind][place, slot].astype(f32) + lasts[kind][place, entry].astype(f32)
            if step:
                lines[kind][place, slot] = value.astype(bf16)
            elif begin + value.shape[1] > target.shape[1]:
                cut = target.shape[1] - begin
                target[:, begin:] = value[:, :cut]
                out_bo[...] = value[:, cut:]
            else:
                target[:, begin : begin + value.shape[1]] = value
        if step:
            line_start(number, step - 1)

    stages = [core_start, core_add]
    for step in range(len(tail))[::-1]:
        stages.append(functools.partial(side_add, step=step))
    for step in range(len(masks))[::-1]:
        stages.append(functools.partial(line_add, step=step))

    def finish_small():
        for copy in second:
            copy.wait_recv()
        rows = grad_ada.shape[0]
        for number in range(9):
            terms = [
                gathered[peer, local * 9 + number : local * 9 + number + 1, :]
                for peer in range(clips)
                for local in range(clip_count)
            ]
            terms = jnp.concatenate(terms, axis=0)
            grad_ada[:, number * width : (number + 1) * width] = lax.dot_general(
                chosen[...], terms, (((1,), (0,)), ((), ())), precision=highest,
                preferred_element_type=f32,
            )[:rows, :]
            bias_sums[number : number + 1, :] = column_sum(terms)
        base = clip_count * 9
        summed = gathered[0, base : base + 7, :]
        for peer in range(1, clips):
            summed = summed + gathered[peer, base : base + 7, :]
        bias_sums[9:16, :] = summed

    for step in range(SLOTS - 1):
        for copy in load(0, step, step):
            copy.start()
    second = None
    lags = [0, 1, 3]
    while len(lags) < len(stages):
        lags.append(lags[-1] + 1)
    for turn in range(len(chunks) + lags[-1]):
        for depth in range(len(stages))[::-1]:
            if depth > 0 and 0 <= turn - lags[depth] < len(chunks):
                stages[depth](turn - lags[depth])
        if turn < clip_count * frame_count:
            send_output(turn)
        if turn < len(chunks):
            multiply(turn)
            core_start(turn)
        if turn == len(chunks):
            finish_small()
        if turn == 0:
            for copy in first:
                copy.wait_recv()
            summed = lined[0]
            for peer in range(1, frames):
                summed = summed + lined[peer]
            held[...] = summed
            second = spread("clip", clips, lambda peer: held, gathered, ps, pr)
            gathered[clip] = summed
    for copy in own_outs:
        copy.wait()
    for copy in out_copies:
        copy.wait_recv()
        copy.wait_send()
    for copy in first + second:
        copy.wait_send()
    for copies in flights.values():
        for copy in copies:
            copy.wait_send()


def grad_call(clips, frames, clip_count, small, chosen, out_all, *operands):
    h3, gup, act = operands[:3]
    _, _, frame_count, part, _ = out_all.shape
    width, hidden = h3.shape[1], act.shape[1]
    owners = clips * frames
    wide, narrow = hidden // 2, width // 2
    rows_w, rows_d = width // owners, hidden // owners
    peers = max(clips // 2 - 1, 1)
    vmem = pl.BlockSpec(memory_space=VMEM)
    hbm = pl.BlockSpec(memory_space=pl.ANY)

    return pl.pallas_call(
        functools.partial(grad_kernel, clips, frames, clip_count),
        out_shape=(
            jax.ShapeDtypeStruct((clip_count, frame_count, frames * part, width), bf16),
            jax.ShapeDtypeStruct((rows_w, 9 * width), f32),
            jax.ShapeDtypeStruct((16, width), f32),
            jax.ShapeDtypeStruct((rows_w, hidden), f32),
            jax.ShapeDtypeStruct((rows_d, width), f32),
            jax.ShapeDtypeStruct((rows_w, 3 * width), f32),
            jax.ShapeDtypeStruct((rows_w, width), f32),
            jax.ShapeDtypeStruct((rows_w, 3 * width), f32),
            jax.ShapeDtypeStruct((rows_w, width), f32),
        ),
        in_specs=[vmem, vmem] + [hbm] * (1 + len(operands)),
        out_specs=(hbm,) + (vmem,) * 8,
        scratch_shapes=[
            VMEM((5, clips, rows_w * frames, wide), bf16),
            VMEM((2, clips, rows_d * frames, narrow), bf16),
            VMEM((2, clips, rows_w * frames, width), bf16),
            VMEM((5, clips // 2, rows_w * frames, wide), bf16),
            VMEM((2, clips // 2, rows_d * frames, narrow), bf16),
            VMEM((2, clips // 2, rows_w * frames, width), bf16),
            VMEM((5, 2, peers, rows_w * frames, wide // 2), bf16),
            VMEM((2, 2, peers, rows_d * frames // 2, narrow), bf16),
            VMEM((2, 2, peers, rows_w * frames, width // 2), bf16),
            VMEM((5, frames, rows_w, wide), bf16),
            VMEM((2, frames, rows_d, narrow), bf16),
            VMEM((2, frames, rows_w, width), bf16),
            VMEM((5, frames - 1, rows_w, wide), bf16),
            VMEM((2, frames - 1, rows_d, narrow), bf16),
            VMEM((2, frames - 1, rows_w, width), bf16),
            VMEM((SLOTS, STEP, width), bf16),
            VMEM((SLOTS, STEP, wide), bf16),
            VMEM((width, wide), f32),
            VMEM((clips,) + small.shape, f32),
            VMEM((frames,) + small.shape, f32),
            VMEM(small.shape, f32),
            DMA((SLOTS,)), DMA((SLOTS,)),
            DMA((9, clips // 2)), DMA((9, clips // 2)),
            DMA((9, 2, peers)), DMA((9, 2, peers)),
            DMA((9, frames - 1)), DMA((9, frames - 1)),
            DMA((frames - 1,)), DMA((frames - 1,)),
            DMA((clips - 1,)), DMA((clips - 1,)),
            DMA((clip_count * frame_count, frames - 1)),
            DMA((clip_count * frame_count, frames - 1)),
            DMA((clip_count,)),
        ],
        compiler_params=pltpu.CompilerParams(
            collective_id=1, has_side_effects=True, vmem_limit_bytes=VMEM_LIMIT
        ),
    )(small, chosen, out_all, *operands)


def normed(values):
    centred = values - jnp.mean(values, axis=-1, keepdims=True)
    scale = lax.rsqrt(jnp.mean(centred * centred, axis=-1, keepdims=True) + 1e-06)
    return centred * scale, scale


def norm_back(grad, scaled, norm, scale):
    inner = grad * scaled
    return scale * (
        inner
        - jnp.mean(inner, axis=-1, keepdims=True)
        - norm * jnp.mean(inner * norm, axis=-1, keepdims=True)
    )


def column_sum(values):
    return jnp.sum(values, axis=0, keepdims=True)


def head_lanes(tokens):
    lane = lax.broadcasted_iota(jnp.int32, (tokens, GROUP * HEAD), 1)
    return [(lane >= HEAD * head) & (lane < HEAD * (head + 1)) for head in range(GROUP)]


def stacked(values, picks):
    return jnp.concatenate([jnp.where(pick, values, bf16(0)) for pick in picks], axis=0)


def unstacked(values, picks, tokens):
    result = values[(GROUP - 1) * tokens :]
    for head in range(GROUP - 1):
        result = jnp.where(picks[head], values[head * tokens : (head + 1) * tokens], result)
    return result


def masked_scores(keys, own, mask):
    scores = dot(keys, own, 1, 1)
    if mask is not None:
        scores = scores + jnp.concatenate([mask[...]] * GROUP, axis=1)
    return scores


def attend(qkv, mixed, totals, width, mask):
    tokens = qkv.shape[0]
    lanes = GROUP * HEAD
    picks = head_lanes(tokens)
    for group in range(HEADS // GROUP):
        at = group * lanes
        own = stacked(qkv[:, at : at + lanes] * bf16(0.125), picks)
        keys = qkv[:, width + at : width + at + lanes]
        values = qkv[:, 2 * width + at : 2 * width + at + lanes]
        scores = masked_scores(keys, own, mask)
        peak = jnp.max(scores, axis=0, keepdims=True)
        terms = jnp.exp(scores - peak)
        total = jnp.sum(terms, axis=0, keepdims=True)
        weights = (terms * (1.0 / total)).astype(bf16)
        logs = peak + jnp.log(total)
        for head in range(GROUP):
            row = group * GROUP + head
            totals[row : row + 1, :] = logs[:, head * tokens : (head + 1) * tokens]
        result = unstacked(dot(weights, values, 0, 0), picks, tokens)
        mixed[:, at : at + lanes] = result.astype(bf16)


def attend_back(qkv, grad_mixed, totals, grad_qkv, width, mask):
    tokens = qkv.shape[0]
    lanes = GROUP * HEAD
    picks = head_lanes(tokens)
    for group in range(HEADS // GROUP):
        at = group * lanes
        own = stacked(qkv[:, at : at + lanes] * bf16(0.125), picks)
        keys = qkv[:, width + at : width + at + lanes]
        values = qkv[:, 2 * width + at : 2 * width + at + lanes]
        own_grads = stacked(grad_mixed[:, at : at + lanes], picks)
        logs = jnp.concatenate(
            [totals[group * GROUP + head : group * GROUP + head + 1, :] for head in range(GROUP)],
            axis=1,
        )
        weights = jnp.exp(masked_scores(keys, own, mask) - logs)
        grad_weights = dot(values, own_grads, 1, 1)
        inner = jnp.sum(weights * grad_weights, axis=0, keepdims=True)
        grad_scores = (weights * (grad_weights - inner)).astype(bf16)
        grad_queries = unstacked(dot(grad_scores, keys, 0, 0), picks, tokens) * 0.125
        grad_keys = dot(grad_scores, own, 1, 0)
        grad_values = dot(weights.astype(bf16), own_grads, 1, 0)
        for part, grad in enumerate((grad_queries, grad_keys, grad_values)):
            start = part * width + at
            grad_qkv[:, start : start + lanes] = grad.astype(bf16)


def full(shape):
    return pl.BlockSpec(shape, lambda *_: (0,) * len(shape), pipeline_mode=pl.Buffered(1))


def middle_kernel(
    clips, frames, tiles,
    after_first, cot_first, after_later, cotangent, loss, mod, w_b, w_u, w_d,
    act_ref, gup_ref, h3_ref, gb3_ref, mixed_ref, gb2_ref, h2_ref, gqkv_ref, sums,
    after_second, cot_second, grad_first, grad_second, grad_later, out_all,
    qkv, totals, mask, gmix, after_tile, cot_tile, grad_stage, out_stage,
    ts, tr, us, ur, gs, gr, hs, hr, ls, ks, ws,
):
    frame = lax.axis_index("frame")
    step = pl.program_id(0)
    last = pl.num_programs(0) - 1
    clip = lax.div(step, tiles)
    tile = lax.rem(step, tiles)
    slot = lax.rem(step, 2)
    width = mod.shape[1]
    frame_count, group = after_tile.shape[2], after_tile.shape[3]
    part = tiles * group
    tokens = frames * frame_count * group
    row = clip * 9
    piece = lambda number: mod[pl.ds(row + number, 1), :]

    def own_part(index):
        return pl.ds(pl.multiple_of(index * part, part), part)

    def later_copies(number):
        copies = []
        for hop in range(frames - 1, 0, -1):
            peer = flip(frame, hop)
            if number:
                source, target, send, recv = cotangent.at[1, :, own_part(peer), :], cot_second, us, ur
            else:
                source, target, send, recv = after_later.at[:, own_part(peer), :], after_second, ts, tr
            copies.append(
                pltpu.make_async_remote_copy(
                    src_ref=source,
                    dst_ref=target.at[frame],
                    send_sem=send.at[hop - 1],
                    recv_sem=recv.at[hop - 1],
                    device_id={"frame": peer},
                    device_id_type=MESH,
                )
            )
        return copies

    def own_copy(number):
        source = cotangent.at[1] if number else after_later
        target = cot_second if number else after_second
        return pltpu.make_async_copy(
            source.at[:, own_part(frame), :], target.at[frame], ks.at[number]
        )

    def load(source, number, index, place):
        rows = pl.ds(pl.multiple_of(index * group, group), group)
        target = (after_tile, cot_tile)[number].at[place]
        return pltpu.make_async_copy(source.at[:, :, rows, :], target, ls.at[place, number])

    early = tiles // 2

    def grad_copies(index, later=False):
        place = index + tiles if later else index
        target, send, recv = (grad_second, hs, hr) if later else (grad_first, gs, gr)
        rows = pl.ds(pl.multiple_of(index * group, group), group)
        copies = []
        for hop in range(frames - 1, 0, -1):
            peer = flip(frame, hop)
            copies.append(
                pltpu.make_async_remote_copy(
                    src_ref=grad_stage.at[place, peer],
                    dst_ref=target.at[frame, :, rows, :],
                    send_sem=send.at[index, hop - 1],
                    recv_sem=recv.at[index, hop - 1],
                    device_id={"frame": peer},
                    device_id_type=MESH,
                )
            )
        return copies

    def grad_own(index, later=False):
        place = index + tiles if later else index
        target = grad_second if later else grad_first
        rows = pl.ds(pl.multiple_of(index * group, group), group)
        return pltpu.make_async_copy(
            grad_stage.at[place, frame], target.at[frame, :, rows, :], ws.at[0, place]
        )

    def grad_keep(index):
        place = index + tiles
        rows = pl.ds(pl.multiple_of((index - early) * group, group), group)
        return pltpu.make_async_copy(
            grad_stage.at[place], grad_later.at[:, :, rows, :], ws.at[0, place]
        )

    def out_keep(number):
        rows = pl.ds(pl.multiple_of(lax.rem(number, tiles) * group, group), group)
        return pltpu.make_async_copy(
            out_stage.at[number], out_all.at[lax.div(number, tiles), :, :, rows, :], ws.at[1, number]
        )

    @pl.when(step == 0)
    def _():
        barrier = pltpu.get_barrier_semaphore()
        for hop in range(1, frames):
            pl.semaphore_signal(
                barrier,
                inc=1,
                device_id={"frame": lax.rem(frame + hop, frames)},
                device_id_type=MESH,
            )
        pl.semaphore_wait(barrier, frames - 1)
        load(after_first, 0, 0, 0).start()
        load(cot_first, 1, 0, 0).start()
        for number in range(2):
            for copy in later_copies(number):
                copy.start()
            own_copy(number).start()
        first = lax.broadcasted_iota(jnp.int32, (tokens, tokens), 0)
        second = lax.broadcasted_iota(jnp.int32, (tokens, tokens), 1)
        mask[...] = jnp.where(lax.rem(first, group) == lax.rem(second, group), 0.0, -1e30)

    @pl.when(step == tiles)
    def _():
        for copy in later_copies(0):
            copy.wait_recv()
        own_copy(0).wait()
        load(after_second, 0, 0, slot).start()

    load(after_first, 0, 0, slot).wait()

    @pl.when(step + 1 < tiles)
    def _():
        load(after_first, 0, step + 1, 1 - slot).start()
        load(cot_first, 1, step + 1, 1 - slot).start()

    @pl.when((step >= tiles) & (step < last))
    def _():
        load(after_second, 0, tile + 1, 1 - slot).start()

    @pl.when((step > tiles) & (step < last))
    def _():
        load(cot_second, 1, tile + 1, 1 - slot).start()

    @pl.when(tile == 0)
    def _():
        sums[...] = jnp.zeros_like(sums)

    def add(place, values):
        sums[place : place + 1, :] += values

    after = after_tile[slot].reshape(tokens, width).astype(f32)
    norm, scale = normed(after)
    hidden = (norm * (1.0 + piece(4)) + piece(3)).astype(bf16)
    h2_ref[...] = hidden
    qkv[...] = dot(hidden, w_b[:, : 3 * width], 1, 0).astype(bf16)
    attend(qkv, mixed_ref, totals, width, mask)
    branch_two = dot(mixed_ref[...], w_b[:, 3 * width :], 1, 0) + mod[19:20, :]
    after_two = after + piece(5) * branch_two
    norm_three, scale_three = normed(after_two)
    hidden = (norm_three * (1.0 + piece(7)) + piece(6)).astype(bf16)
    h3_ref[...] = hidden

    @pl.when(step == tiles)
    def _():
        for copy in later_copies(1):
            copy.wait_recv()
        own_copy(1).wait()
        load(cot_second, 1, 0, slot).start()
        if tiles > 1:
            load(cot_second, 1, 1, 1 - slot).start()

        def send(index, carry):
            for copy in grad_copies(index):
                copy.start()
            return carry

        lax.fori_loop(0, tiles, send, 0)

    load(cot_first, 1, 0, slot).wait()
    grad_out = cot_tile[slot].reshape(tokens, width).astype(f32) * loss[pl.ds(clip, 1), :]
    grad_branch = (grad_out * piece(8)).astype(bf16)
    gb3_ref[...] = grad_branch
    add(11, column_sum(grad_branch.astype(f32)))
    branch_three = jnp.zeros((tokens, width), f32)
    grad_hidden = jnp.zeros((tokens, width), f32)
    for chunk in range(w_u.shape[1] // width):
        cut = slice(chunk * width, (chunk + 1) * width)
        upper = dot(hidden, w_u[:, cut], 1, 0) + mod[20 + chunk : 21 + chunk, :]
        square = upper * upper
        bend = jnp.tanh(upper * (GELU_C + (GELU_C * GELU_A) * square))
        half = 0.5 + 0.5 * bend
        act = (upper * half).astype(bf16)
        slope = half + (0.5 * upper) * (1.0 - bend * bend) * (
            GELU_C + (3.0 * GELU_C * GELU_A) * square
        )
        act_ref[:, cut] = act
        branch_three += dot(act, w_d[cut, :], 1, 0)
        grad_upper = (dot(grad_branch, w_d[cut, :], 1, 1) * slope).astype(bf16)
        gup_ref[:, cut] = grad_upper
        add(7 + chunk, column_sum(grad_upper.astype(f32)))
        grad_hidden += dot(grad_upper, w_u[:, cut], 1, 1)
    branch_three += mod[24:25, :]
    out = (after_two + piece(8) * branch_three).astype(bf16)
    out_stage[step] = out.reshape(out_stage.shape[1:])
    add(5, column_sum(grad_out * branch_three))
    add(3, column_sum(grad_hidden))
    add(4, column_sum(grad_hidden * norm_three))
    grad_two = grad_out + norm_back(grad_hidden, 1.0 + piece(7), norm_three, scale_three)
    add(2, column_sum(grad_two * branch_two))
    grad_branch = (grad_two * piece(5)).astype(bf16)
    gb2_ref[...] = grad_branch
    add(6, column_sum(grad_branch.astype(f32)))
    gmix[...] = dot(grad_branch, w_b[:, 3 * width :], 1, 1).astype(bf16)
    attend_back(qkv, gmix, totals, gqkv_ref, width, mask)
    grad_hidden = dot(gqkv_ref[...], w_b[:, : 3 * width], 1, 1).astype(bf16).astype(f32)
    add(0, column_sum(grad_hidden))
    add(1, column_sum(grad_hidden * norm))
    grad_one = grad_two + norm_back(grad_hidden, 1.0 + piece(4), norm, scale)
    grad_stage[step] = grad_one.astype(bf16).reshape(grad_stage.shape[1:])

    out_keep(step).start()

    @pl.when(step < tiles)
    def _():
        grad_own(tile).start()

    if early:

        @pl.when((step >= tiles) & (tile < early))
        def _():
            for copy in grad_copies(tile, True):
                copy.start()
            grad_own(tile, True).start()

    @pl.when((step >= tiles) & (tile >= early))
    def _():
        grad_keep(tile).start()

    @pl.when(step == last)
    def _():
        for copy in later_copies(0) + later_copies(1):
            copy.wait_send()

        def settle(index, carry):
            for copy in grad_copies(index):
                copy.wait_send()
                copy.wait_recv()
            grad_own(index).wait()
            out_keep(index).wait()
            out_keep(index + tiles).wait()
            return carry

        lax.fori_loop(0, tiles, settle, 0)

        def settle_early(index, carry):
            for copy in grad_copies(index, True):
                copy.wait_send()
                copy.wait_recv()
            grad_own(index, True).wait()
            return carry

        if early:
            lax.fori_loop(0, early, settle_early, 0)

        def settle_kept(index, carry):
            grad_keep(index).wait()
            return carry

        lax.fori_loop(early, tiles, settle_kept, 0)


def middle_call(
    clips, frames, after_first, cot_first, after_later, cotangent, loss, mod, w_b, w_u, w_d
):
    _, frame_count, part, width = after_first.shape
    group = min(16, part)
    tiles = part // group
    tokens = frames * frame_count * group
    hidden_width = w_u.shape[1]
    widths = (hidden_width, hidden_width, width, width, width, width, width, 3 * width)
    own = lambda columns: pl.BlockSpec((tokens, columns), lambda t: (t, 0))
    hbm = pl.BlockSpec(memory_space=pl.ANY)
    rows = 2 * tiles * tokens
    traded = jax.ShapeDtypeStruct(after_first.shape, bf16)
    slab = (frames, frame_count, group, width)
    return pl.pallas_call(
        functools.partial(middle_kernel, clips, frames, tiles),
        grid=(2 * tiles,),
        in_specs=[
            hbm, hbm, hbm, hbm, full(loss.shape), full(mod.shape), full(w_b.shape),
            full(w_u.shape), full(w_d.shape),
        ],
        out_specs=[own(columns) for columns in widths]
        + [pl.BlockSpec((None, 16, width), lambda t: (t // tiles, 0, 0))]
        + [hbm] * 6,
        out_shape=[jax.ShapeDtypeStruct((rows, columns), bf16) for columns in widths]
        + [
            jax.ShapeDtypeStruct((2, 16, width), f32),
            traded, traded, traded, traded,
            jax.ShapeDtypeStruct(
                (frames, frame_count, part - tiles // 2 * group, width), bf16
            ),
            jax.ShapeDtypeStruct((2,) + after_first.shape, bf16),
        ],
        scratch_shapes=[
            VMEM((tokens, 3 * width), bf16),
            VMEM((16, tokens), f32),
            VMEM((tokens, tokens), f32),
            VMEM((tokens, width), bf16),
            VMEM((2,) + slab, bf16),
            VMEM((2,) + slab, bf16),
            VMEM((2 * tiles,) + slab, bf16),
            VMEM((2 * tiles,) + slab, bf16),
            DMA((frames - 1,)), DMA((frames - 1,)),
            DMA((frames - 1,)), DMA((frames - 1,)),
            DMA((tiles, frames - 1)), DMA((tiles, frames - 1)),
            DMA((max(tiles // 2, 1), frames - 1)), DMA((max(tiles // 2, 1), frames - 1)),
            DMA((2, 2)), DMA((2,)), DMA((2, 2 * tiles)),
        ],
        compiler_params=pltpu.CompilerParams(
            collective_id=2, has_side_effects=True, vmem_limit_bytes=VMEM_LIMIT
        ),
    )(after_first, cot_first, after_later, cotangent, loss, mod, w_b, w_u, w_d)


def space_back_kernel(
    clip, grad_refs, x_ref, mod, w_c, qkv, branch, totals,
    out_ref, gb_ref, gqkv_ref, sums, gmix,
):
    width = x_ref.shape[-1]
    tokens = x_ref.shape[-2]
    row = clip * 9
    piece = lambda number: mod[row + number : row + number + 1, :]

    @pl.when(pl.program_id(0) == 0)
    def _():
        sums[...] = jnp.zeros_like(sums)

    joined = [grad_ref[...] for grad_ref in grad_refs]
    joined = joined[0] if len(joined) == 1 else jnp.concatenate(joined, axis=2)
    grad = joined.reshape(tokens, width).astype(f32)
    grad_branch = (grad * piece(2)).astype(bf16)
    gb_ref[...] = grad_branch
    sums[2:3, :] += column_sum(grad * branch[...].astype(f32))
    sums[3:4, :] += column_sum(grad_branch.astype(f32))
    gmix[...] = dot(grad_branch, w_c[:, 3 * width :], 1, 1).astype(bf16)
    attend_back(qkv, gmix, totals, gqkv_ref, width, None)
    grad_hidden = dot(gqkv_ref[...], w_c[:, : 3 * width], 1, 1)
    norm, scale = normed(x_ref[...].reshape(tokens, width).astype(f32))
    sums[0:1, :] += column_sum(grad_hidden)
    sums[1:2, :] += column_sum(grad_hidden * norm)
    result = grad + norm_back(grad_hidden, 1.0 + piece(1), norm, scale)
    out_ref[...] = result.reshape(out_ref.shape)


def space_back_entry(count, parts, clip, *refs):
    base = 6 + parts
    space_back_kernel(clip, refs[:parts], *refs[parts:base], *refs[base + count :])


def space_back_call(clip, grad, x, mod, w_c, qkv, branch, totals, earlier):
    clip_count, frame_count, tokens, width = x.shape
    frames = grad[0].shape[0]
    part = tokens // frames
    rest = [entry.shape[2] for entry in grad[1:]]
    heights = [part - sum(rest)] + rest
    if heights[0] == 0:
        grad, heights = grad[1:], heights[1:]
    rows = frame_count * tokens
    by_frame = lambda columns: pl.BlockSpec(
        (None, tokens, columns), lambda f: (clip * frame_count + f, 0, 0)
    )
    own = lambda columns: pl.BlockSpec((tokens, columns), lambda f: (clip * frame_count + f, 0))
    in_specs = [
        pl.BlockSpec((frames, 1, height, width), lambda f: (0, f, 0, 0)) for height in heights
    ] + [
        pl.BlockSpec((1, 1, tokens, width), lambda f: (clip, f, 0, 0)),
        full(mod.shape),
        full(w_c.shape),
        by_frame(3 * width),
        by_frame(width),
        pl.BlockSpec((None, 16, tokens), lambda f: (clip * frame_count + f, 0, 0)),
    ]
    args = list(grad) + [x, mod, w_c, qkv, branch, totals]
    begin = len(args)
    body = functools.partial(space_back_entry, len(earlier or ()), len(grad), clip)
    aliases = {}
    if earlier is not None:
        in_specs += [pl.BlockSpec(memory_space=pl.ANY)] * len(earlier)
        args += list(earlier)
        aliases = {begin + number: number for number in range(len(earlier))}
    return pl.pallas_call(
        body,
        grid=(frame_count,),
        in_specs=in_specs,
        out_specs=[
            pl.BlockSpec((1, 1, tokens, width), lambda f: (clip, f, 0, 0)),
            own(width),
            own(3 * width),
            pl.BlockSpec((8, width), lambda f: (0, 0)),
        ],
        out_shape=[
            jax.ShapeDtypeStruct(x.shape, f32),
            jax.ShapeDtypeStruct((clip_count * rows, width), bf16),
            jax.ShapeDtypeStruct((clip_count * rows, 3 * width), bf16),
            jax.ShapeDtypeStruct((8, width), f32),
        ],
        scratch_shapes=[VMEM((tokens, width), bf16)],
        input_output_aliases=aliases,
        compiler_params=pltpu.CompilerParams(vmem_limit_bytes=VMEM_LIMIT),
        cost_estimate=pl.CostEstimate(
            flops=rows * 20_000_000, bytes_accessed=rows * width * 20, transcendentals=0
        ),
    )(*args)


def shards(
    inputs, cotangent, time_steps, weight_index, ada_weight, ada_bias, space_qkv, space_out,
    space_out_bias, time_qkv, time_out, time_out_bias, up_weight, up_bias, down_weight, down_bias,
):
    clip_count, frame_count, patch_count, width = inputs.shape
    clips, frames = lax.axis_size("clip"), lax.axis_size("frame")
    owners = clips * frames
    owner = lax.axis_index("clip") * frames + lax.axis_index("frame")
    part = patch_count // frames
    rows = ada_weight.shape[0]

    embed = jax.nn.silu(embed_steps(time_steps, width)).astype(bf16)
    embed = jnp.pad(embed, ((0, 16 - clip_count), (0, 0)))
    place = lax.broadcasted_iota(jnp.int32, (width, 128), 0) - owner * rows
    lane = lax.broadcasted_iota(jnp.int32, (width, 128), 1)
    select = ((place == lane) & (lane < rows)).astype(bf16)

    def spread_bias(vector):
        length = vector.shape[0]
        empty = jnp.zeros((owners * length,), f32)
        return lax.dynamic_update_slice(empty, vector.astype(f32), (owner * length,)).reshape(
            -1, width
        )

    bias = jnp.concatenate(
        [
            spread_bias(vector)
            for vector in (ada_bias, space_out_bias, time_out_bias, up_bias, down_bias)
        ],
        axis=0,
    )
    (
        w_c, w_b, w_u, w_d, mod, chosen, totals, hidden_one, qkv_one, mixed_one, branch_one,
        after_first, after_later, cot_first,
    ) = start_call(
        clips, frames, inputs, cotangent, space_qkv, space_out, time_qkv, time_out, up_weight,
        down_weight, embed, select, ada_weight, bias,
    )

    def exchange(values):
        return lax.all_to_all(values, "frame", split_axis=0, concat_axis=0, tiled=True)

    loss = jnp.exp2(weight_index.astype(f32) * 0.5 - 1.0)
    loss = jnp.broadcast_to(loss[:, None], (clip_count, width))
    (
        act, gup, h3, gb3, mixed_two, gb2, h2, gqkv_two, mid_sums, _, _, grad_first,
        grad_second, grad_later, out_all,
    ) = middle_call(
        clips, frames, after_first, cot_first, after_later, cotangent, loss, mod, w_b, w_u, w_d
    )
    grads = [(grad_first,), (grad_second, exchange(grad_later))]

    earlier = None
    space_sums = []
    for clip in range(clip_count):
        *earlier, sums = space_back_call(
            clip, grads[clip], inputs, mod, w_c, qkv_one, branch_one, totals, earlier
        )
        space_sums.append(sums)
    input_grad, gb1, gqkv_one = earlier
    pieces = []
    for clip in range(clip_count):
        pieces += [space_sums[clip][0:3], mid_sums[clip][0:6]]
    pieces.append(sum(entry[3:4] for entry in space_sums))
    pieces.append(sum(entry[6:12] for entry in mid_sums))
    small = jnp.concatenate(pieces, axis=0)
    small = jnp.pad(small, ((0, ROWS - small.shape[0]), (0, 0)))
    picked = chosen.reshape(clips, 16, 128)[:, :clip_count].reshape(clips * clip_count, 128)
    outputs, grad_ada, sums, own_u, own_d, own_b, own_bo, own_c, own_co = grad_call(
        clips, frames, clip_count, small, picked.astype(f32).T, out_all, h3, gup, act, gb3, h2, gqkv_two,
        mixed_two, gb2, hidden_one.reshape(-1, width), gqkv_one, mixed_one.reshape(-1, width), gb1,
    )
    biases = sums[9:]

    def own_slice(vector):
        length = vector.shape[0] // owners
        return lax.dynamic_slice_in_dim(vector, owner * length, length, 0)

    return (
        outputs,
        input_grad,
        grad_ada,
        own_slice(sums[:9].reshape(-1)),
        own_c,
        own_co,
        own_slice(biases[0]),
        own_b,
        own_bo,
        own_slice(biases[1]),
        own_u,
        own_slice(biases[2:6].reshape(-1)),
        own_d,
        own_slice(biases[6]),
    )


def solution(mesh):
    tokens = P("clip", "frame", None, None)
    matrix = P(("clip", "frame"), None)
    vector = P(("clip", "frame"))
    in_specs = (
        tokens, tokens, P("clip"), P("clip"), matrix, vector, matrix, matrix, vector, matrix,
        matrix, vector, matrix, vector, matrix, vector,
    )
    out_specs = (
        tokens, tokens, matrix, vector, matrix, matrix, vector, matrix, matrix, vector, matrix,
        vector, matrix, vector,
    )
    return jax.shard_map(shards, mesh=mesh, in_specs=in_specs, out_specs=out_specs, check_vma=False)
```

```python
import functools
import math

import jax
import jax.numpy as jnp
from jax import lax
from jax.experimental import pallas as pl
from jax.experimental.pallas import tpu as pltpu
from jax.sharding import PartitionSpec as P

HEADS = 12
HEAD = 64
GROUP = 4
ROWS = 32
GELU_C = math.sqrt(2.0 / math.pi)
GELU_A = 0.044715
VMEM_LIMIT = 58 << 20

f32 = jnp.float32
bf16 = jnp.bfloat16
highest = lax.Precision.HIGHEST
MESH = pl.DeviceIdType.MESH
VMEM = pltpu.VMEM
DMA = pltpu.SemaphoreType.DMA


def embed_steps(time_steps, model_width):
    half_width = model_width // 2
    frequencies = jnp.exp(
        -math.log(10000.0) * jnp.arange(half_width, dtype=f32) / half_width
    )
    angles = time_steps.astype(f32)[:, None] * frequencies[None, :]
    return jnp.concatenate([jnp.cos(angles), jnp.sin(angles)], axis=1)


def dot(left, right, left_dim, right_dim):
    return lax.dot_general(
        left, right, (((left_dim,), (right_dim,)), ((), ())), preferred_element_type=f32
    )


def flip(index, mask):
    bit = 1
    while bit <= mask:
        if mask & bit:
            index = index + bit * (1 - 2 * ((index // bit) % 2))
        bit *= 2
    return index


def span(masks):
    out = [0]
    for mask in masks:
        out = out + [entry ^ mask for entry in out]
    return out


def frame_masks(frames):
    masks, bit = [], 1
    while bit < frames:
        masks.append(bit)
        bit *= 2
    if len(masks) > 1:
        masks = [frames - 1] + masks[:-1]
    return masks


def clip_tail_masks(clips):
    masks, bit = [], 2
    while bit < clips:
        masks.append(bit)
        bit *= 2
    return masks


def greet(clips, frames):
    clip, frame = lax.axis_index("clip"), lax.axis_index("frame")
    barrier = pltpu.get_barrier_semaphore()
    for step in range(1, clips):
        pl.semaphore_signal(
            barrier, inc=1, device_id={"clip": lax.rem(clip + step, clips)}, device_id_type=MESH
        )
    for step in range(1, frames):
        pl.semaphore_signal(
            barrier, inc=1, device_id={"frame": lax.rem(frame + step, frames)}, device_id_type=MESH
        )
    pl.semaphore_wait(barrier, clips + frames - 2)


def spread(axis, size, source_of, target, send_sems, recv_sems):
    me = lax.axis_index(axis)
    copies = []
    for step in range(1, size):
        peer = lax.rem(me + step, size)
        copy = pltpu.make_async_remote_copy(
            src_ref=source_of(peer),
            dst_ref=target.at[me],
            send_sem=send_sems.at[step - 1],
            recv_sem=recv_sems.at[step - 1],
            device_id={axis: peer},
            device_id_type=MESH,
        )
        copy.start()
        copies.append(copy)
    return copies


def start_kernel(
    clips, frames, clip_count,
    x_ref, cotangent, sq, so, tq, to, sh_u, sh_d, embed, select, ada, bias,
    w_c, w_b, w_u, w_d, mod, chosen, totals, hidden_out, qkv_out, mixed_out, branch_out,
    after_first, after_later, cot_first,
    v_c, z_c, z_b, z_u, z_d, st_w, b_c, b_b, b_u, b_d,
    ada_full, embeds, parts, terms, arrived, held, lined, hidden, qkv, mixed, branch, after,
    zs, zr, cs, cr, xs, xr, ls, es, er, ps, pr, fs, fr, ts, tr, hs, hr, os, ws,
):
    clip, frame = lax.axis_index("clip"), lax.axis_index("frame")
    zoned = (z_c, z_b, z_u, z_d)
    blocks = (b_c, b_b, b_u, b_d)
    wholes = (v_c, w_b, w_u, w_d)
    width = mod.shape[1]
    frame_count, tokens = x_ref.shape[1], x_ref.shape[2]
    part = tokens // frames
    greet(clips, frames)
    masks = frame_masks(frames)
    sends = []
    stage = {}

    def frame_step(group, step):
        number = (1 << step) - 1
        copies = []
        for offset in span(masks[:step]):
            slot = flip(frame, offset)
            copy = pltpu.make_async_remote_copy(
                src_ref=zoned[group].at[slot],
                dst_ref=zoned[group].at[slot],
                send_sem=zs.at[group, number],
                recv_sem=zr.at[group, number],
                device_id={"frame": flip(frame, masks[step])},
                device_id_type=MESH,
            )
            copy.start()
            copies.append(copy)
            number += 1
        sends.extend(copies)
        stage[group] = copies

    def frame_rest(group):
        for step in range(1, len(masks)):
            for copy in stage[group]:
                copy.wait_recv()
            frame_step(group, step)

    tail = clip_tail_masks(clips)
    steps = len(tail)
    orders = (tail, tail[::-1])
    moving = {}

    def block_send(group, half, step, position, offset):
        whole = wholes[group]
        block_rows = whole.shape[0] // clips
        columns = whole.shape[1] // 2
        rows = pl.ds(pl.multiple_of(flip(clip, offset) * block_rows, block_rows), block_rows)
        lanes = pl.ds(half * columns, columns)
        target = whole.at[rows, lanes]
        number = (1 << step) - 1 + position
        copy = pltpu.make_async_remote_copy(
            src_ref=blocks[group].at[:, lanes] if offset == 0 else target,
            dst_ref=target,
            send_sem=xs.at[group, half, number],
            recv_sem=xr.at[group, half, number],
            device_id={"clip": flip(clip, orders[half][step])},
            device_id_type=MESH,
        )
        copy.start()
        moving[group, half, number] = copy

    core_copies = {group: [] for group in range(4)}

    def core_send(group, offset):
        whole = wholes[group]
        block_rows = whole.shape[0] // clips
        rows = pl.ds(pl.multiple_of(flip(clip, offset) * block_rows, block_rows), block_rows)
        number = len(core_copies[group])
        copy = pltpu.make_async_remote_copy(
            src_ref=blocks[group] if offset == 0 else whole.at[rows, :],
            dst_ref=whole.at[rows, :],
            send_sem=cs.at[group, number],
            recv_sem=cr.at[group, number],
            device_id={"clip": flip(clip, 1)},
            device_id_type=MESH,
        )
        copy.start()
        core_copies[group].append(copy)

    local_copies = []

    def block_ready(group):
        for copy in stage[group]:
            copy.wait_recv()
        rows, columns = zoned[group].shape[1:]
        block_rows = frames * rows
        if rows % 16:
            for slot in range(frames):
                st_w[slot * rows : (slot + 1) * rows, :columns] = zoned[group][slot].astype(f32)
            blocks[group][...] = st_w[:block_rows, :columns].astype(bf16)
        else:
            for slot in range(frames):
                blocks[group][slot * rows : (slot + 1) * rows, :] = zoned[group][slot]
        for step in range(steps):
            for half in range(2):
                block_send(group, half, step, 0, 0)
        core_send(group, 0)
        place = pl.ds(pl.multiple_of(clip * block_rows, block_rows), block_rows)
        keep = pltpu.make_async_copy(blocks[group], wholes[group].at[place, :], ls.at[group])
        keep.start()
        local_copies.append(keep)

    def block_forward(group):
        for step in range(1, steps):
            for half in range(2):
                for position in range(1 << (step - 1), 1 << step):
                    moving[group, half, position - 1].wait_recv()
                for later in range(step, steps):
                    for position, offset in enumerate(span(orders[half][:later])):
                        if (1 << (step - 1)) <= position < (1 << step):
                            block_send(group, half, later, position, offset)

    def block_finish(group):
        last = (1 << (steps - 1)) - 1
        for half in range(2):
            for number in range(last, (1 << steps) - 1):
                moving[group, half, number].wait_recv()
        for offset in span(tail)[1:]:
            core_send(group, offset)

    def core_finish(group):
        for copy in core_copies[group]:
            copy.wait_recv()

    for group, first, second in ((0, sq, so), (1, tq, to)):
        zoned[group][frame, :, : 3 * width] = first[...]
        zoned[group][frame, :, 3 * width :] = second[...]
    frame_step(0, 0)
    own = spread("clip", clips, lambda peer: embed, embeds, es, er)
    sends.extend(own)
    embeds[clip] = embed[...]
    z_u[frame] = sh_u[...]
    z_d[frame] = sh_d[...]
    ada_full[...] = jnp.zeros_like(ada_full)
    ada_full[: ada.shape[0], :] = ada[...]
    frame_rest(0)
    for group in range(1, 4):
        frame_step(group, 0)
    cot_copies = []

    def cot_send(index):
        for step in range(frames - 1, 0, -1):
            peer = flip(frame, step)
            copy = pltpu.make_async_remote_copy(
                src_ref=cotangent.at[0, index, pl.ds(pl.multiple_of(peer * part, part), part), :],
                dst_ref=cot_first.at[frame, index],
                send_sem=ts.at[index, step - 1],
                recv_sem=tr.at[index, step - 1],
                device_id={"frame": peer},
                device_id_type=MESH,
            )
            copy.start()
            cot_copies.append(copy)

    cot_send(0)
    for copy in own:
        copy.wait_recv()
    picked = dot(embeds[...].reshape(clips * 16, width), select[...], 1, 0).astype(bf16)
    chosen[...] = picked
    parts[...] = dot(picked, ada_full[...], 1, 0)
    for peer in range(clips):
        for local in range(clip_count):
            row = peer * 16 + local
            for piece in range(9):
                terms[peer, local * 9 + piece : local * 9 + piece + 1, :] = (
                    parts[row : row + 1, piece * width : (piece + 1) * width]
                    + bias[piece : piece + 1, :]
                )
        base = clip_count * 9
        terms[peer, base : base + 7, :] = bias[9:16, :]
        if base + 7 < ROWS:
            terms[peer, base + 7 : ROWS, :] = jnp.zeros((ROWS - base - 7, width), f32)
    own = spread("clip", clips, lambda peer: terms.at[peer], arrived, ps, pr)
    sends.extend(own)
    arrived[clip] = terms[clip]
    block_ready(0)
    for copy in own:
        copy.wait_recv()
    total = arrived[0]
    for peer in range(1, clips):
        total = total + arrived[peer]
    held[...] = total
    own = spread("frame", frames, lambda peer: held, lined, fs, fr)
    sends.extend(own)
    lined[frame] = total
    for group in range(1, 4):
        frame_rest(group)

    for index in range(1, frame_count):
        cot_send(index)
    keep = pltpu.make_async_copy(
        cotangent.at[0, :, pl.ds(pl.multiple_of(frame * part, part), part), :],
        cot_first.at[frame],
        ls.at[4],
    )
    keep.start()
    local_copies.append(keep)

    for copy in own:
        copy.wait_recv()
    total = lined[0]
    for peer in range(1, frames):
        total = total + lined[peer]
    mod[...] = total
    block_forward(0)
    for group in range(1, 4):
        block_ready(group)
    block_finish(0)
    core_finish(0)
    local_copies[0].wait()

    keep = pltpu.make_async_copy(v_c, w_c, ls.at[5])
    keep.start()
    local_copies.append(keep)

    def after_copy(f, step):
        peer = flip(frame, step)
        return pltpu.make_async_remote_copy(
            src_ref=after.at[f, pl.ds(pl.multiple_of(peer * part, part), part), :],
            dst_ref=after_first.at[frame, f],
            send_sem=hs.at[f, step - 1],
            recv_sem=hr.at[f, step - 1],
            device_id={"frame": peer},
            device_id_type=MESH,
        )

    def own_after(f):
        return pltpu.make_async_copy(
            after.at[f, pl.ds(pl.multiple_of(frame * part, part), part), :],
            after_first.at[frame, f],
            os.at[f],
        )

    def later_after(f):
        return pltpu.make_async_copy(after.at[f], after_later.at[f - frame_count], os.at[f])

    kept = ((hidden, hidden_out), (qkv, qkv_out), (mixed, mixed_out), (branch, branch_out))

    def write_back(f):
        return [
            pltpu.make_async_copy(source.at[f], target.at[f], ws.at[number, f])
            for number, (source, target) in enumerate(kept)
        ]

    for local in range(clip_count):
        row = local * 9

        def one_frame(index, carry):
            f = local * frame_count + index
            values = x_ref[local, index].astype(f32)
            norm, _ = normed(values)
            scaled = norm * (1.0 + mod[row + 1 : row + 2, :]) + mod[row : row + 1, :]
            lowered = scaled.astype(bf16)
            hidden[f] = lowered
            qkv[f] = dot(lowered, v_c[:, : 3 * width], 1, 0).astype(bf16)
            attend(qkv.at[f], mixed.at[f], totals.at[f], width, None)
            grown = dot(mixed[f], v_c[:, 3 * width :], 1, 0) + mod[18:19, :]
            branch[f] = grown.astype(bf16)
            after[f] = (values + mod[row + 2 : row + 3, :] * grown).astype(bf16)
            if local == 0:
                for step in range(frames - 1, 0, -1):
                    after_copy(f, step).start()
                own_after(f).start()
            else:
                later_after(f).start()
            for copy in write_back(f):
                copy.start()
            return carry

        lax.fori_loop(0, frame_count, one_frame, 0)
        if local == 0:
            block_forward(1)
    for group in range(2, 4):
        block_forward(group)
    for group in range(1, 4):
        block_finish(group)
    for group in range(1, 4):
        core_finish(group)

    def settle(f, carry):
        for step in range(1, frames):
            copy = after_copy(f, step)
            copy.wait_recv()
            copy.wait_send()
        own_after(f).wait()
        return carry

    lax.fori_loop(0, frame_count, settle, 0)

    def settle_later(f, carry):
        later_after(f).wait()
        return carry

    lax.fori_loop(frame_count, clip_count * frame_count, settle_later, 0)

    def settle_kept(f, carry):
        for copy in write_back(f):
            copy.wait()
        return carry

    lax.fori_loop(0, clip_count * frame_count, settle_kept, 0)
    for copy in cot_copies:
        copy.wait_recv()
        copy.wait_send()
    for copy in local_copies[1:]:
        copy.wait()
    for copy in moving.values():
        copy.wait_send()
    for group in range(4):
        for copy in core_copies[group]:
            copy.wait_send()
    for copy in sends:
        copy.wait_send()


def start_call(
    clips, frames, inputs, cotangent, sq, so, tq, to, sh_u, sh_d, embed, select, ada, bias
):
    clip_count, frame_count, tokens, width = inputs.shape
    rows, columns = sh_u.shape
    rows_d = sh_d.shape[0]
    block = frames * rows
    block_d = frames * rows_d
    peers = max(clips // 2 - 1, 1)
    total = clip_count * frame_count
    part = tokens // frames
    whole = jax.ShapeDtypeStruct((clips * block, columns), bf16)
    vmem = pl.BlockSpec(memory_space=VMEM)
    hbm = pl.BlockSpec(memory_space=pl.ANY)
    zoned = lambda height, lanes: VMEM((frames, height, lanes), bf16)
    saved = lambda lanes: jax.ShapeDtypeStruct((total, tokens, lanes), bf16)
    lent = lambda lanes: VMEM((total, tokens, lanes), bf16)
    traded = jax.ShapeDtypeStruct((frames, frame_count, part, width), bf16)
    return pl.pallas_call(
        functools.partial(start_kernel, clips, frames, clip_count),
        out_shape=(
            whole, whole, whole,
            jax.ShapeDtypeStruct((clips * block_d, width), bf16),
            jax.ShapeDtypeStruct((ROWS, width), f32),
            jax.ShapeDtypeStruct((clips * 16, 128), bf16),
            jax.ShapeDtypeStruct((total, 16, tokens), f32),
            saved(width), saved(3 * width), saved(width), saved(width),
            traded,
            jax.ShapeDtypeStruct(((clip_count - 1) * frame_count, tokens, width), bf16),
            traded,
        ),
        in_specs=[vmem, hbm] + [vmem] * 10,
        out_specs=(hbm, hbm, hbm, hbm, vmem, vmem, vmem) + (hbm,) * 7,
        scratch_shapes=[
            VMEM((clips * block, columns), bf16),
            zoned(rows, columns), zoned(rows, columns), zoned(rows, columns), zoned(rows_d, width),
            VMEM((max(block, block_d), columns), f32),
            VMEM((block, columns), bf16),
            VMEM((block, columns), bf16),
            VMEM((block, columns), bf16),
            VMEM((block_d, width), bf16),
            VMEM((128, 9 * width), bf16),
            VMEM((clips, 16, width), bf16),
            VMEM((clips * 16, 9 * width), f32),
            VMEM((clips, ROWS, width), f32),
            VMEM((clips, ROWS, width), f32),
            VMEM((ROWS, width), f32),
            VMEM((frames, ROWS, width), f32),
            lent(width), lent(3 * width), lent(width), lent(width), lent(width),
            DMA((4, frames - 1)), DMA((4, frames - 1)),
            DMA((4, clips // 2)), DMA((4, clips // 2)),
            DMA((4, 2, peers)), DMA((4, 2, peers)),
            DMA((6,)),
            DMA((clips - 1,)), DMA((clips - 1,)),
            DMA((clips - 1,)), DMA((clips - 1,)),
            DMA((frames - 1,)), DMA((frames - 1,)),
            DMA((frame_count, frames - 1)), DMA((frame_count, frames - 1)),
            DMA((frame_count, frames - 1)), DMA((frame_count, frames - 1)),
            DMA((total,)),
            DMA((4, total)),
        ],
        compiler_params=pltpu.CompilerParams(
            collective_id=0, has_side_effects=True, vmem_limit_bytes=VMEM_LIMIT
        ),
    )(inputs, cotangent, sq, so, tq, to, sh_u, sh_d, embed, select, ada, bias)


STEP = 512
SLOTS = 3


def grad_kernel(
    clips, frames, clip_count,
    small, chosen, out_all, h3, gup, act, gb3, h2, gqkv2, mix2, gb2, h1, gqkv1, mix1, gb1,
    outputs, grad_ada, bias_sums, out_u, out_d, out_b, out_bo, out_c, out_co,
    sum_w, sum_d, core_w, core_d, side_w, side_d, line_w, line_d, last_w, last_d,
    left, right, total, gathered, lined, held,
    lsem, rsem, cs, cr, xs, xr, zs, zr, fs, fr, ps, pr, os, orr, ks,
):
    clip, frame = lax.axis_index("clip"), lax.axis_index("frame")
    tokens = h3.shape[0]
    width = small.shape[1]
    wide = sum_w.shape[-1]
    narrow = sum_d.shape[-1]
    tail = clip_tail_masks(clips)
    orders = (tail, tail[::-1])
    masks = frame_masks(frames)
    greet(clips, frames)
    first = spread("frame", frames, lambda peer: small, lined, fs, fr)
    lined[frame] = small[...]
    part = out_all.shape[3]
    frame_count = out_all.shape[2]
    out_copies = []
    mine = pl.ds(pl.multiple_of(frame * part, part), part)

    def send_output(number):
        local, index = divmod(number, frame_count)
        for hop in range(frames - 1, 0, -1):
            peer = flip(frame, hop)
            copy = pltpu.make_async_remote_copy(
                src_ref=out_all.at[local, peer, index],
                dst_ref=outputs.at[local, index, mine, :],
                send_sem=os.at[number, hop - 1],
                recv_sem=orr.at[number, hop - 1],
                device_id={"frame": peer},
                device_id_type=MESH,
            )
            copy.start()
            out_copies.append(copy)

    own_outs = []
    for local in range(clip_count):
        copy = pltpu.make_async_copy(
            out_all.at[local, frame], outputs.at[local, :, mine, :], ks.at[local]
        )
        copy.start()
        own_outs.append(copy)

    chunks = [
        (1, 0, [(act, gb3, 0, 0, narrow)], out_d, 0),
        (1, 1, [(act, gb3, narrow, 0, narrow)], out_d, narrow),
        (0, 0, [(h3, gup, 0, 0, wide)], out_u, 0),
        (0, 1, [(h3, gup, wide, 0, wide)], out_u, wide),
        (0, 2, [(h2, gqkv2, 0, 0, wide)], out_b, 0),
        (0, 3, [(h2, gqkv2, wide, 0, width), (mix2, gb2, 0, width, width)], out_b, wide),
        (0, 4, [(h1, gqkv1, 0, 0, wide)], out_c, 0),
        (0, 5, [(h1, gqkv1, wide, 0, width), (mix1, gb1, 0, width, width)], out_c, wide),
    ]
    sums, cores, sides = (sum_w, sum_d), (core_w, core_d), (side_w, side_d)
    lines, lasts = (line_w, line_d), (last_w, last_d)
    flights = {}

    steps = tokens // STEP
    line_up = []
    for kind, _, parts, _, _ in chunks:
        for part in parts:
            for group in range(part[0].shape[1] // width):
                line_up.append(part[:3] + (part[3] + group * part[4], part[4], group))
    begins = [0]
    for kind, _, parts, _, _ in chunks:
        begins.append(begins[-1] + sum(part[0].shape[1] // width for part in parts))

    def load(entry, step, slot):
        one, other, begin, _, lanes, group = line_up[entry]
        rows = pl.ds(pl.multiple_of(step * STEP, STEP), STEP)
        return (
            pltpu.make_async_copy(
                one.at[rows, pl.ds(group * width, width)], left.at[slot], lsem.at[slot]
            ),
            pltpu.make_async_copy(
                other.at[rows, pl.ds(begin, lanes)],
                right.at[slot, :, pl.ds(0, lanes)],
                rsem.at[slot],
            ),
        )

    def place_of(entry, step):
        return lax.rem(entry * steps + step, SLOTS)

    def multiply(number):
        kind, place = chunks[number][:2]
        for entry in range(begins[number], begins[number + 1]):
            at, lanes = line_up[entry][3:5]

            def body(step, carry):
                ahead = step + SLOTS - 1

                @pl.when(ahead < steps)
                def _():
                    for copy in load(entry, ahead, place_of(entry, ahead)):
                        copy.start()

                if entry + 1 < len(line_up):

                    @pl.when(ahead >= steps)
                    def _():
                        for copy in load(entry + 1, ahead - steps, place_of(entry, ahead)):
                            copy.start()

                slot = place_of(entry, step)
                for copy in load(entry, step, slot):
                    copy.wait()
                columns = slice(at, at + lanes)
                before = jnp.where(step > 0, total[:, columns], 0.0)
                total[:, columns] = before + dot(left[slot], right[slot, :, :lanes], 0, 0)
                return carry

            lax.fori_loop(0, steps, body, 0)
        rows, lanes = sums[kind].shape[2:]
        for block in range(clips):
            begin = block * rows
            column = begin // width * lanes
            begin = begin % width
            sums[kind][place, block] = total[begin : begin + rows, column : column + lanes].astype(
                bf16
            )

    def core_start(number):
        kind, place = chunks[number][:2]
        copies = []
        for position, offset in enumerate(span(tail)):
            copy = pltpu.make_async_remote_copy(
                src_ref=sums[kind].at[place, flip(clip, offset ^ 1)],
                dst_ref=cores[kind].at[place, position],
                send_sem=cs.at[number, position],
                recv_sem=cr.at[number, position],
                device_id={"clip": flip(clip, 1)},
                device_id_type=MESH,
            )
            copy.start()
            copies.append(copy)
        flights[number, "core"] = copies

    def half_of(kind, half):
        if kind:
            rows = sums[kind].shape[2] // 2
            return (slice(half * rows, (half + 1) * rows), slice(None))
        lanes = sums[kind].shape[3] // 2
        return (slice(None), slice(half * lanes, (half + 1) * lanes))

    def side_start(number, step):
        kind, place = chunks[number][:2]
        copies = []
        for half in range(2):
            mask = orders[half][step]
            for position, offset in enumerate(span(orders[half][:step])):
                entry = (1 << step) - 1 + position
                copy = pltpu.make_async_remote_copy(
                    src_ref=sums[kind].at[(place, flip(clip, offset ^ mask)) + half_of(kind, half)],
                    dst_ref=sides[kind].at[place, half, entry],
                    send_sem=xs.at[number, half, entry],
                    recv_sem=xr.at[number, half, entry],
                    device_id={"clip": flip(clip, mask)},
                    device_id_type=MESH,
                )
                copy.start()
                copies.append(copy)
        flights[number, "side", step] = copies

    def core_add(number):
        kind, place = chunks[number][:2]
        for copy in flights[number, "core"]:
            copy.wait_recv()
        for position, offset in enumerate(span(tail)):
            block = flip(clip, offset)
            sums[kind][place, block] = (
                sums[kind][place, block].astype(f32) + cores[kind][place, position].astype(f32)
            ).astype(bf16)
        side_start(number, len(tail) - 1)

    def side_add(number, step):
        kind, place = chunks[number][:2]
        for copy in flights[number, "side", step]:
            copy.wait_recv()
        for half in range(2):
            for position, offset in enumerate(span(orders[half][:step])):
                entry = (1 << step) - 1 + position
                block = flip(clip, offset)
                where = (place, block) + half_of(kind, half)
                sums[kind][where] = (
                    sums[kind][where].astype(f32) + sides[kind][place, half, entry].astype(f32)
                ).astype(bf16)
        if step:
            side_start(number, step - 1)
        else:
            rows = lines[kind].shape[2]
            block = sums[kind][place, clip].astype(f32)
            for slot in range(frames):
                lines[kind][place, slot] = block[slot * rows : (slot + 1) * rows, :].astype(bf16)
            line_start(number, len(masks) - 1)

    def line_start(number, step):
        kind, place = chunks[number][:2]
        copies = []
        for position, offset in enumerate(span(masks[:step])):
            entry = (1 << step) - 1 + position
            copy = pltpu.make_async_remote_copy(
                src_ref=lines[kind].at[place, flip(frame, offset ^ masks[step])],
                dst_ref=lasts[kind].at[place, entry],
                send_sem=zs.at[number, entry],
                recv_sem=zr.at[number, entry],
                device_id={"frame": flip(frame, masks[step])},
                device_id_type=MESH,
            )
            copy.start()
            copies.append(copy)
        flights[number, "line", step] = copies

    def line_add(number, step):
        kind, place, _, target, begin = chunks[number]
        for copy in flights[number, "line", step]:
            copy.wait_recv()
        for position, offset in enumerate(span(masks[:step])):
            entry = (1 << step) - 1 + position
            slot = flip(frame, offset)
            value = lines[kind][place, slot].astype(f32) + lasts[kind][place, entry].astype(f32)
            if step:
                lines[kind][place, slot] = value.astype(bf16)
            elif begin + value.shape[1] > target.shape[1]:
                cut = target.shape[1] - begin
                target[:, begin:] = value[:, :cut]
                (out_bo if target is out_b else out_co)[...] = value[:, cut:]
            else:
                target[:, begin : begin + value.shape[1]] = value
        if step:
            line_start(number, step - 1)

    stages = [core_start, core_add]
    for step in range(len(tail))[::-1]:
        stages.append(functools.partial(side_add, step=step))
    for step in range(len(masks))[::-1]:
        stages.append(functools.partial(line_add, step=step))

    def finish_small():
        for copy in second:
            copy.wait_recv()
        rows = grad_ada.shape[0]
        for number in range(9):
            terms = [
                gathered[peer, local * 9 + number : local * 9 + number + 1, :]
                for peer in range(clips)
                for local in range(clip_count)
            ]
            terms = jnp.concatenate(terms, axis=0)
            grad_ada[:, number * width : (number + 1) * width] = lax.dot_general(
                chosen[...], terms, (((1,), (0,)), ((), ())), precision=highest,
                preferred_element_type=f32,
            )[:rows, :]
            bias_sums[number : number + 1, :] = column_sum(terms)
        base = clip_count * 9
        summed = gathered[0, base : base + 7, :]
        for peer in range(1, clips):
            summed = summed + gathered[peer, base : base + 7, :]
        bias_sums[9:16, :] = summed

    for step in range(SLOTS - 1):
        for copy in load(0, step, step):
            copy.start()
    second = None
    lags = [0, 1, 3]
    while len(lags) < len(stages):
        lags.append(lags[-1] + 1)
    for turn in range(len(chunks) + lags[-1]):
        for depth in range(len(stages))[::-1]:
            if depth > 0 and 0 <= turn - lags[depth] < len(chunks):
                stages[depth](turn - lags[depth])
        if turn < clip_count * frame_count:
            send_output(turn)
        if turn < len(chunks):
            multiply(turn)
            core_start(turn)
        if turn == len(chunks):
            finish_small()
        if turn == 0:
            for copy in first:
                copy.wait_recv()
            summed = lined[0]
            for peer in range(1, frames):
                summed = summed + lined[peer]
            held[...] = summed
            second = spread("clip", clips, lambda peer: held, gathered, ps, pr)
            gathered[clip] = summed
    for copy in own_outs:
        copy.wait()
    for copy in out_copies:
        copy.wait_recv()
        copy.wait_send()
    for copy in first + second:
        copy.wait_send()
    for copies in flights.values():
        for copy in copies:
            copy.wait_send()


def grad_call(clips, frames, clip_count, small, chosen, out_all, *operands):
    h3, gup, act = operands[:3]
    _, _, frame_count, part, _ = out_all.shape
    width, hidden = h3.shape[1], act.shape[1]
    owners = clips * frames
    wide, narrow = hidden // 2, width // 2
    rows_w, rows_d = width // owners, hidden // owners
    peers = max(clips // 2 - 1, 1)
    vmem = pl.BlockSpec(memory_space=VMEM)
    hbm = pl.BlockSpec(memory_space=pl.ANY)

    return pl.pallas_call(
        functools.partial(grad_kernel, clips, frames, clip_count),
        out_shape=(
            jax.ShapeDtypeStruct((clip_count, frame_count, frames * part, width), bf16),
            jax.ShapeDtypeStruct((rows_w, 9 * width), f32),
            jax.ShapeDtypeStruct((16, width), f32),
            jax.ShapeDtypeStruct((rows_w, hidden), f32),
            jax.ShapeDtypeStruct((rows_d, width), f32),
            jax.ShapeDtypeStruct((rows_w, 3 * width), f32),
            jax.ShapeDtypeStruct((rows_w, width), f32),
            jax.ShapeDtypeStruct((rows_w, 3 * width), f32),
            jax.ShapeDtypeStruct((rows_w, width), f32),
        ),
        in_specs=[vmem, vmem] + [hbm] * (1 + len(operands)),
        out_specs=(hbm,) + (vmem,) * 8,
        scratch_shapes=[
            VMEM((6, clips, rows_w * frames, wide), bf16),
            VMEM((2, clips, rows_d * frames, narrow), bf16),
            VMEM((6, clips // 2, rows_w * frames, wide), bf16),
            VMEM((2, clips // 2, rows_d * frames, narrow), bf16),
            VMEM((6, 2, peers, rows_w * frames, wide // 2), bf16),
            VMEM((2, 2, peers, rows_d * frames // 2, narrow), bf16),
            VMEM((6, frames, rows_w, wide), bf16),
            VMEM((2, frames, rows_d, narrow), bf16),
            VMEM((6, frames - 1, rows_w, wide), bf16),
            VMEM((2, frames - 1, rows_d, narrow), bf16),
            VMEM((SLOTS, STEP, width), bf16),
            VMEM((SLOTS, STEP, wide), bf16),
            VMEM((width, wide), f32),
            VMEM((clips,) + small.shape, f32),
            VMEM((frames,) + small.shape, f32),
            VMEM(small.shape, f32),
            DMA((SLOTS,)), DMA((SLOTS,)),
            DMA((8, clips // 2)), DMA((8, clips // 2)),
            DMA((8, 2, peers)), DMA((8, 2, peers)),
            DMA((8, frames - 1)), DMA((8, frames - 1)),
            DMA((frames - 1,)), DMA((frames - 1,)),
            DMA((clips - 1,)), DMA((clips - 1,)),
            DMA((clip_count * frame_count, frames - 1)),
            DMA((clip_count * frame_count, frames - 1)),
            DMA((clip_count,)),
        ],
        compiler_params=pltpu.CompilerParams(
            collective_id=1, has_side_effects=True, vmem_limit_bytes=VMEM_LIMIT
        ),
    )(small, chosen, out_all, *operands)


def normed(values):
    centred = values - jnp.mean(values, axis=-1, keepdims=True)
    scale = lax.rsqrt(jnp.mean(centred * centred, axis=-1, keepdims=True) + 1e-06)
    return centred * scale, scale


def norm_back(grad, scaled, norm, scale):
    inner = grad * scaled
    return scale * (
        inner
        - jnp.mean(inner, axis=-1, keepdims=True)
        - norm * jnp.mean(inner * norm, axis=-1, keepdims=True)
    )


def column_sum(values):
    return jnp.sum(values, axis=0, keepdims=True)


def head_lanes(tokens):
    lane = lax.broadcasted_iota(jnp.int32, (tokens, GROUP * HEAD), 1)
    return [(lane >= HEAD * head) & (lane < HEAD * (head + 1)) for head in range(GROUP)]


def stacked(values, picks):
    return jnp.concatenate([jnp.where(pick, values, bf16(0)) for pick in picks], axis=0)


def unstacked(values, picks, tokens):
    result = values[(GROUP - 1) * tokens :]
    for head in range(GROUP - 1):
        result = jnp.where(picks[head], values[head * tokens : (head + 1) * tokens], result)
    return result


def masked_scores(keys, own, mask):
    scores = dot(keys, own, 1, 1)
    if mask is not None:
        scores = scores + jnp.concatenate([mask[...]] * GROUP, axis=1)
    return scores


def attend(qkv, mixed, totals, width, mask):
    tokens = qkv.shape[0]
    lanes = GROUP * HEAD
    picks = head_lanes(tokens)
    for group in range(HEADS // GROUP):
        at = group * lanes
        own = stacked(qkv[:, at : at + lanes] * bf16(0.125), picks)
        keys = qkv[:, width + at : width + at + lanes]
        values = qkv[:, 2 * width + at : 2 * width + at + lanes]
        scores = masked_scores(keys, own, mask)
        peak = jnp.max(scores, axis=0, keepdims=True)
        terms = jnp.exp(scores - peak)
        total = jnp.sum(terms, axis=0, keepdims=True)
        weights = (terms * (1.0 / total)).astype(bf16)
        logs = peak + jnp.log(total)
        for head in range(GROUP):
            row = group * GROUP + head
            totals[row : row + 1, :] = logs[:, head * tokens : (head + 1) * tokens]
        result = unstacked(dot(weights, values, 0, 0), picks, tokens)
        mixed[:, at : at + lanes] = result.astype(bf16)


def attend_back(qkv, grad_mixed, totals, grad_qkv, width, mask):
    tokens = qkv.shape[0]
    lanes = GROUP * HEAD
    picks = head_lanes(tokens)
    for group in range(HEADS // GROUP):
        at = group * lanes
        own = stacked(qkv[:, at : at + lanes] * bf16(0.125), picks)
        keys = qkv[:, width + at : width + at + lanes]
        values = qkv[:, 2 * width + at : 2 * width + at + lanes]
        own_grads = stacked(grad_mixed[:, at : at + lanes], picks)
        logs = jnp.concatenate(
            [totals[group * GROUP + head : group * GROUP + head + 1, :] for head in range(GROUP)],
            axis=1,
        )
        weights = jnp.exp(masked_scores(keys, own, mask) - logs)
        grad_weights = dot(values, own_grads, 1, 1)
        inner = jnp.sum(weights * grad_weights, axis=0, keepdims=True)
        grad_scores = (weights * (grad_weights - inner)).astype(bf16)
        grad_queries = unstacked(dot(grad_scores, keys, 0, 0), picks, tokens) * 0.125
        grad_keys = dot(grad_scores, own, 1, 0)
        grad_values = dot(weights.astype(bf16), own_grads, 1, 0)
        for part, grad in enumerate((grad_queries, grad_keys, grad_values)):
            start = part * width + at
            grad_qkv[:, start : start + lanes] = grad.astype(bf16)


def full(shape):
    return pl.BlockSpec(shape, lambda *_: (0,) * len(shape), pipeline_mode=pl.Buffered(1))


def middle_kernel(
    clips, frames, tiles,
    after_first, cot_first, after_later, cotangent, loss, mod, w_b, w_u, w_d,
    act_ref, gup_ref, h3_ref, gb3_ref, mixed_ref, gb2_ref, h2_ref, gqkv_ref, sums,
    after_second, cot_second, grad_first, grad_second, grad_later, out_all,
    qkv, totals, mask, gmix, after_tile, cot_tile, grad_stage, out_stage,
    ts, tr, us, ur, gs, gr, hs, hr, ls, ks, ws,
):
    frame = lax.axis_index("frame")
    step = pl.program_id(0)
    last = pl.num_programs(0) - 1
    clip = lax.div(step, tiles)
    tile = lax.rem(step, tiles)
    slot = lax.rem(step, 2)
    width = mod.shape[1]
    frame_count, group = after_tile.shape[2], after_tile.shape[3]
    part = tiles * group
    tokens = frames * frame_count * group
    row = clip * 9
    piece = lambda number: mod[pl.ds(row + number, 1), :]

    def own_part(index):
        return pl.ds(pl.multiple_of(index * part, part), part)

    def later_copies(number):
        copies = []
        for hop in range(frames - 1, 0, -1):
            peer = flip(frame, hop)
            if number:
                source, target, send, recv = cotangent.at[1, :, own_part(peer), :], cot_second, us, ur
            else:
                source, target, send, recv = after_later.at[:, own_part(peer), :], after_second, ts, tr
            copies.append(
                pltpu.make_async_remote_copy(
                    src_ref=source,
                    dst_ref=target.at[frame],
                    send_sem=send.at[hop - 1],
                    recv_sem=recv.at[hop - 1],
                    device_id={"frame": peer},
                    device_id_type=MESH,
                )
            )
        return copies

    def own_copy(number):
        source = cotangent.at[1] if number else after_later
        target = cot_second if number else after_second
        return pltpu.make_async_copy(
            source.at[:, own_part(frame), :], target.at[frame], ks.at[number]
        )

    def load(source, number, index, place):
        rows = pl.ds(pl.multiple_of(index * group, group), group)
        target = (after_tile, cot_tile)[number].at[place]
        return pltpu.make_async_copy(source.at[:, :, rows, :], target, ls.at[place, number])

    early = tiles // 2

    def grad_copies(index, later=False):
        place = index + tiles if later else index
        target, send, recv = (grad_second, hs, hr) if later else (grad_first, gs, gr)
        rows = pl.ds(pl.multiple_of(index * group, group), group)
        copies = []
        for hop in range(frames - 1, 0, -1):
            peer = flip(frame, hop)
            copies.append(
                pltpu.make_async_remote_copy(
                    src_ref=grad_stage.at[place, peer],
                    dst_ref=target.at[frame, :, rows, :],
                    send_sem=send.at[index, hop - 1],
                    recv_sem=recv.at[index, hop - 1],
                    device_id={"frame": peer},
                    device_id_type=MESH,
                )
            )
        return copies

    def grad_own(index, later=False):
        place = index + tiles if later else index
        target = grad_second if later else grad_first
        rows = pl.ds(pl.multiple_of(index * group, group), group)
        return pltpu.make_async_copy(
            grad_stage.at[place, frame], target.at[frame, :, rows, :], ws.at[0, place]
        )

    def grad_keep(index):
        place = index + tiles
        rows = pl.ds(pl.multiple_of((index - early) * group, group), group)
        return pltpu.make_async_copy(
            grad_stage.at[place], grad_later.at[:, :, rows, :], ws.at[0, place]
        )

    def out_keep(number):
        rows = pl.ds(pl.multiple_of(lax.rem(number, tiles) * group, group), group)
        return pltpu.make_async_copy(
            out_stage.at[number], out_all.at[lax.div(number, tiles), :, :, rows, :], ws.at[1, number]
        )

    @pl.when(step == 0)
    def _():
        barrier = pltpu.get_barrier_semaphore()
        for hop in range(1, frames):
            pl.semaphore_signal(
                barrier,
                inc=1,
                device_id={"frame": lax.rem(frame + hop, frames)},
                device_id_type=MESH,
            )
        pl.semaphore_wait(barrier, frames - 1)
        load(after_first, 0, 0, 0).start()
        load(cot_first, 1, 0, 0).start()
        for number in range(2):
            for copy in later_copies(number):
                copy.start()
            own_copy(number).start()
        first = lax.broadcasted_iota(jnp.int32, (tokens, tokens), 0)
        second = lax.broadcasted_iota(jnp.int32, (tokens, tokens), 1)
        mask[...] = jnp.where(lax.rem(first, group) == lax.rem(second, group), 0.0, -1e30)

    @pl.when(step == tiles)
    def _():
        for copy in later_copies(0):
            copy.wait_recv()
        own_copy(0).wait()
        load(after_second, 0, 0, slot).start()

    load(after_first, 0, 0, slot).wait()

    @pl.when(step + 1 < tiles)
    def _():
        load(after_first, 0, step + 1, 1 - slot).start()
        load(cot_first, 1, step + 1, 1 - slot).start()

    @pl.when((step >= tiles) & (step < last))
    def _():
        load(after_second, 0, tile + 1, 1 - slot).start()

    @pl.when((step > tiles) & (step < last))
    def _():
        load(cot_second, 1, tile + 1, 1 - slot).start()

    @pl.when(tile == 0)
    def _():
        sums[...] = jnp.zeros_like(sums)

    def add(place, values):
        sums[place : place + 1, :] += values

    after = after_tile[slot].reshape(tokens, width).astype(f32)
    norm, scale = normed(after)
    hidden = (norm * (1.0 + piece(4)) + piece(3)).astype(bf16)
    h2_ref[...] = hidden
    qkv[...] = dot(hidden, w_b[:, : 3 * width], 1, 0).astype(bf16)
    attend(qkv, mixed_ref, totals, width, mask)
    branch_two = dot(mixed_ref[...], w_b[:, 3 * width :], 1, 0) + mod[19:20, :]
    after_two = after + piece(5) * branch_two
    norm_three, scale_three = normed(after_two)
    hidden = (norm_three * (1.0 + piece(7)) + piece(6)).astype(bf16)
    h3_ref[...] = hidden

    @pl.when(step == tiles)
    def _():
        for copy in later_copies(1):
            copy.wait_recv()
        own_copy(1).wait()
        load(cot_second, 1, 0, slot).start()
        if tiles > 1:
            load(cot_second, 1, 1, 1 - slot).start()

        def send(index, carry):
            for copy in grad_copies(index):
                copy.start()
            return carry

        lax.fori_loop(0, tiles, send, 0)

    load(cot_first, 1, 0, slot).wait()
    grad_out = cot_tile[slot].reshape(tokens, width).astype(f32) * loss[pl.ds(clip, 1), :]
    grad_branch = (grad_out * piece(8)).astype(bf16)
    gb3_ref[...] = grad_branch
    add(11, column_sum(grad_branch.astype(f32)))
    branch_three = jnp.zeros((tokens, width), f32)
    grad_hidden = jnp.zeros((tokens, width), f32)
    for chunk in range(w_u.shape[1] // width):
        cut = slice(chunk * width, (chunk + 1) * width)
        upper = dot(hidden, w_u[:, cut], 1, 0) + mod[20 + chunk : 21 + chunk, :]
        square = upper * upper
        bend = jnp.tanh(upper * (GELU_C + (GELU_C * GELU_A) * square))
        half = 0.5 + 0.5 * bend
        act = (upper * half).astype(bf16)
        slope = half + (0.5 * upper) * (1.0 - bend * bend) * (
            GELU_C + (3.0 * GELU_C * GELU_A) * square
        )
        act_ref[:, cut] = act
        branch_three += dot(act, w_d[cut, :], 1, 0)
        grad_upper = (dot(grad_branch, w_d[cut, :], 1, 1) * slope).astype(bf16)
        gup_ref[:, cut] = grad_upper
        add(7 + chunk, column_sum(grad_upper.astype(f32)))
        grad_hidden += dot(grad_upper, w_u[:, cut], 1, 1)
    branch_three += mod[24:25, :]
    out = (after_two + piece(8) * branch_three).astype(bf16)
    out_stage[step] = out.reshape(out_stage.shape[1:])
    add(5, column_sum(grad_out * branch_three))
    add(3, column_sum(grad_hidden))
    add(4, column_sum(grad_hidden * norm_three))
    grad_two = grad_out + norm_back(grad_hidden, 1.0 + piece(7), norm_three, scale_three)
    add(2, column_sum(grad_two * branch_two))
    grad_branch = (grad_two * piece(5)).astype(bf16)
    gb2_ref[...] = grad_branch
    add(6, column_sum(grad_branch.astype(f32)))
    gmix[...] = dot(grad_branch, w_b[:, 3 * width :], 1, 1).astype(bf16)
    attend_back(qkv, gmix, totals, gqkv_ref, width, mask)
    grad_hidden = dot(gqkv_ref[...], w_b[:, : 3 * width], 1, 1).astype(bf16).astype(f32)
    add(0, column_sum(grad_hidden))
    add(1, column_sum(grad_hidden * norm))
    grad_one = grad_two + norm_back(grad_hidden, 1.0 + piece(4), norm, scale)
    grad_stage[step] = grad_one.astype(bf16).reshape(grad_stage.shape[1:])

    out_keep(step).start()

    @pl.when(step < tiles)
    def _():
        grad_own(tile).start()

    if early:

        @pl.when((step >= tiles) & (tile < early))
        def _():
            for copy in grad_copies(tile, True):
                copy.start()
            grad_own(tile, True).start()

    @pl.when((step >= tiles) & (tile >= early))
    def _():
        grad_keep(tile).start()

    @pl.when(step == last)
    def _():
        for copy in later_copies(0) + later_copies(1):
            copy.wait_send()

        def settle(index, carry):
            for copy in grad_copies(index):
                copy.wait_send()
                copy.wait_recv()
            grad_own(index).wait()
            out_keep(index).wait()
            out_keep(index + tiles).wait()
            return carry

        lax.fori_loop(0, tiles, settle, 0)

        def settle_early(index, carry):
            for copy in grad_copies(index, True):
                copy.wait_send()
                copy.wait_recv()
            grad_own(index, True).wait()
            return carry

        if early:
            lax.fori_loop(0, early, settle_early, 0)

        def settle_kept(index, carry):
            grad_keep(index).wait()
            return carry

        lax.fori_loop(early, tiles, settle_kept, 0)


def middle_call(
    clips, frames, after_first, cot_first, after_later, cotangent, loss, mod, w_b, w_u, w_d
):
    _, frame_count, part, width = after_first.shape
    group = min(16, part)
    tiles = part // group
    tokens = frames * frame_count * group
    hidden_width = w_u.shape[1]
    widths = (hidden_width, hidden_width, width, width, width, width, width, 3 * width)
    own = lambda columns: pl.BlockSpec((tokens, columns), lambda t: (t, 0))
    hbm = pl.BlockSpec(memory_space=pl.ANY)
    rows = 2 * tiles * tokens
    traded = jax.ShapeDtypeStruct(after_first.shape, bf16)
    slab = (frames, frame_count, group, width)
    return pl.pallas_call(
        functools.partial(middle_kernel, clips, frames, tiles),
        grid=(2 * tiles,),
        in_specs=[
            hbm, hbm, hbm, hbm, full(loss.shape), full(mod.shape), full(w_b.shape),
            full(w_u.shape), full(w_d.shape),
        ],
        out_specs=[own(columns) for columns in widths]
        + [pl.BlockSpec((None, 16, width), lambda t: (t // tiles, 0, 0))]
        + [hbm] * 6,
        out_shape=[jax.ShapeDtypeStruct((rows, columns), bf16) for columns in widths]
        + [
            jax.ShapeDtypeStruct((2, 16, width), f32),
            traded, traded, traded, traded,
            jax.ShapeDtypeStruct(
                (frames, frame_count, part - tiles // 2 * group, width), bf16
            ),
            jax.ShapeDtypeStruct((2,) + after_first.shape, bf16),
        ],
        scratch_shapes=[
            VMEM((tokens, 3 * width), bf16),
            VMEM((16, tokens), f32),
            VMEM((tokens, tokens), f32),
            VMEM((tokens, width), bf16),
            VMEM((2,) + slab, bf16),
            VMEM((2,) + slab, bf16),
            VMEM((2 * tiles,) + slab, bf16),
            VMEM((2 * tiles,) + slab, bf16),
            DMA((frames - 1,)), DMA((frames - 1,)),
            DMA((frames - 1,)), DMA((frames - 1,)),
            DMA((tiles, frames - 1)), DMA((tiles, frames - 1)),
            DMA((max(tiles // 2, 1), frames - 1)), DMA((max(tiles // 2, 1), frames - 1)),
            DMA((2, 2)), DMA((2,)), DMA((2, 2 * tiles)),
        ],
        compiler_params=pltpu.CompilerParams(
            collective_id=2, has_side_effects=True, vmem_limit_bytes=VMEM_LIMIT
        ),
    )(after_first, cot_first, after_later, cotangent, loss, mod, w_b, w_u, w_d)


def space_back_kernel(
    clip, grad_refs, x_ref, mod, w_c, qkv, branch, totals,
    out_ref, gb_ref, gqkv_ref, sums, gmix,
):
    width = x_ref.shape[-1]
    tokens = x_ref.shape[-2]
    row = clip * 9
    piece = lambda number: mod[row + number : row + number + 1, :]

    @pl.when(pl.program_id(0) == 0)
    def _():
        sums[...] = jnp.zeros_like(sums)

    joined = [grad_ref[...] for grad_ref in grad_refs]
    joined = joined[0] if len(joined) == 1 else jnp.concatenate(joined, axis=2)
    grad = joined.reshape(tokens, width).astype(f32)
    grad_branch = (grad * piece(2)).astype(bf16)
    gb_ref[...] = grad_branch
    sums[2:3, :] += column_sum(grad * branch[...].astype(f32))
    sums[3:4, :] += column_sum(grad_branch.astype(f32))
    gmix[...] = dot(grad_branch, w_c[:, 3 * width :], 1, 1).astype(bf16)
    attend_back(qkv, gmix, totals, gqkv_ref, width, None)
    grad_hidden = dot(gqkv_ref[...], w_c[:, : 3 * width], 1, 1)
    norm, scale = normed(x_ref[...].reshape(tokens, width).astype(f32))
    sums[0:1, :] += column_sum(grad_hidden)
    sums[1:2, :] += column_sum(grad_hidden * norm)
    result = grad + norm_back(grad_hidden, 1.0 + piece(1), norm, scale)
    out_ref[...] = result.reshape(out_ref.shape)


def space_back_entry(count, parts, clip, *refs):
    base = 6 + parts
    space_back_kernel(clip, refs[:parts], *refs[parts:base], *refs[base + count :])


def space_back_call(clip, grad, x, mod, w_c, qkv, branch, totals, earlier):
    clip_count, frame_count, tokens, width = x.shape
    frames = grad[0].shape[0]
    part = tokens // frames
    rest = [entry.shape[2] for entry in grad[1:]]
    heights = [part - sum(rest)] + rest
    if heights[0] == 0:
        grad, heights = grad[1:], heights[1:]
    rows = frame_count * tokens
    by_frame = lambda columns: pl.BlockSpec(
        (None, tokens, columns), lambda f: (clip * frame_count + f, 0, 0)
    )
    own = lambda columns: pl.BlockSpec((tokens, columns), lambda f: (clip * frame_count + f, 0))
    in_specs = [
        pl.BlockSpec((frames, 1, height, width), lambda f: (0, f, 0, 0)) for height in heights
    ] + [
        pl.BlockSpec((1, 1, tokens, width), lambda f: (clip, f, 0, 0)),
        full(mod.shape),
        full(w_c.shape),
        by_frame(3 * width),
        by_frame(width),
        pl.BlockSpec((None, 16, tokens), lambda f: (clip * frame_count + f, 0, 0)),
    ]
    args = list(grad) + [x, mod, w_c, qkv, branch, totals]
    begin = len(args)
    body = functools.partial(space_back_entry, len(earlier or ()), len(grad), clip)
    aliases = {}
    if earlier is not None:
        in_specs += [pl.BlockSpec(memory_space=pl.ANY)] * len(earlier)
        args += list(earlier)
        aliases = {begin + number: number for number in range(len(earlier))}
    return pl.pallas_call(
        body,
        grid=(frame_count,),
        in_specs=in_specs,
        out_specs=[
            pl.BlockSpec((1, 1, tokens, width), lambda f: (clip, f, 0, 0)),
            own(width),
            own(3 * width),
            pl.BlockSpec((8, width), lambda f: (0, 0)),
        ],
        out_shape=[
            jax.ShapeDtypeStruct(x.shape, f32),
            jax.ShapeDtypeStruct((clip_count * rows, width), bf16),
            jax.ShapeDtypeStruct((clip_count * rows, 3 * width), bf16),
            jax.ShapeDtypeStruct((8, width), f32),
        ],
        scratch_shapes=[VMEM((tokens, width), bf16)],
        input_output_aliases=aliases,
        compiler_params=pltpu.CompilerParams(vmem_limit_bytes=VMEM_LIMIT),
        cost_estimate=pl.CostEstimate(
            flops=rows * 20_000_000, bytes_accessed=rows * width * 20, transcendentals=0
        ),
    )(*args)


def shards(
    inputs, cotangent, time_steps, weight_index, ada_weight, ada_bias, space_qkv, space_out,
    space_out_bias, time_qkv, time_out, time_out_bias, up_weight, up_bias, down_weight, down_bias,
):
    clip_count, frame_count, patch_count, width = inputs.shape
    clips, frames = lax.axis_size("clip"), lax.axis_size("frame")
    owners = clips * frames
    owner = lax.axis_index("clip") * frames + lax.axis_index("frame")
    part = patch_count // frames
    rows = ada_weight.shape[0]

    embed = jax.nn.silu(embed_steps(time_steps, width)).astype(bf16)
    embed = jnp.pad(embed, ((0, 16 - clip_count), (0, 0)))
    place = lax.broadcasted_iota(jnp.int32, (width, 128), 0) - owner * rows
    lane = lax.broadcasted_iota(jnp.int32, (width, 128), 1)
    select = ((place == lane) & (lane < rows)).astype(bf16)

    def spread_bias(vector):
        length = vector.shape[0]
        empty = jnp.zeros((owners * length,), f32)
        return lax.dynamic_update_slice(empty, vector.astype(f32), (owner * length,)).reshape(
            -1, width
        )

    bias = jnp.concatenate(
        [
            spread_bias(vector)
            for vector in (ada_bias, space_out_bias, time_out_bias, up_bias, down_bias)
        ],
        axis=0,
    )
    (
        w_c, w_b, w_u, w_d, mod, chosen, totals, hidden_one, qkv_one, mixed_one, branch_one,
        after_first, after_later, cot_first,
    ) = start_call(
        clips, frames, inputs, cotangent, space_qkv, space_out, time_qkv, time_out, up_weight,
        down_weight, embed, select, ada_weight, bias,
    )

    def exchange(values):
        return lax.all_to_all(values, "frame", split_axis=0, concat_axis=0, tiled=True)

    loss = jnp.exp2(weight_index.astype(f32) * 0.5 - 1.0)
    loss = jnp.broadcast_to(loss[:, None], (clip_count, width))
    (
        act, gup, h3, gb3, mixed_two, gb2, h2, gqkv_two, mid_sums, _, _, grad_first,
        grad_second, grad_later, out_all,
    ) = middle_call(
        clips, frames, after_first, cot_first, after_later, cotangent, loss, mod, w_b, w_u, w_d
    )
    grads = [(grad_first,), (grad_second, exchange(grad_later))]

    earlier = None
    space_sums = []
    for clip in range(clip_count):
        *earlier, sums = space_back_call(
            clip, grads[clip], inputs, mod, w_c, qkv_one, branch_one, totals, earlier
        )
        space_sums.append(sums)
    input_grad, gb1, gqkv_one = earlier
    pieces = []
    for clip in range(clip_count):
        pieces += [space_sums[clip][0:3], mid_sums[clip][0:6]]
    pieces.append(sum(entry[3:4] for entry in space_sums))
    pieces.append(sum(entry[6:12] for entry in mid_sums))
    small = jnp.concatenate(pieces, axis=0)
    small = jnp.pad(small, ((0, ROWS - small.shape[0]), (0, 0)))
    picked = chosen.reshape(clips, 16, 128)[:, :clip_count].reshape(clips * clip_count, 128)
    outputs, grad_ada, sums, own_u, own_d, own_b, own_bo, own_c, own_co = grad_call(
        clips, frames, clip_count, small, picked.astype(f32).T, out_all, h3, gup, act, gb3, h2, gqkv_two,
        mixed_two, gb2, hidden_one.reshape(-1, width), gqkv_one, mixed_one.reshape(-1, width), gb1,
    )
    biases = sums[9:]

    def own_slice(vector):
        length = vector.shape[0] // owners
        return lax.dynamic_slice_in_dim(vector, owner * length, length, 0)

    return (
        outputs,
        input_grad,
        grad_ada,
        own_slice(sums[:9].reshape(-1)),
        own_c,
        own_co,
        own_slice(biases[0]),
        own_b,
        own_bo,
        own_slice(biases[1]),
        own_u,
        own_slice(biases[2:6].reshape(-1)),
        own_d,
        own_slice(biases[6]),
    )


def solution(mesh):
    tokens = P("clip", "frame", None, None)
    matrix = P(("clip", "frame"), None)
    vector = P(("clip", "frame"))
    in_specs = (
        tokens, tokens, P("clip"), P("clip"), matrix, vector, matrix, matrix, vector, matrix,
        matrix, vector, matrix, vector, matrix, vector,
    )
    out_specs = (
        tokens, tokens, matrix, vector, matrix, matrix, vector, matrix, matrix, vector, matrix,
        vector, matrix, vector,
    )
    return jax.shard_map(shards, mesh=mesh, in_specs=in_specs, out_specs=out_specs, check_vma=False)
```

```python
import functools
import math

import jax
import jax.numpy as jnp
from jax import lax
from jax.experimental import pallas as pl
from jax.experimental.pallas import tpu as pltpu
from jax.sharding import PartitionSpec as P

HEADS = 12
HEAD = 64
GROUP = 4
ROWS = 32
GELU_C = math.sqrt(2.0 / math.pi)
GELU_A = 0.044715
VMEM_LIMIT = 58 << 20

f32 = jnp.float32
bf16 = jnp.bfloat16
highest = lax.Precision.HIGHEST
MESH = pl.DeviceIdType.MESH
VMEM = pltpu.VMEM
DMA = pltpu.SemaphoreType.DMA


def embed_steps(time_steps, model_width):
    half_width = model_width // 2
    frequencies = jnp.exp(
        -math.log(10000.0) * jnp.arange(half_width, dtype=f32) / half_width
    )
    angles = time_steps.astype(f32)[:, None] * frequencies[None, :]
    return jnp.concatenate([jnp.cos(angles), jnp.sin(angles)], axis=1)


def dot(left, right, left_dim, right_dim):
    return lax.dot_general(
        left, right, (((left_dim,), (right_dim,)), ((), ())), preferred_element_type=f32
    )


def flip(index, mask):
    bit = 1
    while bit <= mask:
        if mask & bit:
            index = index + bit * (1 - 2 * ((index // bit) % 2))
        bit *= 2
    return index


def span(masks):
    out = [0]
    for mask in masks:
        out = out + [entry ^ mask for entry in out]
    return out


def frame_masks(frames):
    masks, bit = [], 1
    while bit < frames:
        masks.append(bit)
        bit *= 2
    if len(masks) > 1:
        masks = [frames - 1] + masks[:-1]
    return masks


def clip_tail_masks(clips):
    masks, bit = [], 2
    while bit < clips:
        masks.append(bit)
        bit *= 2
    return masks


def greet(clips, frames):
    clip, frame = lax.axis_index("clip"), lax.axis_index("frame")
    barrier = pltpu.get_barrier_semaphore()
    for step in range(1, clips):
        pl.semaphore_signal(
            barrier, inc=1, device_id={"clip": lax.rem(clip + step, clips)}, device_id_type=MESH
        )
    for step in range(1, frames):
        pl.semaphore_signal(
            barrier, inc=1, device_id={"frame": lax.rem(frame + step, frames)}, device_id_type=MESH
        )
    pl.semaphore_wait(barrier, clips + frames - 2)


def spread(axis, size, source_of, target, send_sems, recv_sems):
    me = lax.axis_index(axis)
    copies = []
    for step in range(1, size):
        peer = lax.rem(me + step, size)
        copy = pltpu.make_async_remote_copy(
            src_ref=source_of(peer),
            dst_ref=target.at[me],
            send_sem=send_sems.at[step - 1],
            recv_sem=recv_sems.at[step - 1],
            device_id={axis: peer},
            device_id_type=MESH,
        )
        copy.start()
        copies.append(copy)
    return copies


def start_kernel(
    clips, frames, clip_count,
    x_ref, cotangent, sq, so, tq, to, sh_u, sh_d, embed, select, ada, bias,
    w_c, w_b, w_u, w_d, mod, chosen, totals, hidden_out, qkv_out, mixed_out, branch_out,
    after_first, after_later, cot_first,
    v_c, z_c, z_b, z_u, z_d, st_w, b_c, b_b, b_u, b_d,
    ada_full, embeds, parts, terms, arrived, held, lined, hidden, qkv, mixed, branch, after,
    zs, zr, cs, cr, xs, xr, ls, es, er, ps, pr, fs, fr, ts, tr, hs, hr, os, ws,
):
    clip, frame = lax.axis_index("clip"), lax.axis_index("frame")
    zoned = (z_c, z_b, z_u, z_d)
    blocks = (b_c, b_b, b_u, b_d)
    wholes = (v_c, w_b, w_u, w_d)
    width = mod.shape[1]
    frame_count, tokens = x_ref.shape[1], x_ref.shape[2]
    part = tokens // frames
    greet(clips, frames)
    masks = frame_masks(frames)
    sends = []
    stage = {}

    def frame_step(group, step):
        number = (1 << step) - 1
        copies = []
        for offset in span(masks[:step]):
            slot = flip(frame, offset)
            copy = pltpu.make_async_remote_copy(
                src_ref=zoned[group].at[slot],
                dst_ref=zoned[group].at[slot],
                send_sem=zs.at[group, number],
                recv_sem=zr.at[group, number],
                device_id={"frame": flip(frame, masks[step])},
                device_id_type=MESH,
            )
            copy.start()
            copies.append(copy)
            number += 1
        sends.extend(copies)
        stage[group] = copies

    def frame_rest(group):
        for step in range(1, len(masks)):
            for copy in stage[group]:
                copy.wait_recv()
            frame_step(group, step)

    tail = clip_tail_masks(clips)
    steps = len(tail)
    orders = (tail, tail[::-1])
    moving = {}

    def block_send(group, half, step, position, offset):
        whole = wholes[group]
        block_rows = whole.shape[0] // clips
        columns = whole.shape[1] // 2
        rows = pl.ds(pl.multiple_of(flip(clip, offset) * block_rows, block_rows), block_rows)
        lanes = pl.ds(half * columns, columns)
        target = whole.at[rows, lanes]
        number = (1 << step) - 1 + position
        copy = pltpu.make_async_remote_copy(
            src_ref=blocks[group].at[:, lanes] if offset == 0 else target,
            dst_ref=target,
            send_sem=xs.at[group, half, number],
            recv_sem=xr.at[group, half, number],
            device_id={"clip": flip(clip, orders[half][step])},
            device_id_type=MESH,
        )
        copy.start()
        moving[group, half, number] = copy

    core_copies = {group: [] for group in range(4)}

    def core_send(group, offset):
        whole = wholes[group]
        block_rows = whole.shape[0] // clips
        rows = pl.ds(pl.multiple_of(flip(clip, offset) * block_rows, block_rows), block_rows)
        number = len(core_copies[group])
        copy = pltpu.make_async_remote_copy(
            src_ref=blocks[group] if offset == 0 else whole.at[rows, :],
            dst_ref=whole.at[rows, :],
            send_sem=cs.at[group, number],
            recv_sem=cr.at[group, number],
            device_id={"clip": flip(clip, 1)},
            device_id_type=MESH,
        )
        copy.start()
        core_copies[group].append(copy)

    local_copies = []

    def block_ready(group):
        for copy in stage[group]:
            copy.wait_recv()
        rows, columns = zoned[group].shape[1:]
        block_rows = frames * rows
        if rows % 16:
            for slot in range(frames):
                st_w[slot * rows : (slot + 1) * rows, :columns] = zoned[group][slot].astype(f32)
            blocks[group][...] = st_w[:block_rows, :columns].astype(bf16)
        else:
            for slot in range(frames):
                blocks[group][slot * rows : (slot + 1) * rows, :] = zoned[group][slot]
        for step in range(steps):
            for half in range(2):
                block_send(group, half, step, 0, 0)
        core_send(group, 0)
        place = pl.ds(pl.multiple_of(clip * block_rows, block_rows), block_rows)
        keep = pltpu.make_async_copy(blocks[group], wholes[group].at[place, :], ls.at[group])
        keep.start()
        local_copies.append(keep)

    def block_forward(group):
        for step in range(1, steps):
            for half in range(2):
                for position in range(1 << (step - 1), 1 << step):
                    moving[group, half, position - 1].wait_recv()
                for later in range(step, steps):
                    for position, offset in enumerate(span(orders[half][:later])):
                        if (1 << (step - 1)) <= position < (1 << step):
                            block_send(group, half, later, position, offset)

    def block_finish(group):
        last = (1 << (steps - 1)) - 1
        for half in range(2):
            for number in range(last, (1 << steps) - 1):
                moving[group, half, number].wait_recv()
        for offset in span(tail)[1:]:
            core_send(group, offset)

    def core_finish(group):
        for copy in core_copies[group]:
            copy.wait_recv()

    for group, first, second in ((0, sq, so), (1, tq, to)):
        zoned[group][frame, :, : 3 * width] = first[...]
        zoned[group][frame, :, 3 * width :] = second[...]
    frame_step(0, 0)
    own = spread("clip", clips, lambda peer: embed, embeds, es, er)
    sends.extend(own)
    embeds[clip] = embed[...]
    z_u[frame] = sh_u[...]
    z_d[frame] = sh_d[...]
    ada_full[...] = jnp.zeros_like(ada_full)
    ada_full[: ada.shape[0], :] = ada[...]
    frame_rest(0)
    for group in range(1, 4):
        frame_step(group, 0)
    cot_copies = []

    def cot_send(index):
        for step in range(frames - 1, 0, -1):
            peer = flip(frame, step)
            copy = pltpu.make_async_remote_copy(
                src_ref=cotangent.at[0, index, pl.ds(pl.multiple_of(peer * part, part), part), :],
                dst_ref=cot_first.at[frame, index],
                send_sem=ts.at[index, step - 1],
                recv_sem=tr.at[index, step - 1],
                device_id={"frame": peer},
                device_id_type=MESH,
            )
            copy.start()
            cot_copies.append(copy)

    cot_send(0)
    for copy in own:
        copy.wait_recv()
    picked = dot(embeds[...].reshape(clips * 16, width), select[...], 1, 0).astype(bf16)
    chosen[...] = picked
    parts[...] = dot(picked, ada_full[...], 1, 0)
    for peer in range(clips):
        for local in range(clip_count):
            row = peer * 16 + local
            for piece in range(9):
                terms[peer, local * 9 + piece : local * 9 + piece + 1, :] = (
                    parts[row : row + 1, piece * width : (piece + 1) * width]
                    + bias[piece : piece + 1, :]
                )
        base = clip_count * 9
        terms[peer, base : base + 7, :] = bias[9:16, :]
        if base + 7 < ROWS:
            terms[peer, base + 7 : ROWS, :] = jnp.zeros((ROWS - base - 7, width), f32)
    own = spread("clip", clips, lambda peer: terms.at[peer], arrived, ps, pr)
    sends.extend(own)
    arrived[clip] = terms[clip]
    block_ready(0)
    for copy in own:
        copy.wait_recv()
    total = arrived[0]
    for peer in range(1, clips):
        total = total + arrived[peer]
    held[...] = total
    own = spread("frame", frames, lambda peer: held, lined, fs, fr)
    sends.extend(own)
    lined[frame] = total
    for group in range(1, 4):
        frame_rest(group)

    for index in range(1, frame_count):
        cot_send(index)
    keep = pltpu.make_async_copy(
        cotangent.at[0, :, pl.ds(pl.multiple_of(frame * part, part), part), :],
        cot_first.at[frame],
        ls.at[4],
    )
    keep.start()
    local_copies.append(keep)

    for copy in own:
        copy.wait_recv()
    total = lined[0]
    for peer in range(1, frames):
        total = total + lined[peer]
    mod[...] = total
    block_forward(0)
    for group in range(1, 4):
        block_ready(group)
    block_finish(0)
    core_finish(0)
    local_copies[0].wait()

    keep = pltpu.make_async_copy(v_c, w_c, ls.at[5])
    keep.start()
    local_copies.append(keep)

    def after_copy(f, step):
        peer = flip(frame, step)
        return pltpu.make_async_remote_copy(
            src_ref=after.at[f, pl.ds(pl.multiple_of(peer * part, part), part), :],
            dst_ref=after_first.at[frame, f],
            send_sem=hs.at[f, step - 1],
            recv_sem=hr.at[f, step - 1],
            device_id={"frame": peer},
            device_id_type=MESH,
        )

    def own_after(f):
        return pltpu.make_async_copy(
            after.at[f, pl.ds(pl.multiple_of(frame * part, part), part), :],
            after_first.at[frame, f],
            os.at[f],
        )

    def later_after(f):
        return pltpu.make_async_copy(after.at[f], after_later.at[f - frame_count], os.at[f])

    kept = ((hidden, hidden_out), (qkv, qkv_out), (mixed, mixed_out), (branch, branch_out))

    def write_back(f):
        return [
            pltpu.make_async_copy(source.at[f], target.at[f], ws.at[number, f])
            for number, (source, target) in enumerate(kept)
        ]

    for local in range(clip_count):
        row = local * 9

        def one_frame(index, carry):
            f = local * frame_count + index
            values = x_ref[local, index].astype(f32)
            norm, _ = normed(values)
            scaled = norm * (1.0 + mod[row + 1 : row + 2, :]) + mod[row : row + 1, :]
            lowered = scaled.astype(bf16)
            hidden[f] = lowered
            qkv[f] = dot(lowered, v_c[:, : 3 * width], 1, 0).astype(bf16)
            attend(qkv.at[f], mixed.at[f], totals.at[f], width, None)
            grown = dot(mixed[f], v_c[:, 3 * width :], 1, 0) + mod[18:19, :]
            branch[f] = grown.astype(bf16)
            after[f] = (values + mod[row + 2 : row + 3, :] * grown).astype(bf16)
            if local == 0:
                for step in range(frames - 1, 0, -1):
                    after_copy(f, step).start()
                own_after(f).start()
            else:
                later_after(f).start()
            for copy in write_back(f):
                copy.start()
            return carry

        lax.fori_loop(0, frame_count, one_frame, 0)
        if local == 0:
            block_forward(1)
    for group in range(2, 4):
        block_forward(group)
    for group in range(1, 4):
        block_finish(group)
    for group in range(1, 4):
        core_finish(group)

    def settle(f, carry):
        for step in range(1, frames):
            copy = after_copy(f, step)
            copy.wait_recv()
            copy.wait_send()
        own_after(f).wait()
        return carry

    lax.fori_loop(0, frame_count, settle, 0)

    def settle_later(f, carry):
        later_after(f).wait()
        return carry

    lax.fori_loop(frame_count, clip_count * frame_count, settle_later, 0)

    def settle_kept(f, carry):
        for copy in write_back(f):
            copy.wait()
        return carry

    lax.fori_loop(0, clip_count * frame_count, settle_kept, 0)
    for copy in cot_copies:
        copy.wait_recv()
        copy.wait_send()
    for copy in local_copies[1:]:
        copy.wait()
    for copy in moving.values():
        copy.wait_send()
    for group in range(4):
        for copy in core_copies[group]:
            copy.wait_send()
    for copy in sends:
        copy.wait_send()


def start_call(
    clips, frames, inputs, cotangent, sq, so, tq, to, sh_u, sh_d, embed, select, ada, bias
):
    clip_count, frame_count, tokens, width = inputs.shape
    rows, columns = sh_u.shape
    rows_d = sh_d.shape[0]
    block = frames * rows
    block_d = frames * rows_d
    peers = max(clips // 2 - 1, 1)
    total = clip_count * frame_count
    part = tokens // frames
    whole = jax.ShapeDtypeStruct((clips * block, columns), bf16)
    vmem = pl.BlockSpec(memory_space=VMEM)
    hbm = pl.BlockSpec(memory_space=pl.ANY)
    zoned = lambda height, lanes: VMEM((frames, height, lanes), bf16)
    saved = lambda lanes: jax.ShapeDtypeStruct((total, tokens, lanes), bf16)
    lent = lambda lanes: VMEM((total, tokens, lanes), bf16)
    traded = jax.ShapeDtypeStruct((frames, frame_count, part, width), bf16)
    return pl.pallas_call(
        functools.partial(start_kernel, clips, frames, clip_count),
        out_shape=(
            whole, whole, whole,
            jax.ShapeDtypeStruct((clips * block_d, width), bf16),
            jax.ShapeDtypeStruct((ROWS, width), f32),
            jax.ShapeDtypeStruct((clips * 16, 128), bf16),
            jax.ShapeDtypeStruct((total, 16, tokens), f32),
            saved(width), saved(3 * width), saved(width), saved(width),
            traded,
            jax.ShapeDtypeStruct(((clip_count - 1) * frame_count, tokens, width), bf16),
            traded,
        ),
        in_specs=[vmem, hbm] + [vmem] * 10,
        out_specs=(hbm, hbm, hbm, hbm, vmem, vmem, vmem) + (hbm,) * 7,
        scratch_shapes=[
            VMEM((clips * block, columns), bf16),
            zoned(rows, columns), zoned(rows, columns), zoned(rows, columns), zoned(rows_d, width),
            VMEM((max(block, block_d), columns), f32),
            VMEM((block, columns), bf16),
            VMEM((block, columns), bf16),
            VMEM((block, columns), bf16),
            VMEM((block_d, width), bf16),
            VMEM((128, 9 * width), bf16),
            VMEM((clips, 16, width), bf16),
            VMEM((clips * 16, 9 * width), f32),
            VMEM((clips, ROWS, width), f32),
            VMEM((clips, ROWS, width), f32),
            VMEM((ROWS, width), f32),
            VMEM((frames, ROWS, width), f32),
            lent(width), lent(3 * width), lent(width), lent(width), lent(width),
            DMA((4, frames - 1)), DMA((4, frames - 1)),
            DMA((4, clips // 2)), DMA((4, clips // 2)),
            DMA((4, 2, peers)), DMA((4, 2, peers)),
            DMA((6,)),
            DMA((clips - 1,)), DMA((clips - 1,)),
            DMA((clips - 1,)), DMA((clips - 1,)),
            DMA((frames - 1,)), DMA((frames - 1,)),
            DMA((frame_count, frames - 1)), DMA((frame_count, frames - 1)),
            DMA((frame_count, frames - 1)), DMA((frame_count, frames - 1)),
            DMA((total,)),
            DMA((4, total)),
        ],
        compiler_params=pltpu.CompilerParams(
            collective_id=0, has_side_effects=True, vmem_limit_bytes=VMEM_LIMIT
        ),
    )(inputs, cotangent, sq, so, tq, to, sh_u, sh_d, embed, select, ada, bias)


STEP = 512
SLOTS = 3


def grad_kernel(
    clips, frames, clip_count,
    small, chosen, out_all, h3, gup, act, gb3, h2, gqkv2, mix2, gb2, h1, gqkv1, mix1, gb1,
    outputs, grad_ada, bias_sums, out_u, out_d, out_b, out_bo, out_c, out_co,
    sum_w, sum_d, core_w, core_d, side_w, side_d, line_w, line_d, last_w, last_d,
    left, right, total, gathered, lined, held,
    lsem, rsem, cs, cr, xs, xr, zs, zr, fs, fr, ps, pr, os, orr, ks,
):
    clip, frame = lax.axis_index("clip"), lax.axis_index("frame")
    tokens = h3.shape[0]
    width = small.shape[1]
    wide = sum_w.shape[-1]
    narrow = sum_d.shape[-1]
    tail = clip_tail_masks(clips)
    orders = (tail, tail[::-1])
    masks = frame_masks(frames)
    greet(clips, frames)
    first = spread("frame", frames, lambda peer: small, lined, fs, fr)
    lined[frame] = small[...]
    part = out_all.shape[3]
    frame_count = out_all.shape[2]
    out_copies = []
    mine = pl.ds(pl.multiple_of(frame * part, part), part)

    def send_output(number):
        local, index = divmod(number, frame_count)
        for hop in range(frames - 1, 0, -1):
            peer = flip(frame, hop)
            copy = pltpu.make_async_remote_copy(
                src_ref=out_all.at[local, peer, index],
                dst_ref=outputs.at[local, index, mine, :],
                send_sem=os.at[number, hop - 1],
                recv_sem=orr.at[number, hop - 1],
                device_id={"frame": peer},
                device_id_type=MESH,
            )
            copy.start()
            out_copies.append(copy)

    own_outs = []
    for local in range(clip_count):
        copy = pltpu.make_async_copy(
            out_all.at[local, frame], outputs.at[local, :, mine, :], ks.at[local]
        )
        copy.start()
        own_outs.append(copy)

    chunks = [
        (1, 0, [(act, gb3, 0, 0, narrow)], out_d, 0),
        (1, 1, [(act, gb3, narrow, 0, narrow)], out_d, narrow),
        (0, 0, [(h3, gup, 0, 0, wide)], out_u, 0),
        (0, 1, [(h3, gup, wide, 0, wide)], out_u, wide),
        (0, 2, [(h2, gqkv2, 0, 0, wide)], out_b, 0),
        (0, 3, [(h2, gqkv2, wide, 0, width), (mix2, gb2, 0, width, width)], out_b, wide),
        (0, 4, [(h1, gqkv1, 0, 0, wide)], out_c, 0),
        (0, 5, [(h1, gqkv1, wide, 0, width), (mix1, gb1, 0, width, width)], out_c, wide),
    ]
    sums, cores, sides = (sum_w, sum_d), (core_w, core_d), (side_w, side_d)
    lines, lasts = (line_w, line_d), (last_w, last_d)
    flights = {}

    steps = tokens // STEP
    line_up = []
    for kind, _, parts, _, _ in chunks:
        for part in parts:
            for group in range(part[0].shape[1] // width):
                line_up.append(part[:3] + (part[3] + group * part[4], part[4], group))
    begins = [0]
    for kind, _, parts, _, _ in chunks:
        begins.append(begins[-1] + sum(part[0].shape[1] // width for part in parts))

    def load(entry, step, slot):
        one, other, begin, _, lanes, group = line_up[entry]
        rows = pl.ds(pl.multiple_of(step * STEP, STEP), STEP)
        return (
            pltpu.make_async_copy(
                one.at[rows, pl.ds(group * width, width)], left.at[slot], lsem.at[slot]
            ),
            pltpu.make_async_copy(
                other.at[rows, pl.ds(begin, lanes)],
                right.at[slot, :, pl.ds(0, lanes)],
                rsem.at[slot],
            ),
        )

    def place_of(entry, step):
        return lax.rem(entry * steps + step, SLOTS)

    def multiply(number):
        kind, place = chunks[number][:2]
        for entry in range(begins[number], begins[number + 1]):
            at, lanes = line_up[entry][3:5]

            def body(step, carry):
                ahead = step + SLOTS - 1

                @pl.when(ahead < steps)
                def _():
                    for copy in load(entry, ahead, place_of(entry, ahead)):
                        copy.start()

                if entry + 1 < len(line_up):

                    @pl.when(ahead >= steps)
                    def _():
                        for copy in load(entry + 1, ahead - steps, place_of(entry, ahead)):
                            copy.start()

                slot = place_of(entry, step)
                for copy in load(entry, step, slot):
                    copy.wait()
                columns = slice(at, at + lanes)
                before = jnp.where(step > 0, total[:, columns], 0.0)
                total[:, columns] = before + dot(left[slot], right[slot, :, :lanes], 0, 0)
                return carry

            lax.fori_loop(0, steps, body, 0)
        rows, lanes = sums[kind].shape[2:]
        for block in range(clips):
            begin = block * rows
            column = begin // width * lanes
            begin = begin % width
            sums[kind][place, block] = total[begin : begin + rows, column : column + lanes].astype(
                bf16
            )

    def core_start(number):
        kind, place = chunks[number][:2]
        copies = []
        for position, offset in enumerate(span(tail)):
            copy = pltpu.make_async_remote_copy(
                src_ref=sums[kind].at[place, flip(clip, offset ^ 1)],
                dst_ref=cores[kind].at[place, position],
                send_sem=cs.at[number, position],
                recv_sem=cr.at[number, position],
                device_id={"clip": flip(clip, 1)},
                device_id_type=MESH,
            )
            copy.start()
            copies.append(copy)
        flights[number, "core"] = copies

    def half_of(kind, half):
        if kind:
            rows = sums[kind].shape[2] // 2
            return (slice(half * rows, (half + 1) * rows), slice(None))
        lanes = sums[kind].shape[3] // 2
        return (slice(None), slice(half * lanes, (half + 1) * lanes))

    def side_start(number, step):
        kind, place = chunks[number][:2]
        copies = []
        for half in range(2):
            mask = orders[half][step]
            for position, offset in enumerate(span(orders[half][:step])):
                entry = (1 << step) - 1 + position
                copy = pltpu.make_async_remote_copy(
                    src_ref=sums[kind].at[(place, flip(clip, offset ^ mask)) + half_of(kind, half)],
                    dst_ref=sides[kind].at[place, half, entry],
                    send_sem=xs.at[number, half, entry],
                    recv_sem=xr.at[number, half, entry],
                    device_id={"clip": flip(clip, mask)},
                    device_id_type=MESH,
                )
                copy.start()
                copies.append(copy)
        flights[number, "side", step] = copies

    def core_add(number):
        kind, place = chunks[number][:2]
        for copy in flights[number, "core"]:
            copy.wait_recv()
        for position, offset in enumerate(span(tail)):
            block = flip(clip, offset)
            sums[kind][place, block] = (
                sums[kind][place, block].astype(f32) + cores[kind][place, position].astype(f32)
            ).astype(bf16)
        side_start(number, len(tail) - 1)

    def side_add(number, step):
        kind, place = chunks[number][:2]
        for copy in flights[number, "side", step]:
            copy.wait_recv()
        for half in range(2):
            for position, offset in enumerate(span(orders[half][:step])):
                entry = (1 << step) - 1 + position
                block = flip(clip, offset)
                where = (place, block) + half_of(kind, half)
                sums[kind][where] = (
                    sums[kind][where].astype(f32) + sides[kind][place, half, entry].astype(f32)
                ).astype(bf16)
        if step:
            side_start(number, step - 1)
        else:
            rows = lines[kind].shape[2]
            block = sums[kind][place, clip].astype(f32)
            for slot in range(frames):
                lines[kind][place, slot] = block[slot * rows : (slot + 1) * rows, :].astype(bf16)
            line_start(number, len(masks) - 1)

    def line_start(number, step):
        kind, place = chunks[number][:2]
        copies = []
        for position, offset in enumerate(span(masks[:step])):
            entry = (1 << step) - 1 + position
            copy = pltpu.make_async_remote_copy(
                src_ref=lines[kind].at[place, flip(frame, offset ^ masks[step])],
                dst_ref=lasts[kind].at[place, entry],
                send_sem=zs.at[number, entry],
                recv_sem=zr.at[number, entry],
                device_id={"frame": flip(frame, masks[step])},
                device_id_type=MESH,
            )
            copy.start()
            copies.append(copy)
        flights[number, "line", step] = copies

    def line_add(number, step):
        kind, place, _, target, begin = chunks[number]
        for copy in flights[number, "line", step]:
            copy.wait_recv()
        for position, offset in enumerate(span(masks[:step])):
            entry = (1 << step) - 1 + position
            slot = flip(frame, offset)
            value = lines[kind][place, slot].astype(f32) + lasts[kind][place, entry].astype(f32)
            if step:
                lines[kind][place, slot] = value.astype(bf16)
            elif begin + value.shape[1] > target.shape[1]:
                cut = target.shape[1] - begin
                target[:, begin:] = value[:, :cut]
                (out_bo if target is out_b else out_co)[...] = value[:, cut:]
            else:
                target[:, begin : begin + value.shape[1]] = value
        if step:
            line_start(number, step - 1)

    stages = [core_start, core_add]
    for step in range(len(tail))[::-1]:
        stages.append(functools.partial(side_add, step=step))
    for step in range(len(masks))[::-1]:
        stages.append(functools.partial(line_add, step=step))

    def finish_small():
        for copy in second:
            copy.wait_recv()
        rows = grad_ada.shape[0]
        for number in range(9):
            terms = [
                gathered[peer, local * 9 + number : local * 9 + number + 1, :]
                for peer in range(clips)
                for local in range(clip_count)
            ]
            terms = jnp.concatenate(terms, axis=0)
            grad_ada[:, number * width : (number + 1) * width] = lax.dot_general(
                chosen[...], terms, (((1,), (0,)), ((), ())), precision=highest,
                preferred_element_type=f32,
            )[:rows, :]
            bias_sums[number : number + 1, :] = column_sum(terms)
        base = clip_count * 9
        summed = gathered[0, base : base + 7, :]
        for peer in range(1, clips):
            summed = summed + gathered[peer, base : base + 7, :]
        bias_sums[9:16, :] = summed

    for step in range(SLOTS - 1):
        for copy in load(0, step, step):
            copy.start()
    second = None
    lags = [0, 1, 3]
    while len(lags) < len(stages):
        lags.append(lags[-1] + 1)
    for turn in range(len(chunks) + lags[-1]):
        for depth in range(len(stages))[::-1]:
            if depth > 0 and 0 <= turn - lags[depth] < len(chunks):
                stages[depth](turn - lags[depth])
        if turn < clip_count * frame_count:
            send_output(turn)
        if turn < len(chunks):
            multiply(turn)
            core_start(turn)
        if turn == len(chunks):
            finish_small()
        if turn == 0:
            for copy in first:
                copy.wait_recv()
            summed = lined[0]
            for peer in range(1, frames):
                summed = summed + lined[peer]
            held[...] = summed
            second = spread("clip", clips, lambda peer: held, gathered, ps, pr)
            gathered[clip] = summed
    for copy in own_outs:
        copy.wait()
    for copy in out_copies:
        copy.wait_recv()
        copy.wait_send()
    for copy in first + second:
        copy.wait_send()
    for copies in flights.values():
        for copy in copies:
            copy.wait_send()


def grad_call(clips, frames, clip_count, small, chosen, out_all, *operands):
    h3, gup, act = operands[:3]
    _, _, frame_count, part, _ = out_all.shape
    width, hidden = h3.shape[1], act.shape[1]
    owners = clips * frames
    wide, narrow = hidden // 2, width // 2
    rows_w, rows_d = width // owners, hidden // owners
    peers = max(clips // 2 - 1, 1)
    vmem = pl.BlockSpec(memory_space=VMEM)
    hbm = pl.BlockSpec(memory_space=pl.ANY)

    return pl.pallas_call(
        functools.partial(grad_kernel, clips, frames, clip_count),
        out_shape=(
            jax.ShapeDtypeStruct((clip_count, frame_count, frames * part, width), bf16),
            jax.ShapeDtypeStruct((rows_w, 9 * width), f32),
            jax.ShapeDtypeStruct((16, width), f32),
            jax.ShapeDtypeStruct((rows_w, hidden), f32),
            jax.ShapeDtypeStruct((rows_d, width), f32),
            jax.ShapeDtypeStruct((rows_w, 3 * width), f32),
            jax.ShapeDtypeStruct((rows_w, width), f32),
            jax.ShapeDtypeStruct((rows_w, 3 * width), f32),
            jax.ShapeDtypeStruct((rows_w, width), f32),
        ),
        in_specs=[vmem, vmem] + [hbm] * (1 + len(operands)),
        out_specs=(hbm,) + (vmem,) * 8,
        scratch_shapes=[
            VMEM((6, clips, rows_w * frames, wide), bf16),
            VMEM((2, clips, rows_d * frames, narrow), bf16),
            VMEM((6, clips // 2, rows_w * frames, wide), bf16),
            VMEM((2, clips // 2, rows_d * frames, narrow), bf16),
            VMEM((6, 2, peers, rows_w * frames, wide // 2), bf16),
            VMEM((2, 2, peers, rows_d * frames // 2, narrow), bf16),
            VMEM((6, frames, rows_w, wide), bf16),
            VMEM((2, frames, rows_d, narrow), bf16),
            VMEM((6, frames - 1, rows_w, wide), bf16),
            VMEM((2, frames - 1, rows_d, narrow), bf16),
            VMEM((SLOTS, STEP, width), bf16),
            VMEM((SLOTS, STEP, wide), bf16),
            VMEM((width, wide), f32),
            VMEM((clips,) + small.shape, f32),
            VMEM((frames,) + small.shape, f32),
            VMEM(small.shape, f32),
            DMA((SLOTS,)), DMA((SLOTS,)),
            DMA((8, clips // 2)), DMA((8, clips // 2)),
            DMA((8, 2, peers)), DMA((8, 2, peers)),
            DMA((8, frames - 1)), DMA((8, frames - 1)),
            DMA((frames - 1,)), DMA((frames - 1,)),
            DMA((clips - 1,)), DMA((clips - 1,)),
            DMA((clip_count * frame_count, frames - 1)),
            DMA((clip_count * frame_count, frames - 1)),
            DMA((clip_count,)),
        ],
        compiler_params=pltpu.CompilerParams(
            collective_id=1, has_side_effects=True, vmem_limit_bytes=VMEM_LIMIT
        ),
    )(small, chosen, out_all, *operands)


def normed(values):
    centred = values - jnp.mean(values, axis=-1, keepdims=True)
    scale = lax.rsqrt(jnp.mean(centred * centred, axis=-1, keepdims=True) + 1e-06)
    return centred * scale, scale


def norm_back(grad, scaled, norm, scale):
    inner = grad * scaled
    return scale * (
        inner
        - jnp.mean(inner, axis=-1, keepdims=True)
        - norm * jnp.mean(inner * norm, axis=-1, keepdims=True)
    )


def column_sum(values):
    return jnp.sum(values, axis=0, keepdims=True)


def head_lanes(tokens):
    lane = lax.broadcasted_iota(jnp.int32, (tokens, GROUP * HEAD), 1)
    return [(lane >= HEAD * head) & (lane < HEAD * (head + 1)) for head in range(GROUP)]


def stacked(values, picks):
    return jnp.concatenate([jnp.where(pick, values, bf16(0)) for pick in picks], axis=0)


def unstacked(values, picks, tokens):
    result = values[(GROUP - 1) * tokens :]
    for head in range(GROUP - 1):
        result = jnp.where(picks[head], values[head * tokens : (head + 1) * tokens], result)
    return result


def masked_scores(keys, own, mask):
    scores = dot(keys, own, 1, 1)
    if mask is not None:
        scores = scores + jnp.concatenate([mask[...]] * GROUP, axis=1)
    return scores


def attend(qkv, mixed, totals, width, mask):
    tokens = qkv.shape[0]
    lanes = GROUP * HEAD
    picks = head_lanes(tokens)
    for group in range(HEADS // GROUP):
        at = group * lanes
        own = stacked(qkv[:, at : at + lanes] * bf16(0.125), picks)
        keys = qkv[:, width + at : width + at + lanes]
        values = qkv[:, 2 * width + at : 2 * width + at + lanes]
        scores = masked_scores(keys, own, mask)
        peak = jnp.max(scores, axis=0, keepdims=True)
        terms = jnp.exp(scores - peak)
        total = jnp.sum(terms, axis=0, keepdims=True)
        weights = (terms * (1.0 / total)).astype(bf16)
        logs = peak + jnp.log(total)
        for head in range(GROUP):
            row = group * GROUP + head
            totals[row : row + 1, :] = logs[:, head * tokens : (head + 1) * tokens]
        result = unstacked(dot(weights, values, 0, 0), picks, tokens)
        mixed[:, at : at + lanes] = result.astype(bf16)


def attend_back(qkv, grad_mixed, totals, grad_qkv, width, mask):
    tokens = qkv.shape[0]
    lanes = GROUP * HEAD
    picks = head_lanes(tokens)
    for group in range(HEADS // GROUP):
        at = group * lanes
        own = stacked(qkv[:, at : at + lanes] * bf16(0.125), picks)
        keys = qkv[:, width + at : width + at + lanes]
        values = qkv[:, 2 * width + at : 2 * width + at + lanes]
        own_grads = stacked(grad_mixed[:, at : at + lanes], picks)
        logs = jnp.concatenate(
            [totals[group * GROUP + head : group * GROUP + head + 1, :] for head in range(GROUP)],
            axis=1,
        )
        weights = jnp.exp(masked_scores(keys, own, mask) - logs)
        grad_weights = dot(values, own_grads, 1, 1)
        inner = jnp.sum(weights * grad_weights, axis=0, keepdims=True)
        grad_scores = (weights * (grad_weights - inner)).astype(bf16)
        grad_queries = unstacked(dot(grad_scores, keys, 0, 0), picks, tokens) * 0.125
        grad_keys = dot(grad_scores, own, 1, 0)
        grad_values = dot(weights.astype(bf16), own_grads, 1, 0)
        for part, grad in enumerate((grad_queries, grad_keys, grad_values)):
            start = part * width + at
            grad_qkv[:, start : start + lanes] = grad.astype(bf16)


def full(shape):
    return pl.BlockSpec(shape, lambda *_: (0,) * len(shape), pipeline_mode=pl.Buffered(1))


def middle_kernel(
    clips, frames, tiles,
    after_first, cot_first, after_later, cotangent, loss, mod, w_b, w_u, w_d,
    act_ref, gup_ref, h3_ref, gb3_ref, mixed_ref, gb2_ref, h2_ref, gqkv_ref, sums,
    after_second, cot_second, grad_first, grad_second, grad_later, out_all,
    qkv, totals, mask, gmix, after_tile, cot_tile, grad_stage, out_stage,
    ts, tr, us, ur, gs, gr, hs, hr, ls, ks, ws,
):
    frame = lax.axis_index("frame")
    step = pl.program_id(0)
    last = pl.num_programs(0) - 1
    clip = lax.div(step, tiles)
    tile = lax.rem(step, tiles)
    slot = lax.rem(step, 2)
    width = mod.shape[1]
    frame_count, group = after_tile.shape[2], after_tile.shape[3]
    part = tiles * group
    tokens = frames * frame_count * group
    row = clip * 9
    piece = lambda number: mod[pl.ds(row + number, 1), :]

    def own_part(index):
        return pl.ds(pl.multiple_of(index * part, part), part)

    def later_copies(number):
        copies = []
        for hop in range(frames - 1, 0, -1):
            peer = flip(frame, hop)
            if number:
                source, target, send, recv = cotangent.at[1, :, own_part(peer), :], cot_second, us, ur
            else:
                source, target, send, recv = after_later.at[:, own_part(peer), :], after_second, ts, tr
            copies.append(
                pltpu.make_async_remote_copy(
                    src_ref=source,
                    dst_ref=target.at[frame],
                    send_sem=send.at[hop - 1],
                    recv_sem=recv.at[hop - 1],
                    device_id={"frame": peer},
                    device_id_type=MESH,
                )
            )
        return copies

    def own_copy(number):
        source = cotangent.at[1] if number else after_later
        target = cot_second if number else after_second
        return pltpu.make_async_copy(
            source.at[:, own_part(frame), :], target.at[frame], ks.at[number]
        )

    def load(source, number, index, place):
        rows = pl.ds(pl.multiple_of(index * group, group), group)
        target = (after_tile, cot_tile)[number].at[place]
        return pltpu.make_async_copy(source.at[:, :, rows, :], target, ls.at[place, number])

    early = tiles // 4

    def grad_copies(index, later=False):
        place = index + tiles if later else index
        target, send, recv = (grad_second, hs, hr) if later else (grad_first, gs, gr)
        rows = pl.ds(pl.multiple_of(index * group, group), group)
        copies = []
        for hop in range(frames - 1, 0, -1):
            peer = flip(frame, hop)
            copies.append(
                pltpu.make_async_remote_copy(
                    src_ref=grad_stage.at[place, peer],
                    dst_ref=target.at[frame, :, rows, :],
                    send_sem=send.at[index, hop - 1],
                    recv_sem=recv.at[index, hop - 1],
                    device_id={"frame": peer},
                    device_id_type=MESH,
                )
            )
        return copies

    def grad_own(index, later=False):
        place = index + tiles if later else index
        target = grad_second if later else grad_first
        rows = pl.ds(pl.multiple_of(index * group, group), group)
        return pltpu.make_async_copy(
            grad_stage.at[place, frame], target.at[frame, :, rows, :], ws.at[0, place]
        )

    def grad_keep(index):
        place = index + tiles
        rows = pl.ds(pl.multiple_of((index - early) * group, group), group)
        return pltpu.make_async_copy(
            grad_stage.at[place], grad_later.at[:, :, rows, :], ws.at[0, place]
        )

    def out_keep(number):
        rows = pl.ds(pl.multiple_of(lax.rem(number, tiles) * group, group), group)
        return pltpu.make_async_copy(
            out_stage.at[number], out_all.at[lax.div(number, tiles), :, :, rows, :], ws.at[1, number]
        )

    @pl.when(step == 0)
    def _():
        barrier = pltpu.get_barrier_semaphore()
        for hop in range(1, frames):
            pl.semaphore_signal(
                barrier,
                inc=1,
                device_id={"frame": lax.rem(frame + hop, frames)},
                device_id_type=MESH,
            )
        pl.semaphore_wait(barrier, frames - 1)
        load(after_first, 0, 0, 0).start()
        load(cot_first, 1, 0, 0).start()
        for number in range(2):
            for copy in later_copies(number):
                copy.start()
            own_copy(number).start()
        first = lax.broadcasted_iota(jnp.int32, (tokens, tokens), 0)
        second = lax.broadcasted_iota(jnp.int32, (tokens, tokens), 1)
        mask[...] = jnp.where(lax.rem(first, group) == lax.rem(second, group), 0.0, -1e30)

    @pl.when(step == tiles)
    def _():
        for copy in later_copies(0):
            copy.wait_recv()
        own_copy(0).wait()
        load(after_second, 0, 0, slot).start()

    load(after_first, 0, 0, slot).wait()

    @pl.when(step + 1 < tiles)
    def _():
        load(after_first, 0, step + 1, 1 - slot).start()
        load(cot_first, 1, step + 1, 1 - slot).start()

    @pl.when((step >= tiles) & (step < last))
    def _():
        load(after_second, 0, tile + 1, 1 - slot).start()

    @pl.when((step > tiles) & (step < last))
    def _():
        load(cot_second, 1, tile + 1, 1 - slot).start()

    @pl.when(tile == 0)
    def _():
        sums[...] = jnp.zeros_like(sums)

    def add(place, values):
        sums[place : place + 1, :] += values

    after = after_tile[slot].reshape(tokens, width).astype(f32)
    norm, scale = normed(after)
    hidden = (norm * (1.0 + piece(4)) + piece(3)).astype(bf16)
    h2_ref[...] = hidden
    qkv[...] = dot(hidden, w_b[:, : 3 * width], 1, 0).astype(bf16)
    attend(qkv, mixed_ref, totals, width, mask)
    branch_two = dot(mixed_ref[...], w_b[:, 3 * width :], 1, 0) + mod[19:20, :]
    after_two = after + piece(5) * branch_two
    norm_three, scale_three = normed(after_two)
    hidden = (norm_three * (1.0 + piece(7)) + piece(6)).astype(bf16)
    h3_ref[...] = hidden

    @pl.when(step == tiles)
    def _():
        for copy in later_copies(1):
            copy.wait_recv()
        own_copy(1).wait()
        load(cot_second, 1, 0, slot).start()
        if tiles > 1:
            load(cot_second, 1, 1, 1 - slot).start()

        def send(index, carry):
            for copy in grad_copies(index):
                copy.start()
            return carry

        lax.fori_loop(0, tiles, send, 0)

    load(cot_first, 1, 0, slot).wait()
    grad_out = cot_tile[slot].reshape(tokens, width).astype(f32) * loss[pl.ds(clip, 1), :]
    grad_branch = (grad_out * piece(8)).astype(bf16)
    gb3_ref[...] = grad_branch
    add(11, column_sum(grad_branch.astype(f32)))
    branch_three = jnp.zeros((tokens, width), f32)
    grad_hidden = jnp.zeros((tokens, width), f32)
    for chunk in range(w_u.shape[1] // width):
        cut = slice(chunk * width, (chunk + 1) * width)
        upper = dot(hidden, w_u[:, cut], 1, 0) + mod[20 + chunk : 21 + chunk, :]
        square = upper * upper
        bend = jnp.tanh(upper * (GELU_C + (GELU_C * GELU_A) * square))
        half = 0.5 + 0.5 * bend
        act = (upper * half).astype(bf16)
        slope = half + (0.5 * upper) * (1.0 - bend * bend) * (
            GELU_C + (3.0 * GELU_C * GELU_A) * square
        )
        act_ref[:, cut] = act
        branch_three += dot(act, w_d[cut, :], 1, 0)
        grad_upper = (dot(grad_branch, w_d[cut, :], 1, 1) * slope).astype(bf16)
        gup_ref[:, cut] = grad_upper
        add(7 + chunk, column_sum(grad_upper.astype(f32)))
        grad_hidden += dot(grad_upper, w_u[:, cut], 1, 1)
    branch_three += mod[24:25, :]
    out = (after_two + piece(8) * branch_three).astype(bf16)
    out_stage[step] = out.reshape(out_stage.shape[1:])
    add(5, column_sum(grad_out * branch_three))
    add(3, column_sum(grad_hidden))
    add(4, column_sum(grad_hidden * norm_three))
    grad_two = grad_out + norm_back(grad_hidden, 1.0 + piece(7), norm_three, scale_three)
    add(2, column_sum(grad_two * branch_two))
    grad_branch = (grad_two * piece(5)).astype(bf16)
    gb2_ref[...] = grad_branch
    add(6, column_sum(grad_branch.astype(f32)))
    gmix[...] = dot(grad_branch, w_b[:, 3 * width :], 1, 1).astype(bf16)
    attend_back(qkv, gmix, totals, gqkv_ref, width, mask)
    grad_hidden = dot(gqkv_ref[...], w_b[:, : 3 * width], 1, 1).astype(bf16).astype(f32)
    add(0, column_sum(grad_hidden))
    add(1, column_sum(grad_hidden * norm))
    grad_one = grad_two + norm_back(grad_hidden, 1.0 + piece(4), norm, scale)
    grad_stage[step] = grad_one.astype(bf16).reshape(grad_stage.shape[1:])

    out_keep(step).start()

    @pl.when(step < tiles)
    def _():
        grad_own(tile).start()

    if early:

        @pl.when((step >= tiles) & (tile < early))
        def _():
            for copy in grad_copies(tile, True):
                copy.start()
            grad_own(tile, True).start()

    @pl.when((step >= tiles) & (tile >= early))
    def _():
        grad_keep(tile).start()

    @pl.when(step == last)
    def _():
        for copy in later_copies(0) + later_copies(1):
            copy.wait_send()

        def settle(index, carry):
            for copy in grad_copies(index):
                copy.wait_send()
                copy.wait_recv()
            grad_own(index).wait()
            out_keep(index).wait()
            out_keep(index + tiles).wait()
            return carry

        lax.fori_loop(0, tiles, settle, 0)

        def settle_early(index, carry):
            for copy in grad_copies(index, True):
                copy.wait_send()
                copy.wait_recv()
            grad_own(index, True).wait()
            return carry

        if early:
            lax.fori_loop(0, early, settle_early, 0)

        def settle_kept(index, carry):
            grad_keep(index).wait()
            return carry

        lax.fori_loop(early, tiles, settle_kept, 0)


def middle_call(
    clips, frames, after_first, cot_first, after_later, cotangent, loss, mod, w_b, w_u, w_d
):
    _, frame_count, part, width = after_first.shape
    group = min(16, part)
    tiles = part // group
    tokens = frames * frame_count * group
    hidden_width = w_u.shape[1]
    widths = (hidden_width, hidden_width, width, width, width, width, width, 3 * width)
    own = lambda columns: pl.BlockSpec((tokens, columns), lambda t: (t, 0))
    hbm = pl.BlockSpec(memory_space=pl.ANY)
    rows = 2 * tiles * tokens
    traded = jax.ShapeDtypeStruct(after_first.shape, bf16)
    slab = (frames, frame_count, group, width)
    return pl.pallas_call(
        functools.partial(middle_kernel, clips, frames, tiles),
        grid=(2 * tiles,),
        in_specs=[
            hbm, hbm, hbm, hbm, full(loss.shape), full(mod.shape), full(w_b.shape),
            full(w_u.shape), full(w_d.shape),
        ],
        out_specs=[own(columns) for columns in widths]
        + [pl.BlockSpec((None, 16, width), lambda t: (t // tiles, 0, 0))]
        + [hbm] * 6,
        out_shape=[jax.ShapeDtypeStruct((rows, columns), bf16) for columns in widths]
        + [
            jax.ShapeDtypeStruct((2, 16, width), f32),
            traded, traded, traded, traded,
            jax.ShapeDtypeStruct(
                (frames, frame_count, part - tiles // 4 * group, width), bf16
            ),
            jax.ShapeDtypeStruct((2,) + after_first.shape, bf16),
        ],
        scratch_shapes=[
            VMEM((tokens, 3 * width), bf16),
            VMEM((16, tokens), f32),
            VMEM((tokens, tokens), f32),
            VMEM((tokens, width), bf16),
            VMEM((2,) + slab, bf16),
            VMEM((2,) + slab, bf16),
            VMEM((2 * tiles,) + slab, bf16),
            VMEM((2 * tiles,) + slab, bf16),
            DMA((frames - 1,)), DMA((frames - 1,)),
            DMA((frames - 1,)), DMA((frames - 1,)),
            DMA((tiles, frames - 1)), DMA((tiles, frames - 1)),
            DMA((max(tiles // 4, 1), frames - 1)), DMA((max(tiles // 4, 1), frames - 1)),
            DMA((2, 2)), DMA((2,)), DMA((2, 2 * tiles)),
        ],
        compiler_params=pltpu.CompilerParams(
            collective_id=2, has_side_effects=True, vmem_limit_bytes=VMEM_LIMIT
        ),
    )(after_first, cot_first, after_later, cotangent, loss, mod, w_b, w_u, w_d)


def space_back_kernel(
    clip, grad_refs, x_ref, mod, w_c, qkv, branch, totals,
    out_ref, gb_ref, gqkv_ref, sums, gmix,
):
    width = x_ref.shape[-1]
    tokens = x_ref.shape[-2]
    row = clip * 9
    piece = lambda number: mod[row + number : row + number + 1, :]

    @pl.when(pl.program_id(0) == 0)
    def _():
        sums[...] = jnp.zeros_like(sums)

    joined = [grad_ref[...] for grad_ref in grad_refs]
    joined = joined[0] if len(joined) == 1 else jnp.concatenate(joined, axis=2)
    grad = joined.reshape(tokens, width).astype(f32)
    grad_branch = (grad * piece(2)).astype(bf16)
    gb_ref[...] = grad_branch
    sums[2:3, :] += column_sum(grad * branch[...].astype(f32))
    sums[3:4, :] += column_sum(grad_branch.astype(f32))
    gmix[...] = dot(grad_branch, w_c[:, 3 * width :], 1, 1).astype(bf16)
    attend_back(qkv, gmix, totals, gqkv_ref, width, None)
    grad_hidden = dot(gqkv_ref[...], w_c[:, : 3 * width], 1, 1)
    norm, scale = normed(x_ref[...].reshape(tokens, width).astype(f32))
    sums[0:1, :] += column_sum(grad_hidden)
    sums[1:2, :] += column_sum(grad_hidden * norm)
    result = grad + norm_back(grad_hidden, 1.0 + piece(1), norm, scale)
    out_ref[...] = result.reshape(out_ref.shape)


def space_back_entry(count, parts, clip, *refs):
    base = 6 + parts
    space_back_kernel(clip, refs[:parts], *refs[parts:base], *refs[base + count :])


def space_back_call(clip, grad, x, mod, w_c, qkv, branch, totals, earlier):
    clip_count, frame_count, tokens, width = x.shape
    frames = grad[0].shape[0]
    part = tokens // frames
    rest = [entry.shape[2] for entry in grad[1:]]
    heights = [part - sum(rest)] + rest
    if heights[0] == 0:
        grad, heights = grad[1:], heights[1:]
    rows = frame_count * tokens
    by_frame = lambda columns: pl.BlockSpec(
        (None, tokens, columns), lambda f: (clip * frame_count + f, 0, 0)
    )
    own = lambda columns: pl.BlockSpec((tokens, columns), lambda f: (clip * frame_count + f, 0))
    in_specs = [
        pl.BlockSpec((frames, 1, height, width), lambda f: (0, f, 0, 0)) for height in heights
    ] + [
        pl.BlockSpec((1, 1, tokens, width), lambda f: (clip, f, 0, 0)),
        full(mod.shape),
        full(w_c.shape),
        by_frame(3 * width),
        by_frame(width),
        pl.BlockSpec((None, 16, tokens), lambda f: (clip * frame_count + f, 0, 0)),
    ]
    args = list(grad) + [x, mod, w_c, qkv, branch, totals]
    begin = len(args)
    body = functools.partial(space_back_entry, len(earlier or ()), len(grad), clip)
    aliases = {}
    if earlier is not None:
        in_specs += [pl.BlockSpec(memory_space=pl.ANY)] * len(earlier)
        args += list(earlier)
        aliases = {begin + number: number for number in range(len(earlier))}
    return pl.pallas_call(
        body,
        grid=(frame_count,),
        in_specs=in_specs,
        out_specs=[
            pl.BlockSpec((1, 1, tokens, width), lambda f: (clip, f, 0, 0)),
            own(width),
            own(3 * width),
            pl.BlockSpec((8, width), lambda f: (0, 0)),
        ],
        out_shape=[
            jax.ShapeDtypeStruct(x.shape, f32),
            jax.ShapeDtypeStruct((clip_count * rows, width), bf16),
            jax.ShapeDtypeStruct((clip_count * rows, 3 * width), bf16),
            jax.ShapeDtypeStruct((8, width), f32),
        ],
        scratch_shapes=[VMEM((tokens, width), bf16)],
        input_output_aliases=aliases,
        compiler_params=pltpu.CompilerParams(vmem_limit_bytes=VMEM_LIMIT),
        cost_estimate=pl.CostEstimate(
            flops=rows * 20_000_000, bytes_accessed=rows * width * 20, transcendentals=0
        ),
    )(*args)


def shards(
    inputs, cotangent, time_steps, weight_index, ada_weight, ada_bias, space_qkv, space_out,
    space_out_bias, time_qkv, time_out, time_out_bias, up_weight, up_bias, down_weight, down_bias,
):
    clip_count, frame_count, patch_count, width = inputs.shape
    clips, frames = lax.axis_size("clip"), lax.axis_size("frame")
    owners = clips * frames
    owner = lax.axis_index("clip") * frames + lax.axis_index("frame")
    part = patch_count // frames
    rows = ada_weight.shape[0]

    embed = jax.nn.silu(embed_steps(time_steps, width)).astype(bf16)
    embed = jnp.pad(embed, ((0, 16 - clip_count), (0, 0)))
    place = lax.broadcasted_iota(jnp.int32, (width, 128), 0) - owner * rows
    lane = lax.broadcasted_iota(jnp.int32, (width, 128), 1)
    select = ((place == lane) & (lane < rows)).astype(bf16)

    def spread_bias(vector):
        length = vector.shape[0]
        empty = jnp.zeros((owners * length,), f32)
        return lax.dynamic_update_slice(empty, vector.astype(f32), (owner * length,)).reshape(
            -1, width
        )

    bias = jnp.concatenate(
        [
            spread_bias(vector)
            for vector in (ada_bias, space_out_bias, time_out_bias, up_bias, down_bias)
        ],
        axis=0,
    )
    (
        w_c, w_b, w_u, w_d, mod, chosen, totals, hidden_one, qkv_one, mixed_one, branch_one,
        after_first, after_later, cot_first,
    ) = start_call(
        clips, frames, inputs, cotangent, space_qkv, space_out, time_qkv, time_out, up_weight,
        down_weight, embed, select, ada_weight, bias,
    )

    def exchange(values):
        return lax.all_to_all(values, "frame", split_axis=0, concat_axis=0, tiled=True)

    loss = jnp.exp2(weight_index.astype(f32) * 0.5 - 1.0)
    loss = jnp.broadcast_to(loss[:, None], (clip_count, width))
    (
        act, gup, h3, gb3, mixed_two, gb2, h2, gqkv_two, mid_sums, _, _, grad_first,
        grad_second, grad_later, out_all,
    ) = middle_call(
        clips, frames, after_first, cot_first, after_later, cotangent, loss, mod, w_b, w_u, w_d
    )
    grads = [(grad_first,), (grad_second, exchange(grad_later))]

    earlier = None
    space_sums = []
    for clip in range(clip_count):
        *earlier, sums = space_back_call(
            clip, grads[clip], inputs, mod, w_c, qkv_one, branch_one, totals, earlier
        )
        space_sums.append(sums)
    input_grad, gb1, gqkv_one = earlier
    pieces = []
    for clip in range(clip_count):
        pieces += [space_sums[clip][0:3], mid_sums[clip][0:6]]
    pieces.append(sum(entry[3:4] for entry in space_sums))
    pieces.append(sum(entry[6:12] for entry in mid_sums))
    small = jnp.concatenate(pieces, axis=0)
    small = jnp.pad(small, ((0, ROWS - small.shape[0]), (0, 0)))
    picked = chosen.reshape(clips, 16, 128)[:, :clip_count].reshape(clips * clip_count, 128)
    outputs, grad_ada, sums, own_u, own_d, own_b, own_bo, own_c, own_co = grad_call(
        clips, frames, clip_count, small, picked.astype(f32).T, out_all, h3, gup, act, gb3, h2, gqkv_two,
        mixed_two, gb2, hidden_one.reshape(-1, width), gqkv_one, mixed_one.reshape(-1, width), gb1,
    )
    biases = sums[9:]

    def own_slice(vector):
        length = vector.shape[0] // owners
        return lax.dynamic_slice_in_dim(vector, owner * length, length, 0)

    return (
        outputs,
        input_grad,
        grad_ada,
        own_slice(sums[:9].reshape(-1)),
        own_c,
        own_co,
        own_slice(biases[0]),
        own_b,
        own_bo,
        own_slice(biases[1]),
        own_u,
        own_slice(biases[2:6].reshape(-1)),
        own_d,
        own_slice(biases[6]),
    )


def solution(mesh):
    tokens = P("clip", "frame", None, None)
    matrix = P(("clip", "frame"), None)
    vector = P(("clip", "frame"))
    in_specs = (
        tokens, tokens, P("clip"), P("clip"), matrix, vector, matrix, matrix, vector, matrix,
        matrix, vector, matrix, vector, matrix, vector,
    )
    out_specs = (
        tokens, tokens, matrix, vector, matrix, matrix, vector, matrix, matrix, vector, matrix,
        vector, matrix, vector,
    )
    return jax.shard_map(shards, mesh=mesh, in_specs=in_specs, out_specs=out_specs, check_vma=False)
```
